32 devices in a mesh: groups: 2 (over y), batch: 8 (over z, x), tensor: 2 (over core).
Axes of the slice: x: 2, y: 2, z: 4, core: 2. Of those that a mesh axis runs over, the one named last changes fastest.
Arguments:
- hidden: bfloat16 [4096, 8192], P(('groups', 'batch'), 'tensor'), parts along dimension 0, may hold values from -6 to 6
- demand: int32 [16, 4], P(('groups', 'batch')), parts along dimension 0, may hold values from 0 to 7, as said below
- lengths: int32 [16, 4], P(('groups', 'batch')), parts along dimension 0, may hold values from 62 to 66, as said below
- holder_slot: int32 [8], replicated, may hold values from 0 to 7, each once
- value_weight: bfloat16 [8192, 1024], P('tensor'), may hold values from -0.0625 to 0.0625
- factor_in: bfloat16 [8, 8192, 64], P('batch', 'tensor'), may hold values from -0.0625 to 0.0625
- factor_out: bfloat16 [8, 64, 1024], P('batch', None, 'tensor'), may hold values from -0.75 to 0.75
Outputs:
- values: bfloat16 [4096, 1024], P(('groups', 'batch'), 'tensor'), parts along dimension 0
The draws below stay inside these ranges and needn't reach their ends.
There are 2 independent parts, one for each index of `groups`. The reference program is written for one: setup_inputs(seed, part) draws one part's arguments, and reference() takes and returns one part's arrays. A program takes and returns all parts, laid end to end along the dimension named above; an argument that names none is the same for every part. Nothing has to cross between parts.
Inputs may be any that keep to these rules, and one draw needn't show every extreme that they name: `demand`: each row lists 4 different adapters in rising order; one adapter is listed in every row. `lengths`: each row sums to 256; the adapter listed in every row of demand has exactly 66 rows in each block. `holder_slot`: A permutation.
All inputs are finite; a program needn't handle non-finite values.
Results may differ from the reference program's by a relative error of at most 0.005.
Values may be sent and summed in bfloat16 or wider, within the bound.
No kernel may reach another device: no remote copies, remote signals or barrier semaphores. Data moves between devices by JAX's collectives and lax.ppermute only.
A program may use at most 128 MiB of HBM per device.

```python
import jax
import jax.numpy as jnp
from jax import lax

D = 8192
KVW = 1024
R = 64
TOK_DEV = 256
DEMAND = 4
CAP = 66
ADAPTERS = 8
TOKENS = 2048
N_BATCH = 8


def draw_plan(key):
    popular = jax.random.randint(jax.random.fold_in(key, 11), (), 0, ADAPTERS)
    adapter_index = jnp.arange(ADAPTERS, dtype=jnp.int32)
    ranking = jax.random.randint(jax.random.fold_in(key, 12), (N_BATCH, ADAPTERS), 0, 1024) * ADAPTERS + adapter_index[None, :]
    ranking = jnp.where(adapter_index[None, :] == popular, 2048 * ADAPTERS, ranking)
    chosen = lax.top_k(ranking, DEMAND)[1]
    wanted = jnp.sort(chosen, axis=1).astype(jnp.int32)
    position = jnp.sum((wanted < popular).astype(jnp.int32), axis=1)
    mean_len = TOK_DEV // DEMAND
    swing = jax.random.randint(jax.random.fold_in(key, 13), (N_BATCH, (DEMAND - 2) // 2), -2, 3)
    paired = jnp.stack([mean_len + swing, mean_len - swing], axis=2).reshape(N_BATCH, DEMAND - 2)
    others = jnp.concatenate([paired.astype(jnp.int32), jnp.full((N_BATCH, 1), mean_len - 2, jnp.int32)], axis=1)
    column = jnp.arange(DEMAND, dtype=jnp.int32)[None, :]
    pick = jnp.clip(jnp.where(column < position[:, None], column, column - 1), 0, DEMAND - 2)
    spread = jnp.take_along_axis(others, pick, axis=1)
    seg_lengths = jnp.where(column == position[:, None], mean_len + 2, spread).astype(jnp.int32)
    return (wanted, seg_lengths)


def draw_demand(key, part):
    wanted, seg_lengths = draw_plan(key)
    return wanted


def draw_lengths(key, part):
    wanted, seg_lengths = draw_plan(key)
    return seg_lengths


def block_levels(own_key, dims, shards, smallest, largest):
    level, own = 1.0, jax.random.fold_in(own_key, 6)
    for dim, blocks in shards:
        heights = jnp.exp(jax.random.uniform(jax.random.fold_in(own, dim), (blocks,), jnp.float32, smallest / len(shards), largest / len(shards)))
        level = level * jnp.repeat(heights, dims[dim] // blocks).reshape([-1 if axis == dim else 1 for axis in range(len(dims))])
    return level


def normal_values(own_key, shape, scale, most, cuts=(), kind=jnp.bfloat16):
    entries = scale * jax.random.normal(own_key, shape, jnp.float32)
    if cuts:
        entries = entries * block_levels(own_key, shape, cuts, -0.22, 0.18)
    return jnp.clip(entries, -most, most).astype(kind)


def setup_inputs(seed: int = 0, part: int = 0) -> dict:
    arg_keys = jax.random.split(jax.random.key(seed), 8)
    part_splits = jax.random.split(jax.random.fold_in(arg_keys[7], part), 8)
    hidden = normal_values(part_splits[0], (TOKENS, D), 1.0, 6.0, ((0, 8), (1, 2)))
    demand = draw_demand(jax.random.fold_in(jax.random.fold_in(arg_keys[7], part), 71), part)
    lengths = draw_lengths(jax.random.fold_in(jax.random.fold_in(arg_keys[7], part), 71), part)
    holder_slot = jax.random.permutation(arg_keys[3], ADAPTERS).astype(jnp.int32)
    value_weight = normal_values(arg_keys[4], (D, KVW), D ** -0.5, 0.0625, ((0, 2),))
    factor_in = normal_values(arg_keys[5], (ADAPTERS, D, R), D ** -0.5, 0.0625, ((0, 8), (1, 2)))
    factor_out = normal_values(arg_keys[6], (ADAPTERS, R, KVW), R ** -0.5, 0.75, ((0, 8), (2, 2)))
    return {"hidden": hidden, "demand": demand, "lengths": lengths, "holder_slot": holder_slot, "value_weight": value_weight, "factor_in": factor_in, "factor_out": factor_out}


def reference(hidden, demand, lengths, holder_slot, value_weight, factor_in, factor_out):
    base_part = jnp.dot(hidden, value_weight, preferred_element_type=jnp.float32)
    seg_ends = jnp.cumsum(lengths, axis=1).astype(jnp.int32)
    seg_starts = (seg_ends - lengths).astype(jnp.int32)
    row_index = jnp.arange(TOK_DEV, dtype=jnp.int32)
    slot_index = jnp.arange(CAP, dtype=jnp.int32)

    def per_device(device_item):
        tokens_dev, wanted, begin, finish = device_item
        row_segment = jnp.sum((row_index[:, None] >= finish[None, :]).astype(jnp.int32), axis=1).astype(jnp.int32)
        gather_rows = jnp.clip(begin[:, None] + slot_index[None, :], 0, TOK_DEV - 1).astype(jnp.int32)
        padded = tokens_dev[gather_rows]
        held_slot = holder_slot[wanted]
        a_stack = factor_in[held_slot].astype(jnp.float32)
        b_stack = factor_out[held_slot].astype(jnp.float32)
        rank_pad = jnp.einsum('scd,sdr->scr', padded.astype(jnp.float32), a_stack, precision=lax.Precision.HIGHEST)
        rank_pad = lax.optimization_barrier(rank_pad.astype(jnp.bfloat16))
        adapted = jnp.einsum('scr,srk->sck', rank_pad.astype(jnp.float32), b_stack, precision=lax.Precision.HIGHEST)
        adapted = adapted.astype(jnp.bfloat16)
        within = (row_index - begin[row_segment]).astype(jnp.int32)
        return adapted[row_segment, within]

    low_rank = lax.map(per_device, (hidden.reshape(N_BATCH, TOK_DEV, D), demand, seg_starts, seg_ends))
    total = base_part + low_rank.reshape(TOKENS, KVW).astype(jnp.float32)
    return total.astype(jnp.bfloat16)
```

```python
import functools

import jax
import jax.numpy as jnp
from jax import lax
from jax.experimental import pallas as pl
from jax.experimental.pallas import tpu as pltpu
from jax.sharding import PartitionSpec as P

F32, BF16 = jnp.float32, jnp.bfloat16
VMEM_LIMIT = 40 * 1024 * 1024


def ring_order(size):
    if size % 4:
        return list(range(size))
    columns = size // 4
    order = [0]
    for row in range(4):
        across = range(1, columns) if row % 2 == 0 else range(columns - 1, 0, -1)
        order += [row * columns + column for column in across]
    return order + [row * columns for row in (3, 2, 1)]


def contract(left, right):
    return lax.dot_general(left, right, (((1,), (1,)), ((), ())), preferred_element_type=F32)


def base_kernel(side_ref, rows_ref, weight_ref, out_ref):
    part = jnp.dot(rows_ref[...], weight_ref[...], preferred_element_type=F32)

    @pl.when(pl.program_id(0) == 0)
    def first():
        out_ref[...] = part

    @pl.when(pl.program_id(0) > 0)
    def later():
        out_ref[...] += part


def base_half(side, hidden, weight):
    rows, depth = hidden.shape
    width = weight.shape[1] // 2
    step = min(depth, 1024)
    return pl.pallas_call(
        base_kernel,
        out_shape=jax.ShapeDtypeStruct((rows, width), F32),
        grid_spec=pltpu.PrefetchScalarGridSpec(
            num_scalar_prefetch=1,
            grid=(depth // step,),
            in_specs=[
                pl.BlockSpec((rows, step), lambda k, side: (0, k)),
                pl.BlockSpec((step, width), lambda k, side: (k, side[0])),
            ],
            out_specs=pl.BlockSpec((rows, width), lambda k, side: (0, 0)),
        ),
        compiler_params=pltpu.CompilerParams(vmem_limit_bytes=VMEM_LIMIT),
        cost_estimate=pl.CostEstimate(
            flops=2 * rows * depth * width,
            bytes_accessed=2 * depth * (rows + width) + 4 * rows * width,
            transcendentals=0,
        ),
    )(side, hidden, weight)


def row_mask(bounds_ref, side, chunk, shape):
    row = lax.broadcasted_iota(jnp.int32, shape, 0)
    return (row >= bounds_ref[side, 0, chunk]) & (row < bounds_ref[side, 1, chunk])


def pack(part):
    half = part.shape[0] // 2
    return jnp.concatenate([part[:half], part[half:]], axis=1)


def unpack(packed):
    half = packed.shape[1] // 2
    return jnp.concatenate([packed[:, :half], packed[:, half:]], axis=0)


def rank_kernel(chunks, depth, has_start, pieces, bounds_ref, group_ref, *refs):
    refs = list(refs)
    own_ref, other_ref = refs[0], refs[1]
    factors = refs[2 : 2 + pieces]
    rest = refs[2 + pieces :]
    start_ref = rest.pop(0) if has_start else None
    out_ref = rest[0]
    offset = pl.multiple_of(group_ref[0] * depth, 128)
    own = own_ref[:, pl.ds(offset, depth)]
    other = other_ref[...]
    rank = out_ref.shape[-1] if not has_start else start_ref.shape[-1]
    for side, rows in ((0, own), (1, other)):
        total = start_ref[side] if has_start else jnp.zeros((rows.shape[0], rank), F32)
        for chunk, spans in chunks:
            part = None
            for piece, begin, size in spans:
                product = contract(rows[:, begin : begin + size], factors[piece][:, :size])
                part = product if part is None else part + product
            total = total + jnp.where(row_mask(bounds_ref, side, chunk, part.shape), part, 0.0)
        out_ref[side] = pack(total) if has_start else total


def rank_call(chunks, depth, bounds, group, own, other, factors, start, rank):
    rows = own.shape[0]
    vmem, smem = pl.BlockSpec(memory_space=pltpu.VMEM), pl.BlockSpec(memory_space=pltpu.SMEM)
    operands = [bounds, group, own, other, *factors]
    if start is None:
        shape = (2, rows, rank)
    else:
        operands.append(start)
        shape = (2, rows // 2, 2 * rank)
    return pl.pallas_call(
        functools.partial(rank_kernel, chunks, depth, start is not None, len(factors)),
        out_shape=jax.ShapeDtypeStruct(shape, F32),
        in_specs=[smem, smem] + [vmem] * (len(operands) - 2),
        out_specs=vmem,
        compiler_params=pltpu.CompilerParams(vmem_limit_bytes=VMEM_LIMIT),
        cost_estimate=pl.CostEstimate(
            flops=4 * rows * depth * rank * len(chunks),
            bytes_accessed=2 * depth * (2 * rows + rank * len(chunks)),
            transcendentals=0,
        ),
    )(*operands)


def final_kernel(count, bounds_ref, mine_ref, one_ref, two_ref, three_ref, base_ref, far_ref, *refs):
    outs, out_ref = refs[:count], refs[count]
    rank = unpack((mine_ref[0] + one_ref[...]) + (two_ref[...] + three_ref[...])).astype(BF16)
    total = jnp.zeros(out_ref.shape, F32)
    for chunk in range(count):
        chosen = jnp.where(row_mask(bounds_ref, 0, chunk, rank.shape), rank, jnp.zeros_like(rank))
        total = total + jnp.dot(chosen, outs[chunk][...], preferred_element_type=F32)
    adapted = total.astype(BF16).astype(F32)
    out_ref[...] = ((base_ref[...] + far_ref[...]) + adapted).astype(BF16)


def per_device(hidden, demand, lengths, holder_slot, value_weight, factor_in, factor_out):
    rows, features = hidden.shape
    owners = lax.axis_size("batch")
    rank, width = factor_out.shape[1:]
    depth = features // 2
    group, core = lax.axis_index("groups"), lax.axis_index("tensor")
    order = ring_order(owners)
    forward = [(order[i], order[(i + 1) % owners]) for i in range(owners)]
    backward = [(b, a) for a, b in forward]
    swap = [(0, 1), (1, 0)]

    to_other = lax.dynamic_slice(hidden, (0, (1 - group) * depth), (rows, depth))
    factor = lax.dynamic_slice(factor_in[0].T, (0, group * depth), (rank, depth))
    own = jnp.concatenate([factor, factor_out[0]], axis=1)
    other = lax.ppermute(to_other, "groups", swap)

    full = (owners - 1) // 2
    ahead = behind = own
    chunks = [(0, [(own, 0, depth)], own[:, depth:])]
    for step in range(1, full + 1):
        ahead = lax.ppermute(ahead, "batch", forward)
        behind = lax.ppermute(behind, "batch", backward)
        chunks.append((step, [(ahead, 0, depth)], ahead[:, depth:]))
        chunks.append((-step, [(behind, 0, depth)], behind[:, depth:]))
    if owners % 2 == 0:
        cut = (depth + width) // 2
        first = lax.ppermute(ahead[:, :cut], "batch", forward)
        second = lax.ppermute(behind[:, cut:], "batch", backward)
        chunks.append(
            (owners // 2, [(first, 0, cut), (second, cut, depth - cut)], second[:, depth - cut :])
        )

    position = jnp.asarray([order.index(i) for i in range(owners)], jnp.int32)
    place = position[lax.axis_index("batch")]
    distance = jnp.asarray([c[0] for c in chunks], jnp.int32)
    slots = jnp.asarray(order, jnp.int32)[(place - distance + owners) % owners]
    wanted = demand[0]
    adapter = jnp.arange(holder_slot.shape[0], dtype=jnp.int32)
    holder = jnp.sum(jnp.where(wanted[:, None] == adapter[None, :], holder_slot[None, :], 0), axis=1)
    hits = slots[:, None] == holder[None, :]
    item = jnp.arange(wanted.shape[0])
    before = item[:, None] > item[None, :]
    starts = jnp.sum(jnp.where(before, lengths[0][None, :], 0), axis=1)
    low = jnp.sum(jnp.where(hits, starts[None, :], 0), axis=1)
    high = low + jnp.sum(jnp.where(hits, lengths[0][None, :], 0), axis=1)
    bounds = jnp.stack([low, high]).astype(jnp.int32)
    bounds = jnp.stack([bounds, lax.ppermute(bounds, "groups", swap)])

    far = base_half((1 - core).reshape(1), hidden, value_weight)
    far = lax.ppermute(far, "tensor", swap)
    near = base_half(core.reshape(1), hidden, value_weight)

    def listing(items, first):
        arrays, spans = [], []
        for i, (_, pieces, _) in enumerate(items):
            span = []
            for array, begin, size in pieces:
                span.append((len(arrays), begin, size))
                arrays.append(array)
            spans.append((first + i, span))
        return spans, arrays

    early = len(chunks) - 1
    group_index = group.reshape(1)
    spans, arrays = listing(chunks[:early], 0)
    started = rank_call(spans, depth, bounds, group_index, hidden, other, arrays, None, rank)
    spans, arrays = listing(chunks[early:], early)
    mine = rank_call(spans, depth, bounds, group_index, hidden, other, arrays, started, rank)

    one = lax.ppermute(mine[0], "tensor", swap)
    two = lax.ppermute(mine[1], "groups", swap)
    three = lax.ppermute(mine[1], ("groups", "tensor"), [(0, 3), (1, 2), (2, 1), (3, 0)])

    vmem, smem = pl.BlockSpec(memory_space=pltpu.VMEM), pl.BlockSpec(memory_space=pltpu.SMEM)
    outs = [c[2] for c in chunks]
    return pl.pallas_call(
        functools.partial(final_kernel, len(outs)),
        out_shape=jax.ShapeDtypeStruct((rows, width), BF16),
        in_specs=[smem] + [vmem] * (6 + len(outs)),
        out_specs=vmem,
        compiler_params=pltpu.CompilerParams(vmem_limit_bytes=VMEM_LIMIT),
    )(bounds, mine, one, two, three, near, far, *outs)


def solution(mesh):
    return jax.shard_map(
        per_device,
        mesh=mesh,
        in_specs=(
            P(("groups", "batch"), "tensor"),
            P(("groups", "batch"), None),
            P(("groups", "batch"), None),
            P(),
            P("tensor", None),
            P("batch", "tensor", None),
            P("batch", None, "tensor"),
        ),
        out_specs=P(("groups", "batch"), "tensor"),
        check_vma=False,
    )
```

```python
import functools

import jax
import jax.numpy as jnp
from jax import lax
from jax.experimental import pallas as pl
from jax.experimental.pallas import tpu as pltpu
from jax.sharding import PartitionSpec as P

F32, BF16, I32 = jnp.float32, jnp.bfloat16, jnp.int32
VMEM_LIMIT = 40 * 1024 * 1024
GROUP = 4
VMEM = pl.BlockSpec(memory_space=pltpu.VMEM)
HBM = pl.BlockSpec(memory_space=pltpu.HBM)


def in_hbm(array):
    return pltpu.with_memory_space_constraint(array, pltpu.HBM)


def params():
    return pltpu.CompilerParams(vmem_limit_bytes=VMEM_LIMIT)


def ring_order(size):
    if size % 4:
        return list(range(size))
    columns = size // 4
    order = [0]
    for row in range(4):
        across = range(1, columns) if row % 2 == 0 else range(columns - 1, 0, -1)
        order += [row * columns + column for column in across]
    return order + [row * columns for row in (3, 2, 1)]


def contract(left, right):
    return lax.dot_general(left, right, (((1,), (1,)), ((), ())), preferred_element_type=F32)


def prologue_kernel(
    depth,
    rank,
    hidden_ref,
    factor_ref,
    factor_out_ref,
    demand_ref,
    lengths_ref,
    holder_ref,
    slots_ref,
    to_other_ref,
    first_ref,
    second_ref,
    bounds_ref,
    demand,
    lengths,
    holder,
    slots,
    sems,
):
    group, place = lax.axis_index("groups"), lax.axis_index("batch")
    cut = first_ref.shape[1]
    here = pl.multiple_of(group * depth, 128)
    there = pl.multiple_of((1 - group) * depth, 128)
    after = pl.multiple_of(group * depth + cut, 128)
    small = [
        pltpu.make_async_copy(demand_ref, demand, sems.at[0]),
        pltpu.make_async_copy(lengths_ref, lengths, sems.at[1]),
        pltpu.make_async_copy(holder_ref, holder, sems.at[2]),
        pltpu.make_async_copy(slots_ref.at[pl.ds(place, 1)], slots, sems.at[3]),
    ]
    large = [
        pltpu.make_async_copy(factor_ref.at[:, pl.ds(here, cut)], first_ref, sems.at[4]),
        pltpu.make_async_copy(
            factor_ref.at[:, pl.ds(after, depth - cut)], second_ref.at[:, : depth - cut], sems.at[5]
        ),
        pltpu.make_async_copy(factor_out_ref, second_ref.at[:, depth - cut :], sems.at[6]),
        pltpu.make_async_copy(hidden_ref.at[:, pl.ds(there, depth)], to_other_ref, sems.at[7]),
    ]
    for copy in small + large:
        copy.start()
    for copy in small:
        copy.wait()
    count = slots.shape[2]
    column = lax.broadcasted_iota(I32, (1, count * rank), 1)

    def chunk_bounds(chunk, carry):
        low, high = carry
        slot = slots[0, 0, chunk]

        def item_bounds(item, state):
            start, begin, end = state
            length = lengths[0, item]
            hit = holder[demand[0, item]] == slot
            begin = jnp.where(hit, start, begin)
            end = jnp.where(hit, start + length, end)
            return start + length, begin, end

        zero = jnp.int32(0)
        state = (zero, zero, zero)
        if demand.shape[1] <= 4:
            for item in range(demand.shape[1]):
                state = item_bounds(item, state)
        else:
            state = lax.fori_loop(0, demand.shape[1], item_bounds, state)
        inside = (column >= chunk * rank) & (column < (chunk + 1) * rank)
        return jnp.where(inside, state[1], low), jnp.where(inside, state[2], high)

    none = jnp.zeros((1, count * rank), I32)
    carry = (none, none)
    if count <= 8:
        for chunk in range(count):
            carry = chunk_bounds(chunk, carry)
    else:
        carry = lax.fori_loop(0, count, chunk_bounds, carry)
    bounds_ref[0:1, :] = carry[0]
    bounds_ref[1:2, :] = carry[1]
    bounds_ref[2:8, :] = jnp.zeros((6, count * rank), I32)
    for copy in large:
        copy.wait()


def prologue(hidden, factor, factor_out, demand, lengths, holder_slot, slots):
    rows, features = hidden.shape
    rank, width = factor_out.shape
    depth = features // 2
    cut = (depth + width) // 2
    count = slots.shape[2]
    return pl.pallas_call(
        functools.partial(prologue_kernel, depth, rank),
        out_shape=(
            jax.ShapeDtypeStruct((rows, depth), hidden.dtype),
            jax.ShapeDtypeStruct((rank, cut), factor.dtype),
            jax.ShapeDtypeStruct((rank, cut), factor.dtype),
            jax.ShapeDtypeStruct((8, count * rank), I32),
        ),
        in_specs=[HBM] * 7,
        out_specs=(VMEM,) * 4,
        scratch_shapes=[
            pltpu.SMEM(demand.shape, I32),
            pltpu.SMEM(lengths.shape, I32),
            pltpu.SMEM(holder_slot.shape, I32),
            pltpu.SMEM((1, 1, count), I32),
            pltpu.SemaphoreType.DMA((8,)),
        ],
        compiler_params=params(),
    )(*map(in_hbm, (hidden, factor, factor_out, demand, lengths, holder_slot, slots)))


def base_kernel(rows_ref, weight_ref, near_ref, far_ref, buffer, sems):
    width = near_ref.shape[1]
    core = lax.axis_index("tensor")
    here = pl.multiple_of(core * width, 128)
    there = pl.multiple_of((1 - core) * width, 128)
    step = buffer.shape[1]
    steps = weight_ref.shape[0] // step

    def fetch(k):
        return pltpu.make_async_copy(
            weight_ref.at[pl.ds(k * step, step)], buffer.at[k % 3], sems.at[k % 3]
        )

    fetch(0).start()
    if steps > 1:
        fetch(1).start()
    for k in range(steps):
        if k + 2 < steps:
            fetch(k + 2).start()
        fetch(k).wait()
        rows = rows_ref[:, k * step : (k + 1) * step]
        weight = buffer.at[k % 3]
        for out_ref, offset in ((far_ref, there), (near_ref, here)):
            part = jnp.dot(rows, weight[:, pl.ds(offset, width)], preferred_element_type=F32)
            if k == 0:
                out_ref[...] = part
            else:
                out_ref[...] += part


def base_call(hidden, weight):
    rows, depth = hidden.shape
    width = weight.shape[1] // 2
    step = 1024
    out = jax.ShapeDtypeStruct((rows, width), F32)
    return pl.pallas_call(
        base_kernel,
        out_shape=(out, out),
        in_specs=[VMEM, HBM],
        out_specs=(VMEM, VMEM),
        scratch_shapes=[
            pltpu.VMEM((3, step, 2 * width), weight.dtype),
            pltpu.SemaphoreType.DMA((3,)),
        ],
        compiler_params=params(),
        cost_estimate=pl.CostEstimate(
            flops=4 * rows * depth * width,
            bytes_accessed=2 * depth * (rows + 2 * width) + 8 * rows * width,
            transcendentals=0,
        ),
    )(hidden, in_hbm(weight))


def group_mask(bounds_ref, group, size, shape):
    row = lax.broadcasted_iota(I32, shape, 0)
    columns = pl.ds(group * size, shape[1])
    return (row >= bounds_ref[0:1, columns]) & (row < bounds_ref[1:2, columns])


def fold(masked):
    total = masked[:, :128]
    for begin in range(128, masked.shape[1], 128):
        total = total + masked[:, begin : begin + 128]
    return total


def rank_kernel(groups, depth, last, *refs):
    refs = list(refs)
    own_ref, other_ref, own_bounds, other_bounds = refs[:4]
    pieces = refs[4:]
    pieces, rest = pieces[: 2 * GROUP * len(groups)], pieces[2 * GROUP * len(groups) :]
    starts, outs = (rest[:2], rest[2:]) if last else ((None, None), rest)
    cut = pieces[0].shape[1]
    offset = pl.multiple_of(lax.axis_index("groups") * depth, 128)
    own = own_ref[:, pl.ds(offset, depth)]
    other = other_ref[...]
    rank = pieces[0].shape[0]
    size = GROUP * rank
    sides = ((own, own_bounds, starts[0], outs[0]), (other, other_bounds, starts[1], outs[1]))
    totals = [start_ref[...] if last else None for _, _, start_ref, _ in sides]
    for i, group in enumerate(groups):
        held = pieces[2 * GROUP * i : 2 * GROUP * (i + 1)]
        first = jnp.concatenate([ref[...] for ref in held[:GROUP]], axis=0)
        second = jnp.concatenate([ref[:, : depth - cut] for ref in held[GROUP:]], axis=0)
        for s, (rows, bounds, _, _) in enumerate(sides):
            part = contract(rows[:, :cut], first) + contract(rows[:, cut:], second)
            kept = fold(jnp.where(group_mask(bounds, group, size, part.shape), part, 0.0))
            totals[s] = kept if totals[s] is None else totals[s] + kept
    for total, (_, _, _, out_ref) in zip(totals, sides):
        if last:
            total = total + pltpu.roll(total, rank, 1)
            half = total.shape[0] // 2
            lane = lax.broadcasted_iota(I32, (half, 2 * rank), 1)
            total = jnp.where(lane < rank, total[:half], total[half:])
        out_ref[...] = total


def rank_call(groups, depth, own, other, own_bounds, other_bounds, pieces, starts):
    rows = own.shape[0]
    rank = pieces[0].shape[0]
    last = starts is not None
    shape = (rows // 2, 2 * rank) if last else (rows, 2 * rank)
    out = jax.ShapeDtypeStruct(shape, F32)
    operands = [own, other, own_bounds, other_bounds, *pieces, *(starts or ())]
    return pl.pallas_call(
        functools.partial(rank_kernel, groups, depth, last),
        out_shape=(out, out),
        in_specs=[VMEM] * len(operands),
        out_specs=(VMEM, VMEM),
        compiler_params=params(),
        cost_estimate=pl.CostEstimate(
            flops=4 * rows * depth * rank * GROUP * len(groups),
            bytes_accessed=2 * depth * (2 * rows + rank * GROUP * len(groups)),
            transcendentals=0,
        ),
    )(*operands)


def final_kernel(bounds_ref, mine, one, two, three, near_ref, far_ref, *refs):
    factors, out_ref = refs[:-1], refs[-1]
    rank, width = factors[0].shape[0], out_ref.shape[1]
    begin = factors[0].shape[1] - width
    packed = (mine[...] + one[...]) + (two[...] + three[...])
    turned = pltpu.roll(packed, rank, 1)
    lane = lax.broadcasted_iota(I32, packed.shape, 1)
    values = jnp.concatenate(
        [jnp.where(lane < rank, packed, turned), jnp.where(lane < rank, turned, packed)], axis=0
    )
    wide = jnp.concatenate([values] * (GROUP // 2), axis=1)
    total = None
    for group in range(len(factors) // GROUP):
        mask = group_mask(bounds_ref, group, GROUP * rank, wide.shape)
        chosen = jnp.where(mask, wide, 0.0).astype(BF16)
        factor = jnp.concatenate(
            [ref[:, begin:] for ref in factors[group * GROUP : (group + 1) * GROUP]], axis=0
        )
        part = jnp.dot(chosen, factor, preferred_element_type=F32)
        total = part if total is None else total + part
    adapted = total.astype(BF16).astype(F32)
    out_ref[...] = ((near_ref[...] + far_ref[...]) + adapted).astype(BF16)


def per_device(hidden, demand, lengths, holder_slot, value_weight, factor_in, factor_out):
    rows, features = hidden.shape
    owners = lax.axis_size("batch")
    rank, width = factor_out.shape[1:]
    depth = features // 2
    order = ring_order(owners)
    forward = [(order[i], order[(i + 1) % owners]) for i in range(owners)]
    backward = [(b, a) for a, b in forward]
    swap = [(0, 1), (1, 0)]

    full = (owners - 1) // 2
    distances = [0]
    for step in range(1, full + 1):
        distances += [step, -step]
    distances.append(owners // 2)
    table = [
        [[order[(order.index(me) - distance) % owners] for distance in distances]]
        for me in range(owners)
    ]
    to_other, first, second, bounds = prologue(
        hidden,
        factor_in[0].T,
        factor_out[0],
        demand,
        lengths,
        holder_slot,
        jnp.asarray(table, I32),
    )

    firsts, seconds = [first], [second]
    ahead, behind = (first, second), (first, second)
    for step in range(1, full + 1):
        a = lax.ppermute(ahead[0], "batch", forward)
        b = lax.ppermute(behind[1], "batch", backward)
        ahead = (a, lax.ppermute(ahead[1], "batch", forward))
        behind = (lax.ppermute(behind[0], "batch", backward), b)
        firsts += [ahead[0], behind[0]]
        seconds += [ahead[1], behind[1]]
    firsts.append(lax.ppermute(ahead[0], "batch", forward))
    seconds.append(lax.ppermute(behind[1], "batch", backward))
    other = lax.ppermute(to_other, "groups", swap)
    other_bounds = lax.ppermute(bounds, "groups", swap)

    near, far = base_call(hidden, value_weight)
    far = lax.ppermute(far, "tensor", swap)

    count = owners // GROUP
    early = range(count - 1)
    pieces = []
    for group in early:
        pieces += firsts[group * GROUP : (group + 1) * GROUP]
        pieces += seconds[group * GROUP : (group + 1) * GROUP]
    sides = (hidden, other, bounds, other_bounds)
    starts = rank_call(tuple(early), depth, *sides, pieces, None)
    pieces = firsts[-GROUP:] + seconds[-GROUP:]
    mine, theirs = rank_call((count - 1,), depth, *sides, pieces, starts)

    two = lax.ppermute(theirs, "groups", swap)
    three = lax.ppermute(theirs, ("groups", "tensor"), [(0, 3), (1, 2), (2, 1), (3, 0)])
    one = lax.ppermute(mine, "tensor", swap)

    operands = [bounds, mine, one, two, three, near, far, *seconds]
    return pl.pallas_call(
        final_kernel,
        out_shape=jax.ShapeDtypeStruct((rows, width), BF16),
        in_specs=[VMEM] * len(operands),
        out_specs=VMEM,
        compiler_params=params(),
    )(*operands)


def solution(mesh):
    return jax.shard_map(
        per_device,
        mesh=mesh,
        in_specs=(
            P(("groups", "batch"), "tensor"),
            P(("groups", "batch"), None),
            P(("groups", "batch"), None),
            P(),
            P("tensor", None),
            P("batch", "tensor", None),
            P("batch", None, "tensor"),
        ),
        out_specs=P(("groups", "batch"), "tensor"),
        check_vma=False,
    )
```

```python
import functools

import jax
import jax.numpy as jnp
from jax import lax
from jax.experimental import pallas as pl
from jax.experimental.pallas import tpu as pltpu
from jax.sharding import PartitionSpec as P

F32, BF16, I32 = jnp.float32, jnp.bfloat16, jnp.int32
VMEM_LIMIT = 40 * 1024 * 1024
GROUP = 4
VMEM = pl.BlockSpec(memory_space=pltpu.VMEM)
HBM = pl.BlockSpec(memory_space=pltpu.HBM)


def in_hbm(array):
    return pltpu.with_memory_space_constraint(array, pltpu.HBM)


def params():
    return pltpu.CompilerParams(vmem_limit_bytes=VMEM_LIMIT)


def ring_order(size):
    if size % 4:
        return list(range(size))
    columns = size // 4
    order = [0]
    for row in range(4):
        across = range(1, columns) if row % 2 == 0 else range(columns - 1, 0, -1)
        order += [row * columns + column for column in across]
    return order + [row * columns for row in (3, 2, 1)]


def contract(left, right):
    return lax.dot_general(left, right, (((1,), (1,)), ((), ())), preferred_element_type=F32)


def prologue_kernel(
    depth,
    rank,
    hidden_ref,
    factor_ref,
    factor_out_ref,
    demand_ref,
    lengths_ref,
    holder_ref,
    slots_ref,
    to_other_ref,
    first_ref,
    second_ref,
    bounds_ref,
    demand,
    lengths,
    holder,
    slots,
    sems,
):
    group, place = lax.axis_index("groups"), lax.axis_index("batch")
    cut = first_ref.shape[1]
    here = pl.multiple_of(group * depth, 128)
    there = pl.multiple_of((1 - group) * depth, 128)
    after = pl.multiple_of(group * depth + cut, 128)
    small = [
        pltpu.make_async_copy(demand_ref, demand, sems.at[0]),
        pltpu.make_async_copy(lengths_ref, lengths, sems.at[1]),
        pltpu.make_async_copy(holder_ref, holder, sems.at[2]),
        pltpu.make_async_copy(slots_ref.at[pl.ds(place, 1)], slots, sems.at[3]),
    ]
    large = [
        pltpu.make_async_copy(factor_ref.at[:, pl.ds(here, cut)], first_ref, sems.at[4]),
        pltpu.make_async_copy(
            factor_ref.at[:, pl.ds(after, depth - cut)], second_ref.at[:, : depth - cut], sems.at[5]
        ),
        pltpu.make_async_copy(factor_out_ref, second_ref.at[:, depth - cut :], sems.at[6]),
        pltpu.make_async_copy(hidden_ref.at[:, pl.ds(there, depth)], to_other_ref.at[:-16], sems.at[7]),
    ]
    for copy in small + large:
        copy.start()
    for copy in small:
        copy.wait()
    count = slots.shape[2]
    column = lax.broadcasted_iota(I32, (1, count * rank), 1)

    def chunk_bounds(chunk, carry):
        low, high = carry
        slot = slots[0, 0, chunk]

        def item_bounds(item, state):
            start, begin, end = state
            length = lengths[0, item]
            hit = holder[demand[0, item]] == slot
            begin = jnp.where(hit, start, begin)
            end = jnp.where(hit, start + length, end)
            return start + length, begin, end

        zero = jnp.int32(0)
        state = (zero, zero, zero)
        if demand.shape[1] <= 4:
            for item in range(demand.shape[1]):
                state = item_bounds(item, state)
        else:
            state = lax.fori_loop(0, demand.shape[1], item_bounds, state)
        inside = (column >= chunk * rank) & (column < (chunk + 1) * rank)
        return jnp.where(inside, state[1], low), jnp.where(inside, state[2], high)

    none = jnp.zeros((1, count * rank), I32)
    carry = (none, none)
    if count <= 8:
        for chunk in range(count):
            carry = chunk_bounds(chunk, carry)
    else:
        carry = lax.fori_loop(0, count, chunk_bounds, carry)
    bounds_ref[0:1, :] = carry[0]
    bounds_ref[1:2, :] = carry[1]
    bounds_ref[2:8, :] = jnp.zeros((6, count * rank), I32)
    span = min(depth, count * rank)
    line = lax.broadcasted_iota(I32, (16, span), 0)
    extra = jnp.zeros((16, span), I32)
    for i in range(count * rank // span):
        for first_line, ends in ((0, carry[0]), (8, carry[1])):
            extra = jnp.where(line == first_line + i, ends[:, i * span : (i + 1) * span], extra)
    to_other_ref[-16:, :span] = extra.astype(F32).astype(BF16)
    for copy in large:
        copy.wait()


def prologue(hidden, factor, factor_out, demand, lengths, holder_slot, slots):
    rows, features = hidden.shape
    rank, width = factor_out.shape
    depth = features // 2
    cut = (depth + width) // 2
    count = slots.shape[2]
    return pl.pallas_call(
        functools.partial(prologue_kernel, depth, rank),
        out_shape=(
            jax.ShapeDtypeStruct((rows + 16, depth), hidden.dtype),
            jax.ShapeDtypeStruct((rank, cut), factor.dtype),
            jax.ShapeDtypeStruct((rank, cut), factor.dtype),
            jax.ShapeDtypeStruct((8, count * rank), I32),
        ),
        in_specs=[HBM] * 7,
        out_specs=(VMEM,) * 4,
        scratch_shapes=[
            pltpu.SMEM(demand.shape, I32),
            pltpu.SMEM(lengths.shape, I32),
            pltpu.SMEM(holder_slot.shape, I32),
            pltpu.SMEM((1, 1, count), I32),
            pltpu.SemaphoreType.DMA((8,)),
        ],
        compiler_params=params(),
    )(*map(in_hbm, (hidden, factor, factor_out, demand, lengths, holder_slot, slots)))


def base_kernel(hidden_ref, weight_ref, near_ref, far_ref, rows_ref, buffer, sems):
    width = near_ref.shape[1]
    core = lax.axis_index("tensor")
    here = pl.multiple_of(core * width, 128)
    there = pl.multiple_of((1 - core) * width, 128)
    steps, step = buffer.shape[:2]
    copies = []
    for k in range(steps):
        span = pl.ds(k * step, step)
        copies.append(
            (
                pltpu.make_async_copy(hidden_ref.at[:, span], rows_ref.at[:, span], sems.at[0, k]),
                pltpu.make_async_copy(weight_ref.at[span], buffer.at[k], sems.at[1, k]),
            )
        )
    for pair in copies:
        for copy in pair:
            copy.start()
    for k, pair in enumerate(copies):
        for copy in pair:
            copy.wait()
        rows = rows_ref[:, k * step : (k + 1) * step]
        for out_ref, offset in ((far_ref, there), (near_ref, here)):
            part = jnp.dot(rows, buffer[k, :, pl.ds(offset, width)], preferred_element_type=F32)
            if k == 0:
                out_ref[...] = part
            else:
                out_ref[...] += part


def base_call(hidden, weight):
    rows, depth = hidden.shape
    width = weight.shape[1] // 2
    steps = 8
    out = jax.ShapeDtypeStruct((rows, width), F32)
    return pl.pallas_call(
        base_kernel,
        out_shape=(out, out, jax.ShapeDtypeStruct(hidden.shape, hidden.dtype)),
        in_specs=[HBM, HBM],
        out_specs=(VMEM,) * 3,
        scratch_shapes=[
            pltpu.VMEM((steps, depth // steps, 2 * width), weight.dtype),
            pltpu.SemaphoreType.DMA((2, steps)),
        ],
        compiler_params=params(),
        cost_estimate=pl.CostEstimate(
            flops=4 * rows * depth * width,
            bytes_accessed=2 * depth * (rows + 2 * width) + 8 * rows * width,
            transcendentals=0,
        ),
    )(in_hbm(hidden), in_hbm(weight))


def group_mask(low, high, shape):
    row = lax.broadcasted_iota(I32, shape, 0)
    return (row >= low) & (row < high)


def own_ends(bounds_ref, group, size):
    columns = slice(group * size, (group + 1) * size)
    return bounds_ref[0:1, columns], bounds_ref[1:2, columns]


def other_ends(other_ref, group, size):
    line, column = divmod(group * size, other_ref.shape[1])
    ends = other_ref[-16:, column : column + size].astype(F32).astype(I32)
    return ends[line : line + 1], ends[8 + line : 9 + line]


def fold(masked):
    total = masked[:, :128]
    for begin in range(128, masked.shape[1], 128):
        total = total + masked[:, begin : begin + 128]
    return total


def rank_kernel(groups, depth, last, *refs):
    refs = list(refs)
    own_ref, other_ref, bounds_ref = refs[:3]
    pieces = refs[3:]
    pieces, rest = pieces[: 2 * GROUP * len(groups)], pieces[2 * GROUP * len(groups) :]
    starts, outs = (rest[:2], rest[2:]) if last else ((None, None), rest)
    cut = pieces[0].shape[1]
    offset = pl.multiple_of(lax.axis_index("groups") * depth, 128)
    own = own_ref[:, pl.ds(offset, depth)]
    other = other_ref[:-16]
    rank = pieces[0].shape[0]
    size = GROUP * rank
    totals = [start_ref[...] if last else None for start_ref in starts]
    for i, group in enumerate(groups):
        held = pieces[2 * GROUP * i : 2 * GROUP * (i + 1)]
        first = jnp.concatenate([ref[...] for ref in held[:GROUP]], axis=0)
        second = jnp.concatenate([ref[:, : depth - cut] for ref in held[GROUP:]], axis=0)
        ends = (own_ends(bounds_ref, group, size), other_ends(other_ref, group, size))
        for s, rows in enumerate((own, other)):
            part = contract(rows[:, :cut], first) + contract(rows[:, cut:], second)
            kept = fold(jnp.where(group_mask(*ends[s], part.shape), part, 0.0))
            totals[s] = kept if totals[s] is None else totals[s] + kept
    for total, out_ref in zip(totals, outs):
        if last:
            total = total + pltpu.roll(total, rank, 1)
            half = total.shape[0] // 2
            lane = lax.broadcasted_iota(I32, (half, 2 * rank), 1)
            total = jnp.where(lane < rank, total[:half], total[half:])
        out_ref[...] = total


def rank_call(groups, depth, own, other, bounds, pieces, starts):
    rows = own.shape[0]
    rank = pieces[0].shape[0]
    last = starts is not None
    shape = (rows // 2, 2 * rank) if last else (rows, 2 * rank)
    out = jax.ShapeDtypeStruct(shape, F32)
    operands = [own, other, bounds, *pieces, *(starts or ())]
    return pl.pallas_call(
        functools.partial(rank_kernel, groups, depth, last),
        out_shape=(out, out),
        in_specs=[VMEM] * len(operands),
        out_specs=(VMEM, VMEM),
        compiler_params=params(),
        cost_estimate=pl.CostEstimate(
            flops=4 * rows * depth * rank * GROUP * len(groups),
            bytes_accessed=2 * depth * (2 * rows + rank * GROUP * len(groups)),
            transcendentals=0,
        ),
    )(*operands)


def final_kernel(bounds_ref, mine, one, two, three, near_ref, far_ref, *refs):
    factors, out_ref = refs[:-1], refs[-1]
    rank, width = factors[0].shape[0], out_ref.shape[1]
    begin = factors[0].shape[1] - width
    packed = (mine[...] + one[...]) + (two[...] + three[...])
    turned = pltpu.roll(packed, rank, 1)
    lane = lax.broadcasted_iota(I32, packed.shape, 1)
    values = jnp.concatenate(
        [jnp.where(lane < rank, packed, turned), jnp.where(lane < rank, turned, packed)], axis=0
    )
    wide = jnp.concatenate([values] * (GROUP // 2), axis=1)
    total = None
    for group in range(len(factors) // GROUP):
        mask = group_mask(*own_ends(bounds_ref, group, GROUP * rank), wide.shape)
        chosen = jnp.where(mask, wide, 0.0).astype(BF16)
        factor = jnp.concatenate(
            [ref[:, begin:] for ref in factors[group * GROUP : (group + 1) * GROUP]], axis=0
        )
        part = jnp.dot(chosen, factor, preferred_element_type=F32)
        total = part if total is None else total + part
    adapted = total.astype(BF16).astype(F32)
    out_ref[...] = ((near_ref[...] + far_ref[...]) + adapted).astype(BF16)


def per_device(hidden, demand, lengths, holder_slot, value_weight, factor_in, factor_out):
    rows, features = hidden.shape
    owners = lax.axis_size("batch")
    rank, width = factor_out.shape[1:]
    depth = features // 2
    order = ring_order(owners)
    forward = [(order[i], order[(i + 1) % owners]) for i in range(owners)]
    backward = [(b, a) for a, b in forward]
    swap = [(0, 1), (1, 0)]

    full = (owners - 1) // 2
    distances = [0]
    for step in range(1, full + 1):
        distances += [step, -step]
    distances.append(owners // 2)
    table = [
        [[order[(order.index(me) - distance) % owners] for distance in distances]]
        for me in range(owners)
    ]
    to_other, first, second, bounds = prologue(
        hidden,
        factor_in[0].T,
        factor_out[0],
        demand,
        lengths,
        holder_slot,
        jnp.asarray(table, I32),
    )

    firsts, seconds = [first], [second]
    ahead, behind = (first, second), (first, second)
    for step in range(1, full + 1):
        a = lax.ppermute(ahead[0], "batch", forward)
        b = lax.ppermute(behind[1], "batch", backward)
        ahead = (a, lax.ppermute(ahead[1], "batch", forward))
        behind = (lax.ppermute(behind[0], "batch", backward), b)
        firsts += [ahead[0], behind[0]]
        seconds += [ahead[1], behind[1]]
    firsts.append(lax.ppermute(ahead[0], "batch", forward))
    seconds.append(lax.ppermute(behind[1], "batch", backward))
    other = lax.ppermute(to_other, "groups", swap)

    near, far, held = base_call(hidden, value_weight)
    far = lax.ppermute(far, "tensor", swap)

    count = owners // GROUP
    early = range(count - 1)
    pieces = []
    for group in early:
        pieces += firsts[group * GROUP : (group + 1) * GROUP]
        pieces += seconds[group * GROUP : (group + 1) * GROUP]
    sides = (held, other, bounds)
    starts = rank_call(tuple(early), depth, *sides, pieces, None)
    pieces = firsts[-GROUP:] + seconds[-GROUP:]
    mine, theirs = rank_call((count - 1,), depth, *sides, pieces, starts)

    two = lax.ppermute(theirs, "groups", swap)
    one = lax.ppermute(mine, "tensor", swap)
    three = lax.ppermute(two, "tensor", swap)

    operands = [bounds, mine, one, two, three, near, far, *seconds]
    return pl.pallas_call(
        final_kernel,
        out_shape=jax.ShapeDtypeStruct((rows, width), BF16),
        in_specs=[VMEM] * len(operands),
        out_specs=VMEM,
        compiler_params=params(),
    )(*operands)


def solution(mesh):
    return jax.shard_map(
        per_device,
        mesh=mesh,
        in_specs=(
            P(("groups", "batch"), "tensor"),
            P(("groups", "batch"), None),
            P(("groups", "batch"), None),
            P(),
            P("tensor", None),
            P("batch", "tensor", None),
            P("batch", None, "tensor"),
        ),
        out_specs=P(("groups", "batch"), "tensor"),
        check_vma=False,
    )
```

```python
import functools

import jax
import jax.numpy as jnp
from jax import lax
from jax.experimental import pallas as pl
from jax.experimental.pallas import tpu as pltpu
from jax.sharding import PartitionSpec as P

F32, BF16, I32 = jnp.float32, jnp.bfloat16, jnp.int32
VMEM_LIMIT = 40 * 1024 * 1024
HALF = pl.CostEstimate(flops=0, bytes_accessed=1 << 22, transcendentals=0)
LONG = pl.CostEstimate(flops=1 << 33, bytes_accessed=1 << 24, transcendentals=0)
GROUP = 4
VMEM = pl.BlockSpec(memory_space=pltpu.VMEM)
HBM = pl.BlockSpec(memory_space=pltpu.HBM)


def in_hbm(array):
    return pltpu.with_memory_space_constraint(array, pltpu.HBM)


def params():
    return pltpu.CompilerParams(vmem_limit_bytes=VMEM_LIMIT)


def ring_order(size):
    if size % 4:
        return list(range(size))
    columns = size // 4
    order = [0]
    for row in range(4):
        across = range(1, columns) if row % 2 == 0 else range(columns - 1, 0, -1)
        order += [row * columns + column for column in across]
    return order + [row * columns for row in (3, 2, 1)]


def contract(left, right):
    return lax.dot_general(left, right, (((1,), (1,)), ((), ())), preferred_element_type=F32)


def prologue_kernel(
    depth,
    rank,
    hidden_ref,
    factor_ref,
    factor_out_ref,
    demand_ref,
    lengths_ref,
    holder_ref,
    slots_ref,
    to_other_ref,
    first_ref,
    second_ref,
    bounds_ref,
    demand,
    lengths,
    holder,
    slots,
    sems,
):
    group, place = lax.axis_index("groups"), lax.axis_index("batch")
    cut = first_ref.shape[1]
    here = pl.multiple_of(group * depth, 128)
    there = pl.multiple_of((1 - group) * depth, 128)
    after = pl.multiple_of(group * depth + cut, 128)
    small = [
        pltpu.make_async_copy(demand_ref, demand, sems.at[0]),
        pltpu.make_async_copy(lengths_ref, lengths, sems.at[1]),
        pltpu.make_async_copy(holder_ref, holder, sems.at[2]),
        pltpu.make_async_copy(slots_ref.at[pl.ds(place, 1)], slots, sems.at[3]),
    ]
    large = [
        pltpu.make_async_copy(factor_ref.at[:, pl.ds(here, cut)], first_ref, sems.at[4]),
        pltpu.make_async_copy(
            factor_ref.at[:, pl.ds(after, depth - cut)], second_ref.at[:, : depth - cut], sems.at[5]
        ),
        pltpu.make_async_copy(factor_out_ref, second_ref.at[:, depth - cut :], sems.at[6]),
        pltpu.make_async_copy(hidden_ref.at[:, pl.ds(there, depth)], to_other_ref.at[:-16], sems.at[7]),
    ]
    for copy in small + large:
        copy.start()
    for copy in small:
        copy.wait()
    count = slots.shape[2]
    column = lax.broadcasted_iota(I32, (1, count * rank), 1)

    def chunk_bounds(chunk, carry):
        low, high = carry
        slot = slots[0, 0, chunk]

        def item_bounds(item, state):
            start, begin, end = state
            length = lengths[0, item]
            hit = holder[demand[0, item]] == slot
            begin = jnp.where(hit, start, begin)
            end = jnp.where(hit, start + length, end)
            return start + length, begin, end

        zero = jnp.int32(0)
        state = (zero, zero, zero)
        if demand.shape[1] <= 4:
            for item in range(demand.shape[1]):
                state = item_bounds(item, state)
        else:
            state = lax.fori_loop(0, demand.shape[1], item_bounds, state)
        inside = (column >= chunk * rank) & (column < (chunk + 1) * rank)
        return jnp.where(inside, state[1], low), jnp.where(inside, state[2], high)

    none = jnp.zeros((1, count * rank), I32)
    carry = (none, none)
    if count <= 8:
        for chunk in range(count):
            carry = chunk_bounds(chunk, carry)
    else:
        carry = lax.fori_loop(0, count, chunk_bounds, carry)
    bounds_ref[0:1, :] = carry[0]
    bounds_ref[1:2, :] = carry[1]
    bounds_ref[2:8, :] = jnp.zeros((6, count * rank), I32)
    span = min(depth, count * rank)
    line = lax.broadcasted_iota(I32, (16, span), 0)
    extra = jnp.zeros((16, span), I32)
    for i in range(count * rank // span):
        for first_line, ends in ((0, carry[0]), (8, carry[1])):
            extra = jnp.where(line == first_line + i, ends[:, i * span : (i + 1) * span], extra)
    to_other_ref[-16:, :span] = extra.astype(F32).astype(BF16)
    for copy in large:
        copy.wait()


def prologue(hidden, factor, factor_out, demand, lengths, holder_slot, slots):
    rows, features = hidden.shape
    rank, width = factor_out.shape
    depth = features // 2
    cut = (depth + width) // 2
    count = slots.shape[2]
    return pl.pallas_call(
        functools.partial(prologue_kernel, depth, rank),
        out_shape=(
            jax.ShapeDtypeStruct((rows + 16, depth), hidden.dtype),
            jax.ShapeDtypeStruct((rank, cut), factor.dtype),
            jax.ShapeDtypeStruct((rank, cut), factor.dtype),
            jax.ShapeDtypeStruct((8, count * rank), I32),
        ),
        in_specs=[HBM] * 7,
        out_specs=(VMEM,) * 4,
        scratch_shapes=[
            pltpu.SMEM(demand.shape, I32),
            pltpu.SMEM(lengths.shape, I32),
            pltpu.SMEM(holder_slot.shape, I32),
            pltpu.SMEM((1, 1, count), I32),
            pltpu.SemaphoreType.DMA((8,)),
        ],
        compiler_params=params(),
    )(*map(in_hbm, (hidden, factor, factor_out, demand, lengths, holder_slot, slots)))


def base_kernel(side, fetch_rows, rows_in_ref, weight_ref, out_ref, *rest):
    rows_ref = rest[0] if fetch_rows else rows_in_ref
    buffer, sems = rest[-2:]
    width = out_ref.shape[1]
    core = lax.axis_index("tensor")
    offset = pl.multiple_of((core if side == 0 else 1 - core) * width, 128)
    steps, step = buffer.shape[:2]
    copies = []
    for k in range(steps):
        span = pl.ds(k * step, step)
        need = [
            pltpu.make_async_copy(
                weight_ref.at[span, pl.ds(offset, width)], buffer.at[k], sems.at[0, k]
            )
        ]
        if fetch_rows:
            need.append(
                pltpu.make_async_copy(
                    rows_in_ref.at[:, span], rows_ref.at[:, span], sems.at[1, k]
                )
            )
        copies.append(need)
    for need in copies:
        for copy in need:
            copy.start()
    for k, need in enumerate(copies):
        for copy in need:
            copy.wait()
        rows = rows_ref[:, k * step : (k + 1) * step]
        part = jnp.dot(rows, buffer[k], preferred_element_type=F32)
        if k == 0:
            out_ref[...] = part
        else:
            out_ref[...] += part


def base_call(side, fetch_rows, rows, weight):
    count, depth = rows.shape
    width = weight.shape[1] // 2
    steps = 4
    out = (jax.ShapeDtypeStruct((count, width), F32),)
    if fetch_rows:
        out += (jax.ShapeDtypeStruct(rows.shape, rows.dtype),)
    return pl.pallas_call(
        functools.partial(base_kernel, side, fetch_rows),
        out_shape=out,
        in_specs=[HBM if fetch_rows else VMEM, HBM],
        out_specs=(VMEM,) * len(out),
        scratch_shapes=[
            pltpu.VMEM((steps, depth // steps, width), weight.dtype),
            pltpu.SemaphoreType.DMA((2, steps)),
        ],
        compiler_params=params(),
        cost_estimate=HALF,
    )(in_hbm(rows) if fetch_rows else rows, in_hbm(weight))


def group_mask(low, high, shape):
    row = lax.broadcasted_iota(I32, shape, 0)
    return (row >= low) & (row < high)


def own_ends(bounds_ref, group, size):
    columns = slice(group * size, (group + 1) * size)
    return bounds_ref[0:1, columns], bounds_ref[1:2, columns]


def other_ends(other_ref, group, size):
    line, column = divmod(group * size, other_ref.shape[1])
    ends = other_ref[-16:, column : column + size].astype(F32).astype(I32)
    return ends[line : line + 1], ends[8 + line : 9 + line]


def fold(masked):
    total = masked[:, :128]
    for begin in range(128, masked.shape[1], 128):
        total = total + masked[:, begin : begin + 128]
    return total


def rank_kernel(groups, depth, last, *refs):
    refs = list(refs)
    own_ref, other_ref, bounds_ref = refs[:3]
    pieces = refs[3:]
    pieces, rest = pieces[: 2 * GROUP * len(groups)], pieces[2 * GROUP * len(groups) :]
    starts, outs = (rest[:2], rest[2:]) if last else ((None, None), rest)
    cut = pieces[0].shape[1]
    offset = pl.multiple_of(lax.axis_index("groups") * depth, 128)
    own = own_ref[:, pl.ds(offset, depth)]
    other = other_ref[:-16]
    rank = pieces[0].shape[0]
    size = GROUP * rank
    totals = [start_ref[...] if last else None for start_ref in starts]
    for i, group in enumerate(groups):
        held = pieces[2 * GROUP * i : 2 * GROUP * (i + 1)]
        first = jnp.concatenate([ref[...] for ref in held[:GROUP]], axis=0)
        second = jnp.concatenate([ref[:, : depth - cut] for ref in held[GROUP:]], axis=0)
        ends = (own_ends(bounds_ref, group, size), other_ends(other_ref, group, size))
        for s, rows in enumerate((own, other)):
            part = contract(rows[:, :cut], first) + contract(rows[:, cut:], second)
            kept = fold(jnp.where(group_mask(*ends[s], part.shape), part, 0.0))
            totals[s] = kept if totals[s] is None else totals[s] + kept
    for total, out_ref in zip(totals, outs):
        if last:
            total = total + pltpu.roll(total, rank, 1)
            half = total.shape[0] // 2
            lane = lax.broadcasted_iota(I32, (half, 2 * rank), 1)
            total = jnp.where(lane < rank, total[:half], total[half:])
        out_ref[...] = total


def rank_call(groups, depth, own, other, bounds, pieces, starts):
    rows = own.shape[0]
    rank = pieces[0].shape[0]
    last = starts is not None
    shape = (rows // 2, 2 * rank) if last else (rows, 2 * rank)
    out = jax.ShapeDtypeStruct(shape, F32)
    operands = [own, other, bounds, *pieces, *(starts or ())]
    return pl.pallas_call(
        functools.partial(rank_kernel, groups, depth, last),
        out_shape=(out, out),
        in_specs=[VMEM] * len(operands),
        out_specs=(VMEM, VMEM),
        compiler_params=params(),
        cost_estimate=LONG,
    )(*operands)


def final_kernel(bounds_ref, mine, one, two, three, near_ref, far_ref, *refs):
    factors, out_ref = refs[:-1], refs[-1]
    rank, width = factors[0].shape[0], out_ref.shape[1]
    begin = factors[0].shape[1] - width
    packed = (mine[...] + one[...]) + (two[...] + three[...])
    turned = pltpu.roll(packed, rank, 1)
    lane = lax.broadcasted_iota(I32, packed.shape, 1)
    values = jnp.concatenate(
        [jnp.where(lane < rank, packed, turned), jnp.where(lane < rank, turned, packed)], axis=0
    )
    wide = jnp.concatenate([values] * (GROUP // 2), axis=1)
    total = None
    for group in range(len(factors) // GROUP):
        mask = group_mask(*own_ends(bounds_ref, group, GROUP * rank), wide.shape)
        chosen = jnp.where(mask, wide, 0.0).astype(BF16)
        factor = jnp.concatenate(
            [ref[:, begin:] for ref in factors[group * GROUP : (group + 1) * GROUP]], axis=0
        )
        part = jnp.dot(chosen, factor, preferred_element_type=F32)
        total = part if total is None else total + part
    adapted = total.astype(BF16).astype(F32)
    out_ref[...] = ((near_ref[...] + far_ref[...]) + adapted).astype(BF16)


def per_device(hidden, demand, lengths, holder_slot, value_weight, factor_in, factor_out):
    rows, features = hidden.shape
    owners = lax.axis_size("batch")
    rank, width = factor_out.shape[1:]
    depth = features // 2
    order = ring_order(owners)
    forward = [(order[i], order[(i + 1) % owners]) for i in range(owners)]
    backward = [(b, a) for a, b in forward]
    swap = [(0, 1), (1, 0)]

    full = (owners - 1) // 2
    distances = [0]
    for step in range(1, full + 1):
        distances += [step, -step]
    distances.append(owners // 2)
    table = [
        [[order[(order.index(me) - distance) % owners] for distance in distances]]
        for me in range(owners)
    ]
    to_other, first, second, bounds = prologue(
        hidden,
        factor_in[0].T,
        factor_out[0],
        demand,
        lengths,
        holder_slot,
        jnp.asarray(table, I32),
    )

    far, held = base_call(1, True, hidden, value_weight)
    firsts, seconds = [first], [second]
    ahead, behind = (first, second), (first, second)
    for step in range(1, full + 1):
        a = lax.ppermute(ahead[0], "batch", forward)
        d = lax.ppermute(behind[1], "batch", backward)
        b = lax.ppermute(ahead[1], "batch", forward)
        c = lax.ppermute(behind[0], "batch", backward)
        if step == 1:
            a, far = lax.optimization_barrier((a, far))
        ahead, behind = (a, b), (c, d)
        firsts += [a, c]
        seconds += [b, d]
    firsts.append(lax.ppermute(ahead[0], "batch", forward))
    seconds.append(lax.ppermute(behind[1], "batch", backward))
    other = lax.ppermute(to_other, "groups", swap)
    (near,) = base_call(0, False, held, value_weight)
    held, near = lax.optimization_barrier((held, near))

    count = owners // GROUP
    early = range(count - 1)
    pieces = []
    for group in early:
        pieces += firsts[group * GROUP : (group + 1) * GROUP]
        pieces += seconds[group * GROUP : (group + 1) * GROUP]
    sides = (held, other, bounds)
    starts = rank_call(tuple(early), depth, *sides, pieces, None)
    *starts, far = lax.optimization_barrier((*starts, far))
    far = lax.ppermute(far, "tensor", swap)
    pieces = firsts[-GROUP:] + seconds[-GROUP:]
    mine, theirs = rank_call((count - 1,), depth, *sides, pieces, starts)

    two = lax.ppermute(theirs, "groups", swap)
    one = lax.ppermute(mine, "tensor", swap)
    three = lax.ppermute(two, "tensor", swap)

    operands = [bounds, mine, one, two, three, near, far, *seconds]
    return pl.pallas_call(
        final_kernel,
        out_shape=jax.ShapeDtypeStruct((rows, width), BF16),
        in_specs=[VMEM] * len(operands),
        out_specs=VMEM,
        compiler_params=params(),
    )(*operands)


def solution(mesh):
    return jax.shard_map(
        per_device,
        mesh=mesh,
        in_specs=(
            P(("groups", "batch"), "tensor"),
            P(("groups", "batch"), None),
            P(("groups", "batch"), None),
            P(),
            P("tensor", None),
            P("batch", "tensor", None),
            P("batch", None, "tensor"),
        ),
        out_specs=P(("groups", "batch"), "tensor"),
        check_vma=False,
    )
```

```python
import functools

import jax
import jax.numpy as jnp
from jax import lax
from jax.experimental import pallas as pl
from jax.experimental.pallas import tpu as pltpu
from jax.sharding import PartitionSpec as P

F32, BF16, I32 = jnp.float32, jnp.bfloat16, jnp.int32
VMEM_LIMIT = 40 * 1024 * 1024
HALF = pl.CostEstimate(flops=0, bytes_accessed=1 << 22, transcendentals=0)
LONG = pl.CostEstimate(flops=1 << 33, bytes_accessed=1 << 24, transcendentals=0)
GROUP = 4
VMEM = pl.BlockSpec(memory_space=pltpu.VMEM)
HBM = pl.BlockSpec(memory_space=pltpu.HBM)


def in_hbm(array):
    return pltpu.with_memory_space_constraint(array, pltpu.HBM)


def params():
    return pltpu.CompilerParams(vmem_limit_bytes=VMEM_LIMIT)


def ring_order(size):
    if size % 4:
        return list(range(size))
    columns = size // 4
    order = [0]
    for row in range(4):
        across = range(1, columns) if row % 2 == 0 else range(columns - 1, 0, -1)
        order += [row * columns + column for column in across]
    return order + [row * columns for row in (3, 2, 1)]


def contract(left, right):
    return lax.dot_general(left, right, (((1,), (1,)), ((), ())), preferred_element_type=F32)


def extra_rows(columns):
    return 2 * -(-columns // 1024) * 8


def prologue_kernel(
    depth,
    rank,
    hidden_ref,
    factor_ref,
    factor_out_ref,
    demand_ref,
    lengths_ref,
    holder_ref,
    slots_ref,
    to_other_ref,
    first_ref,
    second_ref,
    bounds_ref,
    demand,
    lengths,
    holder,
    slots,
    sems,
    hidden_sem,
):
    group, place = lax.axis_index("groups"), lax.axis_index("batch")
    cut = first_ref.shape[1]
    rows = hidden_ref.shape[0]
    here = pl.multiple_of(group * depth, 128)
    there = pl.multiple_of((1 - group) * depth, 128)
    after = pl.multiple_of(group * depth + cut, 128)
    small = [
        pltpu.make_async_copy(demand_ref, demand, sems.at[0]),
        pltpu.make_async_copy(lengths_ref, lengths, sems.at[1]),
        pltpu.make_async_copy(holder_ref, holder, sems.at[2]),
        pltpu.make_async_copy(slots_ref.at[pl.ds(place, 1)], slots, sems.at[3]),
    ]
    large = [
        pltpu.make_async_copy(factor_ref.at[:, pl.ds(here, cut)], first_ref, sems.at[4]),
        pltpu.make_async_copy(
            factor_ref.at[:, pl.ds(after, depth - cut)], second_ref.at[:, : depth - cut], sems.at[5]
        ),
        pltpu.make_async_copy(factor_out_ref, second_ref.at[:, depth - cut :], sems.at[6]),
    ]
    for i in range(depth // 128):
        large.append(
            pltpu.make_async_copy(
                hidden_ref.at[:, pl.ds(there + i * 128, 128)],
                to_other_ref.at[i * rows : (i + 1) * rows],
                hidden_sem.at[i],
            )
        )
    for copy in small + large:
        copy.start()
    for copy in small:
        copy.wait()
    count = slots.shape[2]
    items = demand.shape[1]
    column = lax.broadcasted_iota(I32, (1, count * rank), 1)
    zero = jnp.int32(0)

    def chunk_mask(chunk):
        return (column >= chunk * rank) & (column < (chunk + 1) * rank)

    low = high = jnp.zeros((1, count * rank), I32)
    if items * count <= 64:
        start = zero
        spans = []
        for item in range(items):
            end = start + lengths[0, item]
            spans.append((holder[demand[0, item]], start, end))
            start = end
        for chunk in range(count):
            slot = slots[0, 0, chunk]
            begin = end = zero
            for owner, first, last in spans:
                begin = jnp.where(owner == slot, first, begin)
                end = jnp.where(owner == slot, last, end)
            low = jnp.where(chunk_mask(chunk), begin, low)
            high = jnp.where(chunk_mask(chunk), end, high)
    else:

        def chunk_ends(chunk, carry):
            low, high = carry
            slot = slots[0, 0, chunk]

            def item_ends(item, state):
                start, begin, end = state
                last = start + lengths[0, item]
                hit = holder[demand[0, item]] == slot
                return last, jnp.where(hit, start, begin), jnp.where(hit, last, end)

            _, begin, end = lax.fori_loop(0, items, item_ends, (zero, zero, zero))
            mask = chunk_mask(chunk)
            return jnp.where(mask, begin, low), jnp.where(mask, end, high)

        low, high = lax.fori_loop(0, count, chunk_ends, (low, high))
    bounds_ref[0:1, :] = low
    bounds_ref[1:2, :] = high
    bounds_ref[2:8, :] = jnp.zeros((6, count * rank), I32)
    extra = extra_rows(count * rank)
    line = lax.broadcasted_iota(I32, (extra, 128), 0)
    ends = jnp.zeros((extra, 128), I32)
    for i in range(count * rank // 128):
        columns = slice(i * 128, (i + 1) * 128)
        ends = jnp.where(line == i, low[:, columns], ends)
        ends = jnp.where(line == extra // 2 + i, high[:, columns], ends)
    to_other_ref[-extra:, :] = ends.astype(F32).astype(BF16)
    for copy in large:
        copy.wait()


def prologue(hidden, factor, factor_out, demand, lengths, holder_slot, slots):
    rows, features = hidden.shape
    rank, width = factor_out.shape
    depth = features // 2
    cut = (depth + width) // 2
    count = slots.shape[2]
    tall = depth // 128 * rows + extra_rows(count * rank)
    return pl.pallas_call(
        functools.partial(prologue_kernel, depth, rank),
        out_shape=(
            jax.ShapeDtypeStruct((tall, 128), hidden.dtype),
            jax.ShapeDtypeStruct((rank, cut), factor.dtype),
            jax.ShapeDtypeStruct((rank, cut), factor.dtype),
            jax.ShapeDtypeStruct((8, count * rank), I32),
        ),
        in_specs=[HBM] * 7,
        out_specs=(VMEM,) * 4,
        scratch_shapes=[
            pltpu.SMEM(demand.shape, I32),
            pltpu.SMEM(lengths.shape, I32),
            pltpu.SMEM(holder_slot.shape, I32),
            pltpu.SMEM((1, 1, count), I32),
            pltpu.SemaphoreType.DMA((7,)),
            pltpu.SemaphoreType.DMA((depth // 128,)),
        ],
        compiler_params=params(),
    )(*map(in_hbm, (hidden, factor, factor_out, demand, lengths, holder_slot, slots)))


def base_kernel(side, fetch_rows, rows_in_ref, weight_ref, out_ref, *rest):
    rows_ref = rest[0] if fetch_rows else rows_in_ref
    buffer, sems = rest[-2:]
    width = out_ref.shape[1]
    core = lax.axis_index("tensor")
    offset = pl.multiple_of((core if side == 0 else 1 - core) * width, 128)
    steps, step = buffer.shape[:2]
    copies = []
    for k in range(steps):
        span = pl.ds(k * step, step)
        need = [
            pltpu.make_async_copy(
                weight_ref.at[span, pl.ds(offset, width)], buffer.at[k], sems.at[0, k]
            )
        ]
        if fetch_rows:
            need.append(
                pltpu.make_async_copy(
                    rows_in_ref.at[:, span], rows_ref.at[:, span], sems.at[1, k]
                )
            )
        copies.append(need)
    for need in copies:
        for copy in need:
            copy.start()
    for k, need in enumerate(copies):
        for copy in need:
            copy.wait()
        rows = rows_ref[:, k * step : (k + 1) * step]
        part = jnp.dot(rows, buffer[k], preferred_element_type=F32)
        if k == 0:
            out_ref[...] = part
        else:
            out_ref[...] += part


def base_call(side, fetch_rows, rows, weight):
    count, depth = rows.shape
    width = weight.shape[1] // 2
    steps = 4
    out = (jax.ShapeDtypeStruct((count, width), F32),)
    if fetch_rows:
        out += (jax.ShapeDtypeStruct(rows.shape, rows.dtype),)
    return pl.pallas_call(
        functools.partial(base_kernel, side, fetch_rows),
        out_shape=out,
        in_specs=[HBM if fetch_rows else VMEM, HBM],
        out_specs=(VMEM,) * len(out),
        scratch_shapes=[
            pltpu.VMEM((steps, depth // steps, width), weight.dtype),
            pltpu.SemaphoreType.DMA((2, steps)),
        ],
        compiler_params=params(),
        cost_estimate=HALF,
    )(in_hbm(rows) if fetch_rows else rows, in_hbm(weight))


def group_mask(low, high, shape):
    row = lax.broadcasted_iota(I32, shape, 0)
    return (row >= low) & (row < high)


def own_ends(bounds_ref, group, size):
    columns = slice(group * size, (group + 1) * size)
    return bounds_ref[0:1, columns], bounds_ref[1:2, columns]


def other_ends(other_ref, extra, group, size):
    ends = other_ref[-extra:, :].astype(F32).astype(I32)
    lines = range(group * size // 128, (group + 1) * size // 128)
    low = jnp.concatenate([ends[i : i + 1] for i in lines], axis=1)
    high = jnp.concatenate([ends[extra // 2 + i : extra // 2 + i + 1] for i in lines], axis=1)
    return low, high


def fold(masked):
    total = masked[:, :128]
    for begin in range(128, masked.shape[1], 128):
        total = total + masked[:, begin : begin + 128]
    return total


def rank_kernel(groups, depth, last, *refs):
    refs = list(refs)
    own_ref, other_ref, bounds_ref = refs[:3]
    pieces = refs[3:]
    pieces, rest = pieces[: 2 * GROUP * len(groups)], pieces[2 * GROUP * len(groups) :]
    starts, outs = (rest[:2], rest[2:]) if last else ((None, None), rest)
    cut = pieces[0].shape[1]
    offset = pl.multiple_of(lax.axis_index("groups") * depth, 128)
    own = own_ref[:, pl.ds(offset, depth)]
    count = own.shape[0]
    other = jnp.concatenate(
        [other_ref[i * count : (i + 1) * count, :] for i in range(depth // 128)], axis=1
    )
    rank = pieces[0].shape[0]
    size = GROUP * rank
    extra = extra_rows(bounds_ref.shape[1])
    totals = [start_ref[...] if last else None for start_ref in starts]
    for i, group in enumerate(groups):
        held = pieces[2 * GROUP * i : 2 * GROUP * (i + 1)]
        first = jnp.concatenate([ref[...] for ref in held[:GROUP]], axis=0)
        second = jnp.concatenate([ref[:, : depth - cut] for ref in held[GROUP:]], axis=0)
        ends = (own_ends(bounds_ref, group, size), other_ends(other_ref, extra, group, size))
        for s, rows in enumerate((own, other)):
            part = contract(rows[:, :cut], first) + contract(rows[:, cut:], second)
            kept = fold(jnp.where(group_mask(*ends[s], part.shape), part, 0.0))
            totals[s] = kept if totals[s] is None else totals[s] + kept
    for total, out_ref in zip(totals, outs):
        if last:
            total = total + pltpu.roll(total, rank, 1)
            half = total.shape[0] // 2
            lane = lax.broadcasted_iota(I32, (half, 2 * rank), 1)
            total = jnp.where(lane < rank, total[:half], total[half:])
        out_ref[...] = total


def rank_call(groups, depth, own, other, bounds, pieces, starts):
    rows = own.shape[0]
    rank = pieces[0].shape[0]
    last = starts is not None
    shape = (rows // 2, 2 * rank) if last else (rows, 2 * rank)
    out = jax.ShapeDtypeStruct(shape, F32)
    operands = [own, other, bounds, *pieces, *(starts or ())]
    return pl.pallas_call(
        functools.partial(rank_kernel, groups, depth, last),
        out_shape=(out, out),
        in_specs=[VMEM] * len(operands),
        out_specs=(VMEM, VMEM),
        compiler_params=params(),
        cost_estimate=LONG,
    )(*operands)


def final_kernel(bounds_ref, mine, one, two, three, near_ref, far_ref, *refs):
    factors, out_ref = refs[:-1], refs[-1]
    rank, width = factors[0].shape[0], out_ref.shape[1]
    begin = factors[0].shape[1] - width
    packed = (mine[...] + one[...]) + (two[...] + three[...])
    turned = pltpu.roll(packed, rank, 1)
    lane = lax.broadcasted_iota(I32, packed.shape, 1)
    values = jnp.concatenate(
        [jnp.where(lane < rank, packed, turned), jnp.where(lane < rank, turned, packed)], axis=0
    )
    wide = jnp.concatenate([values] * (GROUP // 2), axis=1)
    total = None
    for group in range(len(factors) // GROUP):
        mask = group_mask(*own_ends(bounds_ref, group, GROUP * rank), wide.shape)
        chosen = jnp.where(mask, wide, 0.0).astype(BF16)
        factor = jnp.concatenate(
            [ref[:, begin:] for ref in factors[group * GROUP : (group + 1) * GROUP]], axis=0
        )
        part = jnp.dot(chosen, factor, preferred_element_type=F32)
        total = part if total is None else total + part
    adapted = total.astype(BF16).astype(F32)
    out_ref[...] = ((near_ref[...] + far_ref[...]) + adapted).astype(BF16)


def per_device(hidden, demand, lengths, holder_slot, value_weight, factor_in, factor_out):
    rows, features = hidden.shape
    owners = lax.axis_size("batch")
    rank, width = factor_out.shape[1:]
    depth = features // 2
    order = ring_order(owners)
    forward = [(order[i], order[(i + 1) % owners]) for i in range(owners)]
    backward = [(b, a) for a, b in forward]
    swap = [(0, 1), (1, 0)]

    full = (owners - 1) // 2
    distances = [0]
    for step in range(1, full + 1):
        distances += [step, -step]
    distances.append(owners // 2)
    table = [
        [[order[(order.index(me) - distance) % owners] for distance in distances]]
        for me in range(owners)
    ]
    to_other, first, second, bounds = prologue(
        hidden,
        factor_in[0].T,
        factor_out[0],
        demand,
        lengths,
        holder_slot,
        jnp.asarray(table, I32),
    )

    near, held = base_call(0, True, hidden, value_weight)
    firsts, seconds = [first], [second]
    ahead, behind = (first, second), (first, second)
    for step in range(1, full + 1):
        a = lax.ppermute(ahead[0], "batch", forward)
        d = lax.ppermute(behind[1], "batch", backward)
        b = lax.ppermute(ahead[1], "batch", forward)
        c = lax.ppermute(behind[0], "batch", backward)
        ahead, behind = (a, b), (c, d)
        firsts += [a, c]
        seconds += [b, d]
    rows_far, a, d = lax.optimization_barrier((held, ahead[0], behind[1]))
    firsts.append(lax.ppermute(a, "batch", forward))
    seconds.append(lax.ppermute(d, "batch", backward))
    other = lax.ppermute(to_other, "groups", swap)
    (far,) = base_call(1, False, rows_far, value_weight)
    held, near = lax.optimization_barrier((held, near))

    count = owners // GROUP
    early = range(count - 1)
    pieces = []
    for group in early:
        pieces += firsts[group * GROUP : (group + 1) * GROUP]
        pieces += seconds[group * GROUP : (group + 1) * GROUP]
    sides = (held, other, bounds)
    starts = rank_call(tuple(early), depth, *sides, pieces, None)
    *starts, far = lax.optimization_barrier((*starts, far))
    far = lax.ppermute(far, "tensor", swap)
    pieces = firsts[-GROUP:] + seconds[-GROUP:]
    mine, theirs = rank_call((count - 1,), depth, *sides, pieces, starts)

    two = lax.ppermute(theirs, "groups", swap)
    one = lax.ppermute(mine, "tensor", swap)
    three = lax.ppermute(two, "tensor", swap)

    operands = [bounds, mine, one, two, three, near, far, *seconds]
    return pl.pallas_call(
        final_kernel,
        out_shape=jax.ShapeDtypeStruct((rows, width), BF16),
        in_specs=[VMEM] * len(operands),
        out_specs=VMEM,
        compiler_params=params(),
    )(*operands)


def solution(mesh):
    return jax.shard_map(
        per_device,
        mesh=mesh,
        in_specs=(
            P(("groups", "batch"), "tensor"),
            P(("groups", "batch"), None),
            P(("groups", "batch"), None),
            P(),
            P("tensor", None),
            P("batch", "tensor", None),
            P("batch", None, "tensor"),
        ),
        out_specs=P(("groups", "batch"), "tensor"),
        check_vma=False,
    )
```

```python
import functools

import jax
import jax.numpy as jnp
from jax import lax
from jax.experimental import pallas as pl
from jax.experimental.pallas import tpu as pltpu
from jax.sharding import PartitionSpec as P

F32, BF16, I32 = jnp.float32, jnp.bfloat16, jnp.int32
VMEM_LIMIT = 40 * 1024 * 1024
HALF = pl.CostEstimate(flops=0, bytes_accessed=1 << 22, transcendentals=0)
LONG = pl.CostEstimate(flops=1 << 33, bytes_accessed=1 << 24, transcendentals=0)
GROUP = 4
VMEM = pl.BlockSpec(memory_space=pltpu.VMEM)
HBM = pl.BlockSpec(memory_space=pltpu.HBM)


def in_hbm(array):
    return pltpu.with_memory_space_constraint(array, pltpu.HBM)


def params():
    return pltpu.CompilerParams(vmem_limit_bytes=VMEM_LIMIT)


def ring_order(size):
    if size % 4:
        return list(range(size))
    columns = size // 4
    order = [0]
    for row in range(4):
        across = range(1, columns) if row % 2 == 0 else range(columns - 1, 0, -1)
        order += [row * columns + column for column in across]
    return order + [row * columns for row in (3, 2, 1)]


def contract(left, right):
    return lax.dot_general(left, right, (((1,), (1,)), ((), ())), preferred_element_type=F32)


def extra_rows(columns):
    return 2 * -(-columns // 1024) * 8


def prologue_kernel(
    depth,
    rank,
    hidden_ref,
    factor_ref,
    factor_out_ref,
    demand_ref,
    lengths_ref,
    holder_ref,
    slots_ref,
    to_other_ref,
    first_ref,
    second_ref,
    bounds_ref,
    demand,
    lengths,
    holder,
    slots,
    sems,
    hidden_sem,
):
    group, place = lax.axis_index("groups"), lax.axis_index("batch")
    cut = first_ref.shape[1]
    rows = hidden_ref.shape[0]
    here = pl.multiple_of(group * depth, 128)
    there = pl.multiple_of((1 - group) * depth, 128)
    after = pl.multiple_of(group * depth + cut, 128)
    small = [
        pltpu.make_async_copy(demand_ref, demand, sems.at[0]),
        pltpu.make_async_copy(lengths_ref, lengths, sems.at[1]),
        pltpu.make_async_copy(holder_ref, holder, sems.at[2]),
        pltpu.make_async_copy(slots_ref.at[pl.ds(place, 1)], slots, sems.at[3]),
    ]
    large = [
        pltpu.make_async_copy(factor_ref.at[:, pl.ds(here, cut)], first_ref, sems.at[4]),
        pltpu.make_async_copy(
            factor_ref.at[:, pl.ds(after, depth - cut)], second_ref.at[:, : depth - cut], sems.at[5]
        ),
        pltpu.make_async_copy(factor_out_ref, second_ref.at[:, depth - cut :], sems.at[6]),
    ]
    for i in range(depth // 128):
        large.append(
            pltpu.make_async_copy(
                hidden_ref.at[:, pl.ds(there + i * 128, 128)],
                to_other_ref.at[i * rows : (i + 1) * rows],
                hidden_sem.at[i],
            )
        )
    for copy in small + large:
        copy.start()
    for copy in small:
        copy.wait()
    count = slots.shape[2]
    items = demand.shape[1]
    column = lax.broadcasted_iota(I32, (1, count * rank), 1)
    zero = jnp.int32(0)

    def chunk_mask(chunk):
        return (column >= chunk * rank) & (column < (chunk + 1) * rank)

    low = high = jnp.zeros((1, count * rank), I32)
    if items * count <= 64:
        start = zero
        spans = []
        for item in range(items):
            end = start + lengths[0, item]
            spans.append((holder[demand[0, item]], start, end))
            start = end
        for chunk in range(count):
            slot = slots[0, 0, chunk]
            begin = end = zero
            for owner, first, last in spans:
                begin = jnp.where(owner == slot, first, begin)
                end = jnp.where(owner == slot, last, end)
            low = jnp.where(chunk_mask(chunk), begin, low)
            high = jnp.where(chunk_mask(chunk), end, high)
    else:

        def chunk_ends(chunk, carry):
            low, high = carry
            slot = slots[0, 0, chunk]

            def item_ends(item, state):
                start, begin, end = state
                last = start + lengths[0, item]
                hit = holder[demand[0, item]] == slot
                return last, jnp.where(hit, start, begin), jnp.where(hit, last, end)

            _, begin, end = lax.fori_loop(0, items, item_ends, (zero, zero, zero))
            mask = chunk_mask(chunk)
            return jnp.where(mask, begin, low), jnp.where(mask, end, high)

        low, high = lax.fori_loop(0, count, chunk_ends, (low, high))
    bounds_ref[0:1, :] = low
    bounds_ref[1:2, :] = high
    bounds_ref[2:8, :] = jnp.zeros((6, count * rank), I32)
    extra = extra_rows(count * rank)
    line = lax.broadcasted_iota(I32, (extra, 128), 0)
    ends = jnp.zeros((extra, 128), I32)
    for i in range(count * rank // 128):
        columns = slice(i * 128, (i + 1) * 128)
        ends = jnp.where(line == i, low[:, columns], ends)
        ends = jnp.where(line == extra // 2 + i, high[:, columns], ends)
    to_other_ref[-extra:, :] = ends.astype(F32).astype(BF16)
    for copy in large:
        copy.wait()


def prologue(hidden, factor, factor_out, demand, lengths, holder_slot, slots):
    rows, features = hidden.shape
    rank, width = factor_out.shape
    depth = features // 2
    cut = (depth + width) // 2
    count = slots.shape[2]
    tall = depth // 128 * rows + extra_rows(count * rank)
    return pl.pallas_call(
        functools.partial(prologue_kernel, depth, rank),
        out_shape=(
            jax.ShapeDtypeStruct((tall, 128), hidden.dtype),
            jax.ShapeDtypeStruct((rank, cut), factor.dtype),
            jax.ShapeDtypeStruct((rank, cut), factor.dtype),
            jax.ShapeDtypeStruct((8, count * rank), I32),
        ),
        in_specs=[HBM] * 7,
        out_specs=(VMEM,) * 4,
        scratch_shapes=[
            pltpu.SMEM(demand.shape, I32),
            pltpu.SMEM(lengths.shape, I32),
            pltpu.SMEM(holder_slot.shape, I32),
            pltpu.SMEM((1, 1, count), I32),
            pltpu.SemaphoreType.DMA((7,)),
            pltpu.SemaphoreType.DMA((depth // 128,)),
        ],
        compiler_params=params(),
    )(*map(in_hbm, (hidden, factor, factor_out, demand, lengths, holder_slot, slots)))


def base_kernel(side, fetch_rows, rows_in_ref, weight_ref, out_ref, *rest):
    rows_ref = rest[0] if fetch_rows else rows_in_ref
    buffer, sems = rest[-2:]
    width = out_ref.shape[1]
    core = lax.axis_index("tensor")
    offset = pl.multiple_of((core if side == 0 else 1 - core) * width, 128)
    steps, step = buffer.shape[:2]
    copies = []
    for k in range(steps):
        span = pl.ds(k * step, step)
        need = [
            pltpu.make_async_copy(
                weight_ref.at[span, pl.ds(offset, width)], buffer.at[k], sems.at[0, k]
            )
        ]
        if fetch_rows:
            need.append(
                pltpu.make_async_copy(
                    rows_in_ref.at[:, span], rows_ref.at[:, span], sems.at[1, k]
                )
            )
        copies.append(need)
    for need in copies:
        for copy in need:
            copy.start()
    for k, need in enumerate(copies):
        for copy in need:
            copy.wait()
        rows = rows_ref[:, k * step : (k + 1) * step]
        part = jnp.dot(rows, buffer[k], preferred_element_type=F32)
        if k == 0:
            out_ref[...] = part
        else:
            out_ref[...] += part


def base_call(side, fetch_rows, rows, weight):
    count, depth = rows.shape
    width = weight.shape[1] // 2
    steps = 4
    out = (jax.ShapeDtypeStruct((count, width), F32),)
    if fetch_rows:
        out += (jax.ShapeDtypeStruct(rows.shape, rows.dtype),)
    return pl.pallas_call(
        functools.partial(base_kernel, side, fetch_rows),
        out_shape=out,
        in_specs=[HBM if fetch_rows else VMEM, HBM],
        out_specs=(VMEM,) * len(out),
        scratch_shapes=[
            pltpu.VMEM((steps, depth // steps, width), weight.dtype),
            pltpu.SemaphoreType.DMA((2, steps)),
        ],
        compiler_params=params(),
        cost_estimate=HALF,
    )(in_hbm(rows) if fetch_rows else rows, in_hbm(weight))


def group_mask(low, high, shape):
    row = lax.broadcasted_iota(I32, shape, 0)
    return (row >= low) & (row < high)


def own_ends(bounds_ref, group, size):
    columns = slice(group * size, (group + 1) * size)
    return bounds_ref[0:1, columns], bounds_ref[1:2, columns]


def other_ends(other_ref, extra, group, size):
    ends = other_ref[-extra:, :].astype(F32).astype(I32)
    lines = range(group * size // 128, (group + 1) * size // 128)
    low = jnp.concatenate([ends[i : i + 1] for i in lines], axis=1)
    high = jnp.concatenate([ends[extra // 2 + i : extra // 2 + i + 1] for i in lines], axis=1)
    return low, high


def fold(masked):
    total = masked[:, :128]
    for begin in range(128, masked.shape[1], 128):
        total = total + masked[:, begin : begin + 128]
    return total


def rank_kernel(groups, depth, last, *refs):
    refs = list(refs)
    own_ref, other_ref, bounds_ref = refs[:3]
    pieces = refs[3:]
    pieces, rest = pieces[: 2 * GROUP * len(groups)], pieces[2 * GROUP * len(groups) :]
    starts, outs = (rest[:2], rest[2:]) if last else ((None, None), rest)
    cut = pieces[0].shape[1]
    offset = pl.multiple_of(lax.axis_index("groups") * depth, 128)
    own = own_ref[:, pl.ds(offset, depth)]
    count = own.shape[0]
    other = jnp.concatenate(
        [other_ref[i * count : (i + 1) * count, :] for i in range(depth // 128)], axis=1
    )
    rank = pieces[0].shape[0]
    size = GROUP * rank
    extra = extra_rows(bounds_ref.shape[1])
    totals = [start_ref[...] if last else None for start_ref in starts]
    for i, group in enumerate(groups):
        held = pieces[2 * GROUP * i : 2 * GROUP * (i + 1)]
        first = jnp.concatenate([ref[...] for ref in held[:GROUP]], axis=0)
        second = jnp.concatenate([ref[:, : depth - cut] for ref in held[GROUP:]], axis=0)
        ends = (own_ends(bounds_ref, group, size), other_ends(other_ref, extra, group, size))
        for s, rows in enumerate((own, other)):
            part = contract(rows[:, :cut], first) + contract(rows[:, cut:], second)
            kept = fold(jnp.where(group_mask(*ends[s], part.shape), part, 0.0))
            totals[s] = kept if totals[s] is None else totals[s] + kept
    for total, out_ref in zip(totals, outs):
        if last:
            total = total + pltpu.roll(total, rank, 1)
            half = total.shape[0] // 2
            lane = lax.broadcasted_iota(I32, (half, 2 * rank), 1)
            total = jnp.where(lane < rank, total[:half], total[half:])
        out_ref[...] = total


def rank_call(groups, depth, own, other, bounds, pieces, starts):
    rows = own.shape[0]
    rank = pieces[0].shape[0]
    last = starts is not None
    shape = (rows // 2, 2 * rank) if last else (rows, 2 * rank)
    out = jax.ShapeDtypeStruct(shape, F32)
    operands = [own, other, bounds, *pieces, *(starts or ())]
    return pl.pallas_call(
        functools.partial(rank_kernel, groups, depth, last),
        out_shape=(out, out),
        in_specs=[VMEM] * len(operands),
        out_specs=(VMEM, VMEM),
        compiler_params=params(),
        cost_estimate=LONG,
    )(*operands)


def final_kernel(bounds_ref, mine, one, two, three, near_ref, far_ref, *refs):
    factors, out_ref = refs[:-1], refs[-1]
    rank, width = factors[0].shape[0], out_ref.shape[1]
    begin = factors[0].shape[1] - width
    packed = (mine[...] + one[...]) + (two[...] + three[...])
    turned = pltpu.roll(packed, rank, 1)
    lane = lax.broadcasted_iota(I32, packed.shape, 1)
    values = jnp.concatenate(
        [jnp.where(lane < rank, packed, turned), jnp.where(lane < rank, turned, packed)], axis=0
    )
    wide = jnp.concatenate([values] * (GROUP // 2), axis=1)
    total = None
    for group in range(len(factors) // GROUP):
        mask = group_mask(*own_ends(bounds_ref, group, GROUP * rank), wide.shape)
        chosen = jnp.where(mask, wide, 0.0).astype(BF16)
        factor = jnp.concatenate(
            [ref[:, begin:] for ref in factors[group * GROUP : (group + 1) * GROUP]], axis=0
        )
        part = jnp.dot(chosen, factor, preferred_element_type=F32)
        total = part if total is None else total + part
    adapted = total.astype(BF16).astype(F32)
    out_ref[...] = ((near_ref[...] + far_ref[...]) + adapted).astype(BF16)


def per_device(hidden, demand, lengths, holder_slot, value_weight, factor_in, factor_out):
    rows, features = hidden.shape
    owners = lax.axis_size("batch")
    rank, width = factor_out.shape[1:]
    depth = features // 2
    order = ring_order(owners)
    forward = [(order[i], order[(i + 1) % owners]) for i in range(owners)]
    backward = [(b, a) for a, b in forward]
    swap = [(0, 1), (1, 0)]

    full = (owners - 1) // 2
    distances = [0]
    for step in range(1, full + 1):
        distances += [step, -step]
    distances.append(owners // 2)
    table = [
        [[order[(order.index(me) - distance) % owners] for distance in distances]]
        for me in range(owners)
    ]
    to_other, first, second, bounds = prologue(
        hidden,
        factor_in[0].T,
        factor_out[0],
        demand,
        lengths,
        holder_slot,
        jnp.asarray(table, I32),
    )

    far, held = base_call(1, True, hidden, value_weight)
    firsts, seconds = [first], [second]
    ahead, behind = (first, second), (first, second)
    for step in range(1, full + 1):
        a = lax.ppermute(ahead[0], "batch", forward)
        d = lax.ppermute(behind[1], "batch", backward)
        b = lax.ppermute(ahead[1], "batch", forward)
        c = lax.ppermute(behind[0], "batch", backward)
        if step == 1:
            a, far = lax.optimization_barrier((a, far))
        ahead, behind = (a, b), (c, d)
        firsts += [a, c]
        seconds += [b, d]
    rows_near, a, d = lax.optimization_barrier((held, ahead[0], behind[1]))
    firsts.append(lax.ppermute(a, "batch", forward))
    seconds.append(lax.ppermute(d, "batch", backward))
    other = lax.ppermute(to_other, "groups", swap)
    (near,) = base_call(0, False, rows_near, value_weight)

    count = owners // GROUP
    early = range(count - 1)
    pieces = []
    for group in early:
        pieces += firsts[group * GROUP : (group + 1) * GROUP]
        pieces += seconds[group * GROUP : (group + 1) * GROUP]
    sides = (held, other, bounds)
    starts = rank_call(tuple(early), depth, *sides, pieces, None)
    *starts, far, near = lax.optimization_barrier((*starts, far, near))
    far = lax.ppermute(far, "tensor", swap)
    pieces = firsts[-GROUP:] + seconds[-GROUP:]
    mine, theirs = rank_call((count - 1,), depth, *sides, pieces, starts)

    two = lax.ppermute(theirs, "groups", swap)
    one = lax.ppermute(mine, "tensor", swap)
    three = lax.ppermute(two, "tensor", swap)

    operands = [bounds, mine, one, two, three, near, far, *seconds]
    return pl.pallas_call(
        final_kernel,
        out_shape=jax.ShapeDtypeStruct((rows, width), BF16),
        in_specs=[VMEM] * len(operands),
        out_specs=VMEM,
        compiler_params=params(),
    )(*operands)


def solution(mesh):
    return jax.shard_map(
        per_device,
        mesh=mesh,
        in_specs=(
            P(("groups", "batch"), "tensor"),
            P(("groups", "batch"), None),
            P(("groups", "batch"), None),
            P(),
            P("tensor", None),
            P("batch", "tensor", None),
            P("batch", None, "tensor"),
        ),
        out_specs=P(("groups", "batch"), "tensor"),
        check_vma=False,
    )
```

```python
import functools

import jax
import jax.numpy as jnp
from jax import lax
from jax.experimental import pallas as pl
from jax.experimental.pallas import tpu as pltpu
from jax.sharding import PartitionSpec as P

F32, BF16, I32 = jnp.float32, jnp.bfloat16, jnp.int32
VMEM_LIMIT = 40 * 1024 * 1024
HALF = pl.CostEstimate(flops=0, bytes_accessed=1 << 22, transcendentals=0)
LONG = pl.CostEstimate(flops=1 << 33, bytes_accessed=1 << 24, transcendentals=0)
GROUP = 4
VMEM = pl.BlockSpec(memory_space=pltpu.VMEM)
HBM = pl.BlockSpec(memory_space=pltpu.HBM)


def in_hbm(array):
    return pltpu.with_memory_space_constraint(array, pltpu.HBM)


def params():
    return pltpu.CompilerParams(vmem_limit_bytes=VMEM_LIMIT)


def ring_order(size):
    if size % 4:
        return list(range(size))
    columns = size // 4
    order = [0]
    for row in range(4):
        across = range(1, columns) if row % 2 == 0 else range(columns - 1, 0, -1)
        order += [row * columns + column for column in across]
    return order + [row * columns for row in (3, 2, 1)]


def contract(left, right):
    return lax.dot_general(left, right, (((1,), (1,)), ((), ())), preferred_element_type=F32)


def extra_rows(columns):
    return 2 * -(-columns // 1024) * 8


def prologue_kernel(
    depth,
    rank,
    hidden_ref,
    factor_ref,
    factor_out_ref,
    demand_ref,
    lengths_ref,
    holder_ref,
    slots_ref,
    to_other_ref,
    shard_ref,
    bounds_ref,
    demand,
    lengths,
    holder,
    slots,
    sems,
    hidden_sem,
):
    group, place = lax.axis_index("groups"), lax.axis_index("batch")
    core = lax.axis_index("tensor")
    rows = hidden_ref.shape[0]
    here = pl.multiple_of(group * depth, 128)
    there = pl.multiple_of((1 - group) * depth, 128)
    small = [
        pltpu.make_async_copy(demand_ref, demand, sems.at[0]),
        pltpu.make_async_copy(lengths_ref, lengths, sems.at[1]),
        pltpu.make_async_copy(holder_ref, holder, sems.at[2]),
        pltpu.make_async_copy(slots_ref.at[pl.ds(place * 2 + core, 1)], slots, sems.at[3]),
    ]
    large = [
        pltpu.make_async_copy(
            factor_ref.at[:, pl.ds(here, depth)], shard_ref.at[:, :depth], sems.at[4]
        ),
        pltpu.make_async_copy(factor_out_ref, shard_ref.at[:, depth:], sems.at[5]),
    ]
    for i in range(depth // 128):
        large.append(
            pltpu.make_async_copy(
                hidden_ref.at[:, pl.ds(there + i * 128, 128)],
                to_other_ref.at[i * rows : (i + 1) * rows],
                hidden_sem.at[i],
            )
        )
    for copy in small + large:
        copy.start()
    for copy in small:
        copy.wait()
    count = slots.shape[2]
    items = demand.shape[1]
    column = lax.broadcasted_iota(I32, (1, count * rank), 1)
    zero = jnp.int32(0)

    def chunk_mask(chunk):
        return (column >= chunk * rank) & (column < (chunk + 1) * rank)

    low = high = jnp.zeros((1, count * rank), I32)
    if items * count <= 64:
        start = zero
        spans = []
        for item in range(items):
            end = start + lengths[0, item]
            spans.append((holder[demand[0, item]], start, end))
            start = end
        for chunk in range(count):
            slot = slots[0, 0, chunk]
            begin = end = zero
            for owner, first, last in spans:
                begin = jnp.where(owner == slot, first, begin)
                end = jnp.where(owner == slot, last, end)
            low = jnp.where(chunk_mask(chunk), begin, low)
            high = jnp.where(chunk_mask(chunk), end, high)
    else:

        def chunk_ends(chunk, carry):
            low, high = carry
            slot = slots[0, 0, chunk]

            def item_ends(item, state):
                start, begin, end = state
                last = start + lengths[0, item]
                hit = holder[demand[0, item]] == slot
                return last, jnp.where(hit, start, begin), jnp.where(hit, last, end)

            _, begin, end = lax.fori_loop(0, items, item_ends, (zero, zero, zero))
            mask = chunk_mask(chunk)
            return jnp.where(mask, begin, low), jnp.where(mask, end, high)

        low, high = lax.fori_loop(0, count, chunk_ends, (low, high))
    bounds_ref[0:1, :] = low
    bounds_ref[1:2, :] = high
    bounds_ref[2:8, :] = jnp.zeros((6, count * rank), I32)
    extra = extra_rows(count * rank)
    line = lax.broadcasted_iota(I32, (extra, 128), 0)
    ends = jnp.zeros((extra, 128), I32)
    for i in range(count * rank // 128):
        columns = slice(i * 128, (i + 1) * 128)
        ends = jnp.where(line == i, low[:, columns], ends)
        ends = jnp.where(line == extra // 2 + i, high[:, columns], ends)
    to_other_ref[-extra:, :] = ends.astype(F32).astype(BF16)
    for copy in large:
        copy.wait()


def prologue(hidden, factor, factor_out, demand, lengths, holder_slot, slots):
    rows, features = hidden.shape
    rank, width = factor_out.shape
    depth = features // 2
    count = slots.shape[2]
    tall = depth // 128 * rows + extra_rows(count * rank)
    return pl.pallas_call(
        functools.partial(prologue_kernel, depth, rank),
        out_shape=(
            jax.ShapeDtypeStruct((tall, 128), hidden.dtype),
            jax.ShapeDtypeStruct((rank, depth + width), factor.dtype),
            jax.ShapeDtypeStruct((8, count * rank), I32),
        ),
        in_specs=[HBM] * 7,
        out_specs=(VMEM,) * 3,
        scratch_shapes=[
            pltpu.SMEM(demand.shape, I32),
            pltpu.SMEM(lengths.shape, I32),
            pltpu.SMEM(holder_slot.shape, I32),
            pltpu.SMEM((1, 1, count), I32),
            pltpu.SemaphoreType.DMA((6,)),
            pltpu.SemaphoreType.DMA((depth // 128,)),
        ],
        compiler_params=params(),
    )(*map(in_hbm, (hidden, factor, factor_out, demand, lengths, holder_slot, slots)))


def base_kernel(side, fetch_rows, rows_in_ref, weight_ref, out_ref, *rest):
    rows_ref = rest[0] if fetch_rows else rows_in_ref
    buffer, sems = rest[-2:]
    width = out_ref.shape[1]
    core = lax.axis_index("tensor")
    offset = pl.multiple_of((core if side == 0 else 1 - core) * width, 128)
    steps, step = buffer.shape[:2]
    copies = []
    for k in range(steps):
        span = pl.ds(k * step, step)
        need = [
            pltpu.make_async_copy(
                weight_ref.at[span, pl.ds(offset, width)], buffer.at[k], sems.at[0, k]
            )
        ]
        if fetch_rows:
            need.append(
                pltpu.make_async_copy(
                    rows_in_ref.at[:, span], rows_ref.at[:, span], sems.at[1, k]
                )
            )
        copies.append(need)
    for need in copies:
        for copy in need:
            copy.start()
    for k, need in enumerate(copies):
        for copy in need:
            copy.wait()
        rows = rows_ref[:, k * step : (k + 1) * step]
        part = jnp.dot(rows, buffer[k], preferred_element_type=F32)
        if k == 0:
            out_ref[...] = part
        else:
            out_ref[...] += part


def base_call(side, fetch_rows, rows, weight):
    count, depth = rows.shape
    width = weight.shape[1] // 2
    steps = 4
    out = (jax.ShapeDtypeStruct((count, width), F32),)
    if fetch_rows:
        out += (jax.ShapeDtypeStruct(rows.shape, rows.dtype),)
    return pl.pallas_call(
        functools.partial(base_kernel, side, fetch_rows),
        out_shape=out,
        in_specs=[HBM if fetch_rows else VMEM, HBM],
        out_specs=(VMEM,) * len(out),
        scratch_shapes=[
            pltpu.VMEM((steps, depth // steps, width), weight.dtype),
            pltpu.SemaphoreType.DMA((2, steps)),
        ],
        compiler_params=params(),
        cost_estimate=HALF,
    )(in_hbm(rows) if fetch_rows else rows, in_hbm(weight))


def group_mask(low, high, shape):
    row = lax.broadcasted_iota(I32, shape, 0)
    return (row >= low) & (row < high)


def own_ends(bounds_ref, group, size):
    columns = slice(group * size, (group + 1) * size)
    return bounds_ref[0:1, columns], bounds_ref[1:2, columns]


def other_ends(other_ref, extra, group, size):
    ends = other_ref[-extra:, :].astype(F32).astype(I32)
    lines = range(group * size // 128, (group + 1) * size // 128)
    low = jnp.concatenate([ends[i : i + 1] for i in lines], axis=1)
    high = jnp.concatenate([ends[extra // 2 + i : extra // 2 + i + 1] for i in lines], axis=1)
    return low, high


def fold(masked):
    total = masked[:, :128]
    for begin in range(128, masked.shape[1], 128):
        total = total + masked[:, begin : begin + 128]
    return total


def rank_kernel(groups, depth, last, *refs):
    refs = list(refs)
    own_ref, other_ref, bounds_ref = refs[:3]
    shards, rest = refs[3 : 3 + GROUP * len(groups)], refs[3 + GROUP * len(groups) :]
    starts, outs = (rest[:2], rest[2:]) if last else ((None, None), rest)
    offset = pl.multiple_of(lax.axis_index("groups") * depth, 128)
    own = own_ref[:, pl.ds(offset, depth)]
    count = own.shape[0]
    other = jnp.concatenate(
        [other_ref[i * count : (i + 1) * count, :] for i in range(depth // 128)], axis=1
    )
    rank = shards[0].shape[0]
    size = GROUP * rank
    extra = extra_rows(bounds_ref.shape[1])
    totals = [start_ref[...] if last else None for start_ref in starts]
    for i, group in enumerate(groups):
        held = shards[GROUP * i : GROUP * (i + 1)]
        factor = jnp.concatenate([ref[:, :depth] for ref in held], axis=0)
        ends = (own_ends(bounds_ref, group, size), other_ends(other_ref, extra, group, size))
        for s, rows in enumerate((own, other)):
            part = contract(rows, factor)
            kept = fold(jnp.where(group_mask(*ends[s], part.shape), part, 0.0))
            totals[s] = kept if totals[s] is None else totals[s] + kept
    for total, out_ref in zip(totals, outs):
        if last:
            total = total + pltpu.roll(total, rank, 1)
            half = total.shape[0] // 2
            lane = lax.broadcasted_iota(I32, (half, 2 * rank), 1)
            total = jnp.where(lane < rank, total[:half], total[half:])
        out_ref[...] = total


def rank_call(groups, depth, own, other, bounds, shards, starts):
    rows = own.shape[0]
    rank = shards[0].shape[0]
    last = starts is not None
    shape = (rows // 2, 2 * rank) if last else (rows, 2 * rank)
    out = jax.ShapeDtypeStruct(shape, F32)
    operands = [own, other, bounds, *shards, *(starts or ())]
    return pl.pallas_call(
        functools.partial(rank_kernel, groups, depth, last),
        out_shape=(out, out),
        in_specs=[VMEM] * len(operands),
        out_specs=(VMEM, VMEM),
        compiler_params=params(),
        cost_estimate=LONG,
    )(*operands)


def final_kernel(bounds_ref, mine, one, two, three, near_ref, far_ref, *refs):
    factors, out_ref = refs[:-1], refs[-1]
    rank, width = factors[0].shape[0], out_ref.shape[1]
    begin = factors[0].shape[1] - width
    packed = (mine[...] + one[...]) + (two[...] + three[...])
    turned = pltpu.roll(packed, rank, 1)
    lane = lax.broadcasted_iota(I32, packed.shape, 1)
    values = jnp.concatenate(
        [jnp.where(lane < rank, packed, turned), jnp.where(lane < rank, turned, packed)], axis=0
    )
    wide = jnp.concatenate([values] * (GROUP // 2), axis=1)
    total = None
    for group in range(len(factors) // GROUP):
        mask = group_mask(*own_ends(bounds_ref, group, GROUP * rank), wide.shape)
        chosen = jnp.where(mask, wide, 0.0).astype(BF16)
        factor = jnp.concatenate(
            [ref[:, begin:] for ref in factors[group * GROUP : (group + 1) * GROUP]], axis=0
        )
        part = jnp.dot(chosen, factor, preferred_element_type=F32)
        total = part if total is None else total + part
    adapted = total.astype(BF16).astype(F32)
    out_ref[...] = ((near_ref[...] + far_ref[...]) + adapted).astype(BF16)


def per_device(hidden, demand, lengths, holder_slot, value_weight, factor_in, factor_out):
    rows, features = hidden.shape
    owners = lax.axis_size("batch")
    rank, width = factor_out.shape[1:]
    depth = features // 2
    order = ring_order(owners)
    ring = [(order[i], order[(i + 1) % owners]) for i in range(owners)]
    chain = [
        [(2 * a + core, 2 * b + core) if core == side else (2 * b + core, 2 * a + core)
         for a, b in ring for core in (0, 1)]
        for side in (0, 1)
    ]
    swap = [(0, 1), (1, 0)]

    def hop(side, shard):
        return lax.ppermute(shard, ("batch", "tensor"), chain[side])

    full = (owners - 1) // 2
    distances = [0]
    for step in range(1, full + 1):
        distances += [step, -step]
    distances.append(owners // 2)
    table = [
        [[order[(order.index(me) - sign * distance) % owners] for distance in distances]]
        for me in range(owners)
        for sign in (1, -1)
    ]
    to_other, shard, bounds = prologue(
        hidden,
        factor_in[0].T,
        factor_out[0],
        demand,
        lengths,
        holder_slot,
        jnp.asarray(table, I32),
    )

    far, held = base_call(1, True, hidden, value_weight)
    shards = [shard]
    x = y = shard
    for step in range(1, full + 1):
        x, y = hop(0, x), hop(1, y)
        if step == 1:
            x, far = lax.optimization_barrier((x, far))
            (near,) = base_call(0, False, held, value_weight)
            y, near = lax.optimization_barrier((y, near))
        shards += [x, y]
    shards.append(hop(0, x))
    other = lax.ppermute(to_other, "groups", swap)

    count = owners // GROUP
    early = range(count - 1)
    sides = (held, other, bounds)
    starts = rank_call(tuple(early), depth, *sides, shards[:-GROUP], None)
    *starts, far = lax.optimization_barrier((*starts, far))
    far = lax.ppermute(far, "tensor", swap)
    mine, theirs = rank_call((count - 1,), depth, *sides, shards[-GROUP:], starts)

    two = lax.ppermute(theirs, "groups", swap)
    one = lax.ppermute(mine, "tensor", swap)
    three = lax.ppermute(two, "tensor", swap)

    operands = [bounds, mine, one, two, three, near, far, *shards]
    return pl.pallas_call(
        final_kernel,
        out_shape=jax.ShapeDtypeStruct((rows, width), BF16),
        in_specs=[VMEM] * len(operands),
        out_specs=VMEM,
        compiler_params=params(),
    )(*operands)


def solution(mesh):
    return jax.shard_map(
        per_device,
        mesh=mesh,
        in_specs=(
            P(("groups", "batch"), "tensor"),
            P(("groups", "batch"), None),
            P(("groups", "batch"), None),
            P(),
            P("tensor", None),
            P("batch", "tensor", None),
            P("batch", None, "tensor"),
        ),
        out_specs=P(("groups", "batch"), "tensor"),
        check_vma=False,
    )
```

```python
import functools

import jax
import jax.numpy as jnp
from jax import lax
from jax.experimental import pallas as pl
from jax.experimental.pallas import tpu as pltpu
from jax.sharding import PartitionSpec as P

F32, BF16, I32 = jnp.float32, jnp.bfloat16, jnp.int32
VMEM_LIMIT = 40 * 1024 * 1024
HALF = pl.CostEstimate(flops=0, bytes_accessed=1 << 22, transcendentals=0)
LONG = pl.CostEstimate(flops=1 << 33, bytes_accessed=1 << 24, transcendentals=0)
GROUP = 4
VMEM = pl.BlockSpec(memory_space=pltpu.VMEM)
HBM = pl.BlockSpec(memory_space=pltpu.HBM)


def in_hbm(array):
    return pltpu.with_memory_space_constraint(array, pltpu.HBM)


def params():
    return pltpu.CompilerParams(vmem_limit_bytes=VMEM_LIMIT)


def ring_order(size):
    if size % 4:
        return list(range(size))
    columns = size // 4
    order = [0]
    for row in range(4):
        across = range(1, columns) if row % 2 == 0 else range(columns - 1, 0, -1)
        order += [row * columns + column for column in across]
    return order + [row * columns for row in (3, 2, 1)]


def contract(left, right):
    return lax.dot_general(left, right, (((1,), (1,)), ((), ())), preferred_element_type=F32)


def extra_rows(columns):
    return 2 * -(-columns // 1024) * 8


def prologue_kernel(
    depth,
    rank,
    hidden_ref,
    factor_ref,
    factor_out_ref,
    demand_ref,
    lengths_ref,
    holder_ref,
    slots_ref,
    to_other_ref,
    first_ref,
    second_ref,
    bounds_ref,
    demand,
    lengths,
    holder,
    slots,
    sems,
    hidden_sem,
):
    group, place = lax.axis_index("groups"), lax.axis_index("batch")
    cut = first_ref.shape[1]
    rows = hidden_ref.shape[0]
    here = pl.multiple_of(group * depth, 128)
    there = pl.multiple_of((1 - group) * depth, 128)
    after = pl.multiple_of(group * depth + cut, 128)
    small = [
        pltpu.make_async_copy(demand_ref, demand, sems.at[0]),
        pltpu.make_async_copy(lengths_ref, lengths, sems.at[1]),
        pltpu.make_async_copy(holder_ref, holder, sems.at[2]),
        pltpu.make_async_copy(slots_ref.at[pl.ds(place, 1)], slots, sems.at[3]),
    ]
    large = [
        pltpu.make_async_copy(factor_ref.at[:, pl.ds(here, cut)], first_ref, sems.at[4]),
        pltpu.make_async_copy(
            factor_ref.at[:, pl.ds(after, depth - cut)], second_ref.at[:, : depth - cut], sems.at[5]
        ),
        pltpu.make_async_copy(factor_out_ref, second_ref.at[:, depth - cut :], sems.at[6]),
    ]
    for i in range(depth // 128):
        large.append(
            pltpu.make_async_copy(
                hidden_ref.at[:, pl.ds(there + i * 128, 128)],
                to_other_ref.at[i * rows : (i + 1) * rows],
                hidden_sem.at[i],
            )
        )
    for copy in small + large:
        copy.start()
    for copy in small:
        copy.wait()
    count = slots.shape[2]
    items = demand.shape[1]
    column = lax.broadcasted_iota(I32, (1, count * rank), 1)
    zero = jnp.int32(0)

    def chunk_mask(chunk):
        return (column >= chunk * rank) & (column < (chunk + 1) * rank)

    low = high = jnp.zeros((1, count * rank), I32)
    if items * count <= 64:
        start = zero
        spans = []
        for item in range(items):
            end = start + lengths[0, item]
            spans.append((holder[demand[0, item]], start, end))
            start = end
        for chunk in range(count):
            slot = slots[0, 0, chunk]
            begin = end = zero
            for owner, first, last in spans:
                begin = jnp.where(owner == slot, first, begin)
                end = jnp.where(owner == slot, last, end)
            low = jnp.where(chunk_mask(chunk), begin, low)
            high = jnp.where(chunk_mask(chunk), end, high)
    else:

        def chunk_ends(chunk, carry):
            low, high = carry
            slot = slots[0, 0, chunk]

            def item_ends(item, state):
                start, begin, end = state
                last = start + lengths[0, item]
                hit = holder[demand[0, item]] == slot
                return last, jnp.where(hit, start, begin), jnp.where(hit, last, end)

            _, begin, end = lax.fori_loop(0, items, item_ends, (zero, zero, zero))
            mask = chunk_mask(chunk)
            return jnp.where(mask, begin, low), jnp.where(mask, end, high)

        low, high = lax.fori_loop(0, count, chunk_ends, (low, high))
    bounds_ref[0:1, :] = low
    bounds_ref[1:2, :] = high
    bounds_ref[2:8, :] = jnp.zeros((6, count * rank), I32)
    extra = extra_rows(count * rank)
    line = lax.broadcasted_iota(I32, (extra, 128), 0)
    ends = jnp.zeros((extra, 128), I32)
    for i in range(count * rank // 128):
        columns = slice(i * 128, (i + 1) * 128)
        ends = jnp.where(line == i, low[:, columns], ends)
        ends = jnp.where(line == extra // 2 + i, high[:, columns], ends)
    to_other_ref[-extra:, :] = ends.astype(F32).astype(BF16)
    for copy in large:
        copy.wait()


def prologue(hidden, factor, factor_out, demand, lengths, holder_slot, slots):
    rows, features = hidden.shape
    rank, width = factor_out.shape
    depth = features // 2
    cut = (depth + width) // 2
    count = slots.shape[2]
    tall = depth // 128 * rows + extra_rows(count * rank)
    return pl.pallas_call(
        functools.partial(prologue_kernel, depth, rank),
        out_shape=(
            jax.ShapeDtypeStruct((tall, 128), hidden.dtype),
            jax.ShapeDtypeStruct((rank, cut), factor.dtype),
            jax.ShapeDtypeStruct((rank, cut), factor.dtype),
            jax.ShapeDtypeStruct((8, count * rank), I32),
        ),
        in_specs=[HBM] * 7,
        out_specs=(VMEM,) * 4,
        scratch_shapes=[
            pltpu.SMEM(demand.shape, I32),
            pltpu.SMEM(lengths.shape, I32),
            pltpu.SMEM(holder_slot.shape, I32),
            pltpu.SMEM((1, 1, count), I32),
            pltpu.SemaphoreType.DMA((7,)),
            pltpu.SemaphoreType.DMA((depth // 128,)),
        ],
        compiler_params=params(),
    )(*map(in_hbm, (hidden, factor, factor_out, demand, lengths, holder_slot, slots)))


def mark_kernel(bounds_ref, out_ref):
    out_ref[...] = bounds_ref[...]


def mark(bounds):
    return pl.pallas_call(
        mark_kernel,
        out_shape=jax.ShapeDtypeStruct(bounds.shape, bounds.dtype),
        in_specs=[VMEM],
        out_specs=VMEM,
        cost_estimate=LONG,
    )(bounds)


def base_kernel(rows_ref, weight_ref, near_ref, far_ref):
    width = near_ref.shape[1]
    core = lax.axis_index("tensor")
    for out_ref, side in ((near_ref, core), (far_ref, 1 - core)):
        columns = pl.ds(pl.multiple_of(side * width, 128), width)
        out_ref[...] = jnp.dot(
            rows_ref[...], weight_ref[:, columns], preferred_element_type=F32
        )


def base_call(rows, weight):
    out = jax.ShapeDtypeStruct((rows.shape[0], weight.shape[1] // 2), F32)
    return pl.pallas_call(
        base_kernel,
        out_shape=(out, out),
        in_specs=[VMEM] * 2,
        out_specs=(VMEM,) * 2,
        compiler_params=params(),
        cost_estimate=HALF,
    )(rows, weight)


def group_mask(low, high, shape):
    row = lax.broadcasted_iota(I32, shape, 0)
    return (row >= low) & (row < high)


def own_ends(bounds_ref, group, size):
    columns = slice(group * size, (group + 1) * size)
    return bounds_ref[0:1, columns], bounds_ref[1:2, columns]


def other_ends(other_ref, extra, group, size):
    ends = other_ref[-extra:, :].astype(F32).astype(I32)
    lines = range(group * size // 128, (group + 1) * size // 128)
    low = jnp.concatenate([ends[i : i + 1] for i in lines], axis=1)
    high = jnp.concatenate([ends[extra // 2 + i : extra // 2 + i + 1] for i in lines], axis=1)
    return low, high


def fold(masked):
    total = masked[:, :128]
    for begin in range(128, masked.shape[1], 128):
        total = total + masked[:, begin : begin + 128]
    return total


def rank_kernel(groups, depth, last, *refs):
    refs = list(refs)
    own_ref, other_ref, bounds_ref = refs[:3]
    pieces = refs[3:]
    pieces, rest = pieces[: 2 * GROUP * len(groups)], pieces[2 * GROUP * len(groups) :]
    starts, outs = (rest[:2], rest[2:]) if last else ((None, None), rest)
    cut = pieces[0].shape[1]
    offset = pl.multiple_of(lax.axis_index("groups") * depth, 128)
    own = own_ref[:, pl.ds(offset, depth)]
    count = own.shape[0]
    other = jnp.concatenate(
        [other_ref[i * count : (i + 1) * count, :] for i in range(depth // 128)], axis=1
    )
    rank = pieces[0].shape[0]
    size = GROUP * rank
    extra = extra_rows(bounds_ref.shape[1])
    totals = [start_ref[...] if last else None for start_ref in starts]
    for i, group in enumerate(groups):
        held = pieces[2 * GROUP * i : 2 * GROUP * (i + 1)]
        first = jnp.concatenate([ref[...] for ref in held[:GROUP]], axis=0)
        second = jnp.concatenate([ref[:, : depth - cut] for ref in held[GROUP:]], axis=0)
        ends = (own_ends(bounds_ref, group, size), other_ends(other_ref, extra, group, size))
        for s, rows in enumerate((own, other)):
            part = contract(rows[:, :cut], first) + contract(rows[:, cut:], second)
            kept = fold(jnp.where(group_mask(*ends[s], part.shape), part, 0.0))
            totals[s] = kept if totals[s] is None else totals[s] + kept
    for total, out_ref in zip(totals, outs):
        if last:
            total = total + pltpu.roll(total, rank, 1)
            half = total.shape[0] // 2
            lane = lax.broadcasted_iota(I32, (half, 2 * rank), 1)
            total = jnp.where(lane < rank, total[:half], total[half:])
        out_ref[...] = total


def rank_call(groups, depth, own, other, bounds, pieces, starts):
    rows = own.shape[0]
    rank = pieces[0].shape[0]
    last = starts is not None
    shape = (rows // 2, 2 * rank) if last else (rows, 2 * rank)
    out = jax.ShapeDtypeStruct(shape, F32)
    operands = [own, other, bounds, *pieces, *(starts or ())]
    return pl.pallas_call(
        functools.partial(rank_kernel, groups, depth, last),
        out_shape=(out, out),
        in_specs=[VMEM] * len(operands),
        out_specs=(VMEM, VMEM),
        compiler_params=params(),
        cost_estimate=LONG,
    )(*operands)


def final_kernel(bounds_ref, mine, one, two, three, near_ref, far_ref, *refs):
    factors, out_ref = refs[:-1], refs[-1]
    rank, width = factors[0].shape[0], out_ref.shape[1]
    begin = factors[0].shape[1] - width
    packed = (mine[...] + one[...]) + (two[...] + three[...])
    turned = pltpu.roll(packed, rank, 1)
    lane = lax.broadcasted_iota(I32, packed.shape, 1)
    values = jnp.concatenate(
        [jnp.where(lane < rank, packed, turned), jnp.where(lane < rank, turned, packed)], axis=0
    )
    wide = jnp.concatenate([values] * (GROUP // 2), axis=1)
    total = None
    for group in range(len(factors) // GROUP):
        mask = group_mask(*own_ends(bounds_ref, group, GROUP * rank), wide.shape)
        chosen = jnp.where(mask, wide, 0.0).astype(BF16)
        factor = jnp.concatenate(
            [ref[:, begin:] for ref in factors[group * GROUP : (group + 1) * GROUP]], axis=0
        )
        part = jnp.dot(chosen, factor, preferred_element_type=F32)
        total = part if total is None else total + part
    adapted = total.astype(BF16).astype(F32)
    out_ref[...] = ((near_ref[...] + far_ref[...]) + adapted).astype(BF16)


def per_device(hidden, demand, lengths, holder_slot, value_weight, factor_in, factor_out):
    rows, features = hidden.shape
    owners = lax.axis_size("batch")
    rank, width = factor_out.shape[1:]
    depth = features // 2
    order = ring_order(owners)
    forward = [(order[i], order[(i + 1) % owners]) for i in range(owners)]
    backward = [(b, a) for a, b in forward]
    swap = [(0, 1), (1, 0)]

    full = (owners - 1) // 2
    distances = [0]
    for step in range(1, full + 1):
        distances += [step, -step]
    distances.append(owners // 2)
    table = [
        [[order[(order.index(me) - distance) % owners] for distance in distances]]
        for me in range(owners)
    ]
    to_other, first, second, bounds = prologue(
        hidden,
        factor_in[0].T,
        factor_out[0],
        demand,
        lengths,
        holder_slot,
        jnp.asarray(table, I32),
    )

    bounds, first, second = lax.optimization_barrier((mark(bounds), first, second))

    near, far = base_call(hidden, value_weight)
    firsts, seconds = [first], [second]
    ahead, behind = (first, second), (first, second)
    for step in range(1, full + 1):
        a = lax.ppermute(ahead[0], "batch", forward)
        d = lax.ppermute(behind[1], "batch", backward)
        b = lax.ppermute(ahead[1], "batch", forward)
        c = lax.ppermute(behind[0], "batch", backward)
        if step == 1:
            a, far = lax.optimization_barrier((a, far))
        ahead, behind = (a, b), (c, d)
        firsts += [a, c]
        seconds += [b, d]
    firsts.append(lax.ppermute(ahead[0], "batch", forward))
    seconds.append(lax.ppermute(behind[1], "batch", backward))
    other = lax.ppermute(to_other, "groups", swap)

    count = owners // GROUP
    early = range(count - 1)
    pieces = []
    for group in early:
        pieces += firsts[group * GROUP : (group + 1) * GROUP]
        pieces += seconds[group * GROUP : (group + 1) * GROUP]
    sides = (hidden, other, bounds)
    starts = rank_call(tuple(early), depth, *sides, pieces, None)
    *starts, far = lax.optimization_barrier((*starts, far))
    far = lax.ppermute(far, "tensor", swap)
    pieces = firsts[-GROUP:] + seconds[-GROUP:]
    mine, theirs = rank_call((count - 1,), depth, *sides, pieces, starts)

    two = lax.ppermute(theirs, "groups", swap)
    one = lax.ppermute(mine, "tensor", swap)
    three = lax.ppermute(two, "tensor", swap)

    operands = [bounds, mine, one, two, three, near, far, *seconds]
    return pl.pallas_call(
        final_kernel,
        out_shape=jax.ShapeDtypeStruct((rows, width), BF16),
        in_specs=[VMEM] * len(operands),
        out_specs=VMEM,
        compiler_params=params(),
    )(*operands)


def solution(mesh):
    return jax.shard_map(
        per_device,
        mesh=mesh,
        in_specs=(
            P(("groups", "batch"), "tensor"),
            P(("groups", "batch"), None),
            P(("groups", "batch"), None),
            P(),
            P("tensor", None),
            P("batch", "tensor", None),
            P("batch", None, "tensor"),
        ),
        out_specs=P(("groups", "batch"), "tensor"),
        check_vma=False,
    )
```

```python
import functools

import jax
import jax.numpy as jnp
from jax import lax
from jax.experimental import pallas as pl
from jax.experimental.pallas import tpu as pltpu
from jax.sharding import PartitionSpec as P

F32, BF16, I32 = jnp.float32, jnp.bfloat16, jnp.int32
VMEM_LIMIT = 24 * 1024 * 1024
HALF = pl.CostEstimate(flops=0, bytes_accessed=1 << 22, transcendentals=0)
LONG = pl.CostEstimate(flops=1 << 33, bytes_accessed=1 << 24, transcendentals=0)
GROUP = 4
VMEM = pl.BlockSpec(memory_space=pltpu.VMEM)
HBM = pl.BlockSpec(memory_space=pltpu.HBM)


def in_hbm(array):
    return pltpu.with_memory_space_constraint(array, pltpu.HBM)


def params():
    return pltpu.CompilerParams(vmem_limit_bytes=VMEM_LIMIT)


def ring_order(size):
    if size % 4:
        return list(range(size))
    columns = size // 4
    order = [0]
    for row in range(4):
        across = range(1, columns) if row % 2 == 0 else range(columns - 1, 0, -1)
        order += [row * columns + column for column in across]
    return order + [row * columns for row in (3, 2, 1)]


def contract(left, right):
    return lax.dot_general(left, right, (((1,), (1,)), ((), ())), preferred_element_type=F32)


def extra_rows(columns):
    return 2 * -(-columns // 1024) * 8


def prologue_kernel(
    depth,
    rank,
    hidden_ref,
    factor_ref,
    factor_out_ref,
    demand_ref,
    lengths_ref,
    holder_ref,
    slots_ref,
    to_other_ref,
    first_ref,
    second_ref,
    bounds_ref,
    demand,
    lengths,
    holder,
    slots,
    sems,
    hidden_sem,
):
    group, place = lax.axis_index("groups"), lax.axis_index("batch")
    cut = first_ref.shape[1]
    rows = hidden_ref.shape[0]
    here = pl.multiple_of(group * depth, 128)
    there = pl.multiple_of((1 - group) * depth, 128)
    after = pl.multiple_of(group * depth + cut, 128)
    small = [
        pltpu.make_async_copy(demand_ref, demand, sems.at[0]),
        pltpu.make_async_copy(lengths_ref, lengths, sems.at[1]),
        pltpu.make_async_copy(holder_ref, holder, sems.at[2]),
        pltpu.make_async_copy(slots_ref.at[pl.ds(place, 1)], slots, sems.at[3]),
    ]
    large = [
        pltpu.make_async_copy(factor_ref.at[:, pl.ds(here, cut)], first_ref, sems.at[4]),
        pltpu.make_async_copy(
            factor_ref.at[:, pl.ds(after, depth - cut)], second_ref.at[:, : depth - cut], sems.at[5]
        ),
        pltpu.make_async_copy(factor_out_ref, second_ref.at[:, depth - cut :], sems.at[6]),
    ]
    for i in range(depth // 128):
        large.append(
            pltpu.make_async_copy(
                hidden_ref.at[:, pl.ds(there + i * 128, 128)],
                to_other_ref.at[i * rows : (i + 1) * rows],
                hidden_sem.at[i],
            )
        )
    for copy in small + large:
        copy.start()
    for copy in small:
        copy.wait()
    count = slots.shape[2]
    items = demand.shape[1]
    column = lax.broadcasted_iota(I32, (1, count * rank), 1)
    zero = jnp.int32(0)

    def chunk_mask(chunk):
        return (column >= chunk * rank) & (column < (chunk + 1) * rank)

    low = high = jnp.zeros((1, count * rank), I32)
    if items * count <= 64:
        start = zero
        spans = []
        for item in range(items):
            end = start + lengths[0, item]
            spans.append((holder[demand[0, item]], start, end))
            start = end
        for chunk in range(count):
            slot = slots[0, 0, chunk]
            begin = end = zero
            for owner, first, last in spans:
                begin = jnp.where(owner == slot, first, begin)
                end = jnp.where(owner == slot, last, end)
            low = jnp.where(chunk_mask(chunk), begin, low)
            high = jnp.where(chunk_mask(chunk), end, high)
    else:

        def chunk_ends(chunk, carry):
            low, high = carry
            slot = slots[0, 0, chunk]

            def item_ends(item, state):
                start, begin, end = state
                last = start + lengths[0, item]
                hit = holder[demand[0, item]] == slot
                return last, jnp.where(hit, start, begin), jnp.where(hit, last, end)

            _, begin, end = lax.fori_loop(0, items, item_ends, (zero, zero, zero))
            mask = chunk_mask(chunk)
            return jnp.where(mask, begin, low), jnp.where(mask, end, high)

        low, high = lax.fori_loop(0, count, chunk_ends, (low, high))
    bounds_ref[0:1, :] = low
    bounds_ref[1:2, :] = high
    bounds_ref[2:8, :] = jnp.zeros((6, count * rank), I32)
    extra = extra_rows(count * rank)
    line = lax.broadcasted_iota(I32, (extra, 128), 0)
    ends = jnp.zeros((extra, 128), I32)
    for i in range(count * rank // 128):
        columns = slice(i * 128, (i + 1) * 128)
        ends = jnp.where(line == i, low[:, columns], ends)
        ends = jnp.where(line == extra // 2 + i, high[:, columns], ends)
    to_other_ref[-extra:, :] = ends.astype(F32).astype(BF16)
    for copy in large:
        copy.wait()


def prologue(hidden, factor, factor_out, demand, lengths, holder_slot, slots):
    rows, features = hidden.shape
    rank, width = factor_out.shape
    depth = features // 2
    cut = (depth + width) // 2
    count = slots.shape[2]
    tall = depth // 128 * rows + extra_rows(count * rank)
    return pl.pallas_call(
        functools.partial(prologue_kernel, depth, rank),
        out_shape=(
            jax.ShapeDtypeStruct((tall, 128), hidden.dtype),
            jax.ShapeDtypeStruct((rank, cut), factor.dtype),
            jax.ShapeDtypeStruct((rank, cut), factor.dtype),
            jax.ShapeDtypeStruct((8, count * rank), I32),
        ),
        in_specs=[HBM] * 7,
        out_specs=(VMEM,) * 4,
        scratch_shapes=[
            pltpu.SMEM(demand.shape, I32),
            pltpu.SMEM(lengths.shape, I32),
            pltpu.SMEM(holder_slot.shape, I32),
            pltpu.SMEM((1, 1, count), I32),
            pltpu.SemaphoreType.DMA((7,)),
            pltpu.SemaphoreType.DMA((depth // 128,)),
        ],
        compiler_params=params(),
    )(*map(in_hbm, (hidden, factor, factor_out, demand, lengths, holder_slot, slots)))


def mark_kernel(bounds_ref, out_ref):
    out_ref[...] = bounds_ref[...]


def mark(bounds):
    return pl.pallas_call(
        mark_kernel,
        out_shape=jax.ShapeDtypeStruct(bounds.shape, bounds.dtype),
        in_specs=[VMEM],
        out_specs=VMEM,
        compiler_params=params(),
        cost_estimate=LONG,
    )(bounds)


def base_kernel(rows_ref, weight_ref, near_ref, far_ref):
    width = near_ref.shape[1]
    core = lax.axis_index("tensor")
    for out_ref, side in ((near_ref, core), (far_ref, 1 - core)):
        columns = pl.ds(pl.multiple_of(side * width, 128), width)
        out_ref[...] = jnp.dot(
            rows_ref[...], weight_ref[:, columns], preferred_element_type=F32
        )


def base_call(rows, weight):
    out = jax.ShapeDtypeStruct((rows.shape[0], weight.shape[1] // 2), F32)
    return pl.pallas_call(
        base_kernel,
        out_shape=(out, out),
        in_specs=[VMEM] * 2,
        out_specs=(VMEM,) * 2,
        compiler_params=params(),
        cost_estimate=HALF,
    )(rows, weight)


def group_mask(low, high, shape):
    row = lax.broadcasted_iota(I32, shape, 0)
    return (row >= low) & (row < high)


def own_ends(bounds_ref, group, size):
    columns = slice(group * size, (group + 1) * size)
    return bounds_ref[0:1, columns], bounds_ref[1:2, columns]


def other_ends(other_ref, extra, group, size):
    ends = other_ref[-extra:, :].astype(F32).astype(I32)
    lines = range(group * size // 128, (group + 1) * size // 128)
    low = jnp.concatenate([ends[i : i + 1] for i in lines], axis=1)
    high = jnp.concatenate([ends[extra // 2 + i : extra // 2 + i + 1] for i in lines], axis=1)
    return low, high


def fold(masked):
    total = masked[:, :128]
    for begin in range(128, masked.shape[1], 128):
        total = total + masked[:, begin : begin + 128]
    return total


def rank_kernel(groups, depth, last, *refs):
    refs = list(refs)
    own_ref, other_ref, bounds_ref = refs[:3]
    pieces = refs[3:]
    pieces, rest = pieces[: 2 * GROUP * len(groups)], pieces[2 * GROUP * len(groups) :]
    starts, outs = (rest[:2], rest[2:]) if last else ((None, None), rest)
    cut = pieces[0].shape[1]
    offset = pl.multiple_of(lax.axis_index("groups") * depth, 128)
    own = own_ref[:, pl.ds(offset, depth)]
    count = own.shape[0]
    other = jnp.concatenate(
        [other_ref[i * count : (i + 1) * count, :] for i in range(depth // 128)], axis=1
    )
    rank = pieces[0].shape[0]
    size = GROUP * rank
    extra = extra_rows(bounds_ref.shape[1])
    totals = [start_ref[...] if last else None for start_ref in starts]
    for i, group in enumerate(groups):
        held = pieces[2 * GROUP * i : 2 * GROUP * (i + 1)]
        first = jnp.concatenate([ref[...] for ref in held[:GROUP]], axis=0)
        second = jnp.concatenate([ref[:, : depth - cut] for ref in held[GROUP:]], axis=0)
        ends = (own_ends(bounds_ref, group, size), other_ends(other_ref, extra, group, size))
        for s, rows in enumerate((own, other)):
            part = contract(rows[:, :cut], first) + contract(rows[:, cut:], second)
            kept = fold(jnp.where(group_mask(*ends[s], part.shape), part, 0.0))
            totals[s] = kept if totals[s] is None else totals[s] + kept
    for total, out_ref in zip(totals, outs):
        if last:
            total = total + pltpu.roll(total, rank, 1)
            half = total.shape[0] // 2
            lane = lax.broadcasted_iota(I32, (half, 2 * rank), 1)
            total = jnp.where(lane < rank, total[:half], total[half:])
        out_ref[...] = total


def rank_call(groups, depth, own, other, bounds, pieces, starts):
    rows = own.shape[0]
    rank = pieces[0].shape[0]
    last = starts is not None
    shape = (rows // 2, 2 * rank) if last else (rows, 2 * rank)
    out = jax.ShapeDtypeStruct(shape, F32)
    operands = [own, other, bounds, *pieces, *(starts or ())]
    return pl.pallas_call(
        functools.partial(rank_kernel, groups, depth, last),
        out_shape=(out, out),
        in_specs=[VMEM] * len(operands),
        out_specs=(VMEM, VMEM),
        compiler_params=params(),
        cost_estimate=LONG,
    )(*operands)


def final_kernel(bounds_ref, mine, one, two, three, near_ref, far_ref, *refs):
    factors, out_ref = refs[:-1], refs[-1]
    rank, width = factors[0].shape[0], out_ref.shape[1]
    begin = factors[0].shape[1] - width
    packed = (mine[...] + one[...]) + (two[...] + three[...])
    turned = pltpu.roll(packed, rank, 1)
    lane = lax.broadcasted_iota(I32, packed.shape, 1)
    values = jnp.concatenate(
        [jnp.where(lane < rank, packed, turned), jnp.where(lane < rank, turned, packed)], axis=0
    )
    wide = jnp.concatenate([values] * (GROUP // 2), axis=1)
    total = None
    for group in range(len(factors) // GROUP):
        mask = group_mask(*own_ends(bounds_ref, group, GROUP * rank), wide.shape)
        chosen = jnp.where(mask, wide, 0.0).astype(BF16)
        factor = jnp.concatenate(
            [ref[:, begin:] for ref in factors[group * GROUP : (group + 1) * GROUP]], axis=0
        )
        part = jnp.dot(chosen, factor, preferred_element_type=F32)
        total = part if total is None else total + part
    adapted = total.astype(BF16).astype(F32)
    out_ref[...] = ((near_ref[...] + far_ref[...]) + adapted).astype(BF16)


def per_device(hidden, demand, lengths, holder_slot, value_weight, factor_in, factor_out):
    rows, features = hidden.shape
    owners = lax.axis_size("batch")
    rank, width = factor_out.shape[1:]
    depth = features // 2
    order = ring_order(owners)
    forward = [(order[i], order[(i + 1) % owners]) for i in range(owners)]
    backward = [(b, a) for a, b in forward]
    swap = [(0, 1), (1, 0)]

    full = (owners - 1) // 2
    distances = [0]
    for step in range(1, full + 1):
        distances += [step, -step]
    distances.append(owners // 2)
    table = [
        [[order[(order.index(me) - distance) % owners] for distance in distances]]
        for me in range(owners)
    ]
    to_other, first, second, bounds = prologue(
        hidden,
        factor_in[0].T,
        factor_out[0],
        demand,
        lengths,
        holder_slot,
        jnp.asarray(table, I32),
    )

    bounds, first, second = lax.optimization_barrier((mark(bounds), first, second))

    near, far = base_call(hidden, value_weight)
    firsts, seconds = [first], [second]
    ahead, behind = (first, second), (first, second)
    for step in range(1, full + 1):
        a = lax.ppermute(ahead[0], "batch", forward)
        d = lax.ppermute(behind[1], "batch", backward)
        b = lax.ppermute(ahead[1], "batch", forward)
        c = lax.ppermute(behind[0], "batch", backward)
        if step == 1:
            a, far = lax.optimization_barrier((a, far))
        ahead, behind = (a, b), (c, d)
        firsts += [a, c]
        seconds += [b, d]
    firsts.append(lax.ppermute(ahead[0], "batch", forward))
    seconds.append(lax.ppermute(behind[1], "batch", backward))
    other = lax.ppermute(to_other, "groups", swap)

    count = owners // GROUP
    early = range(count - 1)
    pieces = []
    for group in early:
        pieces += firsts[group * GROUP : (group + 1) * GROUP]
        pieces += seconds[group * GROUP : (group + 1) * GROUP]
    sides = (hidden, other, bounds)
    starts = rank_call(tuple(early), depth, *sides, pieces, None)
    *starts, far = lax.optimization_barrier((*starts, far))
    far = lax.ppermute(far, "tensor", swap)
    pieces = firsts[-GROUP:] + seconds[-GROUP:]
    mine, theirs = rank_call((count - 1,), depth, *sides, pieces, starts)

    two = lax.ppermute(theirs, "groups", swap)
    one = lax.ppermute(mine, "tensor", swap)
    three = lax.ppermute(two, "tensor", swap)

    operands = [bounds, mine, one, two, three, near, far, *seconds]
    return pl.pallas_call(
        final_kernel,
        out_shape=jax.ShapeDtypeStruct((rows, width), BF16),
        in_specs=[VMEM] * len(operands),
        out_specs=VMEM,
        compiler_params=params(),
    )(*operands)


def solution(mesh):
    return jax.shard_map(
        per_device,
        mesh=mesh,
        in_specs=(
            P(("groups", "batch"), "tensor"),
            P(("groups", "batch"), None),
            P(("groups", "batch"), None),
            P(),
            P("tensor", None),
            P("batch", "tensor", None),
            P("batch", None, "tensor"),
        ),
        out_specs=P(("groups", "batch"), "tensor"),
        check_vma=False,
    )
```

```python
import functools

import jax
import jax.numpy as jnp
from jax import lax
from jax.experimental import pallas as pl
from jax.experimental.pallas import tpu as pltpu
from jax.sharding import PartitionSpec as P

F32, BF16, I32 = jnp.float32, jnp.bfloat16, jnp.int32
VMEM_LIMIT = 24 * 1024 * 1024
HALF = pl.CostEstimate(flops=0, bytes_accessed=1 << 22, transcendentals=0)
LONG = pl.CostEstimate(flops=1 << 33, bytes_accessed=1 << 24, transcendentals=0)
GROUP = 4
VMEM = pl.BlockSpec(memory_space=pltpu.VMEM)
HBM = pl.BlockSpec(memory_space=pltpu.HBM)


def in_hbm(array):
    return pltpu.with_memory_space_constraint(array, pltpu.HBM)


def params():
    return pltpu.CompilerParams(vmem_limit_bytes=VMEM_LIMIT)


def ring_order(size):
    if size % 4:
        return list(range(size))
    columns = size // 4
    order = [0]
    for row in range(4):
        across = range(1, columns) if row % 2 == 0 else range(columns - 1, 0, -1)
        order += [row * columns + column for column in across]
    return order + [row * columns for row in (3, 2, 1)]


def contract(left, right):
    return lax.dot_general(left, right, (((1,), (1,)), ((), ())), preferred_element_type=F32)


def extra_rows(columns):
    return 2 * -(-columns // 1024) * 8


def prologue_kernel(
    depth,
    rank,
    hidden_ref,
    factor_ref,
    factor_out_ref,
    demand_ref,
    lengths_ref,
    holder_ref,
    slots_ref,
    to_other_ref,
    first_ref,
    second_ref,
    bounds_ref,
    demand,
    lengths,
    holder,
    slots,
    sems,
    hidden_sem,
):
    group, place = lax.axis_index("groups"), lax.axis_index("batch")
    cut = first_ref.shape[1]
    rows = hidden_ref.shape[0]
    here = pl.multiple_of(group * depth, 128)
    there = pl.multiple_of((1 - group) * depth, 128)
    after = pl.multiple_of(group * depth + cut, 128)
    small = [
        pltpu.make_async_copy(demand_ref, demand, sems.at[0]),
        pltpu.make_async_copy(lengths_ref, lengths, sems.at[1]),
        pltpu.make_async_copy(holder_ref, holder, sems.at[2]),
        pltpu.make_async_copy(slots_ref.at[pl.ds(place, 1)], slots, sems.at[3]),
    ]
    large = [
        pltpu.make_async_copy(factor_ref.at[:, pl.ds(here, cut)], first_ref, sems.at[4]),
        pltpu.make_async_copy(
            factor_ref.at[:, pl.ds(after, depth - cut)], second_ref.at[:, : depth - cut], sems.at[5]
        ),
        pltpu.make_async_copy(factor_out_ref, second_ref.at[:, depth - cut :], sems.at[6]),
    ]
    for i in range(depth // 128):
        large.append(
            pltpu.make_async_copy(
                hidden_ref.at[:, pl.ds(there + i * 128, 128)],
                to_other_ref.at[i * rows : (i + 1) * rows],
                hidden_sem.at[i],
            )
        )
    for copy in small + large:
        copy.start()
    for copy in small:
        copy.wait()
    count = slots.shape[2]
    items = demand.shape[1]
    column = lax.broadcasted_iota(I32, (1, count * rank), 1)
    zero = jnp.int32(0)

    def chunk_mask(chunk):
        return (column >= chunk * rank) & (column < (chunk + 1) * rank)

    low = high = jnp.zeros((1, count * rank), I32)
    if items * count <= 64:
        start = zero
        spans = []
        for item in range(items):
            end = start + lengths[0, item]
            spans.append((holder[demand[0, item]], start, end))
            start = end
        for chunk in range(count):
            slot = slots[0, 0, chunk]
            begin = end = zero
            for owner, first, last in spans:
                begin = jnp.where(owner == slot, first, begin)
                end = jnp.where(owner == slot, last, end)
            low = jnp.where(chunk_mask(chunk), begin, low)
            high = jnp.where(chunk_mask(chunk), end, high)
    else:

        def chunk_ends(chunk, carry):
            low, high = carry
            slot = slots[0, 0, chunk]

            def item_ends(item, state):
                start, begin, end = state
                last = start + lengths[0, item]
                hit = holder[demand[0, item]] == slot
                return last, jnp.where(hit, start, begin), jnp.where(hit, last, end)

            _, begin, end = lax.fori_loop(0, items, item_ends, (zero, zero, zero))
            mask = chunk_mask(chunk)
            return jnp.where(mask, begin, low), jnp.where(mask, end, high)

        low, high = lax.fori_loop(0, count, chunk_ends, (low, high))
    bounds_ref[0:1, :] = low
    bounds_ref[1:2, :] = high
    bounds_ref[2:8, :] = jnp.zeros((6, count * rank), I32)
    extra = extra_rows(count * rank)
    line = lax.broadcasted_iota(I32, (extra, 128), 0)
    ends = jnp.zeros((extra, 128), I32)
    for i in range(count * rank // 128):
        columns = slice(i * 128, (i + 1) * 128)
        ends = jnp.where(line == i, low[:, columns], ends)
        ends = jnp.where(line == extra // 2 + i, high[:, columns], ends)
    to_other_ref[-extra:, :] = ends.astype(F32).astype(BF16)
    for copy in large:
        copy.wait()


def prologue(hidden, factor, factor_out, demand, lengths, holder_slot, slots):
    rows, features = hidden.shape
    rank, width = factor_out.shape
    depth = features // 2
    cut = (depth + width) // 2
    count = slots.shape[2]
    tall = depth // 128 * rows + extra_rows(count * rank)
    return pl.pallas_call(
        functools.partial(prologue_kernel, depth, rank),
        out_shape=(
            jax.ShapeDtypeStruct((tall, 128), hidden.dtype),
            jax.ShapeDtypeStruct((rank, cut), factor.dtype),
            jax.ShapeDtypeStruct((rank, cut), factor.dtype),
            jax.ShapeDtypeStruct((8, count * rank), I32),
        ),
        in_specs=[HBM] * 7,
        out_specs=(VMEM,) * 4,
        scratch_shapes=[
            pltpu.SMEM(demand.shape, I32),
            pltpu.SMEM(lengths.shape, I32),
            pltpu.SMEM(holder_slot.shape, I32),
            pltpu.SMEM((1, 1, count), I32),
            pltpu.SemaphoreType.DMA((7,)),
            pltpu.SemaphoreType.DMA((depth // 128,)),
        ],
        compiler_params=params(),
    )(*map(in_hbm, (hidden, factor, factor_out, demand, lengths, holder_slot, slots)))


def mark_kernel(bounds_ref, out_ref):
    out_ref[...] = bounds_ref[...]


def mark(bounds):
    return pl.pallas_call(
        mark_kernel,
        out_shape=jax.ShapeDtypeStruct(bounds.shape, bounds.dtype),
        in_specs=[VMEM],
        out_specs=VMEM,
        compiler_params=params(),
        cost_estimate=LONG,
    )(bounds)


def base_kernel(rows_ref, weight_ref, near_ref, far_ref):
    width = near_ref.shape[1]
    core = lax.axis_index("tensor")
    for out_ref, side in ((near_ref, core), (far_ref, 1 - core)):
        columns = pl.ds(pl.multiple_of(side * width, 128), width)
        out_ref[...] = jnp.dot(
            rows_ref[...], weight_ref[:, columns], preferred_element_type=F32
        )


def base_call(rows, weight):
    out = jax.ShapeDtypeStruct((rows.shape[0], weight.shape[1] // 2), F32)
    return pl.pallas_call(
        base_kernel,
        out_shape=(out, out),
        in_specs=[VMEM] * 2,
        out_specs=(VMEM,) * 2,
        compiler_params=params(),
        cost_estimate=HALF,
    )(rows, weight)


def group_mask(low, high, shape):
    row = lax.broadcasted_iota(I32, shape, 0)
    return (row >= low) & (row < high)


def own_ends(bounds_ref, group, size):
    columns = slice(group * size, (group + 1) * size)
    return bounds_ref[0:1, columns], bounds_ref[1:2, columns]


def other_ends(other_ref, extra, group, size):
    ends = other_ref[-extra:, :].astype(F32).astype(I32)
    lines = range(group * size // 128, (group + 1) * size // 128)
    low = jnp.concatenate([ends[i : i + 1] for i in lines], axis=1)
    high = jnp.concatenate([ends[extra // 2 + i : extra // 2 + i + 1] for i in lines], axis=1)
    return low, high


def fold(masked):
    total = masked[:, :128]
    for begin in range(128, masked.shape[1], 128):
        total = total + masked[:, begin : begin + 128]
    return total


def rank_kernel(groups, depth, last, *refs):
    refs = list(refs)
    own_ref, other_ref, bounds_ref = refs[:3]
    pieces = refs[3:]
    pieces, rest = pieces[: 2 * GROUP * len(groups)], pieces[2 * GROUP * len(groups) :]
    starts, outs = (rest[:2], rest[2:]) if last else ((None, None), rest)
    cut = pieces[0].shape[1]
    offset = pl.multiple_of(lax.axis_index("groups") * depth, 128)
    own = own_ref[:, pl.ds(offset, depth)]
    count = own.shape[0]
    other = jnp.concatenate(
        [other_ref[i * count : (i + 1) * count, :] for i in range(depth // 128)], axis=1
    )
    rank = pieces[0].shape[0]
    size = GROUP * rank
    extra = extra_rows(bounds_ref.shape[1])
    totals = [start_ref[...] if last else None for start_ref in starts]
    for i, group in enumerate(groups):
        held = pieces[2 * GROUP * i : 2 * GROUP * (i + 1)]
        first = jnp.concatenate([ref[...] for ref in held[:GROUP]], axis=0)
        second = jnp.concatenate([ref[:, : depth - cut] for ref in held[GROUP:]], axis=0)
        ends = (own_ends(bounds_ref, group, size), other_ends(other_ref, extra, group, size))
        for s, rows in enumerate((own, other)):
            part = contract(rows[:, :cut], first) + contract(rows[:, cut:], second)
            kept = fold(jnp.where(group_mask(*ends[s], part.shape), part, 0.0))
            totals[s] = kept if totals[s] is None else totals[s] + kept
    for total, out_ref in zip(totals, outs):
        if last:
            total = total + pltpu.roll(total, rank, 1)
            half = total.shape[0] // 2
            lane = lax.broadcasted_iota(I32, (half, 2 * rank), 1)
            total = jnp.where(lane < rank, total[:half], total[half:])
        out_ref[...] = total


def rank_call(groups, depth, own, other, bounds, pieces, starts):
    rows = own.shape[0]
    rank = pieces[0].shape[0]
    last = starts is not None
    shape = (rows // 2, 2 * rank) if last else (rows, 2 * rank)
    out = jax.ShapeDtypeStruct(shape, F32)
    operands = [own, other, bounds, *pieces, *(starts or ())]
    return pl.pallas_call(
        functools.partial(rank_kernel, groups, depth, last),
        out_shape=(out, out),
        in_specs=[VMEM] * len(operands),
        out_specs=(VMEM, VMEM),
        compiler_params=params(),
        cost_estimate=LONG,
    )(*operands)


def final_kernel(bounds_ref, mine, one, two, three, near_ref, far_ref, *refs):
    factors, out_ref = refs[:-1], refs[-1]
    rank, width = factors[0].shape[0], out_ref.shape[1]
    begin = factors[0].shape[1] - width
    packed = (mine[...] + one[...]) + (two[...] + three[...])
    turned = pltpu.roll(packed, rank, 1)
    lane = lax.broadcasted_iota(I32, packed.shape, 1)
    values = jnp.concatenate(
        [jnp.where(lane < rank, packed, turned), jnp.where(lane < rank, turned, packed)], axis=0
    )
    wide = jnp.concatenate([values] * (GROUP // 2), axis=1)
    total = None
    for group in range(len(factors) // GROUP):
        mask = group_mask(*own_ends(bounds_ref, group, GROUP * rank), wide.shape)
        chosen = jnp.where(mask, wide, 0.0).astype(BF16)
        factor = jnp.concatenate(
            [ref[:, begin:] for ref in factors[group * GROUP : (group + 1) * GROUP]], axis=0
        )
        part = jnp.dot(chosen, factor, preferred_element_type=F32)
        total = part if total is None else total + part
    adapted = total.astype(BF16).astype(F32)
    out_ref[...] = ((near_ref[...] + far_ref[...]) + adapted).astype(BF16)


def per_device(hidden, demand, lengths, holder_slot, value_weight, factor_in, factor_out):
    rows, features = hidden.shape
    owners = lax.axis_size("batch")
    rank, width = factor_out.shape[1:]
    depth = features // 2
    order = ring_order(owners)
    forward = [(order[i], order[(i + 1) % owners]) for i in range(owners)]
    backward = [(b, a) for a, b in forward]
    swap = [(0, 1), (1, 0)]

    full = (owners - 1) // 2
    distances = [0]
    for step in range(1, full + 1):
        distances += [step, -step]
    distances.append(owners // 2)
    table = [
        [[order[(order.index(me) - distance) % owners] for distance in distances]]
        for me in range(owners)
    ]
    to_other, first, second, bounds = prologue(
        hidden,
        factor_in[0].T,
        factor_out[0],
        demand,
        lengths,
        holder_slot,
        jnp.asarray(table, I32),
    )

    bounds, first_later, second_later = lax.optimization_barrier((mark(bounds), first, second))

    firsts, seconds = [first], [second]
    ahead, behind = (first, second_later), (first_later, second)
    for step in range(1, full + 1):
        a = lax.ppermute(ahead[0], "batch", forward)
        d = lax.ppermute(behind[1], "batch", backward)
        b = lax.ppermute(ahead[1], "batch", forward)
        c = lax.ppermute(behind[0], "batch", backward)
        ahead, behind = (a, b), (c, d)
        firsts += [a, c]
        seconds += [b, d]
    rows_base, a, d = lax.optimization_barrier((hidden, ahead[0], behind[1]))
    firsts.append(lax.ppermute(a, "batch", forward))
    seconds.append(lax.ppermute(d, "batch", backward))
    near, far = base_call(rows_base, value_weight)
    other = lax.ppermute(to_other, "groups", swap)

    count = owners // GROUP
    early = range(count - 1)
    pieces = []
    for group in early:
        pieces += firsts[group * GROUP : (group + 1) * GROUP]
        pieces += seconds[group * GROUP : (group + 1) * GROUP]
    sides = (hidden, other, bounds)
    starts = rank_call(tuple(early), depth, *sides, pieces, None)
    *starts, far, near = lax.optimization_barrier((*starts, far, near))
    far = lax.ppermute(far, "tensor", swap)
    pieces = firsts[-GROUP:] + seconds[-GROUP:]
    mine, theirs = rank_call((count - 1,), depth, *sides, pieces, starts)

    two = lax.ppermute(theirs, "groups", swap)
    one = lax.ppermute(mine, "tensor", swap)
    three = lax.ppermute(two, "tensor", swap)

    operands = [bounds, mine, one, two, three, near, far, *seconds]
    return pl.pallas_call(
        final_kernel,
        out_shape=jax.ShapeDtypeStruct((rows, width), BF16),
        in_specs=[VMEM] * len(operands),
        out_specs=VMEM,
        compiler_params=params(),
    )(*operands)


def solution(mesh):
    return jax.shard_map(
        per_device,
        mesh=mesh,
        in_specs=(
            P(("groups", "batch"), "tensor"),
            P(("groups", "batch"), None),
            P(("groups", "batch"), None),
            P(),
            P("tensor", None),
            P("batch", "tensor", None),
            P("batch", None, "tensor"),
        ),
        out_specs=P(("groups", "batch"), "tensor"),
        check_vma=False,
    )
```

```python
import functools

import jax
import jax.numpy as jnp
from jax import lax
from jax.experimental import pallas as pl
from jax.experimental.pallas import tpu as pltpu
from jax.sharding import PartitionSpec as P

F32, BF16, I32 = jnp.float32, jnp.bfloat16, jnp.int32
VMEM_LIMIT = 24 * 1024 * 1024
HALF = pl.CostEstimate(flops=0, bytes_accessed=1 << 22, transcendentals=0)
LONG = pl.CostEstimate(flops=1 << 33, bytes_accessed=1 << 24, transcendentals=0)
GROUP = 4
VMEM = pl.BlockSpec(memory_space=pltpu.VMEM)
HBM = pl.BlockSpec(memory_space=pltpu.HBM)


def in_hbm(array):
    return pltpu.with_memory_space_constraint(array, pltpu.HBM)


def params():
    return pltpu.CompilerParams(vmem_limit_bytes=VMEM_LIMIT)


def ring_order(size):
    if size % 4:
        return list(range(size))
    columns = size // 4
    order = [0]
    for row in range(4):
        across = range(1, columns) if row % 2 == 0 else range(columns - 1, 0, -1)
        order += [row * columns + column for column in across]
    return order + [row * columns for row in (3, 2, 1)]


def contract(left, right):
    return lax.dot_general(left, right, (((1,), (1,)), ((), ())), preferred_element_type=F32)


def extra_rows(columns):
    return 2 * -(-columns // 1024) * 8


def prologue_kernel(
    depth,
    rank,
    hidden_ref,
    factor_ref,
    factor_out_ref,
    demand_ref,
    lengths_ref,
    holder_ref,
    slots_ref,
    to_other_ref,
    first_ref,
    second_ref,
    bounds_ref,
    demand,
    lengths,
    holder,
    slots,
    sems,
    hidden_sem,
):
    group, place = lax.axis_index("groups"), lax.axis_index("batch")
    cut = first_ref.shape[1]
    rows = hidden_ref.shape[0]
    here = pl.multiple_of(group * depth, 128)
    there = pl.multiple_of((1 - group) * depth, 128)
    after = pl.multiple_of(group * depth + cut, 128)
    small = [
        pltpu.make_async_copy(demand_ref, demand, sems.at[0]),
        pltpu.make_async_copy(lengths_ref, lengths, sems.at[1]),
        pltpu.make_async_copy(holder_ref, holder, sems.at[2]),
        pltpu.make_async_copy(slots_ref.at[pl.ds(place, 1)], slots, sems.at[3]),
    ]
    large = [
        pltpu.make_async_copy(factor_ref.at[:, pl.ds(here, cut)], first_ref, sems.at[4]),
        pltpu.make_async_copy(
            factor_ref.at[:, pl.ds(after, depth - cut)], second_ref.at[:, : depth - cut], sems.at[5]
        ),
        pltpu.make_async_copy(factor_out_ref, second_ref.at[:, depth - cut :], sems.at[6]),
    ]
    for i in range(depth // 128):
        large.append(
            pltpu.make_async_copy(
                hidden_ref.at[:, pl.ds(there + i * 128, 128)],
                to_other_ref.at[i * rows : (i + 1) * rows],
                hidden_sem.at[i],
            )
        )
    for copy in small + large:
        copy.start()
    for copy in small:
        copy.wait()
    count = slots.shape[2]
    items = demand.shape[1]
    column = lax.broadcasted_iota(I32, (1, count * rank), 1)
    zero = jnp.int32(0)

    def chunk_mask(chunk):
        return (column >= chunk * rank) & (column < (chunk + 1) * rank)

    low = high = jnp.zeros((1, count * rank), I32)
    if items * count <= 64:
        start = zero
        spans = []
        for item in range(items):
            end = start + lengths[0, item]
            spans.append((holder[demand[0, item]], start, end))
            start = end
        for chunk in range(count):
            slot = slots[0, 0, chunk]
            begin = end = zero
            for owner, first, last in spans:
                begin = jnp.where(owner == slot, first, begin)
                end = jnp.where(owner == slot, last, end)
            low = jnp.where(chunk_mask(chunk), begin, low)
            high = jnp.where(chunk_mask(chunk), end, high)
    else:

        def chunk_ends(chunk, carry):
            low, high = carry
            slot = slots[0, 0, chunk]

            def item_ends(item, state):
                start, begin, end = state
                last = start + lengths[0, item]
                hit = holder[demand[0, item]] == slot
                return last, jnp.where(hit, start, begin), jnp.where(hit, last, end)

            _, begin, end = lax.fori_loop(0, items, item_ends, (zero, zero, zero))
            mask = chunk_mask(chunk)
            return jnp.where(mask, begin, low), jnp.where(mask, end, high)

        low, high = lax.fori_loop(0, count, chunk_ends, (low, high))
    bounds_ref[0:1, :] = low
    bounds_ref[1:2, :] = high
    bounds_ref[2:8, :] = jnp.zeros((6, count * rank), I32)
    extra = extra_rows(count * rank)
    line = lax.broadcasted_iota(I32, (extra, 128), 0)
    ends = jnp.zeros((extra, 128), I32)
    for i in range(count * rank // 128):
        columns = slice(i * 128, (i + 1) * 128)
        ends = jnp.where(line == i, low[:, columns], ends)
        ends = jnp.where(line == extra // 2 + i, high[:, columns], ends)
    to_other_ref[-extra:, :] = ends.astype(F32).astype(BF16)
    for copy in large:
        copy.wait()


def prologue(hidden, factor, factor_out, demand, lengths, holder_slot, slots):
    rows, features = hidden.shape
    rank, width = factor_out.shape
    depth = features // 2
    cut = (depth + width) // 2
    count = slots.shape[2]
    tall = depth // 128 * rows + extra_rows(count * rank)
    return pl.pallas_call(
        functools.partial(prologue_kernel, depth, rank),
        out_shape=(
            jax.ShapeDtypeStruct((tall, 128), hidden.dtype),
            jax.ShapeDtypeStruct((rank, cut), factor.dtype),
            jax.ShapeDtypeStruct((rank, cut), factor.dtype),
            jax.ShapeDtypeStruct((8, count * rank), I32),
        ),
        in_specs=[HBM] * 7,
        out_specs=(VMEM,) * 4,
        scratch_shapes=[
            pltpu.SMEM(demand.shape, I32),
            pltpu.SMEM(lengths.shape, I32),
            pltpu.SMEM(holder_slot.shape, I32),
            pltpu.SMEM((1, 1, count), I32),
            pltpu.SemaphoreType.DMA((7,)),
            pltpu.SemaphoreType.DMA((depth // 128,)),
        ],
        compiler_params=params(),
    )(*map(in_hbm, (hidden, factor, factor_out, demand, lengths, holder_slot, slots)))


def mark_kernel(bounds_ref, out_ref):
    out_ref[...] = bounds_ref[...]


def mark(bounds):
    return pl.pallas_call(
        mark_kernel,
        out_shape=jax.ShapeDtypeStruct(bounds.shape, bounds.dtype),
        in_specs=[VMEM],
        out_specs=VMEM,
        compiler_params=params(),
        cost_estimate=LONG,
    )(bounds)


def base_kernel(rows_ref, weight_ref, near_ref, far_ref):
    width = near_ref.shape[1]
    core = lax.axis_index("tensor")
    for out_ref, side in ((near_ref, core), (far_ref, 1 - core)):
        columns = pl.ds(pl.multiple_of(side * width, 128), width)
        out_ref[...] = jnp.dot(
            rows_ref[...], weight_ref[:, columns], preferred_element_type=F32
        )


def base_call(rows, weight):
    out = jax.ShapeDtypeStruct((rows.shape[0], weight.shape[1] // 2), F32)
    return pl.pallas_call(
        base_kernel,
        out_shape=(out, out),
        in_specs=[VMEM] * 2,
        out_specs=(VMEM,) * 2,
        compiler_params=params(),
        cost_estimate=HALF,
    )(rows, weight)


def group_mask(low, high, shape):
    row = lax.broadcasted_iota(I32, shape, 0)
    return (row >= low) & (row < high)


def own_ends(bounds_ref, group, size):
    columns = slice(group * size, (group + 1) * size)
    return bounds_ref[0:1, columns], bounds_ref[1:2, columns]


def other_ends(other_ref, extra, group, size):
    ends = other_ref[-extra:, :].astype(F32).astype(I32)
    lines = range(group * size // 128, (group + 1) * size // 128)
    low = jnp.concatenate([ends[i : i + 1] for i in lines], axis=1)
    high = jnp.concatenate([ends[extra // 2 + i : extra // 2 + i + 1] for i in lines], axis=1)
    return low, high


def fold(masked):
    total = masked[:, :128]
    for begin in range(128, masked.shape[1], 128):
        total = total + masked[:, begin : begin + 128]
    return total


def rank_kernel(groups, depth, last, *refs):
    refs = list(refs)
    own_ref, other_ref, bounds_ref = refs[:3]
    pieces = refs[3:]
    pieces, rest = pieces[: 2 * GROUP * len(groups)], pieces[2 * GROUP * len(groups) :]
    starts, outs = (rest[:2], rest[2:]) if last else ((None, None), rest)
    cut = pieces[0].shape[1]
    offset = pl.multiple_of(lax.axis_index("groups") * depth, 128)
    own = own_ref[:, pl.ds(offset, depth)]
    count = own.shape[0]
    other = jnp.concatenate(
        [other_ref[i * count : (i + 1) * count, :] for i in range(depth // 128)], axis=1
    )
    rank = pieces[0].shape[0]
    size = GROUP * rank
    extra = extra_rows(bounds_ref.shape[1])
    totals = [start_ref[...] if last else None for start_ref in starts]
    for i, group in enumerate(groups):
        held = pieces[2 * GROUP * i : 2 * GROUP * (i + 1)]
        first = jnp.concatenate([ref[...] for ref in held[:GROUP]], axis=0)
        second = jnp.concatenate([ref[:, : depth - cut] for ref in held[GROUP:]], axis=0)
        ends = (own_ends(bounds_ref, group, size), other_ends(other_ref, extra, group, size))
        for s, rows in enumerate((own, other)):
            part = contract(rows[:, :cut], first) + contract(rows[:, cut:], second)
            kept = fold(jnp.where(group_mask(*ends[s], part.shape), part, 0.0))
            totals[s] = kept if totals[s] is None else totals[s] + kept
    for total, out_ref in zip(totals, outs):
        if last:
            total = total + pltpu.roll(total, rank, 1)
            half = total.shape[0] // 2
            lane = lax.broadcasted_iota(I32, (half, 2 * rank), 1)
            total = jnp.where(lane < rank, total[:half], total[half:])
        out_ref[...] = total


def rank_call(groups, depth, own, other, bounds, pieces, starts):
    rows = own.shape[0]
    rank = pieces[0].shape[0]
    last = starts is not None
    shape = (rows // 2, 2 * rank) if last else (rows, 2 * rank)
    out = jax.ShapeDtypeStruct(shape, F32)
    operands = [own, other, bounds, *pieces, *(starts or ())]
    return pl.pallas_call(
        functools.partial(rank_kernel, groups, depth, last),
        out_shape=(out, out),
        in_specs=[VMEM] * len(operands),
        out_specs=(VMEM, VMEM),
        compiler_params=params(),
        cost_estimate=LONG,
    )(*operands)


def final_kernel(bounds_ref, mine, one, two, three, near_ref, far_ref, *refs):
    factors, out_ref = refs[:-1], refs[-1]
    rank, width = factors[0].shape[0], out_ref.shape[1]
    begin = factors[0].shape[1] - width
    packed = (mine[...] + one[...]) + (two[...] + three[...])
    turned = pltpu.roll(packed, rank, 1)
    lane = lax.broadcasted_iota(I32, packed.shape, 1)
    values = jnp.concatenate(
        [jnp.where(lane < rank, packed, turned), jnp.where(lane < rank, turned, packed)], axis=0
    )
    wide = jnp.concatenate([values] * (GROUP // 2), axis=1)
    total = None
    for group in range(len(factors) // GROUP):
        mask = group_mask(*own_ends(bounds_ref, group, GROUP * rank), wide.shape)
        chosen = jnp.where(mask, wide, 0.0).astype(BF16)
        factor = jnp.concatenate(
            [ref[:, begin:] for ref in factors[group * GROUP : (group + 1) * GROUP]], axis=0
        )
        part = jnp.dot(chosen, factor, preferred_element_type=F32)
        total = part if total is None else total + part
    adapted = total.astype(BF16).astype(F32)
    out_ref[...] = ((near_ref[...] + far_ref[...]) + adapted).astype(BF16)


def per_device(hidden, demand, lengths, holder_slot, value_weight, factor_in, factor_out):
    rows, features = hidden.shape
    owners = lax.axis_size("batch")
    rank, width = factor_out.shape[1:]
    depth = features // 2
    order = ring_order(owners)
    forward = [(order[i], order[(i + 1) % owners]) for i in range(owners)]
    backward = [(b, a) for a, b in forward]
    swap = [(0, 1), (1, 0)]

    full = (owners - 1) // 2
    distances = [0]
    for step in range(1, full + 1):
        distances += [step, -step]
    distances.append(owners // 2)
    table = [
        [[order[(order.index(me) - distance) % owners] for distance in distances]]
        for me in range(owners)
    ]
    to_other, first, second, bounds = prologue(
        hidden,
        factor_in[0].T,
        factor_out[0],
        demand,
        lengths,
        holder_slot,
        jnp.asarray(table, I32),
    )

    bounds, first_later, second_later = lax.optimization_barrier((mark(bounds), first, second))

    firsts, seconds = [first], [second]
    ahead, behind = (first, second_later), (first_later, second)
    for step in range(1, full + 1):
        a = lax.ppermute(ahead[0], "batch", forward)
        d = lax.ppermute(behind[1], "batch", backward)
        b = lax.ppermute(ahead[1], "batch", forward)
        c = lax.ppermute(behind[0], "batch", backward)
        ahead, behind = (a, b), (c, d)
        firsts += [a, c]
        seconds += [b, d]
    firsts.append(lax.ppermute(ahead[0], "batch", forward))
    seconds.append(lax.ppermute(behind[1], "batch", backward))
    near, far = base_call(hidden, value_weight)
    hidden, near, far = lax.optimization_barrier((hidden, near, far))
    other = lax.ppermute(to_other, "groups", swap)

    count = owners // GROUP
    early = range(count - 1)
    pieces = []
    for group in early:
        pieces += firsts[group * GROUP : (group + 1) * GROUP]
        pieces += seconds[group * GROUP : (group + 1) * GROUP]
    sides = (hidden, other, bounds)
    starts = rank_call(tuple(early), depth, *sides, pieces, None)
    *starts, far = lax.optimization_barrier((*starts, far))
    far = lax.ppermute(far, "tensor", swap)
    pieces = firsts[-GROUP:] + seconds[-GROUP:]
    mine, theirs = rank_call((count - 1,), depth, *sides, pieces, starts)

    two = lax.ppermute(theirs, "groups", swap)
    one = lax.ppermute(mine, "tensor", swap)
    three = lax.ppermute(two, "tensor", swap)

    operands = [bounds, mine, one, two, three, near, far, *seconds]
    return pl.pallas_call(
        final_kernel,
        out_shape=jax.ShapeDtypeStruct((rows, width), BF16),
        in_specs=[VMEM] * len(operands),
        out_specs=VMEM,
        compiler_params=params(),
    )(*operands)


def solution(mesh):
    return jax.shard_map(
        per_device,
        mesh=mesh,
        in_specs=(
            P(("groups", "batch"), "tensor"),
            P(("groups", "batch"), None),
            P(("groups", "batch"), None),
            P(),
            P("tensor", None),
            P("batch", "tensor", None),
            P("batch", None, "tensor"),
        ),
        out_specs=P(("groups", "batch"), "tensor"),
        check_vma=False,
    )
```

```python
import functools

import jax
import jax.numpy as jnp
from jax import lax
from jax.experimental import pallas as pl
from jax.experimental.pallas import tpu as pltpu
from jax.sharding import PartitionSpec as P

F32, BF16, I32 = jnp.float32, jnp.bfloat16, jnp.int32
VMEM_LIMIT = 24 * 1024 * 1024
HALF = pl.CostEstimate(flops=0, bytes_accessed=1 << 22, transcendentals=0)
LONG = pl.CostEstimate(flops=1 << 33, bytes_accessed=1 << 24, transcendentals=0)
GROUP = 4
VMEM = pl.BlockSpec(memory_space=pltpu.VMEM)
HBM = pl.BlockSpec(memory_space=pltpu.HBM)


def in_hbm(array):
    return pltpu.with_memory_space_constraint(array, pltpu.HBM)


def params():
    return pltpu.CompilerParams(vmem_limit_bytes=VMEM_LIMIT)


def ring_order(size):
    if size % 4:
        return list(range(size))
    columns = size // 4
    order = [0]
    for row in range(4):
        across = range(1, columns) if row % 2 == 0 else range(columns - 1, 0, -1)
        order += [row * columns + column for column in across]
    return order + [row * columns for row in (3, 2, 1)]


def contract(left, right):
    return lax.dot_general(left, right, (((1,), (1,)), ((), ())), preferred_element_type=F32)


def extra_rows(columns):
    return 2 * -(-columns // 1024) * 8


def shard_kernel(depth, factor_ref, factor_out_ref, first_ref, second_ref, sems):
    cut = first_ref.shape[1]
    here = pl.multiple_of(lax.axis_index("groups") * depth, 128)
    after = pl.multiple_of(lax.axis_index("groups") * depth + cut, 128)
    rest = depth - cut
    copies = (
        pltpu.make_async_copy(factor_ref.at[:, pl.ds(here, cut)], first_ref, sems.at[0]),
        pltpu.make_async_copy(
            factor_ref.at[:, pl.ds(after, rest)], second_ref.at[:, :rest], sems.at[1]
        ),
        pltpu.make_async_copy(factor_out_ref, second_ref.at[:, rest:], sems.at[2]),
    )
    for copy in copies:
        copy.start()
    for copy in copies:
        copy.wait()


def shard_call(factor, factor_out, depth):
    rank, width = factor_out.shape
    out = jax.ShapeDtypeStruct((rank, (depth + width) // 2), factor.dtype)
    return pl.pallas_call(
        functools.partial(shard_kernel, depth),
        out_shape=(out, out),
        in_specs=[HBM] * 2,
        out_specs=(VMEM,) * 2,
        scratch_shapes=[pltpu.SemaphoreType.DMA((3,))],
        compiler_params=params(),
    )(in_hbm(factor), in_hbm(factor_out))


def rows_kernel(
    depth,
    rank,
    hidden_ref,
    demand_ref,
    lengths_ref,
    holder_ref,
    slots_ref,
    to_other_ref,
    bounds_ref,
    demand,
    lengths,
    holder,
    slots,
    sems,
    hidden_sem,
):
    group, place = lax.axis_index("groups"), lax.axis_index("batch")
    rows = hidden_ref.shape[0]
    there = pl.multiple_of((1 - group) * depth, 128)
    small = [
        pltpu.make_async_copy(demand_ref, demand, sems.at[0]),
        pltpu.make_async_copy(lengths_ref, lengths, sems.at[1]),
        pltpu.make_async_copy(holder_ref, holder, sems.at[2]),
        pltpu.make_async_copy(slots_ref.at[pl.ds(place, 1)], slots, sems.at[3]),
    ]
    large = [
        pltpu.make_async_copy(
            hidden_ref.at[:, pl.ds(there + i * 128, 128)],
            to_other_ref.at[i * rows : (i + 1) * rows],
            hidden_sem.at[i],
        )
        for i in range(depth // 128)
    ]
    for copy in small + large:
        copy.start()
    for copy in small:
        copy.wait()
    count = slots.shape[2]
    items = demand.shape[1]
    column = lax.broadcasted_iota(I32, (1, count * rank), 1)
    zero = jnp.int32(0)

    def chunk_mask(chunk):
        return (column >= chunk * rank) & (column < (chunk + 1) * rank)

    low = high = jnp.zeros((1, count * rank), I32)
    if items * count <= 64:
        start = zero
        spans = []
        for item in range(items):
            end = start + lengths[0, item]
            spans.append((holder[demand[0, item]], start, end))
            start = end
        for chunk in range(count):
            slot = slots[0, 0, chunk]
            begin = end = zero
            for owner, first, last in spans:
                begin = jnp.where(owner == slot, first, begin)
                end = jnp.where(owner == slot, last, end)
            low = jnp.where(chunk_mask(chunk), begin, low)
            high = jnp.where(chunk_mask(chunk), end, high)
    else:

        def chunk_ends(chunk, carry):
            low, high = carry
            slot = slots[0, 0, chunk]

            def item_ends(item, state):
                start, begin, end = state
                last = start + lengths[0, item]
                hit = holder[demand[0, item]] == slot
                return last, jnp.where(hit, start, begin), jnp.where(hit, last, end)

            _, begin, end = lax.fori_loop(0, items, item_ends, (zero, zero, zero))
            mask = chunk_mask(chunk)
            return jnp.where(mask, begin, low), jnp.where(mask, end, high)

        low, high = lax.fori_loop(0, count, chunk_ends, (low, high))
    bounds_ref[0:1, :] = low
    bounds_ref[1:2, :] = high
    bounds_ref[2:8, :] = jnp.zeros((6, count * rank), I32)
    extra = extra_rows(count * rank)
    line = lax.broadcasted_iota(I32, (extra, 128), 0)
    ends = jnp.zeros((extra, 128), I32)
    for i in range(count * rank // 128):
        columns = slice(i * 128, (i + 1) * 128)
        ends = jnp.where(line == i, low[:, columns], ends)
        ends = jnp.where(line == extra // 2 + i, high[:, columns], ends)
    to_other_ref[-extra:, :] = ends.astype(F32).astype(BF16)
    for copy in large:
        copy.wait()


def rows_call(hidden, demand, lengths, holder_slot, slots, rank):
    rows, features = hidden.shape
    depth = features // 2
    count = slots.shape[2]
    tall = depth // 128 * rows + extra_rows(count * rank)
    return pl.pallas_call(
        functools.partial(rows_kernel, depth, rank),
        out_shape=(
            jax.ShapeDtypeStruct((tall, 128), hidden.dtype),
            jax.ShapeDtypeStruct((8, count * rank), I32),
        ),
        in_specs=[HBM] * 5,
        out_specs=(VMEM,) * 2,
        scratch_shapes=[
            pltpu.SMEM(demand.shape, I32),
            pltpu.SMEM(lengths.shape, I32),
            pltpu.SMEM(holder_slot.shape, I32),
            pltpu.SMEM((1, 1, count), I32),
            pltpu.SemaphoreType.DMA((4,)),
            pltpu.SemaphoreType.DMA((depth // 128,)),
        ],
        compiler_params=params(),
        cost_estimate=LONG,
    )(*map(in_hbm, (hidden, demand, lengths, holder_slot, slots)))


def mark_kernel(bounds_ref, out_ref):
    out_ref[...] = bounds_ref[...]


def mark(bounds):
    return pl.pallas_call(
        mark_kernel,
        out_shape=jax.ShapeDtypeStruct(bounds.shape, bounds.dtype),
        in_specs=[VMEM],
        out_specs=VMEM,
        compiler_params=params(),
        cost_estimate=LONG,
    )(bounds)


def base_kernel(rows_ref, weight_ref, near_ref, far_ref):
    width = near_ref.shape[1]
    core = lax.axis_index("tensor")
    for out_ref, side in ((near_ref, core), (far_ref, 1 - core)):
        columns = pl.ds(pl.multiple_of(side * width, 128), width)
        out_ref[...] = jnp.dot(
            rows_ref[...], weight_ref[:, columns], preferred_element_type=F32
        )


def base_call(rows, weight):
    out = jax.ShapeDtypeStruct((rows.shape[0], weight.shape[1] // 2), F32)
    return pl.pallas_call(
        base_kernel,
        out_shape=(out, out),
        in_specs=[VMEM] * 2,
        out_specs=(VMEM,) * 2,
        compiler_params=params(),
        cost_estimate=HALF,
    )(rows, weight)


def group_mask(low, high, shape):
    row = lax.broadcasted_iota(I32, shape, 0)
    return (row >= low) & (row < high)


def own_ends(bounds_ref, group, size):
    columns = slice(group * size, (group + 1) * size)
    return bounds_ref[0:1, columns], bounds_ref[1:2, columns]


def other_ends(other_ref, extra, group, size):
    ends = other_ref[-extra:, :].astype(F32).astype(I32)
    lines = range(group * size // 128, (group + 1) * size // 128)
    low = jnp.concatenate([ends[i : i + 1] for i in lines], axis=1)
    high = jnp.concatenate([ends[extra // 2 + i : extra // 2 + i + 1] for i in lines], axis=1)
    return low, high


def fold(masked):
    total = masked[:, :128]
    for begin in range(128, masked.shape[1], 128):
        total = total + masked[:, begin : begin + 128]
    return total


def rank_kernel(groups, depth, last, *refs):
    refs = list(refs)
    own_ref, other_ref, bounds_ref = refs[:3]
    pieces = refs[3:]
    pieces, rest = pieces[: 2 * GROUP * len(groups)], pieces[2 * GROUP * len(groups) :]
    starts, outs = (rest[:2], rest[2:]) if last else ((None, None), rest)
    cut = pieces[0].shape[1]
    offset = pl.multiple_of(lax.axis_index("groups") * depth, 128)
    own = own_ref[:, pl.ds(offset, depth)]
    count = own.shape[0]
    other = jnp.concatenate(
        [other_ref[i * count : (i + 1) * count, :] for i in range(depth // 128)], axis=1
    )
    rank = pieces[0].shape[0]
    size = GROUP * rank
    extra = extra_rows(bounds_ref.shape[1])
    totals = [start_ref[...] if last else None for start_ref in starts]
    for i, group in enumerate(groups):
        held = pieces[2 * GROUP * i : 2 * GROUP * (i + 1)]
        first = jnp.concatenate([ref[...] for ref in held[:GROUP]], axis=0)
        second = jnp.concatenate([ref[:, : depth - cut] for ref in held[GROUP:]], axis=0)
        ends = (own_ends(bounds_ref, group, size), other_ends(other_ref, extra, group, size))
        for s, rows in enumerate((own, other)):
            part = contract(rows[:, :cut], first) + contract(rows[:, cut:], second)
            kept = fold(jnp.where(group_mask(*ends[s], part.shape), part, 0.0))
            totals[s] = kept if totals[s] is None else totals[s] + kept
    for total, out_ref in zip(totals, outs):
        if last:
            total = total + pltpu.roll(total, rank, 1)
            half = total.shape[0] // 2
            lane = lax.broadcasted_iota(I32, (half, 2 * rank), 1)
            total = jnp.where(lane < rank, total[:half], total[half:])
        out_ref[...] = total


def rank_call(groups, depth, own, other, bounds, pieces, starts):
    rows = own.shape[0]
    rank = pieces[0].shape[0]
    last = starts is not None
    shape = (rows // 2, 2 * rank) if last else (rows, 2 * rank)
    out = jax.ShapeDtypeStruct(shape, F32)
    operands = [own, other, bounds, *pieces, *(starts or ())]
    return pl.pallas_call(
        functools.partial(rank_kernel, groups, depth, last),
        out_shape=(out, out),
        in_specs=[VMEM] * len(operands),
        out_specs=(VMEM, VMEM),
        compiler_params=params(),
        cost_estimate=LONG,
    )(*operands)


def final_kernel(bounds_ref, mine, one, two, three, near_ref, far_ref, *refs):
    factors, out_ref = refs[:-1], refs[-1]
    rank, width = factors[0].shape[0], out_ref.shape[1]
    begin = factors[0].shape[1] - width
    packed = (mine[...] + one[...]) + (two[...] + three[...])
    turned = pltpu.roll(packed, rank, 1)
    lane = lax.broadcasted_iota(I32, packed.shape, 1)
    values = jnp.concatenate(
        [jnp.where(lane < rank, packed, turned), jnp.where(lane < rank, turned, packed)], axis=0
    )
    wide = jnp.concatenate([values] * (GROUP // 2), axis=1)
    total = None
    for group in range(len(factors) // GROUP):
        mask = group_mask(*own_ends(bounds_ref, group, GROUP * rank), wide.shape)
        chosen = jnp.where(mask, wide, 0.0).astype(BF16)
        factor = jnp.concatenate(
            [ref[:, begin:] for ref in factors[group * GROUP : (group + 1) * GROUP]], axis=0
        )
        part = jnp.dot(chosen, factor, preferred_element_type=F32)
        total = part if total is None else total + part
    adapted = total.astype(BF16).astype(F32)
    out_ref[...] = ((near_ref[...] + far_ref[...]) + adapted).astype(BF16)


def per_device(hidden, demand, lengths, holder_slot, value_weight, factor_in, factor_out):
    rows, features = hidden.shape
    owners = lax.axis_size("batch")
    rank, width = factor_out.shape[1:]
    depth = features // 2
    order = ring_order(owners)
    forward = [(order[i], order[(i + 1) % owners]) for i in range(owners)]
    backward = [(b, a) for a, b in forward]
    swap = [(0, 1), (1, 0)]

    full = (owners - 1) // 2
    distances = [0]
    for step in range(1, full + 1):
        distances += [step, -step]
    distances.append(owners // 2)
    table = [
        [[order[(order.index(me) - distance) % owners] for distance in distances]]
        for me in range(owners)
    ]
    first, second = shard_call(factor_in[0].T, factor_out[0], depth)
    first, rows_here = lax.optimization_barrier((first, hidden))
    to_other, bounds = rows_call(
        rows_here, demand, lengths, holder_slot, jnp.asarray(table, I32), rank
    )

    bounds, first_later, second_later = lax.optimization_barrier((mark(bounds), first, second))

    firsts, seconds = [first], [second]
    ahead, behind = (first, second_later), (first_later, second)
    for step in range(1, full + 1):
        a = lax.ppermute(ahead[0], "batch", forward)
        d = lax.ppermute(behind[1], "batch", backward)
        b = lax.ppermute(ahead[1], "batch", forward)
        c = lax.ppermute(behind[0], "batch", backward)
        ahead, behind = (a, b), (c, d)
        firsts += [a, c]
        seconds += [b, d]
    firsts.append(lax.ppermute(ahead[0], "batch", forward))
    seconds.append(lax.ppermute(behind[1], "batch", backward))
    near, far = base_call(hidden, value_weight)
    hidden, near, far = lax.optimization_barrier((hidden, near, far))
    other = lax.ppermute(to_other, "groups", swap)

    count = owners // GROUP
    early = range(count - 1)
    pieces = []
    for group in early:
        pieces += firsts[group * GROUP : (group + 1) * GROUP]
        pieces += seconds[group * GROUP : (group + 1) * GROUP]
    sides = (hidden, other, bounds)
    starts = rank_call(tuple(early), depth, *sides, pieces, None)
    *starts, far = lax.optimization_barrier((*starts, far))
    far = lax.ppermute(far, "tensor", swap)
    pieces = firsts[-GROUP:] + seconds[-GROUP:]
    mine, theirs = rank_call((count - 1,), depth, *sides, pieces, starts)

    two = lax.ppermute(theirs, "groups", swap)
    one = lax.ppermute(mine, "tensor", swap)
    three = lax.ppermute(two, "tensor", swap)

    operands = [bounds, mine, one, two, three, near, far, *seconds]
    return pl.pallas_call(
        final_kernel,
        out_shape=jax.ShapeDtypeStruct((rows, width), BF16),
        in_specs=[VMEM] * len(operands),
        out_specs=VMEM,
        compiler_params=params(),
    )(*operands)


def solution(mesh):
    return jax.shard_map(
        per_device,
        mesh=mesh,
        in_specs=(
            P(("groups", "batch"), "tensor"),
            P(("groups", "batch"), None),
            P(("groups", "batch"), None),
            P(),
            P("tensor", None),
            P("batch", "tensor", None),
            P("batch", None, "tensor"),
        ),
        out_specs=P(("groups", "batch"), "tensor"),
        check_vma=False,
    )
```

```python
import functools

import jax
import jax.numpy as jnp
from jax import lax
from jax.experimental import pallas as pl
from jax.experimental.pallas import tpu as pltpu
from jax.sharding import PartitionSpec as P

F32, BF16, I32 = jnp.float32, jnp.bfloat16, jnp.int32
VMEM_LIMIT = 24 * 1024 * 1024
HALF = pl.CostEstimate(flops=0, bytes_accessed=1 << 22, transcendentals=0)
LONG = pl.CostEstimate(flops=1 << 33, bytes_accessed=1 << 24, transcendentals=0)
GROUP = 4
VMEM = pl.BlockSpec(memory_space=pltpu.VMEM)
HBM = pl.BlockSpec(memory_space=pltpu.HBM)


def in_hbm(array):
    return pltpu.with_memory_space_constraint(array, pltpu.HBM)


def params():
    return pltpu.CompilerParams(vmem_limit_bytes=VMEM_LIMIT)


def ring_order(size):
    if size % 4:
        return list(range(size))
    columns = size // 4
    order = [0]
    for row in range(4):
        across = range(1, columns) if row % 2 == 0 else range(columns - 1, 0, -1)
        order += [row * columns + column for column in across]
    return order + [row * columns for row in (3, 2, 1)]


def contract(left, right):
    return lax.dot_general(left, right, (((1,), (1,)), ((), ())), preferred_element_type=F32)


def extra_rows(columns):
    return 2 * -(-columns // 1024) * 8


def prologue_kernel(
    depth,
    rank,
    hidden_ref,
    factor_ref,
    factor_out_ref,
    demand_ref,
    lengths_ref,
    holder_ref,
    slots_ref,
    to_other_ref,
    first_ref,
    second_ref,
    bounds_ref,
    demand,
    lengths,
    holder,
    slots,
    sems,
    hidden_sem,
):
    group, place = lax.axis_index("groups"), lax.axis_index("batch")
    cut = first_ref.shape[1]
    rows = hidden_ref.shape[0]
    here = pl.multiple_of(group * depth, 128)
    there = pl.multiple_of((1 - group) * depth, 128)
    after = pl.multiple_of(group * depth + cut, 128)
    small = [
        pltpu.make_async_copy(demand_ref, demand, sems.at[0]),
        pltpu.make_async_copy(lengths_ref, lengths, sems.at[1]),
        pltpu.make_async_copy(holder_ref, holder, sems.at[2]),
        pltpu.make_async_copy(slots_ref.at[pl.ds(place, 1)], slots, sems.at[3]),
    ]
    large = [
        pltpu.make_async_copy(factor_ref.at[:, pl.ds(here, cut)], first_ref, sems.at[4]),
        pltpu.make_async_copy(
            factor_ref.at[:, pl.ds(after, depth - cut)], second_ref.at[:, : depth - cut], sems.at[5]
        ),
        pltpu.make_async_copy(factor_out_ref, second_ref.at[:, depth - cut :], sems.at[6]),
    ]
    for i in range(depth // 128):
        large.append(
            pltpu.make_async_copy(
                hidden_ref.at[:, pl.ds(there + i * 128, 128)],
                to_other_ref.at[i * rows : (i + 1) * rows],
                hidden_sem.at[i],
            )
        )
    for copy in small + large:
        copy.start()
    for copy in small:
        copy.wait()
    count = slots.shape[2]
    items = demand.shape[1]
    column = lax.broadcasted_iota(I32, (1, count * rank), 1)
    zero = jnp.int32(0)

    def chunk_mask(chunk):
        return (column >= chunk * rank) & (column < (chunk + 1) * rank)

    low = high = jnp.zeros((1, count * rank), I32)
    if items * count <= 64:
        start = zero
        spans = []
        for item in range(items):
            end = start + lengths[0, item]
            spans.append((holder[demand[0, item]], start, end))
            start = end
        for chunk in range(count):
            slot = slots[0, 0, chunk]
            begin = end = zero
            for owner, first, last in spans:
                begin = jnp.where(owner == slot, first, begin)
                end = jnp.where(owner == slot, last, end)
            low = jnp.where(chunk_mask(chunk), begin, low)
            high = jnp.where(chunk_mask(chunk), end, high)
    else:

        def chunk_ends(chunk, carry):
            low, high = carry
            slot = slots[0, 0, chunk]

            def item_ends(item, state):
                start, begin, end = state
                last = start + lengths[0, item]
                hit = holder[demand[0, item]] == slot
                return last, jnp.where(hit, start, begin), jnp.where(hit, last, end)

            _, begin, end = lax.fori_loop(0, items, item_ends, (zero, zero, zero))
            mask = chunk_mask(chunk)
            return jnp.where(mask, begin, low), jnp.where(mask, end, high)

        low, high = lax.fori_loop(0, count, chunk_ends, (low, high))
    bounds_ref[0:1, :] = low
    bounds_ref[1:2, :] = high
    bounds_ref[2:8, :] = jnp.zeros((6, count * rank), I32)
    extra = extra_rows(count * rank)
    line = lax.broadcasted_iota(I32, (extra, 128), 0)
    ends = jnp.zeros((extra, 128), I32)
    for i in range(count * rank // 128):
        columns = slice(i * 128, (i + 1) * 128)
        ends = jnp.where(line == i, low[:, columns], ends)
        ends = jnp.where(line == extra // 2 + i, high[:, columns], ends)
    to_other_ref[-extra:, :] = ends.astype(F32).astype(BF16)
    for copy in large:
        copy.wait()


def prologue(hidden, factor, factor_out, demand, lengths, holder_slot, slots):
    rows, features = hidden.shape
    rank, width = factor_out.shape
    depth = features // 2
    cut = (depth + width) // 2
    count = slots.shape[2]
    tall = depth // 128 * rows + extra_rows(count * rank)
    return pl.pallas_call(
        functools.partial(prologue_kernel, depth, rank),
        out_shape=(
            jax.ShapeDtypeStruct((tall, 128), hidden.dtype),
            jax.ShapeDtypeStruct((rank, cut), factor.dtype),
            jax.ShapeDtypeStruct((rank, cut), factor.dtype),
            jax.ShapeDtypeStruct((8, count * rank), I32),
        ),
        in_specs=[HBM] * 7,
        out_specs=(VMEM,) * 4,
        scratch_shapes=[
            pltpu.SMEM(demand.shape, I32),
            pltpu.SMEM(lengths.shape, I32),
            pltpu.SMEM(holder_slot.shape, I32),
            pltpu.SMEM((1, 1, count), I32),
            pltpu.SemaphoreType.DMA((7,)),
            pltpu.SemaphoreType.DMA((depth // 128,)),
        ],
        compiler_params=params(),
    )(*map(in_hbm, (hidden, factor, factor_out, demand, lengths, holder_slot, slots)))


def mark_kernel(bounds_ref, out_ref):
    out_ref[...] = bounds_ref[...]


def mark(bounds):
    return pl.pallas_call(
        mark_kernel,
        out_shape=jax.ShapeDtypeStruct(bounds.shape, bounds.dtype),
        in_specs=[VMEM],
        out_specs=VMEM,
        compiler_params=params(),
        cost_estimate=LONG,
    )(bounds)


def base_kernel(rows_ref, weight_ref, near_ref, far_ref):
    width = near_ref.shape[1]
    core = lax.axis_index("tensor")
    for out_ref, side in ((near_ref, core), (far_ref, 1 - core)):
        columns = pl.ds(pl.multiple_of(side * width, 128), width)
        out_ref[...] = jnp.dot(
            rows_ref[...], weight_ref[:, columns], preferred_element_type=F32
        )


def base_call(rows, weight):
    out = jax.ShapeDtypeStruct((rows.shape[0], weight.shape[1] // 2), F32)
    return pl.pallas_call(
        base_kernel,
        out_shape=(out, out),
        in_specs=[VMEM] * 2,
        out_specs=(VMEM,) * 2,
        compiler_params=params(),
        cost_estimate=HALF,
    )(rows, weight)


def group_mask(low, high, shape):
    row = lax.broadcasted_iota(I32, shape, 0)
    return (row >= low) & (row < high)


def own_ends(bounds_ref, group, size):
    columns = slice(group * size, (group + 1) * size)
    return bounds_ref[0:1, columns], bounds_ref[1:2, columns]


def other_ends(other_ref, extra, group, size):
    ends = other_ref[-extra:, :].astype(F32).astype(I32)
    lines = range(group * size // 128, (group + 1) * size // 128)
    low = jnp.concatenate([ends[i : i + 1] for i in lines], axis=1)
    high = jnp.concatenate([ends[extra // 2 + i : extra // 2 + i + 1] for i in lines], axis=1)
    return low, high


def fold(masked):
    total = masked[:, :128]
    for begin in range(128, masked.shape[1], 128):
        total = total + masked[:, begin : begin + 128]
    return total


def rank_kernel(groups, depth, last, *refs):
    refs = list(refs)
    own_ref, other_ref, bounds_ref = refs[:3]
    pieces = refs[3:]
    pieces, rest = pieces[: 2 * GROUP * len(groups)], pieces[2 * GROUP * len(groups) :]
    starts, outs = (rest[:2], rest[2:]) if last else ((None, None), rest)
    cut = pieces[0].shape[1]
    offset = pl.multiple_of(lax.axis_index("groups") * depth, 128)
    own = own_ref[:, pl.ds(offset, depth)]
    count = own.shape[0]
    other = jnp.concatenate(
        [other_ref[i * count : (i + 1) * count, :] for i in range(depth // 128)], axis=1
    )
    rows = jnp.concatenate([own, other], axis=0)
    rank = pieces[0].shape[0]
    size = GROUP * rank
    extra = extra_rows(bounds_ref.shape[1])
    totals = [start_ref[...] if last else None for start_ref in starts]
    for i, group in enumerate(groups):
        held = pieces[2 * GROUP * i : 2 * GROUP * (i + 1)]
        first = jnp.concatenate([ref[...] for ref in held[:GROUP]], axis=0)
        second = jnp.concatenate([ref[:, : depth - cut] for ref in held[GROUP:]], axis=0)
        ends = (own_ends(bounds_ref, group, size), other_ends(other_ref, extra, group, size))
        part = contract(rows, jnp.concatenate([first, second], axis=1))
        for s in (0, 1):
            mine = part[s * count : (s + 1) * count]
            kept = fold(jnp.where(group_mask(*ends[s], mine.shape), mine, 0.0))
            totals[s] = kept if totals[s] is None else totals[s] + kept
    for total, out_ref in zip(totals, outs):
        if last:
            total = total + pltpu.roll(total, rank, 1)
            half = total.shape[0] // 2
            lane = lax.broadcasted_iota(I32, (half, 2 * rank), 1)
            total = jnp.where(lane < rank, total[:half], total[half:])
        out_ref[...] = total.astype(out_ref.dtype)


def rank_call(groups, depth, own, other, bounds, pieces, starts):
    rows = own.shape[0]
    rank = pieces[0].shape[0]
    last = starts is not None
    shape = (rows // 2, 2 * rank) if last else (rows, 2 * rank)
    out = jax.ShapeDtypeStruct(shape, F32)
    other_out = jax.ShapeDtypeStruct(shape, BF16 if last else F32)
    operands = [own, other, bounds, *pieces, *(starts or ())]
    return pl.pallas_call(
        functools.partial(rank_kernel, groups, depth, last),
        out_shape=(out, other_out),
        in_specs=[VMEM] * len(operands),
        out_specs=(VMEM, VMEM),
        compiler_params=params(),
        cost_estimate=LONG,
    )(*operands)


def final_kernel(bounds_ref, mine, one, two, three, near_ref, far_ref, *refs):
    factors, out_ref = refs[:-1], refs[-1]
    rank, width = factors[0].shape[0], out_ref.shape[1]
    begin = factors[0].shape[1] - width
    packed = (mine[...] + one[...]) + (two[...].astype(F32) + three[...].astype(F32))
    turned = pltpu.roll(packed, rank, 1)
    lane = lax.broadcasted_iota(I32, packed.shape, 1)
    values = jnp.concatenate(
        [jnp.where(lane < rank, packed, turned), jnp.where(lane < rank, turned, packed)], axis=0
    )
    wide = jnp.concatenate([values] * (GROUP // 2), axis=1)
    total = None
    for group in range(len(factors) // GROUP):
        mask = group_mask(*own_ends(bounds_ref, group, GROUP * rank), wide.shape)
        chosen = jnp.where(mask, wide, 0.0).astype(BF16)
        factor = jnp.concatenate(
            [ref[:, begin:] for ref in factors[group * GROUP : (group + 1) * GROUP]], axis=0
        )
        part = jnp.dot(chosen, factor, preferred_element_type=F32)
        total = part if total is None else total + part
    adapted = total.astype(BF16).astype(F32)
    out_ref[...] = ((near_ref[...] + far_ref[...]) + adapted).astype(BF16)


def per_device(hidden, demand, lengths, holder_slot, value_weight, factor_in, factor_out):
    rows, features = hidden.shape
    owners = lax.axis_size("batch")
    rank, width = factor_out.shape[1:]
    depth = features // 2
    order = ring_order(owners)
    forward = [(order[i], order[(i + 1) % owners]) for i in range(owners)]
    backward = [(b, a) for a, b in forward]
    swap = [(0, 1), (1, 0)]

    full = (owners - 1) // 2
    distances = [0]
    for step in range(1, full + 1):
        distances += [step, -step]
    distances.append(owners // 2)
    table = [
        [[order[(order.index(me) - distance) % owners] for distance in distances]]
        for me in range(owners)
    ]
    to_other, first, second, bounds = prologue(
        hidden,
        factor_in[0].T,
        factor_out[0],
        demand,
        lengths,
        holder_slot,
        jnp.asarray(table, I32),
    )

    bounds, first_later, second_later = lax.optimization_barrier((mark(bounds), first, second))

    firsts, seconds = [first], [second]
    ahead, behind = (first, second_later), (first_later, second)
    for step in range(1, full + 1):
        a = lax.ppermute(ahead[0], "batch", forward)
        d = lax.ppermute(behind[1], "batch", backward)
        b = lax.ppermute(ahead[1], "batch", forward)
        c = lax.ppermute(behind[0], "batch", backward)
        ahead, behind = (a, b), (c, d)
        firsts += [a, c]
        seconds += [b, d]
    firsts.append(lax.ppermute(ahead[0], "batch", forward))
    seconds.append(lax.ppermute(behind[1], "batch", backward))
    near, far = base_call(hidden, value_weight)
    hidden, near, far = lax.optimization_barrier((hidden, near, far))
    other = lax.ppermute(to_other, "groups", swap)

    count = owners // GROUP
    early = range(count - 1)
    pieces = []
    for group in early:
        pieces += firsts[group * GROUP : (group + 1) * GROUP]
        pieces += seconds[group * GROUP : (group + 1) * GROUP]
    sides = (hidden, other, bounds)
    starts = rank_call(tuple(early), depth, *sides, pieces, None)
    *starts, far = lax.optimization_barrier((*starts, far))
    far = lax.ppermute(far, "tensor", swap)
    pieces = firsts[-GROUP:] + seconds[-GROUP:]
    mine, theirs = rank_call((count - 1,), depth, *sides, pieces, starts)

    two = lax.ppermute(theirs, "groups", swap)
    one = lax.ppermute(mine, "tensor", swap)
    three = lax.ppermute(two, "tensor", swap)

    operands = [bounds, mine, one, two, three, near, far, *seconds]
    return pl.pallas_call(
        final_kernel,
        out_shape=jax.ShapeDtypeStruct((rows, width), BF16),
        in_specs=[VMEM] * len(operands),
        out_specs=VMEM,
        compiler_params=params(),
    )(*operands)


def solution(mesh):
    return jax.shard_map(
        per_device,
        mesh=mesh,
        in_specs=(
            P(("groups", "batch"), "tensor"),
            P(("groups", "batch"), None),
            P(("groups", "batch"), None),
            P(),
            P("tensor", None),
            P("batch", "tensor", None),
            P("batch", None, "tensor"),
        ),
        out_specs=P(("groups", "batch"), "tensor"),
        check_vma=False,
    )
```

```python
import functools

import jax
import jax.numpy as jnp
from jax import lax
from jax.experimental import pallas as pl
from jax.experimental.pallas import tpu as pltpu
from jax.sharding import PartitionSpec as P

F32, BF16, I32 = jnp.float32, jnp.bfloat16, jnp.int32
VMEM_LIMIT = 24 * 1024 * 1024
HALF = pl.CostEstimate(flops=0, bytes_accessed=1 << 22, transcendentals=0)
LONG = pl.CostEstimate(flops=1 << 33, bytes_accessed=1 << 24, transcendentals=0)
GROUP = 4
VMEM = pl.BlockSpec(memory_space=pltpu.VMEM)
HBM = pl.BlockSpec(memory_space=pltpu.HBM)


def in_hbm(array):
    return pltpu.with_memory_space_constraint(array, pltpu.HBM)


def params():
    return pltpu.CompilerParams(vmem_limit_bytes=VMEM_LIMIT)


def ring_order(size):
    if size % 4:
        return list(range(size))
    columns = size // 4
    order = [0]
    for row in range(4):
        across = range(1, columns) if row % 2 == 0 else range(columns - 1, 0, -1)
        order += [row * columns + column for column in across]
    return order + [row * columns for row in (3, 2, 1)]


def contract(left, right):
    return lax.dot_general(left, right, (((1,), (1,)), ((), ())), preferred_element_type=F32)


def extra_rows(columns):
    return 2 * -(-columns // 1024) * 8


def prologue_kernel(
    depth,
    rank,
    hidden_ref,
    factor_ref,
    factor_out_ref,
    demand_ref,
    lengths_ref,
    holder_ref,
    slots_ref,
    to_other_ref,
    first_ref,
    second_ref,
    bounds_ref,
    demand,
    lengths,
    holder,
    slots,
    sems,
    hidden_sem,
):
    group, place = lax.axis_index("groups"), lax.axis_index("batch")
    cut = first_ref.shape[1]
    rows = hidden_ref.shape[0]
    here = pl.multiple_of(group * depth, 128)
    there = pl.multiple_of((1 - group) * depth, 128)
    after = pl.multiple_of(group * depth + cut, 128)
    small = [
        pltpu.make_async_copy(demand_ref, demand, sems.at[0]),
        pltpu.make_async_copy(lengths_ref, lengths, sems.at[1]),
        pltpu.make_async_copy(holder_ref, holder, sems.at[2]),
        pltpu.make_async_copy(slots_ref.at[pl.ds(place, 1)], slots, sems.at[3]),
    ]
    large = [
        pltpu.make_async_copy(factor_ref.at[:, pl.ds(here, cut)], first_ref, sems.at[4]),
        pltpu.make_async_copy(
            factor_ref.at[:, pl.ds(after, depth - cut)], second_ref.at[:, : depth - cut], sems.at[5]
        ),
        pltpu.make_async_copy(factor_out_ref, second_ref.at[:, depth - cut :], sems.at[6]),
    ]
    for i in range(depth // 128):
        large.append(
            pltpu.make_async_copy(
                hidden_ref.at[:, pl.ds(there + i * 128, 128)],
                to_other_ref.at[i * rows : (i + 1) * rows],
                hidden_sem.at[i],
            )
        )
    for copy in small + large:
        copy.start()
    for copy in small:
        copy.wait()
    count = slots.shape[2]
    items = demand.shape[1]
    column = lax.broadcasted_iota(I32, (1, count * rank), 1)
    zero = jnp.int32(0)

    def chunk_mask(chunk):
        return (column >= chunk * rank) & (column < (chunk + 1) * rank)

    low = high = jnp.zeros((1, count * rank), I32)
    if items * count <= 64:
        start = zero
        spans = []
        for item in range(items):
            end = start + lengths[0, item]
            spans.append((holder[demand[0, item]], start, end))
            start = end
        for chunk in range(count):
            slot = slots[0, 0, chunk]
            begin = end = zero
            for owner, first, last in spans:
                begin = jnp.where(owner == slot, first, begin)
                end = jnp.where(owner == slot, last, end)
            low = jnp.where(chunk_mask(chunk), begin, low)
            high = jnp.where(chunk_mask(chunk), end, high)
    else:

        def chunk_ends(chunk, carry):
            low, high = carry
            slot = slots[0, 0, chunk]

            def item_ends(item, state):
                start, begin, end = state
                last = start + lengths[0, item]
                hit = holder[demand[0, item]] == slot
                return last, jnp.where(hit, start, begin), jnp.where(hit, last, end)

            _, begin, end = lax.fori_loop(0, items, item_ends, (zero, zero, zero))
            mask = chunk_mask(chunk)
            return jnp.where(mask, begin, low), jnp.where(mask, end, high)

        low, high = lax.fori_loop(0, count, chunk_ends, (low, high))
    bounds_ref[0:1, :] = low
    bounds_ref[1:2, :] = high
    bounds_ref[2:8, :] = jnp.zeros((6, count * rank), I32)
    extra = extra_rows(count * rank)
    line = lax.broadcasted_iota(I32, (extra, 128), 0)
    ends = jnp.zeros((extra, 128), I32)
    for i in range(count * rank // 128):
        columns = slice(i * 128, (i + 1) * 128)
        ends = jnp.where(line == i, low[:, columns], ends)
        ends = jnp.where(line == extra // 2 + i, high[:, columns], ends)
    to_other_ref[-extra:, :] = ends.astype(F32).astype(BF16)
    for copy in large:
        copy.wait()


def prologue(hidden, factor, factor_out, demand, lengths, holder_slot, slots):
    rows, features = hidden.shape
    rank, width = factor_out.shape
    depth = features // 2
    cut = (depth + width) // 2
    count = slots.shape[2]
    tall = depth // 128 * rows + extra_rows(count * rank)
    return pl.pallas_call(
        functools.partial(prologue_kernel, depth, rank),
        out_shape=(
            jax.ShapeDtypeStruct((tall, 128), hidden.dtype),
            jax.ShapeDtypeStruct((rank, cut), factor.dtype),
            jax.ShapeDtypeStruct((rank, cut), factor.dtype),
            jax.ShapeDtypeStruct((8, count * rank), I32),
        ),
        in_specs=[HBM] * 7,
        out_specs=(VMEM,) * 4,
        scratch_shapes=[
            pltpu.SMEM(demand.shape, I32),
            pltpu.SMEM(lengths.shape, I32),
            pltpu.SMEM(holder_slot.shape, I32),
            pltpu.SMEM((1, 1, count), I32),
            pltpu.SemaphoreType.DMA((7,)),
            pltpu.SemaphoreType.DMA((depth // 128,)),
        ],
        compiler_params=params(),
    )(*map(in_hbm, (hidden, factor, factor_out, demand, lengths, holder_slot, slots)))


def mark_kernel(bounds_ref, out_ref):
    out_ref[...] = bounds_ref[...]


def mark(bounds):
    return pl.pallas_call(
        mark_kernel,
        out_shape=jax.ShapeDtypeStruct(bounds.shape, bounds.dtype),
        in_specs=[VMEM],
        out_specs=VMEM,
        compiler_params=params(),
        cost_estimate=LONG,
    )(bounds)


def base_kernel(rows_ref, weight_ref, near_ref, far_ref):
    width = near_ref.shape[1]
    core = lax.axis_index("tensor")
    for out_ref, side in ((near_ref, core), (far_ref, 1 - core)):
        columns = pl.ds(pl.multiple_of(side * width, 128), width)
        out_ref[...] = jnp.dot(
            rows_ref[...], weight_ref[:, columns], preferred_element_type=F32
        )


def base_call(rows, weight):
    out = jax.ShapeDtypeStruct((rows.shape[0], weight.shape[1] // 2), F32)
    return pl.pallas_call(
        base_kernel,
        out_shape=(out, out),
        in_specs=[VMEM] * 2,
        out_specs=(VMEM,) * 2,
        compiler_params=params(),
        cost_estimate=HALF,
    )(rows, weight)


def group_mask(low, high, shape):
    row = lax.broadcasted_iota(I32, shape, 0)
    return (row >= low) & (row < high)


def own_ends(bounds_ref, group, size):
    columns = slice(group * size, (group + 1) * size)
    return bounds_ref[0:1, columns], bounds_ref[1:2, columns]


def other_ends(other_ref, extra, group, size):
    ends = other_ref[-extra:, :].astype(F32).astype(I32)
    lines = range(group * size // 128, (group + 1) * size // 128)
    low = jnp.concatenate([ends[i : i + 1] for i in lines], axis=1)
    high = jnp.concatenate([ends[extra // 2 + i : extra // 2 + i + 1] for i in lines], axis=1)
    return low, high


def fold(masked):
    total = masked[:, :128]
    for begin in range(128, masked.shape[1], 128):
        total = total + masked[:, begin : begin + 128]
    return total


def rank_kernel(sides, groups, depth, last, *refs):
    refs = list(refs)
    rows_refs, refs = refs[: len(sides)], refs[len(sides) :]
    bounds_ref, pieces = refs[0], refs[1:]
    pieces, rest = pieces[: 2 * GROUP * len(groups)], pieces[2 * GROUP * len(groups) :]
    starts, outs = rest[: -len(sides)], rest[-len(sides) :]
    cut = pieces[0].shape[1]
    rank = pieces[0].shape[0]
    size = GROUP * rank
    extra = extra_rows(bounds_ref.shape[1])
    rows = []
    for side, ref in zip(sides, rows_refs):
        if side == 0:
            offset = pl.multiple_of(lax.axis_index("groups") * depth, 128)
            rows.append(ref[:, pl.ds(offset, depth)])
        else:
            blocks = depth // 128
            tall = (ref.shape[0] - extra) // blocks
            rows.append(
                jnp.concatenate([ref[i * tall : (i + 1) * tall, :] for i in range(blocks)], axis=1)
            )
    count = rows[0].shape[0]
    rows = jnp.concatenate(rows, axis=0)
    totals = [ref[...] for ref in starts] if last else [None] * len(sides)
    for i, group in enumerate(groups):
        held = pieces[2 * GROUP * i : 2 * GROUP * (i + 1)]
        first = jnp.concatenate([ref[...] for ref in held[:GROUP]], axis=0)
        second = jnp.concatenate([ref[:, : depth - cut] for ref in held[GROUP:]], axis=0)
        part = contract(rows, jnp.concatenate([first, second], axis=1))
        for s, side in enumerate(sides):
            if side == 0:
                ends = own_ends(bounds_ref, group, size)
            else:
                ends = other_ends(rows_refs[s], extra, group, size)
            here = part[s * count : (s + 1) * count]
            kept = fold(jnp.where(group_mask(*ends, here.shape), here, 0.0))
            totals[s] = kept if totals[s] is None else totals[s] + kept
    for total, out_ref in zip(totals, outs):
        if last:
            total = total + pltpu.roll(total, rank, 1)
            half = count // 2
            lane = lax.broadcasted_iota(I32, (half, 2 * rank), 1)
            total = jnp.where(lane < rank, total[:half], total[half:])
        out_ref[...] = total


def rank_call(sides, groups, depth, count, rows, bounds, pieces, starts):
    rank = pieces[0].shape[0]
    last = len(starts) > 0
    shape = (count // 2, 2 * rank) if last else (count, 2 * rank)
    operands = [*rows, bounds, *pieces, *starts]
    return pl.pallas_call(
        functools.partial(rank_kernel, sides, groups, depth, last),
        out_shape=(jax.ShapeDtypeStruct(shape, F32),) * len(sides),
        in_specs=[VMEM] * len(operands),
        out_specs=(VMEM,) * len(sides),
        compiler_params=params(),
        cost_estimate=LONG,
    )(*operands)


def final_kernel(bounds_ref, mine, one, two, three, near_ref, far_ref, *refs):
    factors, out_ref = refs[:-1], refs[-1]
    rank, width = factors[0].shape[0], out_ref.shape[1]
    begin = factors[0].shape[1] - width
    packed = (mine[...] + one[...]) + (two[...] + three[...])
    turned = pltpu.roll(packed, rank, 1)
    lane = lax.broadcasted_iota(I32, packed.shape, 1)
    values = jnp.concatenate(
        [jnp.where(lane < rank, packed, turned), jnp.where(lane < rank, turned, packed)], axis=0
    )
    wide = jnp.concatenate([values] * (GROUP // 2), axis=1)
    total = None
    for group in range(len(factors) // GROUP):
        mask = group_mask(*own_ends(bounds_ref, group, GROUP * rank), wide.shape)
        chosen = jnp.where(mask, wide, 0.0).astype(BF16)
        factor = jnp.concatenate(
            [ref[:, begin:] for ref in factors[group * GROUP : (group + 1) * GROUP]], axis=0
        )
        part = jnp.dot(chosen, factor, preferred_element_type=F32)
        total = part if total is None else total + part
    adapted = total.astype(BF16).astype(F32)
    out_ref[...] = ((near_ref[...] + far_ref[...]) + adapted).astype(BF16)


def per_device(hidden, demand, lengths, holder_slot, value_weight, factor_in, factor_out):
    rows, features = hidden.shape
    owners = lax.axis_size("batch")
    rank, width = factor_out.shape[1:]
    depth = features // 2
    order = ring_order(owners)
    forward = [(order[i], order[(i + 1) % owners]) for i in range(owners)]
    backward = [(b, a) for a, b in forward]
    swap = [(0, 1), (1, 0)]

    full = (owners - 1) // 2
    distances = [0]
    for step in range(1, full + 1):
        distances += [step, -step]
    distances.append(owners // 2)
    table = [
        [[order[(order.index(me) - distance) % owners] for distance in distances]]
        for me in range(owners)
    ]
    to_other, first, second, bounds = prologue(
        hidden,
        factor_in[0].T,
        factor_out[0],
        demand,
        lengths,
        holder_slot,
        jnp.asarray(table, I32),
    )

    bounds, first_later, second_later = lax.optimization_barrier((mark(bounds), first, second))

    firsts, seconds = [first], [second]
    ahead, behind = (first, second_later), (first_later, second)
    for step in range(1, full + 1):
        a = lax.ppermute(ahead[0], "batch", forward)
        d = lax.ppermute(behind[1], "batch", backward)
        b = lax.ppermute(ahead[1], "batch", forward)
        c = lax.ppermute(behind[0], "batch", backward)
        ahead, behind = (a, b), (c, d)
        firsts += [a, c]
        seconds += [b, d]
    firsts.append(lax.ppermute(ahead[0], "batch", forward))
    seconds.append(lax.ppermute(behind[1], "batch", backward))
    near, far = base_call(hidden, value_weight)
    hidden, near, far = lax.optimization_barrier((hidden, near, far))
    other = lax.ppermute(to_other, "groups", swap)

    count = owners // GROUP
    early = range(count - 1)
    pieces = []
    for group in early:
        pieces += firsts[group * GROUP : (group + 1) * GROUP]
        pieces += seconds[group * GROUP : (group + 1) * GROUP]
    both = (hidden, other)
    start_mine, start_theirs = rank_call(
        (0, 1), tuple(early), depth, rows, both, bounds, pieces, ()
    )
    start_theirs, far = lax.optimization_barrier((start_theirs, far))
    far = lax.ppermute(far, "tensor", swap)
    pieces = firsts[-GROUP:] + seconds[-GROUP:]
    late = (count - 1,)
    (theirs,) = rank_call((1,), late, depth, rows, (other,), bounds, pieces, (start_theirs,))
    (mine,) = rank_call((0,), late, depth, rows, (hidden,), bounds, pieces, (start_mine,))

    two = lax.ppermute(theirs, "groups", swap)
    one = lax.ppermute(mine, "tensor", swap)
    three = lax.ppermute(two, "tensor", swap)

    operands = [bounds, mine, one, two, three, near, far, *seconds]
    return pl.pallas_call(
        final_kernel,
        out_shape=jax.ShapeDtypeStruct((rows, width), BF16),
        in_specs=[VMEM] * len(operands),
        out_specs=VMEM,
        compiler_params=params(),
    )(*operands)


def solution(mesh):
    return jax.shard_map(
        per_device,
        mesh=mesh,
        in_specs=(
            P(("groups", "batch"), "tensor"),
            P(("groups", "batch"), None),
            P(("groups", "batch"), None),
            P(),
            P("tensor", None),
            P("batch", "tensor", None),
            P("batch", None, "tensor"),
        ),
        out_specs=P(("groups", "batch"), "tensor"),
        check_vma=False,
    )
```

```python
import functools

import jax
import jax.numpy as jnp
from jax import lax
from jax.experimental import pallas as pl
from jax.experimental.pallas import tpu as pltpu
from jax.sharding import PartitionSpec as P

F32, BF16, I32 = jnp.float32, jnp.bfloat16, jnp.int32
VMEM_LIMIT = 24 * 1024 * 1024
HALF = pl.CostEstimate(flops=0, bytes_accessed=1 << 22, transcendentals=0)
LONG = pl.CostEstimate(flops=1 << 33, bytes_accessed=1 << 24, transcendentals=0)
GROUP = 4
VMEM = pl.BlockSpec(memory_space=pltpu.VMEM)
HBM = pl.BlockSpec(memory_space=pltpu.HBM)


def in_hbm(array):
    return pltpu.with_memory_space_constraint(array, pltpu.HBM)


def params():
    return pltpu.CompilerParams(vmem_limit_bytes=VMEM_LIMIT)


def ring_order(size):
    if size % 4:
        return list(range(size))
    columns = size // 4
    order = [0]
    for row in range(4):
        across = range(1, columns) if row % 2 == 0 else range(columns - 1, 0, -1)
        order += [row * columns + column for column in across]
    return order + [row * columns for row in (3, 2, 1)]


def contract(left, right):
    return lax.dot_general(left, right, (((1,), (1,)), ((), ())), preferred_element_type=F32)


def extra_rows(columns):
    return 2 * -(-columns // 1024) * 8


def prologue_kernel(
    depth,
    rank,
    hidden_ref,
    factor_ref,
    factor_out_ref,
    demand_ref,
    lengths_ref,
    holder_ref,
    slots_ref,
    to_other_ref,
    first_ref,
    second_ref,
    bounds_ref,
    demand,
    lengths,
    holder,
    slots,
    sems,
    hidden_sem,
):
    group, place = lax.axis_index("groups"), lax.axis_index("batch")
    cut = first_ref.shape[1]
    rows = hidden_ref.shape[0]
    here = pl.multiple_of(group * depth, 128)
    there = pl.multiple_of((1 - group) * depth, 128)
    after = pl.multiple_of(group * depth + cut, 128)
    small = [
        pltpu.make_async_copy(demand_ref, demand, sems.at[0]),
        pltpu.make_async_copy(lengths_ref, lengths, sems.at[1]),
        pltpu.make_async_copy(holder_ref, holder, sems.at[2]),
        pltpu.make_async_copy(slots_ref.at[pl.ds(place, 1)], slots, sems.at[3]),
    ]
    large = [
        pltpu.make_async_copy(factor_ref.at[:, pl.ds(here, cut)], first_ref, sems.at[4]),
        pltpu.make_async_copy(
            factor_ref.at[:, pl.ds(after, depth - cut)], second_ref.at[:, : depth - cut], sems.at[5]
        ),
        pltpu.make_async_copy(factor_out_ref, second_ref.at[:, depth - cut :], sems.at[6]),
    ]
    for i in range(depth // 128):
        large.append(
            pltpu.make_async_copy(
                hidden_ref.at[:, pl.ds(there + i * 128, 128)],
                to_other_ref.at[i * rows : (i + 1) * rows],
                hidden_sem.at[i],
            )
        )
    for copy in small + large:
        copy.start()
    for copy in small:
        copy.wait()
    count = slots.shape[2]
    items = demand.shape[1]
    column = lax.broadcasted_iota(I32, (1, count * rank), 1)
    zero = jnp.int32(0)

    def chunk_mask(chunk):
        return (column >= chunk * rank) & (column < (chunk + 1) * rank)

    low = high = jnp.zeros((1, count * rank), I32)
    if items * count <= 64:
        start = zero
        spans = []
        for item in range(items):
            end = start + lengths[0, item]
            spans.append((holder[demand[0, item]], start, end))
            start = end
        for chunk in range(count):
            slot = slots[0, 0, chunk]
            begin = end = zero
            for owner, first, last in spans:
                begin = jnp.where(owner == slot, first, begin)
                end = jnp.where(owner == slot, last, end)
            low = jnp.where(chunk_mask(chunk), begin, low)
            high = jnp.where(chunk_mask(chunk), end, high)
    else:

        def chunk_ends(chunk, carry):
            low, high = carry
            slot = slots[0, 0, chunk]

            def item_ends(item, state):
                start, begin, end = state
                last = start + lengths[0, item]
                hit = holder[demand[0, item]] == slot
                return last, jnp.where(hit, start, begin), jnp.where(hit, last, end)

            _, begin, end = lax.fori_loop(0, items, item_ends, (zero, zero, zero))
            mask = chunk_mask(chunk)
            return jnp.where(mask, begin, low), jnp.where(mask, end, high)

        low, high = lax.fori_loop(0, count, chunk_ends, (low, high))
    bounds_ref[0:1, :] = low
    bounds_ref[1:2, :] = high
    bounds_ref[2:8, :] = jnp.zeros((6, count * rank), I32)
    extra = extra_rows(count * rank)
    line = lax.broadcasted_iota(I32, (extra, 128), 0)
    ends = jnp.zeros((extra, 128), I32)
    for i in range(count * rank // 128):
        columns = slice(i * 128, (i + 1) * 128)
        ends = jnp.where(line == i, low[:, columns], ends)
        ends = jnp.where(line == extra // 2 + i, high[:, columns], ends)
    to_other_ref[-extra:, :] = ends.astype(F32).astype(BF16)
    for copy in large:
        copy.wait()


def prologue(hidden, factor, factor_out, demand, lengths, holder_slot, slots):
    rows, features = hidden.shape
    rank, width = factor_out.shape
    depth = features // 2
    cut = (depth + width) // 2
    count = slots.shape[2]
    tall = depth // 128 * rows + extra_rows(count * rank)
    return pl.pallas_call(
        functools.partial(prologue_kernel, depth, rank),
        out_shape=(
            jax.ShapeDtypeStruct((tall, 128), hidden.dtype),
            jax.ShapeDtypeStruct((rank, cut), factor.dtype),
            jax.ShapeDtypeStruct((rank, cut), factor.dtype),
            jax.ShapeDtypeStruct((8, count * rank), I32),
        ),
        in_specs=[HBM] * 7,
        out_specs=(VMEM,) * 4,
        scratch_shapes=[
            pltpu.SMEM(demand.shape, I32),
            pltpu.SMEM(lengths.shape, I32),
            pltpu.SMEM(holder_slot.shape, I32),
            pltpu.SMEM((1, 1, count), I32),
            pltpu.SemaphoreType.DMA((7,)),
            pltpu.SemaphoreType.DMA((depth // 128,)),
        ],
        compiler_params=params(),
    )(*map(in_hbm, (hidden, factor, factor_out, demand, lengths, holder_slot, slots)))


def mark_kernel(bounds_ref, out_ref):
    out_ref[...] = bounds_ref[...]


def mark(bounds):
    return pl.pallas_call(
        mark_kernel,
        out_shape=jax.ShapeDtypeStruct(bounds.shape, bounds.dtype),
        in_specs=[VMEM],
        out_specs=VMEM,
        compiler_params=params(),
        cost_estimate=LONG,
    )(bounds)


def base_kernel(rows_ref, weight_ref, near_ref, far_ref):
    width = near_ref.shape[1]
    core = lax.axis_index("tensor")
    for out_ref, side in ((near_ref, core), (far_ref, 1 - core)):
        columns = pl.ds(pl.multiple_of(side * width, 128), width)
        out_ref[...] = jnp.dot(
            rows_ref[...], weight_ref[:, columns], preferred_element_type=F32
        )


def base_call(rows, weight):
    out = jax.ShapeDtypeStruct((rows.shape[0], weight.shape[1] // 2), F32)
    return pl.pallas_call(
        base_kernel,
        out_shape=(out, out),
        in_specs=[VMEM] * 2,
        out_specs=(VMEM,) * 2,
        compiler_params=params(),
        cost_estimate=HALF,
    )(rows, weight)


def group_mask(low, high, shape):
    row = lax.broadcasted_iota(I32, shape, 0)
    return (row >= low) & (row < high)


def own_ends(bounds_ref, group, size):
    columns = slice(group * size, (group + 1) * size)
    return bounds_ref[0:1, columns], bounds_ref[1:2, columns]


def other_ends(other_ref, extra, group, size):
    ends = other_ref[-extra:, :].astype(F32).astype(I32)
    lines = range(group * size // 128, (group + 1) * size // 128)
    low = jnp.concatenate([ends[i : i + 1] for i in lines], axis=1)
    high = jnp.concatenate([ends[extra // 2 + i : extra // 2 + i + 1] for i in lines], axis=1)
    return low, high


def fold(masked):
    total = masked[:, :128]
    for begin in range(128, masked.shape[1], 128):
        total = total + masked[:, begin : begin + 128]
    return total


def rank_kernel(sides, groups, depth, last, *refs):
    refs = list(refs)
    rows_refs, refs = refs[: len(sides)], refs[len(sides) :]
    bounds_ref, pieces = refs[0], refs[1:]
    pieces, rest = pieces[: 2 * GROUP * len(groups)], pieces[2 * GROUP * len(groups) :]
    starts, outs = rest[: -len(sides)], rest[-len(sides) :]
    cut = pieces[0].shape[1]
    rank = pieces[0].shape[0]
    size = GROUP * rank
    extra = extra_rows(bounds_ref.shape[1])
    rows = []
    for side, ref in zip(sides, rows_refs):
        if side == 0:
            offset = pl.multiple_of(lax.axis_index("groups") * depth, 128)
            rows.append(ref[:, pl.ds(offset, depth)])
        else:
            blocks = depth // 128
            tall = (ref.shape[0] - extra) // blocks
            rows.append(
                jnp.concatenate([ref[i * tall : (i + 1) * tall, :] for i in range(blocks)], axis=1)
            )
    count = rows[0].shape[0]
    rows = jnp.concatenate(rows, axis=0)
    totals = [ref[...] for ref in starts] if last else [None] * len(sides)
    for i, group in enumerate(groups):
        held = pieces[2 * GROUP * i : 2 * GROUP * (i + 1)]
        first = jnp.concatenate([ref[...] for ref in held[:GROUP]], axis=0)
        second = jnp.concatenate([ref[:, : depth - cut] for ref in held[GROUP:]], axis=0)
        part = contract(rows, jnp.concatenate([first, second], axis=1))
        for s, side in enumerate(sides):
            if side == 0:
                ends = own_ends(bounds_ref, group, size)
            else:
                ends = other_ends(rows_refs[s], extra, group, size)
            here = part[s * count : (s + 1) * count]
            kept = fold(jnp.where(group_mask(*ends, here.shape), here, 0.0))
            totals[s] = kept if totals[s] is None else totals[s] + kept
    for total, out_ref in zip(totals, outs):
        if last:
            total = total + pltpu.roll(total, rank, 1)
            half = count // 2
            lane = lax.broadcasted_iota(I32, (half, 2 * rank), 1)
            total = jnp.where(lane < rank, total[:half], total[half:])
        out_ref[...] = total


def rank_call(sides, groups, depth, count, rows, bounds, pieces, starts):
    rank = pieces[0].shape[0]
    last = len(starts) > 0
    shape = (count // 2, 2 * rank) if last else (count, 2 * rank)
    operands = [*rows, bounds, *pieces, *starts]
    return pl.pallas_call(
        functools.partial(rank_kernel, sides, groups, depth, last),
        out_shape=(jax.ShapeDtypeStruct(shape, F32),) * len(sides),
        in_specs=[VMEM] * len(operands),
        out_specs=(VMEM,) * len(sides),
        compiler_params=params(),
        cost_estimate=LONG,
    )(*operands)


def final_kernel(bounds_ref, mine, one, two, three, near_ref, far_ref, *refs):
    factors, out_ref = refs[:-1], refs[-1]
    rank, width = factors[0].shape[0], out_ref.shape[1]
    begin = factors[0].shape[1] - width
    packed = (mine[...] + one[...]) + (two[...] + three[...])
    turned = pltpu.roll(packed, rank, 1)
    lane = lax.broadcasted_iota(I32, packed.shape, 1)
    values = jnp.concatenate(
        [jnp.where(lane < rank, packed, turned), jnp.where(lane < rank, turned, packed)], axis=0
    )
    wide = jnp.concatenate([values] * (GROUP // 2), axis=1)
    total = None
    for group in range(len(factors) // GROUP):
        mask = group_mask(*own_ends(bounds_ref, group, GROUP * rank), wide.shape)
        chosen = jnp.where(mask, wide, 0.0).astype(BF16)
        factor = jnp.concatenate(
            [ref[:, begin:] for ref in factors[group * GROUP : (group + 1) * GROUP]], axis=0
        )
        part = jnp.dot(chosen, factor, preferred_element_type=F32)
        total = part if total is None else total + part
    adapted = total.astype(BF16).astype(F32)
    out_ref[...] = ((near_ref[...] + far_ref[...]) + adapted).astype(BF16)


def per_device(hidden, demand, lengths, holder_slot, value_weight, factor_in, factor_out):
    rows, features = hidden.shape
    owners = lax.axis_size("batch")
    rank, width = factor_out.shape[1:]
    depth = features // 2
    order = ring_order(owners)
    forward = [(order[i], order[(i + 1) % owners]) for i in range(owners)]
    backward = [(b, a) for a, b in forward]
    swap = [(0, 1), (1, 0)]

    full = (owners - 1) // 2
    distances = [0]
    for step in range(1, full + 1):
        distances += [step, -step]
    distances.append(owners // 2)
    table = [
        [[order[(order.index(me) - distance) % owners] for distance in distances]]
        for me in range(owners)
    ]
    to_other, first, second, bounds = prologue(
        hidden,
        factor_in[0].T,
        factor_out[0],
        demand,
        lengths,
        holder_slot,
        jnp.asarray(table, I32),
    )

    bounds, first_later, second_later = lax.optimization_barrier((mark(bounds), first, second))

    firsts, seconds = [first], [second]
    ahead, behind = (first, second_later), (first_later, second)
    for step in range(1, full + 1):
        a = lax.ppermute(ahead[0], "batch", forward)
        d = lax.ppermute(behind[1], "batch", backward)
        b = lax.ppermute(ahead[1], "batch", forward)
        c = lax.ppermute(behind[0], "batch", backward)
        ahead, behind = (a, b), (c, d)
        firsts += [a, c]
        seconds += [b, d]
    firsts.append(lax.ppermute(ahead[0], "batch", forward))
    seconds.append(lax.ppermute(behind[1], "batch", backward))
    near, far = base_call(hidden, value_weight)
    hidden, near, far = lax.optimization_barrier((hidden, near, far))
    other = lax.ppermute(to_other, "groups", swap)

    count = owners // GROUP
    early = range(count - 1)
    pieces = []
    for group in early:
        pieces += firsts[group * GROUP : (group + 1) * GROUP]
        pieces += seconds[group * GROUP : (group + 1) * GROUP]
    both = (hidden, other)
    start_mine, start_theirs = rank_call(
        (0, 1), tuple(early), depth, rows, both, bounds, pieces, ()
    )
    start_theirs, far = lax.optimization_barrier((start_theirs, far))
    far = lax.ppermute(far, "tensor", swap)
    pieces = firsts[-GROUP:] + seconds[-GROUP:]
    late = (count - 1,)
    (theirs,) = rank_call((1,), late, depth, rows, (other,), bounds, pieces, (start_theirs,))
    (mine,) = rank_call((0,), late, depth, rows, (hidden,), bounds, pieces, (start_mine,))

    two = lax.ppermute(theirs, "groups", swap)
    three = lax.ppermute(theirs, ("groups", "tensor"), [(0, 3), (1, 2), (2, 1), (3, 0)])
    one = lax.ppermute(mine, "tensor", swap)

    operands = [bounds, mine, one, two, three, near, far, *seconds]
    return pl.pallas_call(
        final_kernel,
        out_shape=jax.ShapeDtypeStruct((rows, width), BF16),
        in_specs=[VMEM] * len(operands),
        out_specs=VMEM,
        compiler_params=params(),
    )(*operands)


def solution(mesh):
    return jax.shard_map(
        per_device,
        mesh=mesh,
        in_specs=(
            P(("groups", "batch"), "tensor"),
            P(("groups", "batch"), None),
            P(("groups", "batch"), None),
            P(),
            P("tensor", None),
            P("batch", "tensor", None),
            P("batch", None, "tensor"),
        ),
        out_specs=P(("groups", "batch"), "tensor"),
        check_vma=False,
    )
```

```python
import functools

import jax
import jax.numpy as jnp
from jax import lax
from jax.experimental import pallas as pl
from jax.experimental.pallas import tpu as pltpu
from jax.sharding import PartitionSpec as P

F32, BF16, I32 = jnp.float32, jnp.bfloat16, jnp.int32
VMEM_LIMIT = 24 * 1024 * 1024
HALF = pl.CostEstimate(flops=0, bytes_accessed=1 << 22, transcendentals=0)
LONG = pl.CostEstimate(flops=1 << 33, bytes_accessed=1 << 24, transcendentals=0)
GROUP = 4
VMEM = pl.BlockSpec(memory_space=pltpu.VMEM)
HBM = pl.BlockSpec(memory_space=pltpu.HBM)


def in_hbm(array):
    return pltpu.with_memory_space_constraint(array, pltpu.HBM)


def params():
    return pltpu.CompilerParams(vmem_limit_bytes=VMEM_LIMIT)


def ring_order(size):
    if size % 4:
        return list(range(size))
    columns = size // 4
    order = [0]
    for row in range(4):
        across = range(1, columns) if row % 2 == 0 else range(columns - 1, 0, -1)
        order += [row * columns + column for column in across]
    return order + [row * columns for row in (3, 2, 1)]


def contract(left, right):
    return lax.dot_general(left, right, (((1,), (1,)), ((), ())), preferred_element_type=F32)


def extra_rows(columns):
    return 2 * -(-columns // 1024) * 8


def prologue_kernel(
    depth,
    rank,
    hidden_ref,
    factor_ref,
    factor_out_ref,
    demand_ref,
    lengths_ref,
    holder_ref,
    slots_ref,
    to_other_ref,
    first_ref,
    second_ref,
    bounds_ref,
    demand,
    lengths,
    holder,
    slots,
    sems,
    hidden_sem,
):
    group, place = lax.axis_index("groups"), lax.axis_index("batch")
    cut = first_ref.shape[1]
    rows = hidden_ref.shape[0]
    here = pl.multiple_of(group * depth, 128)
    there = pl.multiple_of((1 - group) * depth, 128)
    after = pl.multiple_of(group * depth + cut, 128)
    small = [
        pltpu.make_async_copy(demand_ref, demand, sems.at[0]),
        pltpu.make_async_copy(lengths_ref, lengths, sems.at[1]),
        pltpu.make_async_copy(holder_ref, holder, sems.at[2]),
        pltpu.make_async_copy(slots_ref.at[pl.ds(place, 1)], slots, sems.at[3]),
    ]
    large = [
        pltpu.make_async_copy(factor_ref.at[:, pl.ds(here, cut)], first_ref, sems.at[4]),
        pltpu.make_async_copy(
            factor_ref.at[:, pl.ds(after, depth - cut)], second_ref.at[:, : depth - cut], sems.at[5]
        ),
        pltpu.make_async_copy(factor_out_ref, second_ref.at[:, depth - cut :], sems.at[6]),
    ]
    for i in range(depth // 128):
        large.append(
            pltpu.make_async_copy(
                hidden_ref.at[:, pl.ds(there + i * 128, 128)],
                to_other_ref.at[i * rows : (i + 1) * rows],
                hidden_sem.at[i],
            )
        )
    for copy in small + large:
        copy.start()
    for copy in small:
        copy.wait()
    count = slots.shape[2]
    items = demand.shape[1]
    column = lax.broadcasted_iota(I32, (1, count * rank), 1)
    zero = jnp.int32(0)

    def chunk_mask(chunk):
        return (column >= chunk * rank) & (column < (chunk + 1) * rank)

    low = high = jnp.zeros((1, count * rank), I32)
    if items * count <= 64:
        start = zero
        spans = []
        for item in range(items):
            end = start + lengths[0, item]
            spans.append((holder[demand[0, item]], start, end))
            start = end
        for chunk in range(count):
            slot = slots[0, 0, chunk]
            begin = end = zero
            for owner, first, last in spans:
                begin = jnp.where(owner == slot, first, begin)
                end = jnp.where(owner == slot, last, end)
            low = jnp.where(chunk_mask(chunk), begin, low)
            high = jnp.where(chunk_mask(chunk), end, high)
    else:

        def chunk_ends(chunk, carry):
            low, high = carry
            slot = slots[0, 0, chunk]

            def item_ends(item, state):
                start, begin, end = state
                last = start + lengths[0, item]
                hit = holder[demand[0, item]] == slot
                return last, jnp.where(hit, start, begin), jnp.where(hit, last, end)

            _, begin, end = lax.fori_loop(0, items, item_ends, (zero, zero, zero))
            mask = chunk_mask(chunk)
            return jnp.where(mask, begin, low), jnp.where(mask, end, high)

        low, high = lax.fori_loop(0, count, chunk_ends, (low, high))
    bounds_ref[0:1, :] = low
    bounds_ref[1:2, :] = high
    bounds_ref[2:8, :] = jnp.zeros((6, count * rank), I32)
    extra = extra_rows(count * rank)
    line = lax.broadcasted_iota(I32, (extra, 128), 0)
    ends = jnp.zeros((extra, 128), I32)
    for i in range(count * rank // 128):
        columns = slice(i * 128, (i + 1) * 128)
        ends = jnp.where(line == i, low[:, columns], ends)
        ends = jnp.where(line == extra // 2 + i, high[:, columns], ends)
    to_other_ref[-extra:, :] = ends.astype(F32).astype(BF16)
    for copy in large:
        copy.wait()


def prologue(hidden, factor, factor_out, demand, lengths, holder_slot, slots):
    rows, features = hidden.shape
    rank, width = factor_out.shape
    depth = features // 2
    cut = (depth + width) // 2
    count = slots.shape[2]
    tall = depth // 128 * rows + extra_rows(count * rank)
    return pl.pallas_call(
        functools.partial(prologue_kernel, depth, rank),
        out_shape=(
            jax.ShapeDtypeStruct((tall, 128), hidden.dtype),
            jax.ShapeDtypeStruct((rank, cut), factor.dtype),
            jax.ShapeDtypeStruct((rank, cut), factor.dtype),
            jax.ShapeDtypeStruct((8, count * rank), I32),
        ),
        in_specs=[HBM] * 7,
        out_specs=(VMEM,) * 4,
        scratch_shapes=[
            pltpu.SMEM(demand.shape, I32),
            pltpu.SMEM(lengths.shape, I32),
            pltpu.SMEM(holder_slot.shape, I32),
            pltpu.SMEM((1, 1, count), I32),
            pltpu.SemaphoreType.DMA((7,)),
            pltpu.SemaphoreType.DMA((depth // 128,)),
        ],
        compiler_params=params(),
    )(*map(in_hbm, (hidden, factor, factor_out, demand, lengths, holder_slot, slots)))


def mark_kernel(bounds_ref, out_ref):
    out_ref[...] = bounds_ref[...]


def mark(bounds):
    return pl.pallas_call(
        mark_kernel,
        out_shape=jax.ShapeDtypeStruct(bounds.shape, bounds.dtype),
        in_specs=[VMEM],
        out_specs=VMEM,
        compiler_params=params(),
        cost_estimate=LONG,
    )(bounds)


def base_kernel(rows_ref, weight_ref, near_ref, far_ref):
    width = near_ref.shape[1]
    core = lax.axis_index("tensor")
    for out_ref, side in ((near_ref, core), (far_ref, 1 - core)):
        columns = pl.ds(pl.multiple_of(side * width, 128), width)
        out_ref[...] = jnp.dot(
            rows_ref[...], weight_ref[:, columns], preferred_element_type=F32
        )


def base_call(rows, weight):
    out = jax.ShapeDtypeStruct((rows.shape[0], weight.shape[1] // 2), F32)
    return pl.pallas_call(
        base_kernel,
        out_shape=(out, out),
        in_specs=[VMEM] * 2,
        out_specs=(VMEM,) * 2,
        compiler_params=params(),
        cost_estimate=HALF,
    )(rows, weight)


def group_mask(low, high, shape):
    row = lax.broadcasted_iota(I32, shape, 0)
    return (row >= low) & (row < high)


def own_ends(bounds_ref, group, size):
    columns = slice(group * size, (group + 1) * size)
    return bounds_ref[0:1, columns], bounds_ref[1:2, columns]


def other_ends(other_ref, extra, group, size):
    ends = other_ref[-extra:, :].astype(F32).astype(I32)
    lines = range(group * size // 128, (group + 1) * size // 128)
    low = jnp.concatenate([ends[i : i + 1] for i in lines], axis=1)
    high = jnp.concatenate([ends[extra // 2 + i : extra // 2 + i + 1] for i in lines], axis=1)
    return low, high


def fold(masked):
    total = masked[:, :128]
    for begin in range(128, masked.shape[1], 128):
        total = total + masked[:, begin : begin + 128]
    return total


def rank_kernel(sides, groups, depth, last, *refs):
    refs = list(refs)
    rows_refs, refs = refs[: len(sides)], refs[len(sides) :]
    bounds_ref, pieces = refs[0], refs[1:]
    pieces, rest = pieces[: 2 * GROUP * len(groups)], pieces[2 * GROUP * len(groups) :]
    starts, outs = (rest[: len(sides)], rest[len(sides) :]) if last else ((), rest)
    cut = pieces[0].shape[1]
    rank = pieces[0].shape[0]
    size = GROUP * rank
    extra = extra_rows(bounds_ref.shape[1])
    rows = []
    for side, ref in zip(sides, rows_refs):
        if side == 0:
            offset = pl.multiple_of(lax.axis_index("groups") * depth, 128)
            rows.append(ref[:, pl.ds(offset, depth)])
        else:
            blocks = depth // 128
            tall = (ref.shape[0] - extra) // blocks
            rows.append(
                jnp.concatenate([ref[i * tall : (i + 1) * tall, :] for i in range(blocks)], axis=1)
            )
    count = rows[0].shape[0]
    rows = jnp.concatenate(rows, axis=0)
    totals = [ref[...] for ref in starts] if last else [None] * len(sides)
    for i, group in enumerate(groups):
        held = pieces[2 * GROUP * i : 2 * GROUP * (i + 1)]
        first = jnp.concatenate([ref[...] for ref in held[:GROUP]], axis=0)
        second = jnp.concatenate([ref[:, : depth - cut] for ref in held[GROUP:]], axis=0)
        part = contract(rows, jnp.concatenate([first, second], axis=1))
        for s, side in enumerate(sides):
            if side == 0:
                ends = own_ends(bounds_ref, group, size)
            else:
                ends = other_ends(rows_refs[s], extra, group, size)
            here = part[s * count : (s + 1) * count]
            kept = fold(jnp.where(group_mask(*ends, here.shape), here, 0.0))
            totals[s] = kept if totals[s] is None else totals[s] + kept
    if last:
        (total,) = totals
        total = total + pltpu.roll(total, rank, 1)
        half = count // 2
        lane = lax.broadcasted_iota(I32, (half, 2 * rank), 1)
        total = jnp.where(lane < rank, total[:half], total[half:])
        size = outs[0].shape[0]
        totals = [total[i * size : (i + 1) * size] for i in range(len(outs))]
    for total, out_ref in zip(totals, outs):
        out_ref[...] = total.astype(out_ref.dtype)


def rank_call(sides, groups, depth, count, rows, bounds, pieces, starts):
    rank = pieces[0].shape[0]
    last = len(starts) > 0
    if not last:
        out = (jax.ShapeDtypeStruct((count, 2 * rank), F32),) * len(sides)
    elif sides == (1,):
        out = (jax.ShapeDtypeStruct((count // 2, 2 * rank), BF16),)
    else:
        out = (jax.ShapeDtypeStruct((count // 4, 2 * rank), F32),) * 2
    operands = [*rows, bounds, *pieces, *starts]
    return pl.pallas_call(
        functools.partial(rank_kernel, sides, groups, depth, last),
        out_shape=out,
        in_specs=[VMEM] * len(operands),
        out_specs=(VMEM,) * len(out),
        compiler_params=params(),
        cost_estimate=HALF if last and sides == (0,) else LONG,
    )(*operands)


def final_kernel(bounds_ref, top, low, one_top, one_low, two, three, near_ref, far_ref, *refs):
    factors, out_ref = refs[:-1], refs[-1]
    rank, width = factors[0].shape[0], out_ref.shape[1]
    begin = factors[0].shape[1] - width
    here = jnp.concatenate([top[...] + one_top[...], low[...] + one_low[...]], axis=0)
    packed = here + (two[...].astype(F32) + three[...].astype(F32))
    turned = pltpu.roll(packed, rank, 1)
    lane = lax.broadcasted_iota(I32, packed.shape, 1)
    values = jnp.concatenate(
        [jnp.where(lane < rank, packed, turned), jnp.where(lane < rank, turned, packed)], axis=0
    )
    wide = jnp.concatenate([values] * (GROUP // 2), axis=1)
    total = None
    for group in range(len(factors) // GROUP):
        mask = group_mask(*own_ends(bounds_ref, group, GROUP * rank), wide.shape)
        chosen = jnp.where(mask, wide, 0.0).astype(BF16)
        factor = jnp.concatenate(
            [ref[:, begin:] for ref in factors[group * GROUP : (group + 1) * GROUP]], axis=0
        )
        part = jnp.dot(chosen, factor, preferred_element_type=F32)
        total = part if total is None else total + part
    adapted = total.astype(BF16).astype(F32)
    out_ref[...] = ((near_ref[...] + far_ref[...]) + adapted).astype(BF16)


def per_device(hidden, demand, lengths, holder_slot, value_weight, factor_in, factor_out):
    rows, features = hidden.shape
    owners = lax.axis_size("batch")
    rank, width = factor_out.shape[1:]
    depth = features // 2
    order = ring_order(owners)
    forward = [(order[i], order[(i + 1) % owners]) for i in range(owners)]
    backward = [(b, a) for a, b in forward]
    swap = [(0, 1), (1, 0)]

    full = (owners - 1) // 2
    distances = [0]
    for step in range(1, full + 1):
        distances += [step, -step]
    distances.append(owners // 2)
    table = [
        [[order[(order.index(me) - distance) % owners] for distance in distances]]
        for me in range(owners)
    ]
    to_other, first, second, bounds = prologue(
        hidden,
        factor_in[0].T,
        factor_out[0],
        demand,
        lengths,
        holder_slot,
        jnp.asarray(table, I32),
    )

    bounds, first_later, second_later = lax.optimization_barrier((mark(bounds), first, second))

    firsts, seconds = [first], [second]
    ahead, behind = (first, second_later), (first_later, second)
    for step in range(1, full + 1):
        a = lax.ppermute(ahead[0], "batch", forward)
        d = lax.ppermute(behind[1], "batch", backward)
        b = lax.ppermute(ahead[1], "batch", forward)
        c = lax.ppermute(behind[0], "batch", backward)
        ahead, behind = (a, b), (c, d)
        firsts += [a, c]
        seconds += [b, d]
    firsts.append(lax.ppermute(ahead[0], "batch", forward))
    seconds.append(lax.ppermute(behind[1], "batch", backward))
    near, far = base_call(hidden, value_weight)
    hidden, near, far = lax.optimization_barrier((hidden, near, far))
    other = lax.ppermute(to_other, "groups", swap)

    count = owners // GROUP
    early = range(count - 1)
    pieces = []
    for group in early:
        pieces += firsts[group * GROUP : (group + 1) * GROUP]
        pieces += seconds[group * GROUP : (group + 1) * GROUP]
    both = (hidden, other)
    start_mine, start_theirs = rank_call(
        (0, 1), tuple(early), depth, rows, both, bounds, pieces, ()
    )
    start_theirs, far = lax.optimization_barrier((start_theirs, far))
    far = lax.ppermute(far, "tensor", swap)
    pieces = firsts[-GROUP:] + seconds[-GROUP:]
    late = (count - 1,)
    (theirs,) = rank_call((1,), late, depth, rows, (other,), bounds, pieces, (start_theirs,))
    mine = rank_call((0,), late, depth, rows, (hidden,), bounds, pieces, (start_mine,))

    two = lax.ppermute(theirs, "groups", swap)
    three = lax.ppermute(theirs, ("groups", "tensor"), [(0, 3), (1, 2), (2, 1), (3, 0)])
    one = [lax.ppermute(part, "tensor", swap) for part in mine]

    operands = [bounds, *mine, *one, two, three, near, far, *seconds]
    return pl.pallas_call(
        final_kernel,
        out_shape=jax.ShapeDtypeStruct((rows, width), BF16),
        in_specs=[VMEM] * len(operands),
        out_specs=VMEM,
        compiler_params=params(),
    )(*operands)


def solution(mesh):
    return jax.shard_map(
        per_device,
        mesh=mesh,
        in_specs=(
            P(("groups", "batch"), "tensor"),
            P(("groups", "batch"), None),
            P(("groups", "batch"), None),
            P(),
            P("tensor", None),
            P("batch", "tensor", None),
            P("batch", None, "tensor"),
        ),
        out_specs=P(("groups", "batch"), "tensor"),
        check_vma=False,
    )
```

```python
import functools

import jax
import jax.numpy as jnp
from jax import lax
from jax.experimental import pallas as pl
from jax.experimental.pallas import tpu as pltpu
from jax.sharding import PartitionSpec as P

F32, BF16, I32 = jnp.float32, jnp.bfloat16, jnp.int32
VMEM_LIMIT = 24 * 1024 * 1024
HALF = pl.CostEstimate(flops=0, bytes_accessed=1 << 22, transcendentals=0)
LONG = pl.CostEstimate(flops=1 << 33, bytes_accessed=1 << 24, transcendentals=0)
GROUP = 4
VMEM = pl.BlockSpec(memory_space=pltpu.VMEM)
HBM = pl.BlockSpec(memory_space=pltpu.HBM)


def in_hbm(array):
    return pltpu.with_memory_space_constraint(array, pltpu.HBM)


def params():
    return pltpu.CompilerParams(vmem_limit_bytes=VMEM_LIMIT)


def ring_order(size):
    if size % 4:
        return list(range(size))
    columns = size // 4
    order = [0]
    for row in range(4):
        across = range(1, columns) if row % 2 == 0 else range(columns - 1, 0, -1)
        order += [row * columns + column for column in across]
    return order + [row * columns for row in (3, 2, 1)]


def contract(left, right):
    return lax.dot_general(left, right, (((1,), (1,)), ((), ())), preferred_element_type=F32)


def extra_rows(columns):
    return 2 * -(-columns // 1024) * 8


def shard_kernel(
    depth,
    rank,
    factor_ref,
    factor_out_ref,
    demand_ref,
    lengths_ref,
    holder_ref,
    slots_ref,
    first_ref,
    second_ref,
    bounds_ref,
    demand,
    lengths,
    holder,
    slots,
    sems,
):
    group, place = lax.axis_index("groups"), lax.axis_index("batch")
    cut = first_ref.shape[1]
    here = pl.multiple_of(group * depth, 128)
    after = pl.multiple_of(group * depth + cut, 128)
    small = [
        pltpu.make_async_copy(demand_ref, demand, sems.at[0]),
        pltpu.make_async_copy(lengths_ref, lengths, sems.at[1]),
        pltpu.make_async_copy(holder_ref, holder, sems.at[2]),
        pltpu.make_async_copy(slots_ref.at[pl.ds(place, 1)], slots, sems.at[3]),
    ]
    large = [
        pltpu.make_async_copy(factor_ref.at[:, pl.ds(here, cut)], first_ref, sems.at[4]),
        pltpu.make_async_copy(
            factor_ref.at[:, pl.ds(after, depth - cut)], second_ref.at[:, : depth - cut], sems.at[5]
        ),
        pltpu.make_async_copy(factor_out_ref, second_ref.at[:, depth - cut :], sems.at[6]),
    ]
    for copy in small + large:
        copy.start()
    for copy in small:
        copy.wait()
    count = slots.shape[2]
    items = demand.shape[1]
    column = lax.broadcasted_iota(I32, (1, count * rank), 1)
    zero = jnp.int32(0)

    def chunk_mask(chunk):
        return (column >= chunk * rank) & (column < (chunk + 1) * rank)

    low = high = jnp.zeros((1, count * rank), I32)
    if items * count <= 64:
        start = zero
        spans = []
        for item in range(items):
            end = start + lengths[0, item]
            spans.append((holder[demand[0, item]], start, end))
            start = end
        for chunk in range(count):
            slot = slots[0, 0, chunk]
            begin = end = zero
            for owner, first, last in spans:
                begin = jnp.where(owner == slot, first, begin)
                end = jnp.where(owner == slot, last, end)
            low = jnp.where(chunk_mask(chunk), begin, low)
            high = jnp.where(chunk_mask(chunk), end, high)
    else:

        def chunk_ends(chunk, carry):
            low, high = carry
            slot = slots[0, 0, chunk]

            def item_ends(item, state):
                start, begin, end = state
                last = start + lengths[0, item]
                hit = holder[demand[0, item]] == slot
                return last, jnp.where(hit, start, begin), jnp.where(hit, last, end)

            _, begin, end = lax.fori_loop(0, items, item_ends, (zero, zero, zero))
            mask = chunk_mask(chunk)
            return jnp.where(mask, begin, low), jnp.where(mask, end, high)

        low, high = lax.fori_loop(0, count, chunk_ends, (low, high))
    bounds_ref[0:1, :] = low
    bounds_ref[1:2, :] = high
    bounds_ref[2:8, :] = jnp.zeros((6, count * rank), I32)
    for copy in large:
        copy.wait()


def shard_call(factor, factor_out, demand, lengths, holder_slot, slots, depth):
    rank, width = factor_out.shape
    cut = (depth + width) // 2
    count = slots.shape[2]
    return pl.pallas_call(
        functools.partial(shard_kernel, depth, rank),
        out_shape=(
            jax.ShapeDtypeStruct((rank, cut), factor.dtype),
            jax.ShapeDtypeStruct((rank, cut), factor.dtype),
            jax.ShapeDtypeStruct((8, count * rank), I32),
        ),
        in_specs=[HBM] * 6,
        out_specs=(VMEM,) * 3,
        scratch_shapes=[
            pltpu.SMEM(demand.shape, I32),
            pltpu.SMEM(lengths.shape, I32),
            pltpu.SMEM(holder_slot.shape, I32),
            pltpu.SMEM((1, 1, count), I32),
            pltpu.SemaphoreType.DMA((7,)),
        ],
        compiler_params=params(),
        cost_estimate=LONG,
    )(*map(in_hbm, (factor, factor_out, demand, lengths, holder_slot, slots)))


def rows_kernel(depth, hidden_ref, bounds_ref, to_other_ref, bounds_out_ref):
    rows = hidden_ref.shape[0]
    there = pl.multiple_of((1 - lax.axis_index("groups")) * depth, 128)
    for i in range(depth // 128):
        to_other_ref[i * rows : (i + 1) * rows, :] = hidden_ref[:, pl.ds(there + i * 128, 128)]
    columns = bounds_ref.shape[1]
    extra = extra_rows(columns)
    line = lax.broadcasted_iota(I32, (extra, 128), 0)
    ends = jnp.zeros((extra, 128), I32)
    for i in range(columns // 128):
        span = slice(i * 128, (i + 1) * 128)
        ends = jnp.where(line == i, bounds_ref[0:1, span], ends)
        ends = jnp.where(line == extra // 2 + i, bounds_ref[1:2, span], ends)
    to_other_ref[-extra:, :] = ends.astype(F32).astype(BF16)
    bounds_out_ref[...] = bounds_ref[...]


def rows_call(hidden, bounds):
    rows, features = hidden.shape
    depth = features // 2
    tall = depth // 128 * rows + extra_rows(bounds.shape[1])
    return pl.pallas_call(
        functools.partial(rows_kernel, depth),
        out_shape=(
            jax.ShapeDtypeStruct((tall, 128), hidden.dtype),
            jax.ShapeDtypeStruct(bounds.shape, I32),
        ),
        in_specs=[VMEM] * 2,
        out_specs=(VMEM,) * 2,
        compiler_params=params(),
        cost_estimate=LONG,
    )(hidden, bounds)


def mark_kernel(bounds_ref, out_ref):
    out_ref[...] = bounds_ref[...]


def mark(bounds):
    return pl.pallas_call(
        mark_kernel,
        out_shape=jax.ShapeDtypeStruct(bounds.shape, bounds.dtype),
        in_specs=[VMEM],
        out_specs=VMEM,
        compiler_params=params(),
        cost_estimate=LONG,
    )(bounds)


def base_kernel(rows_ref, weight_ref, near_ref, far_ref):
    width = near_ref.shape[1]
    core = lax.axis_index("tensor")
    for out_ref, side in ((near_ref, core), (far_ref, 1 - core)):
        columns = pl.ds(pl.multiple_of(side * width, 128), width)
        out_ref[...] = jnp.dot(
            rows_ref[...], weight_ref[:, columns], preferred_element_type=F32
        )


def base_call(rows, weight):
    out = jax.ShapeDtypeStruct((rows.shape[0], weight.shape[1] // 2), F32)
    return pl.pallas_call(
        base_kernel,
        out_shape=(out, out),
        in_specs=[VMEM] * 2,
        out_specs=(VMEM,) * 2,
        compiler_params=params(),
        cost_estimate=HALF,
    )(rows, weight)


def group_mask(low, high, shape):
    row = lax.broadcasted_iota(I32, shape, 0)
    return (row >= low) & (row < high)


def own_ends(bounds_ref, group, size):
    columns = slice(group * size, (group + 1) * size)
    return bounds_ref[0:1, columns], bounds_ref[1:2, columns]


def other_ends(other_ref, extra, group, size):
    ends = other_ref[-extra:, :].astype(F32).astype(I32)
    lines = range(group * size // 128, (group + 1) * size // 128)
    low = jnp.concatenate([ends[i : i + 1] for i in lines], axis=1)
    high = jnp.concatenate([ends[extra // 2 + i : extra // 2 + i + 1] for i in lines], axis=1)
    return low, high


def fold(masked):
    total = masked[:, :128]
    for begin in range(128, masked.shape[1], 128):
        total = total + masked[:, begin : begin + 128]
    return total


def rank_kernel(sides, groups, depth, last, *refs):
    refs = list(refs)
    rows_refs, refs = refs[: len(sides)], refs[len(sides) :]
    bounds_ref, pieces = refs[0], refs[1:]
    pieces, rest = pieces[: 2 * GROUP * len(groups)], pieces[2 * GROUP * len(groups) :]
    starts, outs = (rest[: len(sides)], rest[len(sides) :]) if last else ((), rest)
    cut = pieces[0].shape[1]
    rank = pieces[0].shape[0]
    size = GROUP * rank
    extra = extra_rows(bounds_ref.shape[1])
    rows = []
    for side, ref in zip(sides, rows_refs):
        if side == 0:
            offset = pl.multiple_of(lax.axis_index("groups") * depth, 128)
            rows.append(ref[:, pl.ds(offset, depth)])
        else:
            blocks = depth // 128
            tall = (ref.shape[0] - extra) // blocks
            rows.append(
                jnp.concatenate([ref[i * tall : (i + 1) * tall, :] for i in range(blocks)], axis=1)
            )
    count = rows[0].shape[0]
    rows = jnp.concatenate(rows, axis=0)
    totals = [ref[...] for ref in starts] if last else [None] * len(sides)
    for i, group in enumerate(groups):
        held = pieces[2 * GROUP * i : 2 * GROUP * (i + 1)]
        first = jnp.concatenate([ref[...] for ref in held[:GROUP]], axis=0)
        second = jnp.concatenate([ref[:, : depth - cut] for ref in held[GROUP:]], axis=0)
        part = contract(rows, jnp.concatenate([first, second], axis=1))
        for s, side in enumerate(sides):
            if side == 0:
                ends = own_ends(bounds_ref, group, size)
            else:
                ends = other_ends(rows_refs[s], extra, group, size)
            here = part[s * count : (s + 1) * count]
            kept = fold(jnp.where(group_mask(*ends, here.shape), here, 0.0))
            totals[s] = kept if totals[s] is None else totals[s] + kept
    if last:
        (total,) = totals
        total = total + pltpu.roll(total, rank, 1)
        half = count // 2
        lane = lax.broadcasted_iota(I32, (half, 2 * rank), 1)
        total = jnp.where(lane < rank, total[:half], total[half:])
        size = outs[0].shape[0]
        totals = [total[i * size : (i + 1) * size] for i in range(len(outs))]
    for total, out_ref in zip(totals, outs):
        out_ref[...] = total.astype(out_ref.dtype)


def rank_call(sides, groups, depth, count, rows, bounds, pieces, starts):
    rank = pieces[0].shape[0]
    last = len(starts) > 0
    if not last:
        out = (jax.ShapeDtypeStruct((count, 2 * rank), F32),) * len(sides)
    elif sides == (1,):
        out = (jax.ShapeDtypeStruct((count // 2, 2 * rank), BF16),)
    else:
        out = (jax.ShapeDtypeStruct((count // 4, 2 * rank), F32),) * 2
    operands = [*rows, bounds, *pieces, *starts]
    return pl.pallas_call(
        functools.partial(rank_kernel, sides, groups, depth, last),
        out_shape=out,
        in_specs=[VMEM] * len(operands),
        out_specs=(VMEM,) * len(out),
        compiler_params=params(),
        cost_estimate=HALF if last and sides == (0,) else LONG,
    )(*operands)


def final_kernel(bounds_ref, top, low, one_top, one_low, two, three, near_ref, far_ref, *refs):
    factors, out_ref = refs[:-1], refs[-1]
    rank, width = factors[0].shape[0], out_ref.shape[1]
    begin = factors[0].shape[1] - width
    here = jnp.concatenate([top[...] + one_top[...], low[...] + one_low[...]], axis=0)
    packed = here + (two[...].astype(F32) + three[...].astype(F32))
    turned = pltpu.roll(packed, rank, 1)
    lane = lax.broadcasted_iota(I32, packed.shape, 1)
    values = jnp.concatenate(
        [jnp.where(lane < rank, packed, turned), jnp.where(lane < rank, turned, packed)], axis=0
    )
    wide = jnp.concatenate([values] * (GROUP // 2), axis=1)
    total = None
    for group in range(len(factors) // GROUP):
        mask = group_mask(*own_ends(bounds_ref, group, GROUP * rank), wide.shape)
        chosen = jnp.where(mask, wide, 0.0).astype(BF16)
        factor = jnp.concatenate(
            [ref[:, begin:] for ref in factors[group * GROUP : (group + 1) * GROUP]], axis=0
        )
        part = jnp.dot(chosen, factor, preferred_element_type=F32)
        total = part if total is None else total + part
    adapted = total.astype(BF16).astype(F32)
    out_ref[...] = ((near_ref[...] + far_ref[...]) + adapted).astype(BF16)


def per_device(hidden, demand, lengths, holder_slot, value_weight, factor_in, factor_out):
    rows, features = hidden.shape
    owners = lax.axis_size("batch")
    rank, width = factor_out.shape[1:]
    depth = features // 2
    order = ring_order(owners)
    forward = [(order[i], order[(i + 1) % owners]) for i in range(owners)]
    backward = [(b, a) for a, b in forward]
    swap = [(0, 1), (1, 0)]

    full = (owners - 1) // 2
    distances = [0]
    for step in range(1, full + 1):
        distances += [step, -step]
    distances.append(owners // 2)
    table = [
        [[order[(order.index(me) - distance) % owners] for distance in distances]]
        for me in range(owners)
    ]
    first, second, bounds = shard_call(
        factor_in[0].T, factor_out[0], demand, lengths, holder_slot, jnp.asarray(table, I32), depth
    )
    to_other, bounds = rows_call(hidden, bounds)
    bounds, first_later, second_later = lax.optimization_barrier((mark(bounds), first, second))

    firsts, seconds = [first], [second]
    ahead, behind = (first, second_later), (first_later, second)
    for step in range(1, full + 1):
        a = lax.ppermute(ahead[0], "batch", forward)
        d = lax.ppermute(behind[1], "batch", backward)
        b = lax.ppermute(ahead[1], "batch", forward)
        c = lax.ppermute(behind[0], "batch", backward)
        ahead, behind = (a, b), (c, d)
        firsts += [a, c]
        seconds += [b, d]
    firsts.append(lax.ppermute(ahead[0], "batch", forward))
    seconds.append(lax.ppermute(behind[1], "batch", backward))
    near, far = base_call(hidden, value_weight)
    hidden, near, far = lax.optimization_barrier((hidden, near, far))
    other = lax.ppermute(to_other, "groups", swap)

    count = owners // GROUP
    early = range(count - 1)
    pieces = []
    for group in early:
        pieces += firsts[group * GROUP : (group + 1) * GROUP]
        pieces += seconds[group * GROUP : (group + 1) * GROUP]
    both = (hidden, other)
    start_mine, start_theirs = rank_call(
        (0, 1), tuple(early), depth, rows, both, bounds, pieces, ()
    )
    start_theirs, far = lax.optimization_barrier((start_theirs, far))
    far = lax.ppermute(far, "tensor", swap)
    pieces = firsts[-GROUP:] + seconds[-GROUP:]
    late = (count - 1,)
    (theirs,) = rank_call((1,), late, depth, rows, (other,), bounds, pieces, (start_theirs,))
    mine = rank_call((0,), late, depth, rows, (hidden,), bounds, pieces, (start_mine,))

    two = lax.ppermute(theirs, "groups", swap)
    three = lax.ppermute(theirs, ("groups", "tensor"), [(0, 3), (1, 2), (2, 1), (3, 0)])
    one = [lax.ppermute(part, "tensor", swap) for part in mine]

    operands = [bounds, *mine, *one, two, three, near, far, *seconds]
    return pl.pallas_call(
        final_kernel,
        out_shape=jax.ShapeDtypeStruct((rows, width), BF16),
        in_specs=[VMEM] * len(operands),
        out_specs=VMEM,
        compiler_params=params(),
    )(*operands)


def solution(mesh):
    return jax.shard_map(
        per_device,
        mesh=mesh,
        in_specs=(
            P(("groups", "batch"), "tensor"),
            P(("groups", "batch"), None),
            P(("groups", "batch"), None),
            P(),
            P("tensor", None),
            P("batch", "tensor", None),
            P("batch", None, "tensor"),
        ),
        out_specs=P(("groups", "batch"), "tensor"),
        check_vma=False,
    )
```

```python
import functools

import jax
import jax.numpy as jnp
from jax import lax
from jax.experimental import pallas as pl
from jax.experimental.pallas import tpu as pltpu
from jax.sharding import PartitionSpec as P

F32, BF16, I32 = jnp.float32, jnp.bfloat16, jnp.int32
VMEM_LIMIT = 24 * 1024 * 1024
HALF = pl.CostEstimate(flops=0, bytes_accessed=1 << 22, transcendentals=0)
LONG = pl.CostEstimate(flops=1 << 33, bytes_accessed=1 << 24, transcendentals=0)
GROUP = 4
VMEM = pl.BlockSpec(memory_space=pltpu.VMEM)
HBM = pl.BlockSpec(memory_space=pltpu.HBM)


def in_hbm(array):
    return pltpu.with_memory_space_constraint(array, pltpu.HBM)


def params():
    return pltpu.CompilerParams(vmem_limit_bytes=VMEM_LIMIT)


def ring_order(size):
    if size % 4:
        return list(range(size))
    columns = size // 4
    order = [0]
    for row in range(4):
        across = range(1, columns) if row % 2 == 0 else range(columns - 1, 0, -1)
        order += [row * columns + column for column in across]
    return order + [row * columns for row in (3, 2, 1)]


def contract(left, right):
    return lax.dot_general(left, right, (((1,), (1,)), ((), ())), preferred_element_type=F32)


def extra_rows(columns):
    return 2 * -(-columns // 1024) * 8


def shard_kernel(
    depth,
    rank,
    factor_ref,
    factor_out_ref,
    demand_ref,
    lengths_ref,
    holder_ref,
    slots_ref,
    first_ref,
    second_ref,
    bounds_ref,
    demand,
    lengths,
    holder,
    slots,
    sems,
):
    group, place = lax.axis_index("groups"), lax.axis_index("batch")
    cut = first_ref.shape[1]
    here = pl.multiple_of(group * depth, 128)
    after = pl.multiple_of(group * depth + cut, 128)
    small = [
        pltpu.make_async_copy(demand_ref, demand, sems.at[0]),
        pltpu.make_async_copy(lengths_ref, lengths, sems.at[1]),
        pltpu.make_async_copy(holder_ref, holder, sems.at[2]),
        pltpu.make_async_copy(slots_ref.at[pl.ds(place, 1)], slots, sems.at[3]),
    ]
    large = [
        pltpu.make_async_copy(factor_ref.at[:, pl.ds(here, cut)], first_ref, sems.at[4]),
        pltpu.make_async_copy(
            factor_ref.at[:, pl.ds(after, depth - cut)], second_ref.at[:, : depth - cut], sems.at[5]
        ),
        pltpu.make_async_copy(factor_out_ref, second_ref.at[:, depth - cut :], sems.at[6]),
    ]
    for copy in small + large:
        copy.start()
    for copy in small:
        copy.wait()
    count = slots.shape[2]
    items = demand.shape[1]
    column = lax.broadcasted_iota(I32, (1, count * rank), 1)
    zero = jnp.int32(0)

    def chunk_mask(chunk):
        return (column >= chunk * rank) & (column < (chunk + 1) * rank)

    low = high = jnp.zeros((1, count * rank), I32)
    if items * count <= 64:
        start = zero
        spans = []
        for item in range(items):
            end = start + lengths[0, item]
            spans.append((holder[demand[0, item]], start, end))
            start = end
        for chunk in range(count):
            slot = slots[0, 0, chunk]
            begin = end = zero
            for owner, first, last in spans:
                begin = jnp.where(owner == slot, first, begin)
                end = jnp.where(owner == slot, last, end)
            low = jnp.where(chunk_mask(chunk), begin, low)
            high = jnp.where(chunk_mask(chunk), end, high)
    else:

        def chunk_ends(chunk, carry):
            low, high = carry
            slot = slots[0, 0, chunk]

            def item_ends(item, state):
                start, begin, end = state
                last = start + lengths[0, item]
                hit = holder[demand[0, item]] == slot
                return last, jnp.where(hit, start, begin), jnp.where(hit, last, end)

            _, begin, end = lax.fori_loop(0, items, item_ends, (zero, zero, zero))
            mask = chunk_mask(chunk)
            return jnp.where(mask, begin, low), jnp.where(mask, end, high)

        low, high = lax.fori_loop(0, count, chunk_ends, (low, high))
    bounds_ref[0:1, :] = low
    bounds_ref[1:2, :] = high
    bounds_ref[2:8, :] = jnp.zeros((6, count * rank), I32)
    for copy in large:
        copy.wait()


def shard_call(factor, factor_out, demand, lengths, holder_slot, slots, depth):
    rank, width = factor_out.shape
    cut = (depth + width) // 2
    count = slots.shape[2]
    return pl.pallas_call(
        functools.partial(shard_kernel, depth, rank),
        out_shape=(
            jax.ShapeDtypeStruct((rank, cut), factor.dtype),
            jax.ShapeDtypeStruct((rank, cut), factor.dtype),
            jax.ShapeDtypeStruct((8, count * rank), I32),
        ),
        in_specs=[HBM] * 6,
        out_specs=(VMEM,) * 3,
        scratch_shapes=[
            pltpu.SMEM(demand.shape, I32),
            pltpu.SMEM(lengths.shape, I32),
            pltpu.SMEM(holder_slot.shape, I32),
            pltpu.SMEM((1, 1, count), I32),
            pltpu.SemaphoreType.DMA((7,)),
        ],
        compiler_params=params(),
        cost_estimate=LONG,
    )(*map(in_hbm, (factor, factor_out, demand, lengths, holder_slot, slots)))


def rows_kernel(depth, hidden_ref, bounds_ref, to_other_ref, bounds_out_ref):
    rows = hidden_ref.shape[0]
    there = pl.multiple_of((1 - lax.axis_index("groups")) * depth, 128)
    for i in range(depth // 128):
        to_other_ref[i * rows : (i + 1) * rows, :] = hidden_ref[:, pl.ds(there + i * 128, 128)]
    columns = bounds_ref.shape[1]
    extra = extra_rows(columns)
    line = lax.broadcasted_iota(I32, (extra, 128), 0)
    ends = jnp.zeros((extra, 128), I32)
    for i in range(columns // 128):
        span = slice(i * 128, (i + 1) * 128)
        ends = jnp.where(line == i, bounds_ref[0:1, span], ends)
        ends = jnp.where(line == extra // 2 + i, bounds_ref[1:2, span], ends)
    to_other_ref[-extra:, :] = ends.astype(F32).astype(BF16)
    bounds_out_ref[...] = bounds_ref[...]


def rows_call(hidden, bounds):
    rows, features = hidden.shape
    depth = features // 2
    tall = depth // 128 * rows + extra_rows(bounds.shape[1])
    return pl.pallas_call(
        functools.partial(rows_kernel, depth),
        out_shape=(
            jax.ShapeDtypeStruct((tall, 128), hidden.dtype),
            jax.ShapeDtypeStruct(bounds.shape, I32),
        ),
        in_specs=[VMEM] * 2,
        out_specs=(VMEM,) * 2,
        compiler_params=params(),
        cost_estimate=LONG,
    )(hidden, bounds)


def mark_kernel(bounds_ref, out_ref):
    out_ref[...] = bounds_ref[...]


def mark(bounds):
    return pl.pallas_call(
        mark_kernel,
        out_shape=jax.ShapeDtypeStruct(bounds.shape, bounds.dtype),
        in_specs=[VMEM],
        out_specs=VMEM,
        compiler_params=params(),
        cost_estimate=LONG,
    )(bounds)


def base_kernel(size, rows_ref, weight_ref, bounds_ref, near_ref, far_ref, mask_ref):
    width = near_ref.shape[1]
    core = lax.axis_index("tensor")
    for out_ref, side in ((near_ref, core), (far_ref, 1 - core)):
        columns = pl.ds(pl.multiple_of(side * width, 128), width)
        out_ref[...] = jnp.dot(
            rows_ref[...], weight_ref[:, columns], preferred_element_type=F32
        )
    for group in range(mask_ref.shape[1] // size):
        mask = group_mask(*own_ends(bounds_ref, group, size), (rows_ref.shape[0], size))
        mask_ref[:, group * size : (group + 1) * size] = jnp.where(mask, 1.0, 0.0).astype(BF16)


def base_call(rows, weight, bounds, size):
    mask = jax.ShapeDtypeStruct((rows.shape[0], bounds.shape[1]), BF16)
    out = jax.ShapeDtypeStruct((rows.shape[0], weight.shape[1] // 2), F32)
    return pl.pallas_call(
        functools.partial(base_kernel, size),
        out_shape=(out, out, mask),
        in_specs=[VMEM] * 3,
        out_specs=(VMEM,) * 3,
        compiler_params=params(),
        cost_estimate=HALF,
    )(rows, weight, bounds)


def group_mask(low, high, shape):
    row = lax.broadcasted_iota(I32, shape, 0)
    return (row >= low) & (row < high)


def own_ends(bounds_ref, group, size):
    columns = slice(group * size, (group + 1) * size)
    return bounds_ref[0:1, columns], bounds_ref[1:2, columns]


def other_ends(other_ref, extra, group, size):
    ends = other_ref[-extra:, :].astype(F32).astype(I32)
    lines = range(group * size // 128, (group + 1) * size // 128)
    low = jnp.concatenate([ends[i : i + 1] for i in lines], axis=1)
    high = jnp.concatenate([ends[extra // 2 + i : extra // 2 + i + 1] for i in lines], axis=1)
    return low, high


def fold(masked):
    total = masked[:, :128]
    for begin in range(128, masked.shape[1], 128):
        total = total + masked[:, begin : begin + 128]
    return total


def rank_kernel(sides, groups, depth, last, *refs):
    refs = list(refs)
    rows_refs, refs = refs[: len(sides)], refs[len(sides) :]
    bounds_ref, pieces = refs[0], refs[1:]
    pieces, rest = pieces[: 2 * GROUP * len(groups)], pieces[2 * GROUP * len(groups) :]
    starts, outs = (rest[: len(sides)], rest[len(sides) :]) if last else ((), rest)
    cut = pieces[0].shape[1]
    rank = pieces[0].shape[0]
    size = GROUP * rank
    extra = extra_rows(bounds_ref.shape[1])
    rows = []
    for side, ref in zip(sides, rows_refs):
        if side == 0:
            offset = pl.multiple_of(lax.axis_index("groups") * depth, 128)
            rows.append(ref[:, pl.ds(offset, depth)])
        else:
            blocks = depth // 128
            tall = (ref.shape[0] - extra) // blocks
            rows.append(
                jnp.concatenate([ref[i * tall : (i + 1) * tall, :] for i in range(blocks)], axis=1)
            )
    count = rows[0].shape[0]
    rows = jnp.concatenate(rows, axis=0)
    totals = [ref[...] for ref in starts] if last else [None] * len(sides)
    for i, group in enumerate(groups):
        held = pieces[2 * GROUP * i : 2 * GROUP * (i + 1)]
        first = jnp.concatenate([ref[...] for ref in held[:GROUP]], axis=0)
        second = jnp.concatenate([ref[:, : depth - cut] for ref in held[GROUP:]], axis=0)
        part = contract(rows, jnp.concatenate([first, second], axis=1))
        for s, side in enumerate(sides):
            if side == 0:
                ends = own_ends(bounds_ref, group, size)
            else:
                ends = other_ends(rows_refs[s], extra, group, size)
            here = part[s * count : (s + 1) * count]
            kept = fold(jnp.where(group_mask(*ends, here.shape), here, 0.0))
            totals[s] = kept if totals[s] is None else totals[s] + kept
    if last:
        (total,) = totals
        total = total + pltpu.roll(total, rank, 1)
        half = count // 2
        lane = lax.broadcasted_iota(I32, (half, 2 * rank), 1)
        total = jnp.where(lane < rank, total[:half], total[half:])
        size = outs[0].shape[0]
        totals = [total[i * size : (i + 1) * size] for i in range(len(outs))]
    for total, out_ref in zip(totals, outs):
        out_ref[...] = total.astype(out_ref.dtype)


def rank_call(sides, groups, depth, count, rows, bounds, pieces, starts):
    rank = pieces[0].shape[0]
    last = len(starts) > 0
    if not last:
        out = (jax.ShapeDtypeStruct((count, 2 * rank), F32),) * len(sides)
    elif sides == (1,):
        out = (jax.ShapeDtypeStruct((count // 2, 2 * rank), BF16),)
    else:
        out = (jax.ShapeDtypeStruct((count // 4, 2 * rank), F32),) * 2
    operands = [*rows, bounds, *pieces, *starts]
    return pl.pallas_call(
        functools.partial(rank_kernel, sides, groups, depth, last),
        out_shape=out,
        in_specs=[VMEM] * len(operands),
        out_specs=(VMEM,) * len(out),
        compiler_params=params(),
        cost_estimate=HALF if last and sides == (0,) else LONG,
    )(*operands)


def final_kernel(mask_ref, top, low, one_top, one_low, three, two, near_ref, far_ref, *refs):
    factors, out_ref = refs[:-1], refs[-1]
    rank, width = factors[0].shape[0], out_ref.shape[1]
    begin = factors[0].shape[1] - width
    here = jnp.concatenate([top[...] + one_top[...], low[...] + one_low[...]], axis=0)
    packed = here + (two[...].astype(F32) + three[...].astype(F32))
    turned = pltpu.roll(packed, rank, 1)
    lane = lax.broadcasted_iota(I32, packed.shape, 1)
    values = jnp.concatenate(
        [jnp.where(lane < rank, packed, turned), jnp.where(lane < rank, turned, packed)], axis=0
    )
    wide = jnp.concatenate([values.astype(BF16)] * (GROUP // 2), axis=1)
    total = None
    for group in range(len(factors) // GROUP):
        chosen = wide * mask_ref[:, group * GROUP * rank : (group + 1) * GROUP * rank]
        factor = jnp.concatenate(
            [ref[:, begin:] for ref in factors[group * GROUP : (group + 1) * GROUP]], axis=0
        )
        part = jnp.dot(chosen, factor, preferred_element_type=F32)
        total = part if total is None else total + part
    adapted = total.astype(BF16).astype(F32)
    out_ref[...] = ((near_ref[...] + far_ref[...]) + adapted).astype(BF16)


def per_device(hidden, demand, lengths, holder_slot, value_weight, factor_in, factor_out):
    rows, features = hidden.shape
    owners = lax.axis_size("batch")
    rank, width = factor_out.shape[1:]
    depth = features // 2
    order = ring_order(owners)
    forward = [(order[i], order[(i + 1) % owners]) for i in range(owners)]
    backward = [(b, a) for a, b in forward]
    swap = [(0, 1), (1, 0)]

    full = (owners - 1) // 2
    distances = [0]
    for step in range(1, full + 1):
        distances += [step, -step]
    distances.append(owners // 2)
    table = [
        [[order[(order.index(me) - distance) % owners] for distance in distances]]
        for me in range(owners)
    ]
    first, second, bounds = shard_call(
        factor_in[0].T, factor_out[0], demand, lengths, holder_slot, jnp.asarray(table, I32), depth
    )
    to_other, bounds = rows_call(hidden, bounds)
    bounds, first_later, second_later = lax.optimization_barrier((mark(bounds), first, second))

    firsts, seconds = [first], [second]
    ahead, behind = (first, second_later), (first_later, second)
    for step in range(1, full + 1):
        a = lax.ppermute(ahead[0], "batch", forward)
        d = lax.ppermute(behind[1], "batch", backward)
        b = lax.ppermute(ahead[1], "batch", forward)
        c = lax.ppermute(behind[0], "batch", backward)
        ahead, behind = (a, b), (c, d)
        firsts += [a, c]
        seconds += [b, d]
    firsts.append(lax.ppermute(ahead[0], "batch", forward))
    seconds.append(lax.ppermute(behind[1], "batch", backward))
    near, far, mask = base_call(hidden, value_weight, bounds, GROUP * rank)
    hidden, near, far = lax.optimization_barrier((hidden, near, far))
    other = lax.ppermute(to_other, "groups", swap)

    count = owners // GROUP
    early = range(count - 1)
    pieces = []
    for group in early:
        pieces += firsts[group * GROUP : (group + 1) * GROUP]
        pieces += seconds[group * GROUP : (group + 1) * GROUP]
    both = (hidden, other)
    start_mine, start_theirs = rank_call(
        (0, 1), tuple(early), depth, rows, both, bounds, pieces, ()
    )
    start_theirs, far = lax.optimization_barrier((start_theirs, far))
    far = lax.ppermute(far, "tensor", swap)
    pieces = firsts[-GROUP:] + seconds[-GROUP:]
    late = (count - 1,)
    (theirs,) = rank_call((1,), late, depth, rows, (other,), bounds, pieces, (start_theirs,))
    mine = rank_call((0,), late, depth, rows, (hidden,), bounds, pieces, (start_mine,))

    three = lax.ppermute(theirs, ("groups", "tensor"), [(0, 3), (1, 2), (2, 1), (3, 0)])
    two = lax.ppermute(theirs, "groups", swap)
    one = [lax.ppermute(part, "tensor", swap) for part in mine]

    operands = [mask, *mine, *one, three, two, near, far, *seconds]
    return pl.pallas_call(
        final_kernel,
        out_shape=jax.ShapeDtypeStruct((rows, width), BF16),
        in_specs=[VMEM] * len(operands),
        out_specs=VMEM,
        compiler_params=params(),
    )(*operands)


def solution(mesh):
    return jax.shard_map(
        per_device,
        mesh=mesh,
        in_specs=(
            P(("groups", "batch"), "tensor"),
            P(("groups", "batch"), None),
            P(("groups", "batch"), None),
            P(),
            P("tensor", None),
            P("batch", "tensor", None),
            P("batch", None, "tensor"),
        ),
        out_specs=P(("groups", "batch"), "tensor"),
        check_vma=False,
    )
```

```python
import functools

import jax
import jax.numpy as jnp
from jax import lax
from jax.experimental import pallas as pl
from jax.experimental.pallas import tpu as pltpu
from jax.sharding import PartitionSpec as P

F32, BF16, I32 = jnp.float32, jnp.bfloat16, jnp.int32
VMEM_LIMIT = 24 * 1024 * 1024
HALF = pl.CostEstimate(flops=0, bytes_accessed=1 << 22, transcendentals=0)
LONG = pl.CostEstimate(flops=1 << 33, bytes_accessed=1 << 24, transcendentals=0)
GROUP = 4
VMEM = pl.BlockSpec(memory_space=pltpu.VMEM)
HBM = pl.BlockSpec(memory_space=pltpu.HBM)


def in_hbm(array):
    return pltpu.with_memory_space_constraint(array, pltpu.HBM)


def params():
    return pltpu.CompilerParams(vmem_limit_bytes=VMEM_LIMIT)


def ring_order(size):
    if size % 4:
        return list(range(size))
    columns = size // 4
    order = [0]
    for row in range(4):
        across = range(1, columns) if row % 2 == 0 else range(columns - 1, 0, -1)
        order += [row * columns + column for column in across]
    return order + [row * columns for row in (3, 2, 1)]


def contract(left, right):
    return lax.dot_general(left, right, (((1,), (1,)), ((), ())), preferred_element_type=F32)


def extra_rows(columns):
    return 2 * -(-columns // 1024) * 8


def shard_kernel(
    depth,
    rank,
    factor_ref,
    factor_out_ref,
    demand_ref,
    lengths_ref,
    holder_ref,
    slots_ref,
    first_ref,
    second_ref,
    bounds_ref,
    demand,
    lengths,
    holder,
    slots,
    sems,
):
    group, place = lax.axis_index("groups"), lax.axis_index("batch")
    cut = first_ref.shape[1]
    here = pl.multiple_of(group * depth, 128)
    after = pl.multiple_of(group * depth + cut, 128)
    small = [
        pltpu.make_async_copy(demand_ref, demand, sems.at[0]),
        pltpu.make_async_copy(lengths_ref, lengths, sems.at[1]),
        pltpu.make_async_copy(holder_ref, holder, sems.at[2]),
        pltpu.make_async_copy(slots_ref.at[pl.ds(place, 1)], slots, sems.at[3]),
    ]
    large = [
        pltpu.make_async_copy(factor_ref.at[:, pl.ds(here, cut)], first_ref, sems.at[4]),
        pltpu.make_async_copy(
            factor_ref.at[:, pl.ds(after, depth - cut)], second_ref.at[:, : depth - cut], sems.at[5]
        ),
        pltpu.make_async_copy(factor_out_ref, second_ref.at[:, depth - cut :], sems.at[6]),
    ]
    for copy in small + large:
        copy.start()
    for copy in small:
        copy.wait()
    count = slots.shape[2]
    items = demand.shape[1]
    column = lax.broadcasted_iota(I32, (1, count * rank), 1)
    zero = jnp.int32(0)

    def chunk_mask(chunk):
        return (column >= chunk * rank) & (column < (chunk + 1) * rank)

    low = high = jnp.zeros((1, count * rank), I32)
    if items * count <= 64:
        start = zero
        spans = []
        for item in range(items):
            end = start + lengths[0, item]
            spans.append((holder[demand[0, item]], start, end))
            start = end
        for chunk in range(count):
            slot = slots[0, 0, chunk]
            begin = end = zero
            for owner, first, last in spans:
                begin = jnp.where(owner == slot, first, begin)
                end = jnp.where(owner == slot, last, end)
            low = jnp.where(chunk_mask(chunk), begin, low)
            high = jnp.where(chunk_mask(chunk), end, high)
    else:

        def chunk_ends(chunk, carry):
            low, high = carry
            slot = slots[0, 0, chunk]

            def item_ends(item, state):
                start, begin, end = state
                last = start + lengths[0, item]
                hit = holder[demand[0, item]] == slot
                return last, jnp.where(hit, start, begin), jnp.where(hit, last, end)

            _, begin, end = lax.fori_loop(0, items, item_ends, (zero, zero, zero))
            mask = chunk_mask(chunk)
            return jnp.where(mask, begin, low), jnp.where(mask, end, high)

        low, high = lax.fori_loop(0, count, chunk_ends, (low, high))
    bounds_ref[0:1, :] = low
    bounds_ref[1:2, :] = high
    bounds_ref[2:8, :] = jnp.zeros((6, count * rank), I32)
    for copy in large:
        copy.wait()


def shard_call(factor, factor_out, demand, lengths, holder_slot, slots, depth):
    rank, width = factor_out.shape
    cut = (depth + width) // 2
    count = slots.shape[2]
    return pl.pallas_call(
        functools.partial(shard_kernel, depth, rank),
        out_shape=(
            jax.ShapeDtypeStruct((rank, cut), factor.dtype),
            jax.ShapeDtypeStruct((rank, cut), factor.dtype),
            jax.ShapeDtypeStruct((8, count * rank), I32),
        ),
        in_specs=[HBM] * 6,
        out_specs=(VMEM,) * 3,
        scratch_shapes=[
            pltpu.SMEM(demand.shape, I32),
            pltpu.SMEM(lengths.shape, I32),
            pltpu.SMEM(holder_slot.shape, I32),
            pltpu.SMEM((1, 1, count), I32),
            pltpu.SemaphoreType.DMA((7,)),
        ],
        compiler_params=params(),
        cost_estimate=LONG,
    )(*map(in_hbm, (factor, factor_out, demand, lengths, holder_slot, slots)))


def rows_kernel(depth, hidden_ref, bounds_ref, to_other_ref, bounds_out_ref):
    rows = hidden_ref.shape[0]
    there = pl.multiple_of((1 - lax.axis_index("groups")) * depth, 128)
    for i in range(depth // 128):
        to_other_ref[i * rows : (i + 1) * rows, :] = hidden_ref[:, pl.ds(there + i * 128, 128)]
    columns = bounds_ref.shape[1]
    extra = extra_rows(columns)
    line = lax.broadcasted_iota(I32, (extra, 128), 0)
    ends = jnp.zeros((extra, 128), I32)
    for i in range(columns // 128):
        span = slice(i * 128, (i + 1) * 128)
        ends = jnp.where(line == i, bounds_ref[0:1, span], ends)
        ends = jnp.where(line == extra // 2 + i, bounds_ref[1:2, span], ends)
    to_other_ref[-extra:, :] = ends.astype(F32).astype(BF16)
    bounds_out_ref[...] = bounds_ref[...]


def rows_call(hidden, bounds):
    rows, features = hidden.shape
    depth = features // 2
    tall = depth // 128 * rows + extra_rows(bounds.shape[1])
    return pl.pallas_call(
        functools.partial(rows_kernel, depth),
        out_shape=(
            jax.ShapeDtypeStruct((tall, 128), hidden.dtype),
            jax.ShapeDtypeStruct(bounds.shape, I32),
        ),
        in_specs=[VMEM] * 2,
        out_specs=(VMEM,) * 2,
        compiler_params=params(),
        cost_estimate=LONG,
    )(hidden, bounds)


def mark_kernel(bounds_ref, out_ref):
    out_ref[...] = bounds_ref[...]


def mark(bounds):
    return pl.pallas_call(
        mark_kernel,
        out_shape=jax.ShapeDtypeStruct(bounds.shape, bounds.dtype),
        in_specs=[VMEM],
        out_specs=VMEM,
        compiler_params=params(),
        cost_estimate=LONG,
    )(bounds)


def base_kernel(size, rows_ref, weight_ref, bounds_ref, near_ref, far_ref, mask_ref):
    width = near_ref.shape[1]
    core = lax.axis_index("tensor")
    for out_ref, side in ((near_ref, core), (far_ref, 1 - core)):
        columns = pl.ds(pl.multiple_of(side * width, 128), width)
        out_ref[...] = jnp.dot(
            rows_ref[...], weight_ref[:, columns], preferred_element_type=F32
        )
    for group in range(mask_ref.shape[1] // size):
        mask = group_mask(*own_ends(bounds_ref, group, size), (rows_ref.shape[0], size))
        mask_ref[:, group * size : (group + 1) * size] = jnp.where(mask, 1.0, 0.0).astype(BF16)


def base_call(rows, weight, bounds, size):
    mask = jax.ShapeDtypeStruct((rows.shape[0], bounds.shape[1]), BF16)
    out = jax.ShapeDtypeStruct((rows.shape[0], weight.shape[1] // 2), F32)
    return pl.pallas_call(
        functools.partial(base_kernel, size),
        out_shape=(out, out, mask),
        in_specs=[VMEM] * 3,
        out_specs=(VMEM,) * 3,
        compiler_params=params(),
        cost_estimate=HALF,
    )(rows, weight, bounds)


def group_mask(low, high, shape):
    row = lax.broadcasted_iota(I32, shape, 0)
    return (row >= low) & (row < high)


def own_ends(bounds_ref, group, size):
    columns = slice(group * size, (group + 1) * size)
    return bounds_ref[0:1, columns], bounds_ref[1:2, columns]


def other_ends(other_ref, extra, group, size):
    ends = other_ref[-extra:, :].astype(F32).astype(I32)
    lines = range(group * size // 128, (group + 1) * size // 128)
    low = jnp.concatenate([ends[i : i + 1] for i in lines], axis=1)
    high = jnp.concatenate([ends[extra // 2 + i : extra // 2 + i + 1] for i in lines], axis=1)
    return low, high


def fold(masked):
    total = masked[:, :128]
    for begin in range(128, masked.shape[1], 128):
        total = total + masked[:, begin : begin + 128]
    return total


def rank_kernel(sides, groups, depth, last, *refs):
    refs = list(refs)
    rows_refs, refs = refs[: len(sides)], refs[len(sides) :]
    bounds_ref, pieces = refs[0], refs[1:]
    pieces, rest = pieces[: 2 * GROUP * len(groups)], pieces[2 * GROUP * len(groups) :]
    starts, outs = (rest[: len(sides)], rest[len(sides) :]) if last else ((), rest)
    cut = pieces[0].shape[1]
    rank = pieces[0].shape[0]
    size = GROUP * rank
    extra = extra_rows(bounds_ref.shape[1])
    rows = []
    for side, ref in zip(sides, rows_refs):
        if side == 0:
            offset = pl.multiple_of(lax.axis_index("groups") * depth, 128)
            rows.append(ref[:, pl.ds(offset, depth)])
        else:
            blocks = depth // 128
            tall = (ref.shape[0] - extra) // blocks
            rows.append(
                jnp.concatenate([ref[i * tall : (i + 1) * tall, :] for i in range(blocks)], axis=1)
            )
    count = rows[0].shape[0]
    rows = jnp.concatenate(rows, axis=0)
    totals = [ref[...] for ref in starts] if last else [None] * len(sides)
    for i, group in enumerate(groups):
        held = pieces[2 * GROUP * i : 2 * GROUP * (i + 1)]
        first = jnp.concatenate([ref[...] for ref in held[:GROUP]], axis=0)
        second = jnp.concatenate([ref[:, : depth - cut] for ref in held[GROUP:]], axis=0)
        part = contract(rows, jnp.concatenate([first, second], axis=1))
        for s, side in enumerate(sides):
            if side == 0:
                ends = own_ends(bounds_ref, group, size)
            else:
                ends = other_ends(rows_refs[s], extra, group, size)
            here = part[s * count : (s + 1) * count]
            kept = fold(jnp.where(group_mask(*ends, here.shape), here, 0.0))
            totals[s] = kept if totals[s] is None else totals[s] + kept
    if last:
        (total,) = totals
        total = total + pltpu.roll(total, rank, 1)
        half = count // 2
        lane = lax.broadcasted_iota(I32, (half, 2 * rank), 1)
        total = jnp.where(lane < rank, total[:half], total[half:])
        size = outs[0].shape[0]
        totals = [total[i * size : (i + 1) * size] for i in range(len(outs))]
    for total, out_ref in zip(totals, outs):
        out_ref[...] = total.astype(out_ref.dtype)


def rank_call(sides, groups, depth, count, rows, bounds, pieces, starts):
    rank = pieces[0].shape[0]
    last = len(starts) > 0
    if not last:
        out = (jax.ShapeDtypeStruct((count, 2 * rank), F32),) * len(sides)
    elif sides == (1,):
        out = (jax.ShapeDtypeStruct((count // 2, 2 * rank), F32),)
    else:
        out = (jax.ShapeDtypeStruct((count // 2, 2 * rank), F32),)
    operands = [*rows, bounds, *pieces, *starts]
    return pl.pallas_call(
        functools.partial(rank_kernel, sides, groups, depth, last),
        out_shape=out,
        in_specs=[VMEM] * len(operands),
        out_specs=(VMEM,) * len(out),
        compiler_params=params(),
        cost_estimate=HALF if last and sides == (0,) else LONG,
    )(*operands)


def final_kernel(mask_ref, mine, one, three, two, near_ref, far_ref, *refs):
    factors, out_ref = refs[:-1], refs[-1]
    rank, width = factors[0].shape[0], out_ref.shape[1]
    begin = factors[0].shape[1] - width
    packed = (mine[...] + one[...]) + (two[...] + three[...])
    turned = pltpu.roll(packed, rank, 1)
    lane = lax.broadcasted_iota(I32, packed.shape, 1)
    values = jnp.concatenate(
        [jnp.where(lane < rank, packed, turned), jnp.where(lane < rank, turned, packed)], axis=0
    )
    wide = jnp.concatenate([values.astype(BF16)] * (GROUP // 2), axis=1)
    total = None
    for group in range(len(factors) // GROUP):
        chosen = wide * mask_ref[:, group * GROUP * rank : (group + 1) * GROUP * rank]
        factor = jnp.concatenate(
            [ref[:, begin:] for ref in factors[group * GROUP : (group + 1) * GROUP]], axis=0
        )
        part = jnp.dot(chosen, factor, preferred_element_type=F32)
        total = part if total is None else total + part
    adapted = total.astype(BF16).astype(F32)
    out_ref[...] = ((near_ref[...] + far_ref[...]) + adapted).astype(BF16)


def per_device(hidden, demand, lengths, holder_slot, value_weight, factor_in, factor_out):
    rows, features = hidden.shape
    owners = lax.axis_size("batch")
    rank, width = factor_out.shape[1:]
    depth = features // 2
    order = ring_order(owners)
    forward = [(order[i], order[(i + 1) % owners]) for i in range(owners)]
    backward = [(b, a) for a, b in forward]
    swap = [(0, 1), (1, 0)]

    full = (owners - 1) // 2
    distances = [0]
    for step in range(1, full + 1):
        distances += [step, -step]
    distances.append(owners // 2)
    table = [
        [[order[(order.index(me) - distance) % owners] for distance in distances]]
        for me in range(owners)
    ]
    first, second, bounds = shard_call(
        factor_in[0].T, factor_out[0], demand, lengths, holder_slot, jnp.asarray(table, I32), depth
    )
    to_other, bounds = rows_call(hidden, bounds)
    bounds, first_later, second_later = lax.optimization_barrier((mark(bounds), first, second))

    firsts, seconds = [first], [second]
    ahead, behind = (first, second_later), (first_later, second)
    for step in range(1, full + 1):
        a = lax.ppermute(ahead[0], "batch", forward)
        d = lax.ppermute(behind[1], "batch", backward)
        b = lax.ppermute(ahead[1], "batch", forward)
        c = lax.ppermute(behind[0], "batch", backward)
        ahead, behind = (a, b), (c, d)
        firsts += [a, c]
        seconds += [b, d]
    firsts.append(lax.ppermute(ahead[0], "batch", forward))
    seconds.append(lax.ppermute(behind[1], "batch", backward))
    near, far, mask = base_call(hidden, value_weight, bounds, GROUP * rank)
    hidden, near, far = lax.optimization_barrier((hidden, near, far))
    other = lax.ppermute(to_other, "groups", swap)

    count = owners // GROUP
    early = range(count - 1)
    pieces = []
    for group in early:
        pieces += firsts[group * GROUP : (group + 1) * GROUP]
        pieces += seconds[group * GROUP : (group + 1) * GROUP]
    both = (hidden, other)
    start_mine, start_theirs = rank_call(
        (0, 1), tuple(early), depth, rows, both, bounds, pieces, ()
    )
    start_theirs, far = lax.optimization_barrier((start_theirs, far))
    far = lax.ppermute(far, "tensor", swap)
    pieces = firsts[-GROUP:] + seconds[-GROUP:]
    late = (count - 1,)
    (theirs,) = rank_call((1,), late, depth, rows, (other,), bounds, pieces, (start_theirs,))
    mine = rank_call((0,), late, depth, rows, (hidden,), bounds, pieces, (start_mine,))

    three = lax.ppermute(theirs, ("groups", "tensor"), [(0, 3), (1, 2), (2, 1), (3, 0)])
    two = lax.ppermute(theirs, "groups", swap)
    one = [lax.ppermute(part, "tensor", swap) for part in mine]

    operands = [mask, *mine, *one, three, two, near, far, *seconds]
    return pl.pallas_call(
        final_kernel,
        out_shape=jax.ShapeDtypeStruct((rows, width), BF16),
        in_specs=[VMEM] * len(operands),
        out_specs=VMEM,
        compiler_params=params(),
    )(*operands)


def solution(mesh):
    return jax.shard_map(
        per_device,
        mesh=mesh,
        in_specs=(
            P(("groups", "batch"), "tensor"),
            P(("groups", "batch"), None),
            P(("groups", "batch"), None),
            P(),
            P("tensor", None),
            P("batch", "tensor", None),
            P("batch", None, "tensor"),
        ),
        out_specs=P(("groups", "batch"), "tensor"),
        check_vma=False,
    )
```

```python
import functools

import jax
import jax.numpy as jnp
from jax import lax
from jax.experimental import pallas as pl
from jax.experimental.pallas import tpu as pltpu
from jax.sharding import PartitionSpec as P

F32, BF16, I32 = jnp.float32, jnp.bfloat16, jnp.int32
VMEM_LIMIT = 24 * 1024 * 1024
HALF = pl.CostEstimate(flops=0, bytes_accessed=1 << 22, transcendentals=0)
LONG = pl.CostEstimate(flops=1 << 33, bytes_accessed=1 << 24, transcendentals=0)
GROUP = 4
VMEM = pl.BlockSpec(memory_space=pltpu.VMEM)
HBM = pl.BlockSpec(memory_space=pltpu.HBM)


def in_hbm(array):
    return pltpu.with_memory_space_constraint(array, pltpu.HBM)


def params():
    return pltpu.CompilerParams(vmem_limit_bytes=VMEM_LIMIT)


def ring_order(size):
    if size % 4:
        return list(range(size))
    columns = size // 4
    order = [0]
    for row in range(4):
        across = range(1, columns) if row % 2 == 0 else range(columns - 1, 0, -1)
        order += [row * columns + column for column in across]
    return order + [row * columns for row in (3, 2, 1)]


def contract(left, right):
    return lax.dot_general(left, right, (((1,), (1,)), ((), ())), preferred_element_type=F32)


def extra_rows(columns):
    return 2 * -(-columns // 1024) * 8


def shard_kernel(
    depth,
    rank,
    factor_ref,
    factor_out_ref,
    demand_ref,
    lengths_ref,
    holder_ref,
    slots_ref,
    first_ref,
    second_ref,
    bounds_ref,
    demand,
    lengths,
    holder,
    slots,
    sems,
):
    group, place = lax.axis_index("groups"), lax.axis_index("batch")
    cut = first_ref.shape[1]
    here = pl.multiple_of(group * depth, 128)
    after = pl.multiple_of(group * depth + cut, 128)
    small = [
        pltpu.make_async_copy(demand_ref, demand, sems.at[0]),
        pltpu.make_async_copy(lengths_ref, lengths, sems.at[1]),
        pltpu.make_async_copy(holder_ref, holder, sems.at[2]),
        pltpu.make_async_copy(slots_ref.at[pl.ds(place, 1)], slots, sems.at[3]),
    ]
    large = [
        pltpu.make_async_copy(factor_ref.at[:, pl.ds(here, cut)], first_ref, sems.at[4]),
        pltpu.make_async_copy(
            factor_ref.at[:, pl.ds(after, depth - cut)], second_ref.at[:, : depth - cut], sems.at[5]
        ),
        pltpu.make_async_copy(factor_out_ref, second_ref.at[:, depth - cut :], sems.at[6]),
    ]
    for copy in small + large:
        copy.start()
    for copy in small:
        copy.wait()
    count = slots.shape[2]
    items = demand.shape[1]
    column = lax.broadcasted_iota(I32, (1, count * rank), 1)
    zero = jnp.int32(0)

    def chunk_mask(chunk):
        return (column >= chunk * rank) & (column < (chunk + 1) * rank)

    low = high = jnp.zeros((1, count * rank), I32)
    if items * count <= 64:
        start = zero
        spans = []
        for item in range(items):
            end = start + lengths[0, item]
            spans.append((holder[demand[0, item]], start, end))
            start = end
        for chunk in range(count):
            slot = slots[0, 0, chunk]
            begin = end = zero
            for owner, first, last in spans:
                begin = jnp.where(owner == slot, first, begin)
                end = jnp.where(owner == slot, last, end)
            low = jnp.where(chunk_mask(chunk), begin, low)
            high = jnp.where(chunk_mask(chunk), end, high)
    else:

        def chunk_ends(chunk, carry):
            low, high = carry
            slot = slots[0, 0, chunk]

            def item_ends(item, state):
                start, begin, end = state
                last = start + lengths[0, item]
                hit = holder[demand[0, item]] == slot
                return last, jnp.where(hit, start, begin), jnp.where(hit, last, end)

            _, begin, end = lax.fori_loop(0, items, item_ends, (zero, zero, zero))
            mask = chunk_mask(chunk)
            return jnp.where(mask, begin, low), jnp.where(mask, end, high)

        low, high = lax.fori_loop(0, count, chunk_ends, (low, high))
    bounds_ref[0:1, :] = low
    bounds_ref[1:2, :] = high
    bounds_ref[2:8, :] = jnp.zeros((6, count * rank), I32)
    for copy in large:
        copy.wait()


def shard_call(factor, factor_out, demand, lengths, holder_slot, slots, depth):
    rank, width = factor_out.shape
    cut = (depth + width) // 2
    count = slots.shape[2]
    return pl.pallas_call(
        functools.partial(shard_kernel, depth, rank),
        out_shape=(
            jax.ShapeDtypeStruct((rank, cut), factor.dtype),
            jax.ShapeDtypeStruct((rank, cut), factor.dtype),
            jax.ShapeDtypeStruct((8, count * rank), I32),
        ),
        in_specs=[HBM] * 6,
        out_specs=(VMEM,) * 3,
        scratch_shapes=[
            pltpu.SMEM(demand.shape, I32),
            pltpu.SMEM(lengths.shape, I32),
            pltpu.SMEM(holder_slot.shape, I32),
            pltpu.SMEM((1, 1, count), I32),
            pltpu.SemaphoreType.DMA((7,)),
        ],
        compiler_params=params(),
        cost_estimate=LONG,
    )(*map(in_hbm, (factor, factor_out, demand, lengths, holder_slot, slots)))


def rows_kernel(depth, hidden_ref, bounds_ref, to_other_ref, bounds_out_ref):
    rows = hidden_ref.shape[0]
    there = pl.multiple_of((1 - lax.axis_index("groups")) * depth, 128)
    for i in range(depth // 128):
        to_other_ref[i * rows : (i + 1) * rows, :] = hidden_ref[:, pl.ds(there + i * 128, 128)]
    columns = bounds_ref.shape[1]
    extra = extra_rows(columns)
    line = lax.broadcasted_iota(I32, (extra, 128), 0)
    ends = jnp.zeros((extra, 128), I32)
    for i in range(columns // 128):
        span = slice(i * 128, (i + 1) * 128)
        ends = jnp.where(line == i, bounds_ref[0:1, span], ends)
        ends = jnp.where(line == extra // 2 + i, bounds_ref[1:2, span], ends)
    to_other_ref[-extra:, :] = ends.astype(F32).astype(BF16)
    bounds_out_ref[...] = bounds_ref[...]


def rows_call(hidden, bounds):
    rows, features = hidden.shape
    depth = features // 2
    tall = depth // 128 * rows + extra_rows(bounds.shape[1])
    return pl.pallas_call(
        functools.partial(rows_kernel, depth),
        out_shape=(
            jax.ShapeDtypeStruct((tall, 128), hidden.dtype),
            jax.ShapeDtypeStruct(bounds.shape, I32),
        ),
        in_specs=[VMEM] * 2,
        out_specs=(VMEM,) * 2,
        compiler_params=params(),
        cost_estimate=LONG,
    )(hidden, bounds)


def mark_kernel(bounds_ref, out_ref):
    out_ref[...] = bounds_ref[...]


def mark(bounds):
    return pl.pallas_call(
        mark_kernel,
        out_shape=jax.ShapeDtypeStruct(bounds.shape, bounds.dtype),
        in_specs=[VMEM],
        out_specs=VMEM,
        compiler_params=params(),
        cost_estimate=LONG,
    )(bounds)


def base_kernel(size, rows_ref, weight_ref, bounds_ref, near_ref, far_ref, mask_ref):
    width = near_ref.shape[1]
    core = lax.axis_index("tensor")
    for out_ref, side in ((near_ref, core), (far_ref, 1 - core)):
        columns = pl.ds(pl.multiple_of(side * width, 128), width)
        out_ref[...] = jnp.dot(
            rows_ref[...], weight_ref[:, columns], preferred_element_type=F32
        )
    for group in range(mask_ref.shape[1] // size):
        mask = group_mask(*own_ends(bounds_ref, group, size), (rows_ref.shape[0], size))
        mask_ref[:, group * size : (group + 1) * size] = jnp.where(mask, 1.0, 0.0).astype(BF16)


def base_call(rows, weight, bounds, size):
    mask = jax.ShapeDtypeStruct((rows.shape[0], bounds.shape[1]), BF16)
    out = jax.ShapeDtypeStruct((rows.shape[0], weight.shape[1] // 2), F32)
    return pl.pallas_call(
        functools.partial(base_kernel, size),
        out_shape=(out, out, mask),
        in_specs=[VMEM] * 3,
        out_specs=(VMEM,) * 3,
        compiler_params=params(),
        cost_estimate=HALF,
    )(rows, weight, bounds)


def group_mask(low, high, shape):
    row = lax.broadcasted_iota(I32, shape, 0)
    return (row >= low) & (row < high)


def own_ends(bounds_ref, group, size):
    columns = slice(group * size, (group + 1) * size)
    return bounds_ref[0:1, columns], bounds_ref[1:2, columns]


def other_ends(other_ref, extra, group, size):
    ends = other_ref[-extra:, :].astype(F32).astype(I32)
    lines = range(group * size // 128, (group + 1) * size // 128)
    low = jnp.concatenate([ends[i : i + 1] for i in lines], axis=1)
    high = jnp.concatenate([ends[extra // 2 + i : extra // 2 + i + 1] for i in lines], axis=1)
    return low, high


def fold(masked):
    total = masked[:, :128]
    for begin in range(128, masked.shape[1], 128):
        total = total + masked[:, begin : begin + 128]
    return total


def rank_kernel(sides, groups, depth, last, *refs):
    refs = list(refs)
    rows_refs, refs = refs[: len(sides)], refs[len(sides) :]
    bounds_ref, pieces = refs[0], refs[1:]
    pieces, rest = pieces[: 2 * GROUP * len(groups)], pieces[2 * GROUP * len(groups) :]
    starts, outs = (rest[: len(sides)], rest[len(sides) :]) if last else ((), rest)
    cut = pieces[0].shape[1]
    rank = pieces[0].shape[0]
    size = GROUP * rank
    extra = extra_rows(bounds_ref.shape[1])
    rows = []
    for side, ref in zip(sides, rows_refs):
        if side == 0:
            offset = pl.multiple_of(lax.axis_index("groups") * depth, 128)
            rows.append(ref[:, pl.ds(offset, depth)])
        else:
            blocks = depth // 128
            tall = (ref.shape[0] - extra) // blocks
            rows.append(
                jnp.concatenate([ref[i * tall : (i + 1) * tall, :] for i in range(blocks)], axis=1)
            )
    count = rows[0].shape[0]
    rows = jnp.concatenate(rows, axis=0)
    totals = [ref[...] for ref in starts] if last else [None] * len(sides)
    for i, group in enumerate(groups):
        held = pieces[2 * GROUP * i : 2 * GROUP * (i + 1)]
        first = jnp.concatenate([ref[...] for ref in held[:GROUP]], axis=0)
        second = jnp.concatenate([ref[:, : depth - cut] for ref in held[GROUP:]], axis=0)
        part = contract(rows, jnp.concatenate([first, second], axis=1))
        for s, side in enumerate(sides):
            if side == 0:
                ends = own_ends(bounds_ref, group, size)
            else:
                ends = other_ends(rows_refs[s], extra, group, size)
            here = part[s * count : (s + 1) * count]
            kept = fold(jnp.where(group_mask(*ends, here.shape), here, 0.0))
            totals[s] = kept if totals[s] is None else totals[s] + kept
    if last:
        (total,) = totals
        total = total + pltpu.roll(total, rank, 1)
        half = count // 2
        lane = lax.broadcasted_iota(I32, (half, 2 * rank), 1)
        total = jnp.where(lane < rank, total[:half], total[half:])
        size = outs[0].shape[0]
        totals = [total[i * size : (i + 1) * size] for i in range(len(outs))]
    for total, out_ref in zip(totals, outs):
        out_ref[...] = total.astype(out_ref.dtype)


def rank_call(sides, groups, depth, count, rows, bounds, pieces, starts):
    rank = pieces[0].shape[0]
    last = len(starts) > 0
    if not last:
        out = (jax.ShapeDtypeStruct((count, 2 * rank), F32),) * len(sides)
    elif sides == (1,):
        out = (jax.ShapeDtypeStruct((count // 2, 2 * rank), BF16),)
    else:
        out = (jax.ShapeDtypeStruct((count // 4, 2 * rank), F32),) * 2
    operands = [*rows, bounds, *pieces, *starts]
    return pl.pallas_call(
        functools.partial(rank_kernel, sides, groups, depth, last),
        out_shape=out,
        in_specs=[VMEM] * len(operands),
        out_specs=(VMEM,) * len(out),
        compiler_params=params(),
        cost_estimate=HALF if last and sides == (0,) else LONG,
    )(*operands)


def final_kernel(mask_ref, top, low, one_top, one_low, three, two, near_ref, far_ref, *refs):
    factors, out_ref = refs[:-1], refs[-1]
    rank, width = factors[0].shape[0], out_ref.shape[1]
    begin = factors[0].shape[1] - width
    here = jnp.concatenate([top[...] + one_top[...], low[...] + one_low[...]], axis=0)
    packed = here + (two[...].astype(F32) + three[...].astype(F32))
    turned = pltpu.roll(packed, rank, 1)
    lane = lax.broadcasted_iota(I32, packed.shape, 1)
    values = jnp.concatenate(
        [jnp.where(lane < rank, packed, turned), jnp.where(lane < rank, turned, packed)], axis=0
    )
    wide = jnp.concatenate([values.astype(BF16)] * (GROUP // 2), axis=1)
    total = None
    for group in range(len(factors) // GROUP):
        chosen = wide * mask_ref[:, group * GROUP * rank : (group + 1) * GROUP * rank]
        factor = jnp.concatenate(
            [ref[:, begin:] for ref in factors[group * GROUP : (group + 1) * GROUP]], axis=0
        )
        part = jnp.dot(chosen, factor, preferred_element_type=F32)
        total = part if total is None else total + part
    adapted = total.astype(BF16).astype(F32)
    out_ref[...] = ((near_ref[...] + far_ref[...]) + adapted).astype(BF16)


def per_device(hidden, demand, lengths, holder_slot, value_weight, factor_in, factor_out):
    rows, features = hidden.shape
    owners = lax.axis_size("batch")
    rank, width = factor_out.shape[1:]
    depth = features // 2
    order = ring_order(owners)
    swap = [(0, 1), (1, 0)]
    edges = [[], []]
    for i in range(owners):
        a, b = order[i], order[(i + 1) % owners]
        edges[i % 2] += [(a, b), (b, a)]

    full = (owners - 1) // 2
    held = [list(range(owners)), list(range(owners))]
    table = [[[me]] for me in range(owners)]
    for step in range(1, owners // 2 + 1):
        for chain in (0, 1):
            came = dict((b, a) for a, b in edges[(step - 1 + chain) % 2])
            held[chain] = [held[chain][came[me]] for me in range(owners)]
        for me in range(owners):
            table[me][0] += [held[0][me], held[1][me]] if step <= full else [held[0][me]]
    first, second, bounds = shard_call(
        factor_in[0].T, factor_out[0], demand, lengths, holder_slot, jnp.asarray(table, I32), depth
    )
    to_other, bounds = rows_call(hidden, bounds)
    bounds, first_later, second_later = lax.optimization_barrier((mark(bounds), first, second))

    firsts, seconds = [first], [second]
    ahead, behind = (first, second_later), (first_later, second)
    for step in range(1, full + 1):
        first_edges, second_edges = edges[(step - 1) % 2], edges[step % 2]
        a = lax.ppermute(ahead[0], "batch", first_edges)
        d = lax.ppermute(behind[1], "batch", second_edges)
        b = lax.ppermute(ahead[1], "batch", first_edges)
        c = lax.ppermute(behind[0], "batch", second_edges)
        ahead, behind = (a, b), (c, d)
        firsts += [a, c]
        seconds += [b, d]
    firsts.append(lax.ppermute(ahead[0], "batch", edges[full % 2]))
    seconds.append(lax.ppermute(behind[1], "batch", edges[(full + 1) % 2]))
    near, far, mask = base_call(hidden, value_weight, bounds, GROUP * rank)
    hidden, near, far = lax.optimization_barrier((hidden, near, far))
    other = lax.ppermute(to_other, "groups", swap)

    count = owners // GROUP
    early = range(count - 1)
    pieces = []
    for group in early:
        pieces += firsts[group * GROUP : (group + 1) * GROUP]
        pieces += seconds[group * GROUP : (group + 1) * GROUP]
    both = (hidden, other)
    start_mine, start_theirs = rank_call(
        (0, 1), tuple(early), depth, rows, both, bounds, pieces, ()
    )
    start_theirs, far = lax.optimization_barrier((start_theirs, far))
    far = lax.ppermute(far, "tensor", swap)
    pieces = firsts[-GROUP:] + seconds[-GROUP:]
    late = (count - 1,)
    (theirs,) = rank_call((1,), late, depth, rows, (other,), bounds, pieces, (start_theirs,))
    mine = rank_call((0,), late, depth, rows, (hidden,), bounds, pieces, (start_mine,))

    three = lax.ppermute(theirs, ("groups", "tensor"), [(0, 3), (1, 2), (2, 1), (3, 0)])
    two = lax.ppermute(theirs, "groups", swap)
    one = [lax.ppermute(part, "tensor", swap) for part in mine]

    operands = [mask, *mine, *one, three, two, near, far, *seconds]
    return pl.pallas_call(
        final_kernel,
        out_shape=jax.ShapeDtypeStruct((rows, width), BF16),
        in_specs=[VMEM] * len(operands),
        out_specs=VMEM,
        compiler_params=params(),
    )(*operands)


def solution(mesh):
    return jax.shard_map(
        per_device,
        mesh=mesh,
        in_specs=(
            P(("groups", "batch"), "tensor"),
            P(("groups", "batch"), None),
            P(("groups", "batch"), None),
            P(),
            P("tensor", None),
            P("batch", "tensor", None),
            P("batch", None, "tensor"),
        ),
        out_specs=P(("groups", "batch"), "tensor"),
        check_vma=False,
    )
```

```python
import functools

import jax
import jax.numpy as jnp
from jax import lax
from jax.experimental import pallas as pl
from jax.experimental.pallas import tpu as pltpu
from jax.sharding import PartitionSpec as P

F32, BF16, I32 = jnp.float32, jnp.bfloat16, jnp.int32
VMEM_LIMIT = 24 * 1024 * 1024
HALF = pl.CostEstimate(flops=0, bytes_accessed=1 << 22, transcendentals=0)
LONG = pl.CostEstimate(flops=1 << 33, bytes_accessed=1 << 24, transcendentals=0)
GROUP = 4
VMEM = pl.BlockSpec(memory_space=pltpu.VMEM)
HBM = pl.BlockSpec(memory_space=pltpu.HBM)


def in_hbm(array):
    return pltpu.with_memory_space_constraint(array, pltpu.HBM)


def params():
    return pltpu.CompilerParams(vmem_limit_bytes=VMEM_LIMIT)


def ring_order(size):
    if size % 4:
        return list(range(size))
    columns = size // 4
    order = [0]
    for row in range(4):
        across = range(1, columns) if row % 2 == 0 else range(columns - 1, 0, -1)
        order += [row * columns + column for column in across]
    return order + [row * columns for row in (3, 2, 1)]


def contract(left, right):
    return lax.dot_general(left, right, (((1,), (1,)), ((), ())), preferred_element_type=F32)


def extra_rows(columns):
    return 2 * -(-columns // 1024) * 8


def shard_kernel(
    depth,
    rank,
    factor_ref,
    factor_out_ref,
    demand_ref,
    lengths_ref,
    holder_ref,
    slots_ref,
    first_ref,
    second_ref,
    bounds_ref,
    demand,
    lengths,
    holder,
    slots,
    sems,
):
    group, place = lax.axis_index("groups"), lax.axis_index("batch")
    cut = first_ref.shape[1]
    here = pl.multiple_of(group * depth, 128)
    after = pl.multiple_of(group * depth + cut, 128)
    small = [
        pltpu.make_async_copy(demand_ref, demand, sems.at[0]),
        pltpu.make_async_copy(lengths_ref, lengths, sems.at[1]),
        pltpu.make_async_copy(holder_ref, holder, sems.at[2]),
        pltpu.make_async_copy(slots_ref.at[pl.ds(place, 1)], slots, sems.at[3]),
    ]
    large = [
        pltpu.make_async_copy(factor_ref.at[:, pl.ds(here, cut)], first_ref, sems.at[4]),
        pltpu.make_async_copy(
            factor_ref.at[:, pl.ds(after, depth - cut)], second_ref.at[:, : depth - cut], sems.at[5]
        ),
        pltpu.make_async_copy(factor_out_ref, second_ref.at[:, depth - cut :], sems.at[6]),
    ]
    for copy in small + large:
        copy.start()
    for copy in small:
        copy.wait()
    count = slots.shape[2]
    items = demand.shape[1]
    column = lax.broadcasted_iota(I32, (1, count * rank), 1)
    zero = jnp.int32(0)

    def chunk_mask(chunk):
        return (column >= chunk * rank) & (column < (chunk + 1) * rank)

    low = high = jnp.zeros((1, count * rank), I32)
    if items * count <= 64:
        start = zero
        spans = []
        for item in range(items):
            end = start + lengths[0, item]
            spans.append((holder[demand[0, item]], start, end))
            start = end
        for chunk in range(count):
            slot = slots[0, 0, chunk]
            begin = end = zero
            for owner, first, last in spans:
                begin = jnp.where(owner == slot, first, begin)
                end = jnp.where(owner == slot, last, end)
            low = jnp.where(chunk_mask(chunk), begin, low)
            high = jnp.where(chunk_mask(chunk), end, high)
    else:

        def chunk_ends(chunk, carry):
            low, high = carry
            slot = slots[0, 0, chunk]

            def item_ends(item, state):
                start, begin, end = state
                last = start + lengths[0, item]
                hit = holder[demand[0, item]] == slot
                return last, jnp.where(hit, start, begin), jnp.where(hit, last, end)

            _, begin, end = lax.fori_loop(0, items, item_ends, (zero, zero, zero))
            mask = chunk_mask(chunk)
            return jnp.where(mask, begin, low), jnp.where(mask, end, high)

        low, high = lax.fori_loop(0, count, chunk_ends, (low, high))
    bounds_ref[0:1, :] = low
    bounds_ref[1:2, :] = high
    bounds_ref[2:8, :] = jnp.zeros((6, count * rank), I32)
    for copy in large:
        copy.wait()


def shard_call(factor, factor_out, demand, lengths, holder_slot, slots, depth):
    rank, width = factor_out.shape
    cut = (depth + width) // 2
    count = slots.shape[2]
    return pl.pallas_call(
        functools.partial(shard_kernel, depth, rank),
        out_shape=(
            jax.ShapeDtypeStruct((rank, cut), factor.dtype),
            jax.ShapeDtypeStruct((rank, cut), factor.dtype),
            jax.ShapeDtypeStruct((8, count * rank), I32),
        ),
        in_specs=[HBM] * 6,
        out_specs=(VMEM,) * 3,
        scratch_shapes=[
            pltpu.SMEM(demand.shape, I32),
            pltpu.SMEM(lengths.shape, I32),
            pltpu.SMEM(holder_slot.shape, I32),
            pltpu.SMEM((1, 1, count), I32),
            pltpu.SemaphoreType.DMA((7,)),
        ],
        compiler_params=params(),
        cost_estimate=LONG,
    )(*map(in_hbm, (factor, factor_out, demand, lengths, holder_slot, slots)))


def rows_kernel(depth, hidden_ref, bounds_ref, to_other_ref, bounds_out_ref):
    rows = hidden_ref.shape[0]
    there = pl.multiple_of((1 - lax.axis_index("groups")) * depth, 128)
    for i in range(depth // 128):
        to_other_ref[i * rows : (i + 1) * rows, :] = hidden_ref[:, pl.ds(there + i * 128, 128)]
    columns = bounds_ref.shape[1]
    extra = extra_rows(columns)
    line = lax.broadcasted_iota(I32, (extra, 128), 0)
    ends = jnp.zeros((extra, 128), I32)
    for i in range(columns // 128):
        span = slice(i * 128, (i + 1) * 128)
        ends = jnp.where(line == i, bounds_ref[0:1, span], ends)
        ends = jnp.where(line == extra // 2 + i, bounds_ref[1:2, span], ends)
    to_other_ref[-extra:, :] = ends.astype(F32).astype(BF16)
    bounds_out_ref[...] = bounds_ref[...]


def rows_call(hidden, bounds):
    rows, features = hidden.shape
    depth = features // 2
    tall = depth // 128 * rows + extra_rows(bounds.shape[1])
    return pl.pallas_call(
        functools.partial(rows_kernel, depth),
        out_shape=(
            jax.ShapeDtypeStruct((tall, 128), hidden.dtype),
            jax.ShapeDtypeStruct(bounds.shape, I32),
        ),
        in_specs=[VMEM] * 2,
        out_specs=(VMEM,) * 2,
        compiler_params=params(),
        cost_estimate=LONG,
    )(hidden, bounds)


def mark_kernel(bounds_ref, out_ref):
    out_ref[...] = bounds_ref[...]


def mark(bounds):
    return pl.pallas_call(
        mark_kernel,
        out_shape=jax.ShapeDtypeStruct(bounds.shape, bounds.dtype),
        in_specs=[VMEM],
        out_specs=VMEM,
        compiler_params=params(),
        cost_estimate=LONG,
    )(bounds)


def base_kernel(rows_ref, weight_ref, near_ref, far_ref):
    width = near_ref.shape[1]
    core = lax.axis_index("tensor")
    for out_ref, side in ((near_ref, core), (far_ref, 1 - core)):
        columns = pl.ds(pl.multiple_of(side * width, 128), width)
        out_ref[...] = jnp.dot(
            rows_ref[...], weight_ref[:, columns], preferred_element_type=F32
        )


def base_call(rows, weight):
    out = jax.ShapeDtypeStruct((rows.shape[0], weight.shape[1] // 2), F32)
    return pl.pallas_call(
        base_kernel,
        out_shape=(out, out),
        in_specs=[VMEM] * 2,
        out_specs=(VMEM,) * 2,
        compiler_params=params(),
        cost_estimate=HALF,
    )(rows, weight)


def group_mask(low, high, shape):
    row = lax.broadcasted_iota(I32, shape, 0)
    return (row >= low) & (row < high)


def own_ends(bounds_ref, group, size):
    columns = slice(group * size, (group + 1) * size)
    return bounds_ref[0:1, columns], bounds_ref[1:2, columns]


def other_ends(other_ref, extra, group, size):
    ends = other_ref[-extra:, :].astype(F32).astype(I32)
    lines = range(group * size // 128, (group + 1) * size // 128)
    low = jnp.concatenate([ends[i : i + 1] for i in lines], axis=1)
    high = jnp.concatenate([ends[extra // 2 + i : extra // 2 + i + 1] for i in lines], axis=1)
    return low, high


def fold(masked):
    total = masked[:, :128]
    for begin in range(128, masked.shape[1], 128):
        total = total + masked[:, begin : begin + 128]
    return total


def rank_kernel(sides, groups, depth, last, *refs):
    refs = list(refs)
    rows_refs, refs = refs[: len(sides)], refs[len(sides) :]
    bounds_ref, pieces = refs[0], refs[1:]
    pieces, rest = pieces[: 2 * GROUP * len(groups)], pieces[2 * GROUP * len(groups) :]
    starts, outs = (rest[: len(sides)], rest[len(sides) :]) if last else ((), rest)
    cut = pieces[0].shape[1]
    rank = pieces[0].shape[0]
    size = GROUP * rank
    extra = extra_rows(bounds_ref.shape[1])
    rows = []
    for side, ref in zip(sides, rows_refs):
        if side == 0:
            offset = pl.multiple_of(lax.axis_index("groups") * depth, 128)
            rows.append(ref[:, pl.ds(offset, depth)])
        else:
            blocks = depth // 128
            tall = (ref.shape[0] - extra) // blocks
            rows.append(
                jnp.concatenate([ref[i * tall : (i + 1) * tall, :] for i in range(blocks)], axis=1)
            )
    count = rows[0].shape[0]
    rows = jnp.concatenate(rows, axis=0)
    totals = [ref[...] for ref in starts] if last else [None] * len(sides)
    for i, group in enumerate(groups):
        held = pieces[2 * GROUP * i : 2 * GROUP * (i + 1)]
        first = jnp.concatenate([ref[...] for ref in held[:GROUP]], axis=0)
        second = jnp.concatenate([ref[:, : depth - cut] for ref in held[GROUP:]], axis=0)
        part = contract(rows, jnp.concatenate([first, second], axis=1))
        for s, side in enumerate(sides):
            if side == 0:
                ends = own_ends(bounds_ref, group, size)
            else:
                ends = other_ends(rows_refs[s], extra, group, size)
            here = part[s * count : (s + 1) * count]
            kept = fold(jnp.where(group_mask(*ends, here.shape), here, 0.0))
            totals[s] = kept if totals[s] is None else totals[s] + kept
    if last:
        (total,) = totals
        total = total + pltpu.roll(total, rank, 1)
        half = count // 2
        lane = lax.broadcasted_iota(I32, (half, 2 * rank), 1)
        total = jnp.where(lane < rank, total[:half], total[half:])
        size = outs[0].shape[0]
        totals = [total[i * size : (i + 1) * size] for i in range(len(outs))]
    for total, out_ref in zip(totals, outs):
        out_ref[...] = total.astype(out_ref.dtype)


def rank_call(sides, groups, depth, count, rows, bounds, pieces, starts):
    rank = pieces[0].shape[0]
    last = len(starts) > 0
    if not last:
        out = (jax.ShapeDtypeStruct((count, 2 * rank), F32),) * len(sides)
    elif sides == (1,):
        out = (jax.ShapeDtypeStruct((count // 2, 2 * rank), BF16),)
    else:
        out = (jax.ShapeDtypeStruct((count // 2, 2 * rank), F32),)
    operands = [*rows, bounds, *pieces, *starts]
    return pl.pallas_call(
        functools.partial(rank_kernel, sides, groups, depth, last),
        out_shape=out,
        in_specs=[VMEM] * len(operands),
        out_specs=(VMEM,) * len(out),
        compiler_params=params(),
        cost_estimate=HALF if last and sides == (0,) else LONG,
    )(*operands)


def final_kernel(bounds_ref, mine, one, two, three, near_ref, far_ref, *refs):
    factors, out_ref = refs[:-1], refs[-1]
    rank, width = factors[0].shape[0], out_ref.shape[1]
    begin = factors[0].shape[1] - width
    packed = (mine[...] + one[...]) + (two[...].astype(F32) + three[...].astype(F32))
    turned = pltpu.roll(packed, rank, 1)
    lane = lax.broadcasted_iota(I32, packed.shape, 1)
    values = jnp.concatenate(
        [jnp.where(lane < rank, packed, turned), jnp.where(lane < rank, turned, packed)], axis=0
    )
    wide = jnp.concatenate([values] * (GROUP // 2), axis=1)
    total = None
    for group in range(len(factors) // GROUP):
        mask = group_mask(*own_ends(bounds_ref, group, GROUP * rank), wide.shape)
        chosen = jnp.where(mask, wide, 0.0).astype(BF16)
        factor = jnp.concatenate(
            [ref[:, begin:] for ref in factors[group * GROUP : (group + 1) * GROUP]], axis=0
        )
        part = jnp.dot(chosen, factor, preferred_element_type=F32)
        total = part if total is None else total + part
    adapted = total.astype(BF16).astype(F32)
    out_ref[...] = ((near_ref[...] + far_ref[...]) + adapted).astype(BF16)


def per_device(hidden, demand, lengths, holder_slot, value_weight, factor_in, factor_out):
    rows, features = hidden.shape
    owners = lax.axis_size("batch")
    rank, width = factor_out.shape[1:]
    depth = features // 2
    order = ring_order(owners)
    forward = [(order[i], order[(i + 1) % owners]) for i in range(owners)]
    backward = [(b, a) for a, b in forward]
    swap = [(0, 1), (1, 0)]

    full = (owners - 1) // 2
    distances = [0]
    for step in range(1, full + 1):
        distances += [step, -step]
    distances.append(owners // 2)
    table = [
        [[order[(order.index(me) - distance) % owners] for distance in distances]]
        for me in range(owners)
    ]
    first, second, bounds = shard_call(
        factor_in[0].T, factor_out[0], demand, lengths, holder_slot, jnp.asarray(table, I32), depth
    )
    to_other, bounds = rows_call(hidden, bounds)
    bounds, first_later, second_later = lax.optimization_barrier((mark(bounds), first, second))

    firsts, seconds = [first], [second]
    ahead, behind = (first, second_later), (first_later, second)
    for step in range(1, full + 1):
        a = lax.ppermute(ahead[0], "batch", forward)
        d = lax.ppermute(behind[1], "batch", backward)
        b = lax.ppermute(ahead[1], "batch", forward)
        c = lax.ppermute(behind[0], "batch", backward)
        ahead, behind = (a, b), (c, d)
        firsts += [a, c]
        seconds += [b, d]
    firsts.append(lax.ppermute(ahead[0], "batch", forward))
    seconds.append(lax.ppermute(behind[1], "batch", backward))
    near, far = base_call(hidden, value_weight)
    hidden, near, far = lax.optimization_barrier((hidden, near, far))
    other = lax.ppermute(to_other, "groups", swap)

    count = owners // GROUP
    early = range(count - 1)
    pieces = []
    for group in early:
        pieces += firsts[group * GROUP : (group + 1) * GROUP]
        pieces += seconds[group * GROUP : (group + 1) * GROUP]
    both = (hidden, other)
    start_mine, start_theirs = rank_call(
        (0, 1), tuple(early), depth, rows, both, bounds, pieces, ()
    )
    start_theirs, far = lax.optimization_barrier((start_theirs, far))
    far = lax.ppermute(far, "tensor", swap)
    pieces = firsts[-GROUP:] + seconds[-GROUP:]
    late = (count - 1,)
    (theirs,) = rank_call((1,), late, depth, rows, (other,), bounds, pieces, (start_theirs,))
    mine = rank_call((0,), late, depth, rows, (hidden,), bounds, pieces, (start_mine,))

    two = lax.ppermute(theirs, "groups", swap)
    three = lax.ppermute(two, "tensor", swap)
    one = [lax.ppermute(part, "tensor", swap) for part in mine]

    operands = [bounds, *mine, *one, two, three, near, far, *seconds]
    return pl.pallas_call(
        final_kernel,
        out_shape=jax.ShapeDtypeStruct((rows, width), BF16),
        in_specs=[VMEM] * len(operands),
        out_specs=VMEM,
        compiler_params=params(),
    )(*operands)


def solution(mesh):
    return jax.shard_map(
        per_device,
        mesh=mesh,
        in_specs=(
            P(("groups", "batch"), "tensor"),
            P(("groups", "batch"), None),
            P(("groups", "batch"), None),
            P(),
            P("tensor", None),
            P("batch", "tensor", None),
            P("batch", None, "tensor"),
        ),
        out_specs=P(("groups", "batch"), "tensor"),
        check_vma=False,
    )
```

```python
import functools

import jax
import jax.numpy as jnp
from jax import lax
from jax.experimental import pallas as pl
from jax.experimental.pallas import tpu as pltpu
from jax.sharding import PartitionSpec as P

F32, BF16, I32 = jnp.float32, jnp.bfloat16, jnp.int32
VMEM_LIMIT = 24 * 1024 * 1024
HALF = pl.CostEstimate(flops=0, bytes_accessed=1 << 22, transcendentals=0)
LONG = pl.CostEstimate(flops=1 << 33, bytes_accessed=1 << 24, transcendentals=0)
GROUP = 4
VMEM = pl.BlockSpec(memory_space=pltpu.VMEM)
HBM = pl.BlockSpec(memory_space=pltpu.HBM)


def in_hbm(array):
    return pltpu.with_memory_space_constraint(array, pltpu.HBM)


def params():
    return pltpu.CompilerParams(vmem_limit_bytes=VMEM_LIMIT)


def ring_order(size):
    if size % 4:
        return list(range(size))
    columns = size // 4
    order = [0]
    for row in range(4):
        across = range(1, columns) if row % 2 == 0 else range(columns - 1, 0, -1)
        order += [row * columns + column for column in across]
    return order + [row * columns for row in (3, 2, 1)]


def contract(left, right):
    return lax.dot_general(left, right, (((1,), (1,)), ((), ())), preferred_element_type=F32)


def extra_rows(columns):
    return 2 * -(-columns // 1024) * 8


def shard_kernel(
    depth,
    rank,
    factor_ref,
    factor_out_ref,
    demand_ref,
    lengths_ref,
    holder_ref,
    slots_ref,
    first_ref,
    second_ref,
    bounds_ref,
    demand,
    lengths,
    holder,
    slots,
    sems,
):
    group, place = lax.axis_index("groups"), lax.axis_index("batch")
    cut = first_ref.shape[1]
    here = pl.multiple_of(group * depth, 128)
    after = pl.multiple_of(group * depth + cut, 128)
    small = [
        pltpu.make_async_copy(demand_ref, demand, sems.at[0]),
        pltpu.make_async_copy(lengths_ref, lengths, sems.at[1]),
        pltpu.make_async_copy(holder_ref, holder, sems.at[2]),
        pltpu.make_async_copy(slots_ref.at[pl.ds(place, 1)], slots, sems.at[3]),
    ]
    large = [
        pltpu.make_async_copy(factor_ref.at[:, pl.ds(here, cut)], first_ref, sems.at[4]),
        pltpu.make_async_copy(
            factor_ref.at[:, pl.ds(after, depth - cut)], second_ref.at[:, : depth - cut], sems.at[5]
        ),
        pltpu.make_async_copy(factor_out_ref, second_ref.at[:, depth - cut :], sems.at[6]),
    ]
    for copy in small + large:
        copy.start()
    for copy in small:
        copy.wait()
    count = slots.shape[2]
    items = demand.shape[1]
    column = lax.broadcasted_iota(I32, (1, count * rank), 1)
    zero = jnp.int32(0)

    def chunk_mask(chunk):
        return (column >= chunk * rank) & (column < (chunk + 1) * rank)

    low = high = jnp.zeros((1, count * rank), I32)
    if items * count <= 64:
        start = zero
        spans = []
        for item in range(items):
            end = start + lengths[0, item]
            spans.append((holder[demand[0, item]], start, end))
            start = end
        for chunk in range(count):
            slot = slots[0, 0, chunk]
            begin = end = zero
            for owner, first, last in spans:
                begin = jnp.where(owner == slot, first, begin)
                end = jnp.where(owner == slot, last, end)
            low = jnp.where(chunk_mask(chunk), begin, low)
            high = jnp.where(chunk_mask(chunk), end, high)
    else:

        def chunk_ends(chunk, carry):
            low, high = carry
            slot = slots[0, 0, chunk]

            def item_ends(item, state):
                start, begin, end = state
                last = start + lengths[0, item]
                hit = holder[demand[0, item]] == slot
                return last, jnp.where(hit, start, begin), jnp.where(hit, last, end)

            _, begin, end = lax.fori_loop(0, items, item_ends, (zero, zero, zero))
            mask = chunk_mask(chunk)
            return jnp.where(mask, begin, low), jnp.where(mask, end, high)

        low, high = lax.fori_loop(0, count, chunk_ends, (low, high))
    bounds_ref[0:1, :] = low
    bounds_ref[1:2, :] = high
    bounds_ref[2:8, :] = jnp.zeros((6, count * rank), I32)
    for copy in large:
        copy.wait()


def shard_call(factor, factor_out, demand, lengths, holder_slot, slots, depth):
    rank, width = factor_out.shape
    cut = (depth + width) // 2
    count = slots.shape[2]
    return pl.pallas_call(
        functools.partial(shard_kernel, depth, rank),
        out_shape=(
            jax.ShapeDtypeStruct((rank, cut), factor.dtype),
            jax.ShapeDtypeStruct((rank, cut), factor.dtype),
            jax.ShapeDtypeStruct((8, count * rank), I32),
        ),
        in_specs=[HBM] * 6,
        out_specs=(VMEM,) * 3,
        scratch_shapes=[
            pltpu.SMEM(demand.shape, I32),
            pltpu.SMEM(lengths.shape, I32),
            pltpu.SMEM(holder_slot.shape, I32),
            pltpu.SMEM((1, 1, count), I32),
            pltpu.SemaphoreType.DMA((7,)),
        ],
        compiler_params=params(),
        cost_estimate=LONG,
    )(*map(in_hbm, (factor, factor_out, demand, lengths, holder_slot, slots)))


def rows_kernel(depth, hidden_ref, bounds_ref, to_other_ref, bounds_out_ref):
    rows = hidden_ref.shape[0]
    there = pl.multiple_of((1 - lax.axis_index("groups")) * depth, 128)
    for i in range(depth // 128):
        to_other_ref[i * rows : (i + 1) * rows, :] = hidden_ref[:, pl.ds(there + i * 128, 128)]
    columns = bounds_ref.shape[1]
    extra = extra_rows(columns)
    line = lax.broadcasted_iota(I32, (extra, 128), 0)
    ends = jnp.zeros((extra, 128), I32)
    for i in range(columns // 128):
        span = slice(i * 128, (i + 1) * 128)
        ends = jnp.where(line == i, bounds_ref[0:1, span], ends)
        ends = jnp.where(line == extra // 2 + i, bounds_ref[1:2, span], ends)
    to_other_ref[-extra:, :] = ends.astype(F32).astype(BF16)
    bounds_out_ref[...] = bounds_ref[...]


def rows_call(hidden, bounds):
    rows, features = hidden.shape
    depth = features // 2
    tall = depth // 128 * rows + extra_rows(bounds.shape[1])
    return pl.pallas_call(
        functools.partial(rows_kernel, depth),
        out_shape=(
            jax.ShapeDtypeStruct((tall, 128), hidden.dtype),
            jax.ShapeDtypeStruct(bounds.shape, I32),
        ),
        in_specs=[VMEM] * 2,
        out_specs=(VMEM,) * 2,
        compiler_params=params(),
        cost_estimate=LONG,
    )(hidden, bounds)


def mark_kernel(bounds_ref, out_ref):
    out_ref[...] = bounds_ref[...]


def mark(bounds):
    return pl.pallas_call(
        mark_kernel,
        out_shape=jax.ShapeDtypeStruct(bounds.shape, bounds.dtype),
        in_specs=[VMEM],
        out_specs=VMEM,
        compiler_params=params(),
        cost_estimate=LONG,
    )(bounds)


def base_kernel(rows_ref, weight_ref, near_ref, far_ref):
    width = near_ref.shape[1]
    core = lax.axis_index("tensor")
    for out_ref, side in ((near_ref, core), (far_ref, 1 - core)):
        columns = pl.ds(pl.multiple_of(side * width, 128), width)
        out_ref[...] = jnp.dot(
            rows_ref[...], weight_ref[:, columns], preferred_element_type=F32
        )


def base_call(rows, weight):
    out = jax.ShapeDtypeStruct((rows.shape[0], weight.shape[1] // 2), F32)
    return pl.pallas_call(
        base_kernel,
        out_shape=(out, out),
        in_specs=[VMEM] * 2,
        out_specs=(VMEM,) * 2,
        compiler_params=params(),
        cost_estimate=HALF,
    )(rows, weight)


def group_mask(low, high, shape):
    row = lax.broadcasted_iota(I32, shape, 0)
    return (row >= low) & (row < high)


def own_ends(bounds_ref, group, size):
    columns = slice(group * size, (group + 1) * size)
    return bounds_ref[0:1, columns], bounds_ref[1:2, columns]


def other_ends(other_ref, extra, group, size):
    ends = other_ref[-extra:, :].astype(F32).astype(I32)
    lines = range(group * size // 128, (group + 1) * size // 128)
    low = jnp.concatenate([ends[i : i + 1] for i in lines], axis=1)
    high = jnp.concatenate([ends[extra // 2 + i : extra // 2 + i + 1] for i in lines], axis=1)
    return low, high


def fold(masked):
    total = masked[:, :128]
    for begin in range(128, masked.shape[1], 128):
        total = total + masked[:, begin : begin + 128]
    return total


def rank_kernel(sides, groups, depth, last, *refs):
    refs = list(refs)
    rows_refs, refs = refs[: len(sides)], refs[len(sides) :]
    bounds_ref, pieces = refs[0], refs[1:]
    pieces, rest = pieces[: 2 * GROUP * len(groups)], pieces[2 * GROUP * len(groups) :]
    starts, outs = (rest[: len(sides)], rest[len(sides) :]) if last else ((), rest)
    cut = pieces[0].shape[1]
    rank = pieces[0].shape[0]
    size = GROUP * rank
    extra = extra_rows(bounds_ref.shape[1])
    rows = []
    for side, ref in zip(sides, rows_refs):
        if side == 0:
            offset = pl.multiple_of(lax.axis_index("groups") * depth, 128)
            rows.append(ref[:, pl.ds(offset, depth)])
        else:
            blocks = depth // 128
            tall = (ref.shape[0] - extra) // blocks
            rows.append(
                jnp.concatenate([ref[i * tall : (i + 1) * tall, :] for i in range(blocks)], axis=1)
            )
    count = rows[0].shape[0]
    rows = jnp.concatenate(rows, axis=0)
    totals = [ref[...] for ref in starts] if last else [None] * len(sides)
    for i, group in enumerate(groups):
        held = pieces[2 * GROUP * i : 2 * GROUP * (i + 1)]
        first = jnp.concatenate([ref[...] for ref in held[:GROUP]], axis=0)
        second = jnp.concatenate([ref[:, : depth - cut] for ref in held[GROUP:]], axis=0)
        part = contract(rows, jnp.concatenate([first, second], axis=1))
        for s, side in enumerate(sides):
            if side == 0:
                ends = own_ends(bounds_ref, group, size)
            else:
                ends = other_ends(rows_refs[s], extra, group, size)
            here = part[s * count : (s + 1) * count]
            kept = fold(jnp.where(group_mask(*ends, here.shape), here, 0.0))
            totals[s] = kept if totals[s] is None else totals[s] + kept
    if last:
        (total,) = totals
        total = total + pltpu.roll(total, rank, 1)
        half = count // 2
        lane = lax.broadcasted_iota(I32, (half, 2 * rank), 1)
        total = jnp.where(lane < rank, total[:half], total[half:])
        size = outs[0].shape[0]
        totals = [total[i * size : (i + 1) * size] for i in range(len(outs))]
    for total, out_ref in zip(totals, outs):
        out_ref[...] = total.astype(out_ref.dtype)


def rank_call(sides, groups, depth, count, rows, bounds, pieces, starts):
    rank = pieces[0].shape[0]
    last = len(starts) > 0
    if not last:
        out = (jax.ShapeDtypeStruct((count, 2 * rank), F32),) * len(sides)
    elif sides == (1,):
        out = (jax.ShapeDtypeStruct((count // 2, 2 * rank), BF16),)
    else:
        out = (jax.ShapeDtypeStruct((count // 4, 2 * rank), F32),) * 2
    operands = [*rows, bounds, *pieces, *starts]
    return pl.pallas_call(
        functools.partial(rank_kernel, sides, groups, depth, last),
        out_shape=out,
        in_specs=[VMEM] * len(operands),
        out_specs=(VMEM,) * len(out),
        compiler_params=params(),
        cost_estimate=HALF if last and sides == (0,) else LONG,
    )(*operands)


def final_kernel(bounds_ref, top, low, one_top, one_low, two, three, near_ref, far_ref, *refs):
    factors, out_ref = refs[:-1], refs[-1]
    rank, width = factors[0].shape[0], out_ref.shape[1]
    begin = factors[0].shape[1] - width
    here = jnp.concatenate([top[...] + one_top[...], low[...] + one_low[...]], axis=0)
    packed = here + (two[...].astype(F32) + three[...].astype(F32))
    turned = pltpu.roll(packed, rank, 1)
    lane = lax.broadcasted_iota(I32, packed.shape, 1)
    values = jnp.concatenate(
        [jnp.where(lane < rank, packed, turned), jnp.where(lane < rank, turned, packed)], axis=0
    )
    wide = jnp.concatenate([values] * (GROUP // 2), axis=1)
    total = None
    for group in range(len(factors) // GROUP):
        mask = group_mask(*own_ends(bounds_ref, group, GROUP * rank), wide.shape)
        chosen = jnp.where(mask, wide, 0.0).astype(BF16)
        factor = jnp.concatenate(
            [ref[:, begin:] for ref in factors[group * GROUP : (group + 1) * GROUP]], axis=0
        )
        part = jnp.dot(chosen, factor, preferred_element_type=F32)
        total = part if total is None else total + part
    adapted = total.astype(BF16).astype(F32)
    out_ref[...] = ((near_ref[...] + far_ref[...]) + adapted).astype(BF16)


def per_device(hidden, demand, lengths, holder_slot, value_weight, factor_in, factor_out):
    rows, features = hidden.shape
    owners = lax.axis_size("batch")
    rank, width = factor_out.shape[1:]
    depth = features // 2
    order = ring_order(owners)
    forward = [(order[i], order[(i + 1) % owners]) for i in range(owners)]
    backward = [(b, a) for a, b in forward]
    swap = [(0, 1), (1, 0)]

    full = (owners - 1) // 2
    distances = [0]
    for step in range(1, full + 1):
        distances += [step, -step]
    distances.append(owners // 2)
    table = [
        [[order[(order.index(me) - distance) % owners] for distance in distances]]
        for me in range(owners)
    ]
    first, second, bounds = shard_call(
        factor_in[0].T, factor_out[0], demand, lengths, holder_slot, jnp.asarray(table, I32), depth
    )
    to_other, bounds = rows_call(hidden, bounds)
    bounds, first_later = lax.optimization_barrier((mark(bounds), first))

    firsts, seconds = [first], [second]
    ahead, behind = (first, second), (first_later, second)
    for step in range(1, full + 1):
        a = lax.ppermute(ahead[0], "batch", forward)
        d = lax.ppermute(behind[1], "batch", backward)
        b = lax.ppermute(ahead[1], "batch", forward)
        c = lax.ppermute(behind[0], "batch", backward)
        ahead, behind = (a, b), (c, d)
        firsts += [a, c]
        seconds += [b, d]
    firsts.append(lax.ppermute(ahead[0], "batch", forward))
    seconds.append(lax.ppermute(behind[1], "batch", backward))
    near, far = base_call(hidden, value_weight)
    hidden, near, far = lax.optimization_barrier((hidden, near, far))
    other = lax.ppermute(to_other, "groups", swap)

    count = owners // GROUP
    early = range(count - 1)
    pieces = []
    for group in early:
        pieces += firsts[group * GROUP : (group + 1) * GROUP]
        pieces += seconds[group * GROUP : (group + 1) * GROUP]
    both = (hidden, other)
    start_mine, start_theirs = rank_call(
        (0, 1), tuple(early), depth, rows, both, bounds, pieces, ()
    )
    start_theirs, far = lax.optimization_barrier((start_theirs, far))
    far = lax.ppermute(far, "tensor", swap)
    pieces = firsts[-GROUP:] + seconds[-GROUP:]
    late = (count - 1,)
    (theirs,) = rank_call((1,), late, depth, rows, (other,), bounds, pieces, (start_theirs,))
    mine = rank_call((0,), late, depth, rows, (hidden,), bounds, pieces, (start_mine,))

    two = lax.ppermute(theirs, "groups", swap)
    three = lax.ppermute(theirs, ("groups", "tensor"), [(0, 3), (1, 2), (2, 1), (3, 0)])
    one = [lax.ppermute(part, "tensor", swap) for part in mine]

    operands = [bounds, *mine, *one, two, three, near, far, *seconds]
    return pl.pallas_call(
        final_kernel,
        out_shape=jax.ShapeDtypeStruct((rows, width), BF16),
        in_specs=[VMEM] * len(operands),
        out_specs=VMEM,
        compiler_params=params(),
    )(*operands)


def solution(mesh):
    return jax.shard_map(
        per_device,
        mesh=mesh,
        in_specs=(
            P(("groups", "batch"), "tensor"),
            P(("groups", "batch"), None),
            P(("groups", "batch"), None),
            P(),
            P("tensor", None),
            P("batch", "tensor", None),
            P("batch", None, "tensor"),
        ),
        out_specs=P(("groups", "batch"), "tensor"),
        check_vma=False,
    )
```

```python
import functools

import jax
import jax.numpy as jnp
from jax import lax
from jax.experimental import pallas as pl
from jax.experimental.pallas import tpu as pltpu
from jax.sharding import PartitionSpec as P

F32, BF16, I32 = jnp.float32, jnp.bfloat16, jnp.int32
VMEM_LIMIT = 24 * 1024 * 1024
HALF = pl.CostEstimate(flops=0, bytes_accessed=1 << 22, transcendentals=0)
LONG = pl.CostEstimate(flops=1 << 33, bytes_accessed=1 << 24, transcendentals=0)
GROUP = 4
VMEM = pl.BlockSpec(memory_space=pltpu.VMEM)
HBM = pl.BlockSpec(memory_space=pltpu.HBM)


def in_hbm(array):
    return pltpu.with_memory_space_constraint(array, pltpu.HBM)


def params():
    return pltpu.CompilerParams(vmem_limit_bytes=VMEM_LIMIT)


def ring_order(size):
    if size % 4:
        return list(range(size))
    columns = size // 4
    order = [0]
    for row in range(4):
        across = range(1, columns) if row % 2 == 0 else range(columns - 1, 0, -1)
        order += [row * columns + column for column in across]
    return order + [row * columns for row in (3, 2, 1)]


def contract(left, right):
    return lax.dot_general(left, right, (((1,), (1,)), ((), ())), preferred_element_type=F32)


def extra_rows(columns):
    return 2 * -(-columns // 1024) * 8


def shard_kernel(
    depth,
    rank,
    factor_ref,
    factor_out_ref,
    demand_ref,
    lengths_ref,
    holder_ref,
    slots_ref,
    first_ref,
    second_ref,
    bounds_ref,
    demand,
    lengths,
    holder,
    slots,
    sems,
):
    group, place = lax.axis_index("groups"), lax.axis_index("batch")
    cut = first_ref.shape[1]
    here = pl.multiple_of(group * depth, 128)
    after = pl.multiple_of(group * depth + cut, 128)
    small = [
        pltpu.make_async_copy(demand_ref, demand, sems.at[0]),
        pltpu.make_async_copy(lengths_ref, lengths, sems.at[1]),
        pltpu.make_async_copy(holder_ref, holder, sems.at[2]),
        pltpu.make_async_copy(slots_ref.at[pl.ds(place, 1)], slots, sems.at[3]),
    ]
    large = [
        pltpu.make_async_copy(factor_ref.at[:, pl.ds(here, cut)], first_ref, sems.at[4]),
        pltpu.make_async_copy(
            factor_ref.at[:, pl.ds(after, depth - cut)], second_ref.at[:, : depth - cut], sems.at[5]
        ),
        pltpu.make_async_copy(factor_out_ref, second_ref.at[:, depth - cut :], sems.at[6]),
    ]
    for copy in small + large:
        copy.start()
    for copy in small:
        copy.wait()
    count = slots.shape[2]
    items = demand.shape[1]
    column = lax.broadcasted_iota(I32, (1, count * rank), 1)
    zero = jnp.int32(0)

    def chunk_mask(chunk):
        return (column >= chunk * rank) & (column < (chunk + 1) * rank)

    low = high = jnp.zeros((1, count * rank), I32)
    if items * count <= 64:
        start = zero
        spans = []
        for item in range(items):
            end = start + lengths[0, item]
            spans.append((holder[demand[0, item]], start, end))
            start = end
        for chunk in range(count):
            slot = slots[0, 0, chunk]
            begin = end = zero
            for owner, first, last in spans:
                begin = jnp.where(owner == slot, first, begin)
                end = jnp.where(owner == slot, last, end)
            low = jnp.where(chunk_mask(chunk), begin, low)
            high = jnp.where(chunk_mask(chunk), end, high)
    else:

        def chunk_ends(chunk, carry):
            low, high = carry
            slot = slots[0, 0, chunk]

            def item_ends(item, state):
                start, begin, end = state
                last = start + lengths[0, item]
                hit = holder[demand[0, item]] == slot
                return last, jnp.where(hit, start, begin), jnp.where(hit, last, end)

            _, begin, end = lax.fori_loop(0, items, item_ends, (zero, zero, zero))
            mask = chunk_mask(chunk)
            return jnp.where(mask, begin, low), jnp.where(mask, end, high)

        low, high = lax.fori_loop(0, count, chunk_ends, (low, high))
    bounds_ref[0:1, :] = low
    bounds_ref[1:2, :] = high
    bounds_ref[2:8, :] = jnp.zeros((6, count * rank), I32)
    for copy in large:
        copy.wait()


def shard_call(factor, factor_out, demand, lengths, holder_slot, slots, depth):
    rank, width = factor_out.shape
    cut = (depth + width) // 2
    count = slots.shape[2]
    return pl.pallas_call(
        functools.partial(shard_kernel, depth, rank),
        out_shape=(
            jax.ShapeDtypeStruct((rank, cut), factor.dtype),
            jax.ShapeDtypeStruct((rank, cut), factor.dtype),
            jax.ShapeDtypeStruct((8, count * rank), I32),
        ),
        in_specs=[HBM] * 6,
        out_specs=(VMEM,) * 3,
        scratch_shapes=[
            pltpu.SMEM(demand.shape, I32),
            pltpu.SMEM(lengths.shape, I32),
            pltpu.SMEM(holder_slot.shape, I32),
            pltpu.SMEM((1, 1, count), I32),
            pltpu.SemaphoreType.DMA((7,)),
        ],
        compiler_params=params(),
        cost_estimate=LONG,
    )(*map(in_hbm, (factor, factor_out, demand, lengths, holder_slot, slots)))


def rows_kernel(depth, hidden_ref, bounds_ref, to_other_ref, bounds_out_ref):
    rows = hidden_ref.shape[0]
    there = pl.multiple_of((1 - lax.axis_index("groups")) * depth, 128)
    for i in range(depth // 128):
        to_other_ref[i * rows : (i + 1) * rows, :] = hidden_ref[:, pl.ds(there + i * 128, 128)]
    columns = bounds_ref.shape[1]
    extra = extra_rows(columns)
    line = lax.broadcasted_iota(I32, (extra, 128), 0)
    ends = jnp.zeros((extra, 128), I32)
    for i in range(columns // 128):
        span = slice(i * 128, (i + 1) * 128)
        ends = jnp.where(line == i, bounds_ref[0:1, span], ends)
        ends = jnp.where(line == extra // 2 + i, bounds_ref[1:2, span], ends)
    to_other_ref[-extra:, :] = ends.astype(F32).astype(BF16)
    bounds_out_ref[...] = bounds_ref[...]


def rows_call(hidden, bounds):
    rows, features = hidden.shape
    depth = features // 2
    tall = depth // 128 * rows + extra_rows(bounds.shape[1])
    return pl.pallas_call(
        functools.partial(rows_kernel, depth),
        out_shape=(
            jax.ShapeDtypeStruct((tall, 128), hidden.dtype),
            jax.ShapeDtypeStruct(bounds.shape, I32),
        ),
        in_specs=[VMEM] * 2,
        out_specs=(VMEM,) * 2,
        compiler_params=params(),
        cost_estimate=LONG,
    )(hidden, bounds)


def mark_kernel(bounds_ref, out_ref):
    out_ref[...] = bounds_ref[...]


def mark(bounds):
    return pl.pallas_call(
        mark_kernel,
        out_shape=jax.ShapeDtypeStruct(bounds.shape, bounds.dtype),
        in_specs=[VMEM],
        out_specs=VMEM,
        compiler_params=params(),
        cost_estimate=LONG,
    )(bounds)


def base_kernel(rows_ref, weight_ref, near_ref, far_ref):
    width = near_ref.shape[1]
    core = lax.axis_index("tensor")
    for out_ref, side in ((near_ref, core), (far_ref, 1 - core)):
        columns = pl.ds(pl.multiple_of(side * width, 128), width)
        out_ref[...] = jnp.dot(
            rows_ref[...], weight_ref[:, columns], preferred_element_type=F32
        )


def base_call(rows, weight):
    out = jax.ShapeDtypeStruct((rows.shape[0], weight.shape[1] // 2), F32)
    return pl.pallas_call(
        base_kernel,
        out_shape=(out, out),
        in_specs=[VMEM] * 2,
        out_specs=(VMEM,) * 2,
        compiler_params=params(),
        cost_estimate=HALF,
    )(rows, weight)


def group_mask(low, high, shape):
    row = lax.broadcasted_iota(I32, shape, 0)
    return (row >= low) & (row < high)


def own_ends(bounds_ref, begin, end):
    return bounds_ref[0:1, begin:end], bounds_ref[1:2, begin:end]


def other_ends(other_ref, extra, begin, end):
    ends = other_ref[-extra:, :].astype(F32).astype(I32)
    lines = range(begin // 128, end // 128)
    low = jnp.concatenate([ends[i : i + 1] for i in lines], axis=1)
    high = jnp.concatenate([ends[extra // 2 + i : extra // 2 + i + 1] for i in lines], axis=1)
    return low, high


def fold(masked):
    total = masked[:, :128]
    for begin in range(128, masked.shape[1], 128):
        total = total + masked[:, begin : begin + 128]
    return total


def rank_kernel(sides, plan, chunks, depth, last, started, *refs):
    refs = list(refs)
    rows_refs, refs = refs[: len(sides)], refs[len(sides) :]
    bounds_ref, pieces = refs[0], refs[1:]
    firsts = dict(zip(chunks, pieces))
    seconds = dict(zip(chunks, pieces[len(chunks) :]))
    rest = pieces[2 * len(chunks) :]
    outs = rest[started:]
    starts = rest[:started]
    rank, cut = pieces[0].shape
    extra = extra_rows(bounds_ref.shape[1])
    rows = {}
    for side, ref in zip(sides, rows_refs):
        if side == 0:
            offset = pl.multiple_of(lax.axis_index("groups") * depth, 128)
            rows[side] = ref[:, pl.ds(offset, depth)]
        else:
            blocks = depth // 128
            tall = (ref.shape[0] - extra) // blocks
            rows[side] = jnp.concatenate(
                [ref[i * tall : (i + 1) * tall, :] for i in range(blocks)], axis=1
            )
    count = rows[sides[0]].shape[0]
    totals = {side: ref[...] for side, ref in zip(sides, starts)}
    for begin, end, from_chunk, to_chunk, meant in plan:
        held = [chunk if from_chunk <= chunk < to_chunk else from_chunk for chunk in range(begin, end)]
        first = jnp.concatenate([firsts[chunk][...] for chunk in held], axis=0)
        second = jnp.concatenate([seconds[chunk][:, : depth - cut] for chunk in held], axis=0)
        tall = jnp.concatenate([rows[side] for side in meant], axis=0)
        part = contract(tall, jnp.concatenate([first, second], axis=1))
        for i, side in enumerate(meant):
            columns = (begin * rank, end * rank)
            if side == 0:
                ends = own_ends(bounds_ref, *columns)
            else:
                ends = other_ends(rows_refs[sides.index(1)], extra, *columns)
            here = part[i * count : (i + 1) * count]
            mask = group_mask(*ends, here.shape)
            if (from_chunk, to_chunk) != (begin, end):
                lane = lax.broadcasted_iota(I32, here.shape, 1)
                mask = mask & (lane >= (from_chunk - begin) * rank)
                mask = mask & (lane < (to_chunk - begin) * rank)
            kept = fold(jnp.where(mask, here, 0.0))
            totals[side] = totals[side] + kept if side in totals else kept
    totals = [totals[side] for side in sides]
    if last:
        (total,) = totals
        total = total + pltpu.roll(total, rank, 1)
        half = count // 2
        lane = lax.broadcasted_iota(I32, (half, 2 * rank), 1)
        total = jnp.where(lane < rank, total[:half], total[half:])
        size = outs[0].shape[0]
        totals = [total[i * size : (i + 1) * size] for i in range(len(outs))]
    for total, out_ref in zip(totals, outs):
        out_ref[...] = total.astype(out_ref.dtype)


def rank_call(sides, plan, chunks, depth, count, rows, bounds, firsts, seconds, starts, last=True):
    pieces = [firsts[chunk] for chunk in chunks] + [seconds[chunk] for chunk in chunks]
    rank = pieces[0].shape[0]
    last = last and len(starts) > 0
    if not last:
        out = (jax.ShapeDtypeStruct((count, 2 * rank), F32),) * len(sides)
    elif sides == (1,):
        out = (jax.ShapeDtypeStruct((count // 2, 2 * rank), BF16),)
    else:
        out = (jax.ShapeDtypeStruct((count // 4, 2 * rank), F32),) * 2
    operands = [*rows, bounds, *pieces, *starts]
    return pl.pallas_call(
        functools.partial(rank_kernel, sides, plan, chunks, depth, last, len(starts)),
        out_shape=out,
        in_specs=[VMEM] * len(operands),
        out_specs=(VMEM,) * len(out),
        compiler_params=params(),
        cost_estimate=HALF if last and sides == (0,) else LONG,
    )(*operands)


def final_kernel(bounds_ref, top, low, one_top, one_low, two, three, near_ref, far_ref, *refs):
    factors, out_ref = refs[:-1], refs[-1]
    rank, width = factors[0].shape[0], out_ref.shape[1]
    begin = factors[0].shape[1] - width
    here = jnp.concatenate([top[...] + one_top[...], low[...] + one_low[...]], axis=0)
    packed = here + (two[...].astype(F32) + three[...].astype(F32))
    turned = pltpu.roll(packed, rank, 1)
    lane = lax.broadcasted_iota(I32, packed.shape, 1)
    values = jnp.concatenate(
        [jnp.where(lane < rank, packed, turned), jnp.where(lane < rank, turned, packed)], axis=0
    )
    wide = jnp.concatenate([values] * (GROUP // 2), axis=1)
    total = None
    for group in range(len(factors) // GROUP):
        columns = (group * GROUP * rank, (group + 1) * GROUP * rank)
        mask = group_mask(*own_ends(bounds_ref, *columns), wide.shape)
        chosen = jnp.where(mask, wide, 0.0).astype(BF16)
        factor = jnp.concatenate(
            [ref[:, begin:] for ref in factors[group * GROUP : (group + 1) * GROUP]], axis=0
        )
        part = jnp.dot(chosen, factor, preferred_element_type=F32)
        total = part if total is None else total + part
    adapted = total.astype(BF16).astype(F32)
    out_ref[...] = ((near_ref[...] + far_ref[...]) + adapted).astype(BF16)


def per_device(hidden, demand, lengths, holder_slot, value_weight, factor_in, factor_out):
    rows, features = hidden.shape
    owners = lax.axis_size("batch")
    rank, width = factor_out.shape[1:]
    depth = features // 2
    order = ring_order(owners)
    forward = [(order[i], order[(i + 1) % owners]) for i in range(owners)]
    backward = [(b, a) for a, b in forward]
    swap = [(0, 1), (1, 0)]

    full = (owners - 1) // 2
    distances = [0]
    for step in range(1, full + 1):
        distances += [step, -step]
    distances.append(owners // 2)
    table = [
        [[order[(order.index(me) - distance) % owners] for distance in distances]]
        for me in range(owners)
    ]
    first, second, bounds = shard_call(
        factor_in[0].T, factor_out[0], demand, lengths, holder_slot, jnp.asarray(table, I32), depth
    )
    to_other, bounds = rows_call(hidden, bounds)
    bounds, first_later = lax.optimization_barrier((mark(bounds), first))

    firsts, seconds = [first], [second]
    ahead, behind = (first, second), (first_later, second)
    for step in range(1, full + 1):
        a = lax.ppermute(ahead[0], "batch", forward)
        d = lax.ppermute(behind[1], "batch", backward)
        b = lax.ppermute(ahead[1], "batch", forward)
        c = lax.ppermute(behind[0], "batch", backward)
        ahead, behind = (a, b), (c, d)
        firsts += [a, c]
        seconds += [b, d]
    firsts.append(lax.ppermute(ahead[0], "batch", forward))
    seconds.append(lax.ppermute(behind[1], "batch", backward))
    near, far = base_call(hidden, value_weight)
    hidden, near, far = lax.optimization_barrier((hidden, near, far))
    other = lax.ppermute(to_other, "groups", swap)

    before = owners - GROUP
    held = (depth, rows)
    plan = [(i, i + GROUP, i, i + GROUP, (0, 1)) for i in range(0, before, GROUP)]
    start_mine, start_theirs = rank_call(
        (0, 1), plan, range(before), *held, (hidden, other), bounds, firsts, seconds, ()
    )
    plan = [(before, owners, before, owners - 1, (1,))]
    (start_theirs,) = rank_call(
        (1,), plan, range(before, owners - 1), *held, (other,), bounds, firsts, seconds, (start_theirs,), False
    )
    plan = [(owners - 2, owners, owners - 1, owners, (1,))]
    (theirs,) = rank_call(
        (1,), plan, [owners - 1], *held, (other,), bounds, firsts, seconds, (start_theirs,)
    )
    theirs, far = lax.optimization_barrier((theirs, far))
    far = lax.ppermute(far, "tensor", swap)
    plan = [(before, owners, before, owners, (0,))]
    mine = rank_call(
        (0,), plan, range(before, owners), *held, (hidden,), bounds, firsts, seconds, (start_mine,)
    )

    two = lax.ppermute(theirs, "groups", swap)
    three = lax.ppermute(theirs, ("groups", "tensor"), [(0, 3), (1, 2), (2, 1), (3, 0)])
    one = [lax.ppermute(part, "tensor", swap) for part in mine]

    operands = [bounds, *mine, *one, two, three, near, far, *seconds]
    return pl.pallas_call(
        final_kernel,
        out_shape=jax.ShapeDtypeStruct((rows, width), BF16),
        in_specs=[VMEM] * len(operands),
        out_specs=VMEM,
        compiler_params=params(),
    )(*operands)


def solution(mesh):
    return jax.shard_map(
        per_device,
        mesh=mesh,
        in_specs=(
            P(("groups", "batch"), "tensor"),
            P(("groups", "batch"), None),
            P(("groups", "batch"), None),
            P(),
            P("tensor", None),
            P("batch", "tensor", None),
            P("batch", None, "tensor"),
        ),
        out_specs=P(("groups", "batch"), "tensor"),
        check_vma=False,
    )
```

```python
import functools

import jax
import jax.numpy as jnp
from jax import lax
from jax.experimental import pallas as pl
from jax.experimental.pallas import tpu as pltpu
from jax.sharding import PartitionSpec as P

F32, BF16, I32 = jnp.float32, jnp.bfloat16, jnp.int32
VMEM_LIMIT = 24 * 1024 * 1024
HALF = pl.CostEstimate(flops=0, bytes_accessed=1 << 22, transcendentals=0)
LONG = pl.CostEstimate(flops=1 << 33, bytes_accessed=1 << 24, transcendentals=0)
GROUP = 4
VMEM = pl.BlockSpec(memory_space=pltpu.VMEM)
HBM = pl.BlockSpec(memory_space=pltpu.HBM)


def in_hbm(array):
    return pltpu.with_memory_space_constraint(array, pltpu.HBM)


def params():
    return pltpu.CompilerParams(vmem_limit_bytes=VMEM_LIMIT)


def ring_order(size):
    if size % 4:
        return list(range(size))
    columns = size // 4
    order = [0]
    for row in range(4):
        across = range(1, columns) if row % 2 == 0 else range(columns - 1, 0, -1)
        order += [row * columns + column for column in across]
    return order + [row * columns for row in (3, 2, 1)]


def contract(left, right):
    return lax.dot_general(left, right, (((1,), (1,)), ((), ())), preferred_element_type=F32)


def extra_rows(columns):
    return 2 * -(-columns // 1024) * 8


def shard_kernel(
    depth,
    rank,
    factor_ref,
    factor_out_ref,
    demand_ref,
    lengths_ref,
    holder_ref,
    slots_ref,
    first_ref,
    second_ref,
    bounds_ref,
    demand,
    lengths,
    holder,
    slots,
    sems,
):
    group, place = lax.axis_index("groups"), lax.axis_index("batch")
    cut = first_ref.shape[1]
    here = pl.multiple_of(group * depth, 128)
    after = pl.multiple_of(group * depth + cut, 128)
    small = [
        pltpu.make_async_copy(demand_ref, demand, sems.at[0]),
        pltpu.make_async_copy(lengths_ref, lengths, sems.at[1]),
        pltpu.make_async_copy(holder_ref, holder, sems.at[2]),
        pltpu.make_async_copy(slots_ref.at[pl.ds(place, 1)], slots, sems.at[3]),
    ]
    large = [
        pltpu.make_async_copy(factor_ref.at[:, pl.ds(here, cut)], first_ref, sems.at[4]),
        pltpu.make_async_copy(
            factor_ref.at[:, pl.ds(after, depth - cut)], second_ref.at[:, : depth - cut], sems.at[5]
        ),
        pltpu.make_async_copy(factor_out_ref, second_ref.at[:, depth - cut :], sems.at[6]),
    ]
    for copy in small + large:
        copy.start()
    for copy in small:
        copy.wait()
    count = slots.shape[2]
    items = demand.shape[1]
    column = lax.broadcasted_iota(I32, (1, count * rank), 1)
    zero = jnp.int32(0)

    def chunk_mask(chunk):
        return (column >= chunk * rank) & (column < (chunk + 1) * rank)

    low = high = jnp.zeros((1, count * rank), I32)
    if items * count <= 64:
        start = zero
        spans = []
        for item in range(items):
            end = start + lengths[0, item]
            spans.append((holder[demand[0, item]], start, end))
            start = end
        for chunk in range(count):
            slot = slots[0, 0, chunk]
            begin = end = zero
            for owner, first, last in spans:
                begin = jnp.where(owner == slot, first, begin)
                end = jnp.where(owner == slot, last, end)
            low = jnp.where(chunk_mask(chunk), begin, low)
            high = jnp.where(chunk_mask(chunk), end, high)
    else:

        def chunk_ends(chunk, carry):
            low, high = carry
            slot = slots[0, 0, chunk]

            def item_ends(item, state):
                start, begin, end = state
                last = start + lengths[0, item]
                hit = holder[demand[0, item]] == slot
                return last, jnp.where(hit, start, begin), jnp.where(hit, last, end)

            _, begin, end = lax.fori_loop(0, items, item_ends, (zero, zero, zero))
            mask = chunk_mask(chunk)
            return jnp.where(mask, begin, low), jnp.where(mask, end, high)

        low, high = lax.fori_loop(0, count, chunk_ends, (low, high))
    bounds_ref[0:1, :] = low
    bounds_ref[1:2, :] = high
    bounds_ref[2:8, :] = jnp.zeros((6, count * rank), I32)
    for copy in large:
        copy.wait()


def shard_call(factor, factor_out, demand, lengths, holder_slot, slots, depth):
    rank, width = factor_out.shape
    cut = (depth + width) // 2
    count = slots.shape[2]
    return pl.pallas_call(
        functools.partial(shard_kernel, depth, rank),
        out_shape=(
            jax.ShapeDtypeStruct((rank, cut), factor.dtype),
            jax.ShapeDtypeStruct((rank, cut), factor.dtype),
            jax.ShapeDtypeStruct((8, count * rank), I32),
        ),
        in_specs=[HBM] * 6,
        out_specs=(VMEM,) * 3,
        scratch_shapes=[
            pltpu.SMEM(demand.shape, I32),
            pltpu.SMEM(lengths.shape, I32),
            pltpu.SMEM(holder_slot.shape, I32),
            pltpu.SMEM((1, 1, count), I32),
            pltpu.SemaphoreType.DMA((7,)),
        ],
        compiler_params=params(),
        cost_estimate=LONG,
    )(*map(in_hbm, (factor, factor_out, demand, lengths, holder_slot, slots)))


def rows_kernel(depth, hidden_ref, bounds_ref, to_other_ref, bounds_out_ref):
    rows = hidden_ref.shape[0]
    there = pl.multiple_of((1 - lax.axis_index("groups")) * depth, 128)
    for i in range(depth // 128):
        to_other_ref[i * rows : (i + 1) * rows, :] = hidden_ref[:, pl.ds(there + i * 128, 128)]
    columns = bounds_ref.shape[1]
    extra = extra_rows(columns)
    line = lax.broadcasted_iota(I32, (extra, 128), 0)
    ends = jnp.zeros((extra, 128), I32)
    for i in range(columns // 128):
        span = slice(i * 128, (i + 1) * 128)
        ends = jnp.where(line == i, bounds_ref[0:1, span], ends)
        ends = jnp.where(line == extra // 2 + i, bounds_ref[1:2, span], ends)
    to_other_ref[-extra:, :] = ends.astype(F32).astype(BF16)
    bounds_out_ref[...] = bounds_ref[...]


def rows_call(hidden, bounds):
    rows, features = hidden.shape
    depth = features // 2
    tall = depth // 128 * rows + extra_rows(bounds.shape[1])
    return pl.pallas_call(
        functools.partial(rows_kernel, depth),
        out_shape=(
            jax.ShapeDtypeStruct((tall, 128), hidden.dtype),
            jax.ShapeDtypeStruct(bounds.shape, I32),
        ),
        in_specs=[VMEM] * 2,
        out_specs=(VMEM,) * 2,
        compiler_params=params(),
        cost_estimate=LONG,
    )(hidden, bounds)


def mark_kernel(bounds_ref, out_ref):
    out_ref[...] = bounds_ref[...]


def mark(bounds):
    return pl.pallas_call(
        mark_kernel,
        out_shape=jax.ShapeDtypeStruct(bounds.shape, bounds.dtype),
        in_specs=[VMEM],
        out_specs=VMEM,
        compiler_params=params(),
        cost_estimate=LONG,
    )(bounds)


def base_kernel(rows_ref, weight_ref, near_ref, far_ref):
    width = near_ref.shape[1]
    core = lax.axis_index("tensor")
    for out_ref, side in ((near_ref, core), (far_ref, 1 - core)):
        columns = pl.ds(pl.multiple_of(side * width, 128), width)
        out_ref[...] = jnp.dot(
            rows_ref[...], weight_ref[:, columns], preferred_element_type=F32
        )


def base_call(rows, weight):
    out = jax.ShapeDtypeStruct((rows.shape[0], weight.shape[1] // 2), F32)
    return pl.pallas_call(
        base_kernel,
        out_shape=(out, out),
        in_specs=[VMEM] * 2,
        out_specs=(VMEM,) * 2,
        compiler_params=params(),
        cost_estimate=HALF,
    )(rows, weight)


def group_mask(low, high, shape):
    row = lax.broadcasted_iota(I32, shape, 0)
    return (row >= low) & (row < high)


def own_ends(bounds_ref, begin, end):
    return bounds_ref[0:1, begin:end], bounds_ref[1:2, begin:end]


def other_ends(other_ref, extra, begin, end):
    ends = other_ref[-extra:, :].astype(F32).astype(I32)
    lines = range(begin // 128, end // 128)
    low = jnp.concatenate([ends[i : i + 1] for i in lines], axis=1)
    high = jnp.concatenate([ends[extra // 2 + i : extra // 2 + i + 1] for i in lines], axis=1)
    return low, high


def fold(masked):
    total = masked[:, :128]
    for begin in range(128, masked.shape[1], 128):
        total = total + masked[:, begin : begin + 128]
    return total


def rank_kernel(sides, plan, chunks, depth, last, started, *refs):
    refs = list(refs)
    rows_refs, refs = refs[: len(sides)], refs[len(sides) :]
    bounds_ref, pieces = refs[0], refs[1:]
    firsts = dict(zip(chunks, pieces))
    seconds = dict(zip(chunks, pieces[len(chunks) :]))
    rest = pieces[2 * len(chunks) :]
    outs = rest[started:]
    starts = rest[:started]
    rank, cut = pieces[0].shape
    extra = extra_rows(bounds_ref.shape[1])
    rows = {}
    for side, ref in zip(sides, rows_refs):
        if side == 0:
            offset = pl.multiple_of(lax.axis_index("groups") * depth, 128)
            rows[side] = ref[:, pl.ds(offset, depth)]
        else:
            blocks = depth // 128
            tall = (ref.shape[0] - extra) // blocks
            rows[side] = jnp.concatenate(
                [ref[i * tall : (i + 1) * tall, :] for i in range(blocks)], axis=1
            )
    count = rows[sides[0]].shape[0]
    totals = {side: ref[...] for side, ref in zip(sides, starts)}
    single = None
    for begin, end, from_chunk, to_chunk, meant in plan:
        held = [chunk if from_chunk <= chunk < to_chunk else from_chunk for chunk in range(begin, end)]
        if last and to_chunk - from_chunk == 1:
            factor = jnp.concatenate(
                [firsts[from_chunk][...], seconds[from_chunk][:, : depth - cut]], axis=1
            )
            (side,) = meant
            columns = (begin * rank, end * rank)
            low, high = other_ends(rows_refs[0], extra, *columns)
            low, high = low[:, -rank:], high[:, -rank:]
            here = jnp.transpose(contract(factor, rows[side]))
            single = jnp.where(group_mask(low, high, here.shape), here, 0.0)
            continue
        first = jnp.concatenate([firsts[chunk][...] for chunk in held], axis=0)
        second = jnp.concatenate([seconds[chunk][:, : depth - cut] for chunk in held], axis=0)
        tall = jnp.concatenate([rows[side] for side in meant], axis=0)
        part = contract(tall, jnp.concatenate([first, second], axis=1))
        for i, side in enumerate(meant):
            columns = (begin * rank, end * rank)
            if side == 0:
                ends = own_ends(bounds_ref, *columns)
            else:
                ends = other_ends(rows_refs[sides.index(1)], extra, *columns)
            here = part[i * count : (i + 1) * count]
            mask = group_mask(*ends, here.shape)
            if (from_chunk, to_chunk) != (begin, end):
                lane = lax.broadcasted_iota(I32, here.shape, 1)
                mask = mask & (lane >= (from_chunk - begin) * rank)
                mask = mask & (lane < (to_chunk - begin) * rank)
            kept = fold(jnp.where(mask, here, 0.0))
            totals[side] = totals[side] + kept if side in totals else kept
    totals = [totals[side] for side in sides]
    if last:
        (total,) = totals
        total = total + pltpu.roll(total, rank, 1)
        if single is not None:
            total = total + jnp.concatenate([single, single], axis=1)
        half = count // 2
        lane = lax.broadcasted_iota(I32, (half, 2 * rank), 1)
        total = jnp.where(lane < rank, total[:half], total[half:])
        size = outs[0].shape[0]
        totals = [total[i * size : (i + 1) * size] for i in range(len(outs))]
    for total, out_ref in zip(totals, outs):
        out_ref[...] = total.astype(out_ref.dtype)


def rank_call(sides, plan, chunks, depth, count, rows, bounds, firsts, seconds, starts, last=True):
    pieces = [firsts[chunk] for chunk in chunks] + [seconds[chunk] for chunk in chunks]
    rank = pieces[0].shape[0]
    last = last and len(starts) > 0
    if not last:
        out = (jax.ShapeDtypeStruct((count, 2 * rank), F32),) * len(sides)
    elif sides == (1,):
        out = (jax.ShapeDtypeStruct((count // 2, 2 * rank), BF16),)
    else:
        out = (jax.ShapeDtypeStruct((count // 4, 2 * rank), F32),) * 2
    operands = [*rows, bounds, *pieces, *starts]
    return pl.pallas_call(
        functools.partial(rank_kernel, sides, plan, chunks, depth, last, len(starts)),
        out_shape=out,
        in_specs=[VMEM] * len(operands),
        out_specs=(VMEM,) * len(out),
        compiler_params=params(),
        cost_estimate=HALF if last and sides == (0,) else LONG,
    )(*operands)


def final_kernel(bounds_ref, top, low, one_top, one_low, two, three, near_ref, far_ref, *refs):
    factors, out_ref = refs[:-1], refs[-1]
    rank, width = factors[0].shape[0], out_ref.shape[1]
    begin = factors[0].shape[1] - width
    here = jnp.concatenate([top[...] + one_top[...], low[...] + one_low[...]], axis=0)
    packed = here + (two[...].astype(F32) + three[...].astype(F32))
    turned = pltpu.roll(packed, rank, 1)
    lane = lax.broadcasted_iota(I32, packed.shape, 1)
    values = jnp.concatenate(
        [jnp.where(lane < rank, packed, turned), jnp.where(lane < rank, turned, packed)], axis=0
    )
    wide = jnp.concatenate([values] * (GROUP // 2), axis=1)
    total = None
    for group in range(len(factors) // GROUP):
        columns = (group * GROUP * rank, (group + 1) * GROUP * rank)
        mask = group_mask(*own_ends(bounds_ref, *columns), wide.shape)
        chosen = jnp.where(mask, wide, 0.0).astype(BF16)
        factor = jnp.concatenate(
            [ref[:, begin:] for ref in factors[group * GROUP : (group + 1) * GROUP]], axis=0
        )
        part = jnp.dot(chosen, factor, preferred_element_type=F32)
        total = part if total is None else total + part
    adapted = total.astype(BF16).astype(F32)
    out_ref[...] = ((near_ref[...] + far_ref[...]) + adapted).astype(BF16)


def per_device(hidden, demand, lengths, holder_slot, value_weight, factor_in, factor_out):
    rows, features = hidden.shape
    owners = lax.axis_size("batch")
    rank, width = factor_out.shape[1:]
    depth = features // 2
    order = ring_order(owners)
    forward = [(order[i], order[(i + 1) % owners]) for i in range(owners)]
    backward = [(b, a) for a, b in forward]
    swap = [(0, 1), (1, 0)]

    full = (owners - 1) // 2
    distances = [0]
    for step in range(1, full + 1):
        distances += [step, -step]
    distances.append(owners // 2)
    table = [
        [[order[(order.index(me) - distance) % owners] for distance in distances]]
        for me in range(owners)
    ]
    first, second, bounds = shard_call(
        factor_in[0].T, factor_out[0], demand, lengths, holder_slot, jnp.asarray(table, I32), depth
    )
    to_other, bounds = rows_call(hidden, bounds)
    bounds, first_later = lax.optimization_barrier((mark(bounds), first))

    firsts, seconds = [first], [second]
    ahead, behind = (first, second), (first_later, second)
    for step in range(1, full + 1):
        a = lax.ppermute(ahead[0], "batch", forward)
        d = lax.ppermute(behind[1], "batch", backward)
        b = lax.ppermute(ahead[1], "batch", forward)
        c = lax.ppermute(behind[0], "batch", backward)
        ahead, behind = (a, b), (c, d)
        firsts += [a, c]
        seconds += [b, d]
    firsts.append(lax.ppermute(ahead[0], "batch", forward))
    seconds.append(lax.ppermute(behind[1], "batch", backward))
    near, far = base_call(hidden, value_weight)
    hidden, near, far = lax.optimization_barrier((hidden, near, far))
    other = lax.ppermute(to_other, "groups", swap)

    before = owners - GROUP
    held = (depth, rows)
    plan = [(i, i + GROUP, i, i + GROUP, (0, 1)) for i in range(0, before, GROUP)]
    start_mine, start_theirs = rank_call(
        (0, 1), plan, range(before), *held, (hidden, other), bounds, firsts, seconds, ()
    )
    start_theirs, far = lax.optimization_barrier((start_theirs, far))
    far = lax.ppermute(far, "tensor", swap)
    plan = [(before, owners, before, owners - 1, (1,))]
    (start_theirs,) = rank_call(
        (1,), plan, range(before, owners - 1), *held, (other,), bounds, firsts, seconds, (start_theirs,), False
    )
    plan = [(owners - 2, owners, owners - 1, owners, (1,))]
    (theirs,) = rank_call(
        (1,), plan, [owners - 1], *held, (other,), bounds, firsts, seconds, (start_theirs,)
    )
    plan = [(before, owners, before, owners, (0,))]
    mine = rank_call(
        (0,), plan, range(before, owners), *held, (hidden,), bounds, firsts, seconds, (start_mine,)
    )

    two = lax.ppermute(theirs, "groups", swap)
    three = lax.ppermute(theirs, ("groups", "tensor"), [(0, 3), (1, 2), (2, 1), (3, 0)])
    one = [lax.ppermute(part, "tensor", swap) for part in mine]

    operands = [bounds, *mine, *one, two, three, near, far, *seconds]
    return pl.pallas_call(
        final_kernel,
        out_shape=jax.ShapeDtypeStruct((rows, width), BF16),
        in_specs=[VMEM] * len(operands),
        out_specs=VMEM,
        compiler_params=params(),
    )(*operands)


def solution(mesh):
    return jax.shard_map(
        per_device,
        mesh=mesh,
        in_specs=(
            P(("groups", "batch"), "tensor"),
            P(("groups", "batch"), None),
            P(("groups", "batch"), None),
            P(),
            P("tensor", None),
            P("batch", "tensor", None),
            P("batch", None, "tensor"),
        ),
        out_specs=P(("groups", "batch"), "tensor"),
        check_vma=False,
    )
```

```python
import functools

import jax
import jax.numpy as jnp
from jax import lax
from jax.experimental import pallas as pl
from jax.experimental.pallas import tpu as pltpu
from jax.sharding import PartitionSpec as P

F32, BF16, I32 = jnp.float32, jnp.bfloat16, jnp.int32
VMEM_LIMIT = 24 * 1024 * 1024
HALF = pl.CostEstimate(flops=0, bytes_accessed=1 << 22, transcendentals=0)
LONG = pl.CostEstimate(flops=1 << 33, bytes_accessed=1 << 24, transcendentals=0)
GROUP = 4
VMEM = pl.BlockSpec(memory_space=pltpu.VMEM)
HBM = pl.BlockSpec(memory_space=pltpu.HBM)
SMEM = pl.BlockSpec(memory_space=pltpu.SMEM)


def in_hbm(array):
    return pltpu.with_memory_space_constraint(array, pltpu.HBM)


def params():
    return pltpu.CompilerParams(vmem_limit_bytes=VMEM_LIMIT)


def ring_order(size):
    if size % 4:
        return list(range(size))
    columns = size // 4
    order = [0]
    for row in range(4):
        across = range(1, columns) if row % 2 == 0 else range(columns - 1, 0, -1)
        order += [row * columns + column for column in across]
    return order + [row * columns for row in (3, 2, 1)]


def contract(left, right):
    return lax.dot_general(left, right, (((1,), (1,)), ((), ())), preferred_element_type=F32)


def extra_rows(columns):
    return 2 * -(-columns // 1024) * 8


def shard_kernel(depth, factor_ref, factor_out_ref, first_ref, second_ref, sems):
    group = lax.axis_index("groups")
    cut = first_ref.shape[1]
    here = pl.multiple_of(group * depth, 128)
    after = pl.multiple_of(group * depth + cut, 128)
    copies = (
        pltpu.make_async_copy(factor_ref.at[:, pl.ds(here, cut)], first_ref, sems.at[0]),
        pltpu.make_async_copy(
            factor_ref.at[:, pl.ds(after, depth - cut)], second_ref.at[:, : depth - cut], sems.at[1]
        ),
        pltpu.make_async_copy(factor_out_ref, second_ref.at[:, depth - cut :], sems.at[2]),
    )
    for copy in copies:
        copy.start()
    for copy in copies:
        copy.wait()


def shard_call(factor, factor_out, depth):
    rank, width = factor_out.shape
    out = jax.ShapeDtypeStruct((rank, (depth + width) // 2), factor.dtype)
    return pl.pallas_call(
        functools.partial(shard_kernel, depth),
        out_shape=(out, out),
        in_specs=[HBM] * 2,
        out_specs=(VMEM,) * 2,
        scratch_shapes=[pltpu.SemaphoreType.DMA((3,))],
        compiler_params=params(),
        cost_estimate=LONG,
    )(in_hbm(factor), in_hbm(factor_out))


def row_ends(demand, lengths, holder, slots, rank):
    place = lax.axis_index("batch")
    count = slots.shape[2]
    items = demand.shape[1]
    column = lax.broadcasted_iota(I32, (1, count * rank), 1)
    zero = jnp.int32(0)

    def chunk_mask(chunk):
        return (column >= chunk * rank) & (column < (chunk + 1) * rank)

    low = high = jnp.zeros((1, count * rank), I32)
    if items * count <= 64:
        start = zero
        spans = []
        for item in range(items):
            end = start + lengths[0, item]
            spans.append((holder[demand[0, item]], start, end))
            start = end
        for chunk in range(count):
            slot = slots[place, 0, chunk]
            begin = end = zero
            for owner, first, last in spans:
                begin = jnp.where(owner == slot, first, begin)
                end = jnp.where(owner == slot, last, end)
            low = jnp.where(chunk_mask(chunk), begin, low)
            high = jnp.where(chunk_mask(chunk), end, high)
    else:

        def chunk_ends(chunk, carry):
            low, high = carry
            slot = slots[place, 0, chunk]

            def item_ends(item, state):
                start, begin, end = state
                last = start + lengths[0, item]
                hit = holder[demand[0, item]] == slot
                return last, jnp.where(hit, start, begin), jnp.where(hit, last, end)

            _, begin, end = lax.fori_loop(0, items, item_ends, (zero, zero, zero))
            mask = chunk_mask(chunk)
            return jnp.where(mask, begin, low), jnp.where(mask, end, high)

        low, high = lax.fori_loop(0, count, chunk_ends, (low, high))
    return low, high


def rows_kernel(depth, rank, hidden_ref, demand, lengths, holder, slots, to_other_ref, bounds_ref):
    rows = hidden_ref.shape[0]
    there = pl.multiple_of((1 - lax.axis_index("groups")) * depth, 128)
    for i in range(depth // 128):
        to_other_ref[i * rows : (i + 1) * rows, :] = hidden_ref[:, pl.ds(there + i * 128, 128)]
    columns = bounds_ref.shape[1]
    low, high = row_ends(demand, lengths, holder, slots, rank)
    extra = extra_rows(columns)
    line = lax.broadcasted_iota(I32, (extra, 128), 0)
    ends = jnp.zeros((extra, 128), I32)
    for i in range(columns // 128):
        span = slice(i * 128, (i + 1) * 128)
        ends = jnp.where(line == i, low[:, span], ends)
        ends = jnp.where(line == extra // 2 + i, high[:, span], ends)
    to_other_ref[-extra:, :] = ends.astype(F32).astype(BF16)
    bounds_ref[0:1, :] = low
    bounds_ref[1:2, :] = high
    bounds_ref[2:8, :] = jnp.zeros((6, columns), I32)


def rows_call(hidden, demand, lengths, holder_slot, slots, rank):
    rows, features = hidden.shape
    depth = features // 2
    columns = slots.shape[2] * rank
    tall = depth // 128 * rows + extra_rows(columns)
    return pl.pallas_call(
        functools.partial(rows_kernel, depth, rank),
        out_shape=(
            jax.ShapeDtypeStruct((tall, 128), hidden.dtype),
            jax.ShapeDtypeStruct((8, columns), I32),
        ),
        in_specs=[VMEM] + [SMEM] * 4,
        out_specs=(VMEM,) * 2,
        compiler_params=params(),
        cost_estimate=LONG,
    )(hidden, demand, lengths, holder_slot, slots)


def mark_kernel(bounds_ref, out_ref):
    out_ref[...] = bounds_ref[...]


def mark(bounds):
    return pl.pallas_call(
        mark_kernel,
        out_shape=jax.ShapeDtypeStruct(bounds.shape, bounds.dtype),
        in_specs=[VMEM],
        out_specs=VMEM,
        compiler_params=params(),
        cost_estimate=LONG,
    )(bounds)


def base_kernel(rows_ref, weight_ref, near_ref, far_ref):
    width = near_ref.shape[1]
    core = lax.axis_index("tensor")
    for out_ref, side in ((near_ref, core), (far_ref, 1 - core)):
        columns = pl.ds(pl.multiple_of(side * width, 128), width)
        out_ref[...] = jnp.dot(
            rows_ref[...], weight_ref[:, columns], preferred_element_type=F32
        )


def base_call(rows, weight):
    out = jax.ShapeDtypeStruct((rows.shape[0], weight.shape[1] // 2), F32)
    return pl.pallas_call(
        base_kernel,
        out_shape=(out, out),
        in_specs=[VMEM] * 2,
        out_specs=(VMEM,) * 2,
        compiler_params=params(),
        cost_estimate=HALF,
    )(rows, weight)


def group_mask(low, high, shape):
    row = lax.broadcasted_iota(I32, shape, 0)
    return (row >= low) & (row < high)


def own_ends(bounds_ref, group, size):
    columns = slice(group * size, (group + 1) * size)
    return bounds_ref[0:1, columns], bounds_ref[1:2, columns]


def other_ends(other_ref, extra, group, size):
    ends = other_ref[-extra:, :].astype(F32).astype(I32)
    lines = range(group * size // 128, (group + 1) * size // 128)
    low = jnp.concatenate([ends[i : i + 1] for i in lines], axis=1)
    high = jnp.concatenate([ends[extra // 2 + i : extra // 2 + i + 1] for i in lines], axis=1)
    return low, high


def fold(masked):
    total = masked[:, :128]
    for begin in range(128, masked.shape[1], 128):
        total = total + masked[:, begin : begin + 128]
    return total


def rank_kernel(sides, groups, depth, last, *refs):
    refs = list(refs)
    rows_refs, refs = refs[: len(sides)], refs[len(sides) :]
    bounds_ref, pieces = refs[0], refs[1:]
    pieces, rest = pieces[: 2 * GROUP * len(groups)], pieces[2 * GROUP * len(groups) :]
    starts, outs = (rest[: len(sides)], rest[len(sides) :]) if last else ((), rest)
    cut = pieces[0].shape[1]
    rank = pieces[0].shape[0]
    size = GROUP * rank
    extra = extra_rows(bounds_ref.shape[1])
    rows = []
    for side, ref in zip(sides, rows_refs):
        if side == 0:
            offset = pl.multiple_of(lax.axis_index("groups") * depth, 128)
            rows.append(ref[:, pl.ds(offset, depth)])
        else:
            blocks = depth // 128
            tall = (ref.shape[0] - extra) // blocks
            rows.append(
                jnp.concatenate([ref[i * tall : (i + 1) * tall, :] for i in range(blocks)], axis=1)
            )
    count = rows[0].shape[0]
    rows = jnp.concatenate(rows, axis=0)
    totals = [ref[...] for ref in starts] if last else [None] * len(sides)
    for i, group in enumerate(groups):
        held = pieces[2 * GROUP * i : 2 * GROUP * (i + 1)]
        first = jnp.concatenate([ref[...] for ref in held[:GROUP]], axis=0)
        second = jnp.concatenate([ref[:, : depth - cut] for ref in held[GROUP:]], axis=0)
        part = contract(rows, jnp.concatenate([first, second], axis=1))
        for s, side in enumerate(sides):
            if side == 0:
                ends = own_ends(bounds_ref, group, size)
            else:
                ends = other_ends(rows_refs[s], extra, group, size)
            here = part[s * count : (s + 1) * count]
            kept = fold(jnp.where(group_mask(*ends, here.shape), here, 0.0))
            totals[s] = kept if totals[s] is None else totals[s] + kept
    if last:
        (total,) = totals
        total = total + pltpu.roll(total, rank, 1)
        half = count // 2
        lane = lax.broadcasted_iota(I32, (half, 2 * rank), 1)
        total = jnp.where(lane < rank, total[:half], total[half:])
        size = outs[0].shape[0]
        totals = [total[i * size : (i + 1) * size] for i in range(len(outs))]
    for total, out_ref in zip(totals, outs):
        out_ref[...] = total.astype(out_ref.dtype)


def rank_call(sides, groups, depth, count, rows, bounds, pieces, starts):
    rank = pieces[0].shape[0]
    last = len(starts) > 0
    if not last:
        out = (jax.ShapeDtypeStruct((count, 2 * rank), F32),) * len(sides)
    elif sides == (1,):
        out = (jax.ShapeDtypeStruct((count // 2, 2 * rank), BF16),)
    else:
        out = (jax.ShapeDtypeStruct((count // 4, 2 * rank), F32),) * 2
    operands = [*rows, bounds, *pieces, *starts]
    return pl.pallas_call(
        functools.partial(rank_kernel, sides, groups, depth, last),
        out_shape=out,
        in_specs=[VMEM] * len(operands),
        out_specs=(VMEM,) * len(out),
        compiler_params=params(),
        cost_estimate=HALF if last and sides == (0,) else LONG,
    )(*operands)


def final_kernel(bounds_ref, top, low, one_top, one_low, two, three, near_ref, far_ref, *refs):
    factors, out_ref = refs[:-1], refs[-1]
    rank, width = factors[0].shape[0], out_ref.shape[1]
    begin = factors[0].shape[1] - width
    here = jnp.concatenate([top[...] + one_top[...], low[...] + one_low[...]], axis=0)
    packed = here + (two[...].astype(F32) + three[...].astype(F32))
    turned = pltpu.roll(packed, rank, 1)
    lane = lax.broadcasted_iota(I32, packed.shape, 1)
    values = jnp.concatenate(
        [jnp.where(lane < rank, packed, turned), jnp.where(lane < rank, turned, packed)], axis=0
    )
    wide = jnp.concatenate([values] * (GROUP // 2), axis=1)
    total = None
    for group in range(len(factors) // GROUP):
        mask = group_mask(*own_ends(bounds_ref, group, GROUP * rank), wide.shape)
        chosen = jnp.where(mask, wide, 0.0).astype(BF16)
        factor = jnp.concatenate(
            [ref[:, begin:] for ref in factors[group * GROUP : (group + 1) * GROUP]], axis=0
        )
        part = jnp.dot(chosen, factor, preferred_element_type=F32)
        total = part if total is None else total + part
    adapted = total.astype(BF16).astype(F32)
    out_ref[...] = ((near_ref[...] + far_ref[...]) + adapted).astype(BF16)


def per_device(hidden, demand, lengths, holder_slot, value_weight, factor_in, factor_out):
    rows, features = hidden.shape
    owners = lax.axis_size("batch")
    rank, width = factor_out.shape[1:]
    depth = features // 2
    order = ring_order(owners)
    forward = [(order[i], order[(i + 1) % owners]) for i in range(owners)]
    backward = [(b, a) for a, b in forward]
    swap = [(0, 1), (1, 0)]

    full = (owners - 1) // 2
    distances = [0]
    for step in range(1, full + 1):
        distances += [step, -step]
    distances.append(owners // 2)
    table = [
        [[order[(order.index(me) - distance) % owners] for distance in distances]]
        for me in range(owners)
    ]
    first, second = shard_call(factor_in[0].T, factor_out[0], depth)
    first, rows_here = lax.optimization_barrier((first, hidden))
    to_other, bounds = rows_call(
        rows_here, demand, lengths, holder_slot, jnp.asarray(table, I32), rank
    )
    bounds, first_later = lax.optimization_barrier((mark(bounds), first))

    firsts, seconds = [first], [second]
    ahead, behind = (first, second), (first_later, second)
    for step in range(1, full + 1):
        a = lax.ppermute(ahead[0], "batch", forward)
        d = lax.ppermute(behind[1], "batch", backward)
        b = lax.ppermute(ahead[1], "batch", forward)
        c = lax.ppermute(behind[0], "batch", backward)
        ahead, behind = (a, b), (c, d)
        firsts += [a, c]
        seconds += [b, d]
    firsts.append(lax.ppermute(ahead[0], "batch", forward))
    seconds.append(lax.ppermute(behind[1], "batch", backward))
    near, far = base_call(hidden, value_weight)
    hidden, near, far = lax.optimization_barrier((hidden, near, far))
    other = lax.ppermute(to_other, "groups", swap)

    count = owners // GROUP
    early = range(count - 1)
    pieces = []
    for group in early:
        pieces += firsts[group * GROUP : (group + 1) * GROUP]
        pieces += seconds[group * GROUP : (group + 1) * GROUP]
    both = (hidden, other)
    start_mine, start_theirs = rank_call(
        (0, 1), tuple(early), depth, rows, both, bounds, pieces, ()
    )
    start_theirs, far = lax.optimization_barrier((start_theirs, far))
    far = lax.ppermute(far, "tensor", swap)
    pieces = firsts[-GROUP:] + seconds[-GROUP:]
    late = (count - 1,)
    (theirs,) = rank_call((1,), late, depth, rows, (other,), bounds, pieces, (start_theirs,))
    mine = rank_call((0,), late, depth, rows, (hidden,), bounds, pieces, (start_mine,))

    two = lax.ppermute(theirs, "groups", swap)
    three = lax.ppermute(theirs, ("groups", "tensor"), [(0, 3), (1, 2), (2, 1), (3, 0)])
    one = [lax.ppermute(part, "tensor", swap) for part in mine]

    operands = [bounds, *mine, *one, two, three, near, far, *seconds]
    return pl.pallas_call(
        final_kernel,
        out_shape=jax.ShapeDtypeStruct((rows, width), BF16),
        in_specs=[VMEM] * len(operands),
        out_specs=VMEM,
        compiler_params=params(),
    )(*operands)


def solution(mesh):
    return jax.shard_map(
        per_device,
        mesh=mesh,
        in_specs=(
            P(("groups", "batch"), "tensor"),
            P(("groups", "batch"), None),
            P(("groups", "batch"), None),
            P(),
            P("tensor", None),
            P("batch", "tensor", None),
            P("batch", None, "tensor"),
        ),
        out_specs=P(("groups", "batch"), "tensor"),
        check_vma=False,
    )
```

```python
import functools

import jax
import jax.numpy as jnp
from jax import lax
from jax.experimental import pallas as pl
from jax.experimental.pallas import tpu as pltpu
from jax.sharding import PartitionSpec as P

F32, BF16, I32 = jnp.float32, jnp.bfloat16, jnp.int32
VMEM_LIMIT = 24 * 1024 * 1024
HALF = pl.CostEstimate(flops=0, bytes_accessed=1 << 22, transcendentals=0)
LONG = pl.CostEstimate(flops=1 << 33, bytes_accessed=1 << 24, transcendentals=0)
GROUP = 4
VMEM = pl.BlockSpec(memory_space=pltpu.VMEM)
HBM = pl.BlockSpec(memory_space=pltpu.HBM)


def in_hbm(array):
    return pltpu.with_memory_space_constraint(array, pltpu.HBM)


def params():
    return pltpu.CompilerParams(vmem_limit_bytes=VMEM_LIMIT)


def ring_order(size):
    if size % 4:
        return list(range(size))
    columns = size // 4
    order = [0]
    for row in range(4):
        across = range(1, columns) if row % 2 == 0 else range(columns - 1, 0, -1)
        order += [row * columns + column for column in across]
    return order + [row * columns for row in (3, 2, 1)]


def contract(left, right):
    return lax.dot_general(left, right, (((1,), (1,)), ((), ())), preferred_element_type=F32)


def extra_rows(columns):
    return 2 * -(-columns // 1024) * 8


def shard_kernel(
    depth,
    rank,
    factor_ref,
    factor_out_ref,
    demand_ref,
    lengths_ref,
    holder_ref,
    slots_ref,
    first_ref,
    second_ref,
    bounds_ref,
    demand,
    lengths,
    holder,
    slots,
    sems,
):
    group, place = lax.axis_index("groups"), lax.axis_index("batch")
    cut = first_ref.shape[1]
    here = pl.multiple_of(group * depth, 128)
    after = pl.multiple_of(group * depth + cut, 128)
    small = [
        pltpu.make_async_copy(demand_ref, demand, sems.at[0]),
        pltpu.make_async_copy(lengths_ref, lengths, sems.at[1]),
        pltpu.make_async_copy(holder_ref, holder, sems.at[2]),
        pltpu.make_async_copy(slots_ref.at[pl.ds(place, 1)], slots, sems.at[3]),
    ]
    large = [
        pltpu.make_async_copy(factor_ref.at[:, pl.ds(here, cut)], first_ref, sems.at[4]),
        pltpu.make_async_copy(
            factor_ref.at[:, pl.ds(after, depth - cut)], second_ref.at[:, : depth - cut], sems.at[5]
        ),
        pltpu.make_async_copy(factor_out_ref, second_ref.at[:, depth - cut :], sems.at[6]),
    ]
    for copy in small + large:
        copy.start()
    for copy in small:
        copy.wait()
    count = slots.shape[2]
    items = demand.shape[1]
    column = lax.broadcasted_iota(I32, (1, count * rank), 1)
    zero = jnp.int32(0)

    def chunk_mask(chunk):
        return (column >= chunk * rank) & (column < (chunk + 1) * rank)

    low = high = jnp.zeros((1, count * rank), I32)
    if items * count <= 64:
        start = zero
        spans = []
        for item in range(items):
            end = start + lengths[0, item]
            spans.append((holder[demand[0, item]], start, end))
            start = end
        for chunk in range(count):
            slot = slots[0, 0, chunk]
            begin = end = zero
            for owner, first, last in spans:
                begin = jnp.where(owner == slot, first, begin)
                end = jnp.where(owner == slot, last, end)
            low = jnp.where(chunk_mask(chunk), begin, low)
            high = jnp.where(chunk_mask(chunk), end, high)
    else:

        def chunk_ends(chunk, carry):
            low, high = carry
            slot = slots[0, 0, chunk]

            def item_ends(item, state):
                start, begin, end = state
                last = start + lengths[0, item]
                hit = holder[demand[0, item]] == slot
                return last, jnp.where(hit, start, begin), jnp.where(hit, last, end)

            _, begin, end = lax.fori_loop(0, items, item_ends, (zero, zero, zero))
            mask = chunk_mask(chunk)
            return jnp.where(mask, begin, low), jnp.where(mask, end, high)

        low, high = lax.fori_loop(0, count, chunk_ends, (low, high))
    bounds_ref[0:1, :] = low
    bounds_ref[1:2, :] = high
    bounds_ref[2:8, :] = jnp.zeros((6, count * rank), I32)
    for copy in large:
        copy.wait()


def shard_call(factor, factor_out, demand, lengths, holder_slot, slots, depth):
    rank, width = factor_out.shape
    cut = (depth + width) // 2
    count = slots.shape[2]
    return pl.pallas_call(
        functools.partial(shard_kernel, depth, rank),
        out_shape=(
            jax.ShapeDtypeStruct((rank, cut), factor.dtype),
            jax.ShapeDtypeStruct((rank, cut), factor.dtype),
            jax.ShapeDtypeStruct((8, count * rank), I32),
        ),
        in_specs=[HBM] * 6,
        out_specs=(VMEM,) * 3,
        scratch_shapes=[
            pltpu.SMEM(demand.shape, I32),
            pltpu.SMEM(lengths.shape, I32),
            pltpu.SMEM(holder_slot.shape, I32),
            pltpu.SMEM((1, 1, count), I32),
            pltpu.SemaphoreType.DMA((7,)),
        ],
        compiler_params=params(),
        cost_estimate=LONG,
    )(*map(in_hbm, (factor, factor_out, demand, lengths, holder_slot, slots)))


def rows_kernel(depth, hidden_ref, bounds_ref, to_other_ref, bounds_out_ref):
    rows = hidden_ref.shape[0]
    there = pl.multiple_of((1 - lax.axis_index("groups")) * depth, 128)
    for i in range(depth // 128):
        to_other_ref[i * rows : (i + 1) * rows, :] = hidden_ref[:, pl.ds(there + i * 128, 128)]
    columns = bounds_ref.shape[1]
    extra = extra_rows(columns)
    line = lax.broadcasted_iota(I32, (extra, 128), 0)
    ends = jnp.zeros((extra, 128), I32)
    for i in range(columns // 128):
        span = slice(i * 128, (i + 1) * 128)
        ends = jnp.where(line == i, bounds_ref[0:1, span], ends)
        ends = jnp.where(line == extra // 2 + i, bounds_ref[1:2, span], ends)
    to_other_ref[-extra:, :] = ends.astype(F32).astype(BF16)
    bounds_out_ref[...] = bounds_ref[...]


def rows_call(hidden, bounds):
    rows, features = hidden.shape
    depth = features // 2
    tall = depth // 128 * rows + extra_rows(bounds.shape[1])
    return pl.pallas_call(
        functools.partial(rows_kernel, depth),
        out_shape=(
            jax.ShapeDtypeStruct((tall, 128), hidden.dtype),
            jax.ShapeDtypeStruct(bounds.shape, I32),
        ),
        in_specs=[VMEM] * 2,
        out_specs=(VMEM,) * 2,
        compiler_params=params(),
        cost_estimate=LONG,
    )(hidden, bounds)


def mark_kernel(bounds_ref, out_ref):
    out_ref[...] = bounds_ref[...]


def mark(bounds):
    return pl.pallas_call(
        mark_kernel,
        out_shape=jax.ShapeDtypeStruct(bounds.shape, bounds.dtype),
        in_specs=[VMEM],
        out_specs=VMEM,
        compiler_params=params(),
        cost_estimate=LONG,
    )(bounds)


def base_kernel(rows_ref, weight_ref, near_ref, far_ref):
    width = near_ref.shape[1]
    core = lax.axis_index("tensor")
    for out_ref, side in ((near_ref, core), (far_ref, 1 - core)):
        columns = pl.ds(pl.multiple_of(side * width, 128), width)
        out_ref[...] = jnp.dot(
            rows_ref[...], weight_ref[:, columns], preferred_element_type=F32
        )


def base_call(rows, weight):
    out = jax.ShapeDtypeStruct((rows.shape[0], weight.shape[1] // 2), F32)
    return pl.pallas_call(
        base_kernel,
        out_shape=(out, out),
        in_specs=[VMEM] * 2,
        out_specs=(VMEM,) * 2,
        compiler_params=params(),
        cost_estimate=HALF,
    )(rows, weight)


def group_mask(low, high, shape):
    row = lax.broadcasted_iota(I32, shape, 0)
    return (row >= low) & (row < high)


def own_ends(bounds_ref, group, size):
    columns = slice(group * size, (group + 1) * size)
    return bounds_ref[0:1, columns], bounds_ref[1:2, columns]


def other_ends(other_ref, extra, group, size):
    ends = other_ref[-extra:, :].astype(F32).astype(I32)
    lines = range(group * size // 128, (group + 1) * size // 128)
    low = jnp.concatenate([ends[i : i + 1] for i in lines], axis=1)
    high = jnp.concatenate([ends[extra // 2 + i : extra // 2 + i + 1] for i in lines], axis=1)
    return low, high


def fold(masked):
    total = masked[:, :128]
    for begin in range(128, masked.shape[1], 128):
        total = total + masked[:, begin : begin + 128]
    return total


def rank_kernel(sides, groups, depth, last, *refs):
    refs = list(refs)
    rows_refs, refs = refs[: len(sides)], refs[len(sides) :]
    bounds_ref, pieces = refs[0], refs[1:]
    pieces, rest = pieces[: 2 * GROUP * len(groups)], pieces[2 * GROUP * len(groups) :]
    starts, outs = (rest[: len(sides)], rest[len(sides) :]) if last else ((), rest)
    cut = pieces[0].shape[1]
    rank = pieces[0].shape[0]
    size = GROUP * rank
    extra = extra_rows(bounds_ref.shape[1])
    rows = []
    for side, ref in zip(sides, rows_refs):
        if side == 0:
            offset = pl.multiple_of(lax.axis_index("groups") * depth, 128)
            rows.append(ref[:, pl.ds(offset, depth)])
        else:
            blocks = depth // 128
            tall = (ref.shape[0] - extra) // blocks
            rows.append(
                jnp.concatenate([ref[i * tall : (i + 1) * tall, :] for i in range(blocks)], axis=1)
            )
    count = rows[0].shape[0]
    rows = jnp.concatenate(rows, axis=0)
    totals = [ref[...] for ref in starts] if last else [None] * len(sides)
    for i, group in enumerate(groups):
        held = pieces[2 * GROUP * i : 2 * GROUP * (i + 1)]
        first = jnp.concatenate([ref[...] for ref in held[:GROUP]], axis=0)
        second = jnp.concatenate([ref[:, : depth - cut] for ref in held[GROUP:]], axis=0)
        part = contract(rows, jnp.concatenate([first, second], axis=1))
        for s, side in enumerate(sides):
            if side == 0:
                ends = own_ends(bounds_ref, group, size)
            else:
                ends = other_ends(rows_refs[s], extra, group, size)
            here = part[s * count : (s + 1) * count]
            kept = fold(jnp.where(group_mask(*ends, here.shape), here, 0.0))
            totals[s] = kept if totals[s] is None else totals[s] + kept
    if last:
        (total,) = totals
        total = total + pltpu.roll(total, rank, 1)
        half = count // 2
        lane = lax.broadcasted_iota(I32, (half, 2 * rank), 1)
        total = jnp.where(lane < rank, total[:half], total[half:])
        size = outs[0].shape[0]
        totals = [total[i * size : (i + 1) * size] for i in range(len(outs))]
    for total, out_ref in zip(totals, outs):
        out_ref[...] = total.astype(out_ref.dtype)


def rank_call(sides, groups, depth, count, rows, bounds, pieces, starts):
    rank = pieces[0].shape[0]
    last = len(starts) > 0
    if not last:
        out = (jax.ShapeDtypeStruct((count, 2 * rank), F32),) * len(sides)
    elif sides == (1,):
        out = (jax.ShapeDtypeStruct((count // 2, 2 * rank), BF16),)
    else:
        out = (jax.ShapeDtypeStruct((count // 4, 2 * rank), F32),) * 2
    operands = [*rows, bounds, *pieces, *starts]
    return pl.pallas_call(
        functools.partial(rank_kernel, sides, groups, depth, last),
        out_shape=out,
        in_specs=[VMEM] * len(operands),
        out_specs=(VMEM,) * len(out),
        compiler_params=params(),
        cost_estimate=HALF if last and sides == (0,) else LONG,
    )(*operands)


def final_kernel(bounds_ref, top, low, one_top, one_low, two, three, near_ref, far_ref, *refs):
    factors, out_ref = refs[:-1], refs[-1]
    rank, width = factors[0].shape[0], out_ref.shape[1]
    begin = factors[0].shape[1] - width
    here = jnp.concatenate([top[...] + one_top[...], low[...] + one_low[...]], axis=0)
    packed = here + (two[...].astype(F32) + three[...].astype(F32))
    turned = pltpu.roll(packed, rank, 1)
    lane = lax.broadcasted_iota(I32, packed.shape, 1)
    values = jnp.concatenate(
        [jnp.where(lane < rank, packed, turned), jnp.where(lane < rank, turned, packed)], axis=0
    )
    wide = jnp.concatenate([values] * (GROUP // 2), axis=1)
    total = None
    for group in range(len(factors) // GROUP):
        mask = group_mask(*own_ends(bounds_ref, group, GROUP * rank), wide.shape)
        chosen = jnp.where(mask, wide, 0.0).astype(BF16)
        factor = jnp.concatenate(
            [ref[:, begin:] for ref in factors[group * GROUP : (group + 1) * GROUP]], axis=0
        )
        part = jnp.dot(chosen, factor, preferred_element_type=F32)
        total = part if total is None else total + part
    adapted = total.astype(BF16).astype(F32)
    out_ref[...] = ((near_ref[...] + far_ref[...]) + adapted).astype(BF16)


def per_device(hidden, demand, lengths, holder_slot, value_weight, factor_in, factor_out):
    rows, features = hidden.shape
    owners = lax.axis_size("batch")
    rank, width = factor_out.shape[1:]
    depth = features // 2
    order = ring_order(owners)
    forward = [(order[i], order[(i + 1) % owners]) for i in range(owners)]
    backward = [(b, a) for a, b in forward]
    swap = [(0, 1), (1, 0)]

    full = (owners - 1) // 2
    distances = [0]
    for step in range(1, full + 1):
        distances += [step, -step]
    distances.append(owners // 2)
    table = [
        [[order[(order.index(me) - distance) % owners] for distance in distances]]
        for me in range(owners)
    ]
    first, second, bounds = shard_call(
        factor_in[0].T, factor_out[0], demand, lengths, holder_slot, jnp.asarray(table, I32), depth
    )
    to_other, bounds = rows_call(hidden, bounds)
    to_other, first = lax.optimization_barrier((to_other, first))
    bounds, first_later = lax.optimization_barrier((mark(bounds), first))

    firsts, seconds = [first], [second]
    ahead, behind = (first, second), (first_later, second)
    for step in range(1, full + 1):
        a = lax.ppermute(ahead[0], "batch", forward)
        d = lax.ppermute(behind[1], "batch", backward)
        b = lax.ppermute(ahead[1], "batch", forward)
        c = lax.ppermute(behind[0], "batch", backward)
        ahead, behind = (a, b), (c, d)
        firsts += [a, c]
        seconds += [b, d]
    firsts.append(lax.ppermute(ahead[0], "batch", forward))
    seconds.append(lax.ppermute(behind[1], "batch", backward))
    near, far = base_call(hidden, value_weight)
    hidden, near, far = lax.optimization_barrier((hidden, near, far))
    other = lax.ppermute(to_other, "groups", swap)

    count = owners // GROUP
    early = range(count - 1)
    pieces = []
    for group in early:
        pieces += firsts[group * GROUP : (group + 1) * GROUP]
        pieces += seconds[group * GROUP : (group + 1) * GROUP]
    both = (hidden, other)
    start_mine, start_theirs = rank_call(
        (0, 1), tuple(early), depth, rows, both, bounds, pieces, ()
    )
    start_theirs, far = lax.optimization_barrier((start_theirs, far))
    far = lax.ppermute(far, "tensor", swap)
    pieces = firsts[-GROUP:] + seconds[-GROUP:]
    late = (count - 1,)
    (theirs,) = rank_call((1,), late, depth, rows, (other,), bounds, pieces, (start_theirs,))
    mine = rank_call((0,), late, depth, rows, (hidden,), bounds, pieces, (start_mine,))

    two = lax.ppermute(theirs, "groups", swap)
    three = lax.ppermute(theirs, ("groups", "tensor"), [(0, 3), (1, 2), (2, 1), (3, 0)])
    one = [lax.ppermute(part, "tensor", swap) for part in mine]

    operands = [bounds, *mine, *one, two, three, near, far, *seconds]
    return pl.pallas_call(
        final_kernel,
        out_shape=jax.ShapeDtypeStruct((rows, width), BF16),
        in_specs=[VMEM] * len(operands),
        out_specs=VMEM,
        compiler_params=params(),
    )(*operands)


def solution(mesh):
    return jax.shard_map(
        per_device,
        mesh=mesh,
        in_specs=(
            P(("groups", "batch"), "tensor"),
            P(("groups", "batch"), None),
            P(("groups", "batch"), None),
            P(),
            P("tensor", None),
            P("batch", "tensor", None),
            P("batch", None, "tensor"),
        ),
        out_specs=P(("groups", "batch"), "tensor"),
        check_vma=False,
    )
```

```python
import functools

import jax
import jax.numpy as jnp
from jax import lax
from jax.experimental import pallas as pl
from jax.experimental.pallas import tpu as pltpu
from jax.sharding import PartitionSpec as P

F32, BF16, I32 = jnp.float32, jnp.bfloat16, jnp.int32
VMEM_LIMIT = 24 * 1024 * 1024
HALF = pl.CostEstimate(flops=0, bytes_accessed=1 << 22, transcendentals=0)
LONG = pl.CostEstimate(flops=1 << 33, bytes_accessed=1 << 24, transcendentals=0)
GROUP = 4
VMEM = pl.BlockSpec(memory_space=pltpu.VMEM)
HBM = pl.BlockSpec(memory_space=pltpu.HBM)


def in_hbm(array):
    return pltpu.with_memory_space_constraint(array, pltpu.HBM)


def params():
    return pltpu.CompilerParams(vmem_limit_bytes=VMEM_LIMIT)


def ring_order(size):
    if size % 4:
        return list(range(size))
    columns = size // 4
    order = [0]
    for row in range(4):
        across = range(1, columns) if row % 2 == 0 else range(columns - 1, 0, -1)
        order += [row * columns + column for column in across]
    return order + [row * columns for row in (3, 2, 1)]


def contract(left, right):
    return lax.dot_general(left, right, (((1,), (1,)), ((), ())), preferred_element_type=F32)


def extra_rows(columns):
    return 2 * -(-columns // 1024) * 8


def shard_kernel(
    depth,
    rank,
    factor_ref,
    factor_out_ref,
    demand_ref,
    lengths_ref,
    holder_ref,
    slots_ref,
    first_ref,
    second_ref,
    bounds_ref,
    demand,
    lengths,
    holder,
    slots,
    sems,
):
    group, place = lax.axis_index("groups"), lax.axis_index("batch")
    cut = first_ref.shape[1]
    here = pl.multiple_of(group * depth, 128)
    after = pl.multiple_of(group * depth + cut, 128)
    small = [
        pltpu.make_async_copy(demand_ref, demand, sems.at[0]),
        pltpu.make_async_copy(lengths_ref, lengths, sems.at[1]),
        pltpu.make_async_copy(holder_ref, holder, sems.at[2]),
        pltpu.make_async_copy(slots_ref.at[pl.ds(place, 1)], slots, sems.at[3]),
    ]
    large = [
        pltpu.make_async_copy(factor_ref.at[:, pl.ds(here, cut)], first_ref, sems.at[4]),
        pltpu.make_async_copy(
            factor_ref.at[:, pl.ds(after, depth - cut)], second_ref.at[:, : depth - cut], sems.at[5]
        ),
        pltpu.make_async_copy(factor_out_ref, second_ref.at[:, depth - cut :], sems.at[6]),
    ]
    for copy in small + large:
        copy.start()
    for copy in small:
        copy.wait()
    count = slots.shape[2]
    items = demand.shape[1]
    column = lax.broadcasted_iota(I32, (1, count * rank), 1)
    zero = jnp.int32(0)

    def chunk_mask(chunk):
        return (column >= chunk * rank) & (column < (chunk + 1) * rank)

    low = high = jnp.zeros((1, count * rank), I32)
    if items * count <= 64:
        start = zero
        spans = []
        for item in range(items):
            end = start + lengths[0, item]
            spans.append((holder[demand[0, item]], start, end))
            start = end
        for chunk in range(count):
            slot = slots[0, 0, chunk]
            begin = end = zero
            for owner, first, last in spans:
                begin = jnp.where(owner == slot, first, begin)
                end = jnp.where(owner == slot, last, end)
            low = jnp.where(chunk_mask(chunk), begin, low)
            high = jnp.where(chunk_mask(chunk), end, high)
    else:

        def chunk_ends(chunk, carry):
            low, high = carry
            slot = slots[0, 0, chunk]

            def item_ends(item, state):
                start, begin, end = state
                last = start + lengths[0, item]
                hit = holder[demand[0, item]] == slot
                return last, jnp.where(hit, start, begin), jnp.where(hit, last, end)

            _, begin, end = lax.fori_loop(0, items, item_ends, (zero, zero, zero))
            mask = chunk_mask(chunk)
            return jnp.where(mask, begin, low), jnp.where(mask, end, high)

        low, high = lax.fori_loop(0, count, chunk_ends, (low, high))
    bounds_ref[0:1, :] = low
    bounds_ref[1:2, :] = high
    bounds_ref[2:8, :] = jnp.zeros((6, count * rank), I32)
    for copy in large:
        copy.wait()


def shard_call(factor, factor_out, demand, lengths, holder_slot, slots, depth):
    rank, width = factor_out.shape
    cut = (depth + width) // 2
    count = slots.shape[2]
    return pl.pallas_call(
        functools.partial(shard_kernel, depth, rank),
        out_shape=(
            jax.ShapeDtypeStruct((rank, cut), factor.dtype),
            jax.ShapeDtypeStruct((rank, cut), factor.dtype),
            jax.ShapeDtypeStruct((8, count * rank), I32),
        ),
        in_specs=[HBM] * 6,
        out_specs=(VMEM,) * 3,
        scratch_shapes=[
            pltpu.SMEM(demand.shape, I32),
            pltpu.SMEM(lengths.shape, I32),
            pltpu.SMEM(holder_slot.shape, I32),
            pltpu.SMEM((1, 1, count), I32),
            pltpu.SemaphoreType.DMA((7,)),
        ],
        compiler_params=params(),
        cost_estimate=LONG,
    )(*map(in_hbm, (factor, factor_out, demand, lengths, holder_slot, slots)))


def rows_kernel(depth, hidden_ref, bounds_ref, to_other_ref, bounds_out_ref):
    rows = hidden_ref.shape[0]
    there = pl.multiple_of((1 - lax.axis_index("groups")) * depth, 128)
    for i in range(depth // 128):
        to_other_ref[i * rows : (i + 1) * rows, :] = hidden_ref[:, pl.ds(there + i * 128, 128)]
    columns = bounds_ref.shape[1]
    extra = extra_rows(columns)
    line = lax.broadcasted_iota(I32, (extra, 128), 0)
    ends = jnp.zeros((extra, 128), I32)
    for i in range(columns // 128):
        span = slice(i * 128, (i + 1) * 128)
        ends = jnp.where(line == i, bounds_ref[0:1, span], ends)
        ends = jnp.where(line == extra // 2 + i, bounds_ref[1:2, span], ends)
    to_other_ref[-extra:, :] = ends.astype(F32).astype(BF16)
    bounds_out_ref[...] = bounds_ref[...]


def rows_call(hidden, bounds):
    rows, features = hidden.shape
    depth = features // 2
    tall = depth // 128 * rows + extra_rows(bounds.shape[1])
    return pl.pallas_call(
        functools.partial(rows_kernel, depth),
        out_shape=(
            jax.ShapeDtypeStruct((tall, 128), hidden.dtype),
            jax.ShapeDtypeStruct(bounds.shape, I32),
        ),
        in_specs=[VMEM] * 2,
        out_specs=(VMEM,) * 2,
        compiler_params=params(),
        cost_estimate=LONG,
    )(hidden, bounds)


def mark_kernel(bounds_ref, out_ref):
    out_ref[...] = bounds_ref[...]


def mark(bounds):
    return pl.pallas_call(
        mark_kernel,
        out_shape=jax.ShapeDtypeStruct(bounds.shape, bounds.dtype),
        in_specs=[VMEM],
        out_specs=VMEM,
        compiler_params=params(),
        cost_estimate=LONG,
    )(bounds)


def base_kernel(size, rows_ref, weight_ref, bounds_ref, near_ref, far_ref, mask_ref):
    width = near_ref.shape[1]
    core = lax.axis_index("tensor")
    for out_ref, side in ((near_ref, core), (far_ref, 1 - core)):
        columns = pl.ds(pl.multiple_of(side * width, 128), width)
        out_ref[...] = jnp.dot(
            rows_ref[...], weight_ref[:, columns], preferred_element_type=F32
        )
    for group in range(mask_ref.shape[1] // size):
        mask = group_mask(*own_ends(bounds_ref, group, size), (rows_ref.shape[0], size))
        mask_ref[:, group * size : (group + 1) * size] = jnp.where(mask, 1.0, 0.0).astype(BF16)


def base_call(rows, weight, bounds, size):
    mask = jax.ShapeDtypeStruct((rows.shape[0], bounds.shape[1]), BF16)
    out = jax.ShapeDtypeStruct((rows.shape[0], weight.shape[1] // 2), F32)
    return pl.pallas_call(
        functools.partial(base_kernel, size),
        out_shape=(out, out, mask),
        in_specs=[VMEM] * 3,
        out_specs=(VMEM,) * 3,
        compiler_params=params(),
        cost_estimate=HALF,
    )(rows, weight, bounds)


def group_mask(low, high, shape):
    row = lax.broadcasted_iota(I32, shape, 0)
    return (row >= low) & (row < high)


def own_ends(bounds_ref, group, size):
    columns = slice(group * size, (group + 1) * size)
    return bounds_ref[0:1, columns], bounds_ref[1:2, columns]


def other_ends(other_ref, extra, group, size):
    ends = other_ref[-extra:, :].astype(F32).astype(I32)
    lines = range(group * size // 128, (group + 1) * size // 128)
    low = jnp.concatenate([ends[i : i + 1] for i in lines], axis=1)
    high = jnp.concatenate([ends[extra // 2 + i : extra // 2 + i + 1] for i in lines], axis=1)
    return low, high


def fold(masked):
    total = masked[:, :128]
    for begin in range(128, masked.shape[1], 128):
        total = total + masked[:, begin : begin + 128]
    return total


def rank_kernel(sides, groups, depth, last, *refs):
    refs = list(refs)
    rows_refs, refs = refs[: len(sides)], refs[len(sides) :]
    bounds_ref, pieces = refs[0], refs[1:]
    pieces, rest = pieces[: 2 * GROUP * len(groups)], pieces[2 * GROUP * len(groups) :]
    starts, outs = (rest[: len(sides)], rest[len(sides) :]) if last else ((), rest)
    cut = pieces[0].shape[1]
    rank = pieces[0].shape[0]
    size = GROUP * rank
    extra = extra_rows(bounds_ref.shape[1])
    rows = []
    for side, ref in zip(sides, rows_refs):
        if side == 0:
            offset = pl.multiple_of(lax.axis_index("groups") * depth, 128)
            rows.append(ref[:, pl.ds(offset, depth)])
        else:
            blocks = depth // 128
            tall = (ref.shape[0] - extra) // blocks
            rows.append(
                jnp.concatenate([ref[i * tall : (i + 1) * tall, :] for i in range(blocks)], axis=1)
            )
    count = rows[0].shape[0]
    rows = jnp.concatenate(rows, axis=0)
    totals = [ref[...] for ref in starts] if last else [None] * len(sides)
    for i, group in enumerate(groups):
        held = pieces[2 * GROUP * i : 2 * GROUP * (i + 1)]
        first = jnp.concatenate([ref[...] for ref in held[:GROUP]], axis=0)
        second = jnp.concatenate([ref[:, : depth - cut] for ref in held[GROUP:]], axis=0)
        part = contract(rows, jnp.concatenate([first, second], axis=1))
        for s, side in enumerate(sides):
            if side == 0:
                ends = own_ends(bounds_ref, group, size)
            else:
                ends = other_ends(rows_refs[s], extra, group, size)
            here = part[s * count : (s + 1) * count]
            kept = fold(jnp.where(group_mask(*ends, here.shape), here, 0.0))
            totals[s] = kept if totals[s] is None else totals[s] + kept
    if last:
        (total,) = totals
        total = total + pltpu.roll(total, rank, 1)
        half = count // 2
        lane = lax.broadcasted_iota(I32, (half, 2 * rank), 1)
        total = jnp.where(lane < rank, total[:half], total[half:])
        size = outs[0].shape[0]
        totals = [total[i * size : (i + 1) * size] for i in range(len(outs))]
    for total, out_ref in zip(totals, outs):
        out_ref[...] = total.astype(out_ref.dtype)


def rank_call(sides, groups, depth, count, rows, bounds, pieces, starts):
    rank = pieces[0].shape[0]
    last = len(starts) > 0
    if not last:
        out = (jax.ShapeDtypeStruct((count, 2 * rank), F32),) * len(sides)
    elif sides == (1,):
        out = (jax.ShapeDtypeStruct((count // 2, 2 * rank), BF16),)
    else:
        out = (jax.ShapeDtypeStruct((count // 4, 2 * rank), F32),) * 2
    operands = [*rows, bounds, *pieces, *starts]
    return pl.pallas_call(
        functools.partial(rank_kernel, sides, groups, depth, last),
        out_shape=out,
        in_specs=[VMEM] * len(operands),
        out_specs=(VMEM,) * len(out),
        compiler_params=params(),
        cost_estimate=HALF if last and sides == (0,) else LONG,
    )(*operands)


def final_kernel(mask_ref, top, low, one_top, one_low, three, two, near_ref, far_ref, *refs):
    factors, out_ref = refs[:-1], refs[-1]
    rank, width = factors[0].shape[0], out_ref.shape[1]
    begin = factors[0].shape[1] - width
    here = jnp.concatenate([top[...] + one_top[...], low[...] + one_low[...]], axis=0)
    packed = here + (two[...].astype(F32) + three[...].astype(F32))
    turned = pltpu.roll(packed, rank, 1)
    lane = lax.broadcasted_iota(I32, packed.shape, 1)
    values = jnp.concatenate(
        [jnp.where(lane < rank, packed, turned), jnp.where(lane < rank, turned, packed)], axis=0
    )
    wide = jnp.concatenate([values.astype(BF16)] * (GROUP // 2), axis=1)
    total = None
    for group in range(len(factors) // GROUP):
        chosen = wide * mask_ref[:, group * GROUP * rank : (group + 1) * GROUP * rank]
        factor = jnp.concatenate(
            [ref[:, begin:] for ref in factors[group * GROUP : (group + 1) * GROUP]], axis=0
        )
        part = jnp.dot(chosen, factor, preferred_element_type=F32)
        total = part if total is None else total + part
    adapted = total.astype(BF16).astype(F32)
    out_ref[...] = ((near_ref[...] + far_ref[...]) + adapted).astype(BF16)


def per_device(hidden, demand, lengths, holder_slot, value_weight, factor_in, factor_out):
    rows, features = hidden.shape
    owners = lax.axis_size("batch")
    rank, width = factor_out.shape[1:]
    depth = features // 2
    order = ring_order(owners)
    forward = [(order[i], order[(i + 1) % owners]) for i in range(owners)]
    backward = [(b, a) for a, b in forward]
    swap = [(0, 1), (1, 0)]

    full = (owners - 1) // 2
    distances = [0]
    for step in range(1, full + 1):
        distances += [step, -step]
    distances.append(owners // 2)
    table = [
        [[order[(order.index(me) - distance) % owners] for distance in distances]]
        for me in range(owners)
    ]
    first, second, bounds = shard_call(
        factor_in[0].T, factor_out[0], demand, lengths, holder_slot, jnp.asarray(table, I32), depth
    )
    to_other, bounds = rows_call(hidden, bounds)
    bounds, first_later = lax.optimization_barrier((mark(bounds), first))

    firsts, seconds = [first], [second]
    ahead, behind = (first, second), (first_later, second)
    for step in range(1, full + 1):
        a = lax.ppermute(ahead[0], "batch", forward)
        d = lax.ppermute(behind[1], "batch", backward)
        b = lax.ppermute(ahead[1], "batch", forward)
        c = lax.ppermute(behind[0], "batch", backward)
        ahead, behind = (a, b), (c, d)
        firsts += [a, c]
        seconds += [b, d]
    firsts.append(lax.ppermute(ahead[0], "batch", forward))
    seconds.append(lax.ppermute(behind[1], "batch", backward))
    near, far, mask = base_call(hidden, value_weight, bounds, GROUP * rank)
    hidden, near, far = lax.optimization_barrier((hidden, near, far))
    other = lax.ppermute(to_other, "groups", swap)

    count = owners // GROUP
    early = range(count - 1)
    pieces = []
    for group in early:
        pieces += firsts[group * GROUP : (group + 1) * GROUP]
        pieces += seconds[group * GROUP : (group + 1) * GROUP]
    both = (hidden, other)
    start_mine, start_theirs = rank_call(
        (0, 1), tuple(early), depth, rows, both, bounds, pieces, ()
    )
    start_theirs, far = lax.optimization_barrier((start_theirs, far))
    far = lax.ppermute(far, "tensor", swap)
    pieces = firsts[-GROUP:] + seconds[-GROUP:]
    late = (count - 1,)
    (theirs,) = rank_call((1,), late, depth, rows, (other,), bounds, pieces, (start_theirs,))
    mine = rank_call((0,), late, depth, rows, (hidden,), bounds, pieces, (start_mine,))

    three = lax.ppermute(theirs, ("groups", "tensor"), [(0, 3), (1, 2), (2, 1), (3, 0)])
    two = lax.ppermute(theirs, "groups", swap)
    one = [lax.ppermute(part, "tensor", swap) for part in mine]

    operands = [mask, *mine, *one, three, two, near, far, *seconds]
    return pl.pallas_call(
        final_kernel,
        out_shape=jax.ShapeDtypeStruct((rows, width), BF16),
        in_specs=[VMEM] * len(operands),
        out_specs=VMEM,
        compiler_params=params(),
    )(*operands)


def solution(mesh):
    return jax.shard_map(
        per_device,
        mesh=mesh,
        in_specs=(
            P(("groups", "batch"), "tensor"),
            P(("groups", "batch"), None),
            P(("groups", "batch"), None),
            P(),
            P("tensor", None),
            P("batch", "tensor", None),
            P("batch", None, "tensor"),
        ),
        out_specs=P(("groups", "batch"), "tensor"),
        check_vma=False,
    )
```

```python
import functools

import jax
import jax.numpy as jnp
from jax import lax
from jax.experimental import pallas as pl
from jax.experimental.pallas import tpu as pltpu
from jax.sharding import PartitionSpec as P

F32, BF16, I32 = jnp.float32, jnp.bfloat16, jnp.int32
VMEM_LIMIT = 24 * 1024 * 1024
HALF = pl.CostEstimate(flops=0, bytes_accessed=1 << 22, transcendentals=0)
LONG = pl.CostEstimate(flops=1 << 33, bytes_accessed=1 << 24, transcendentals=0)
GROUP = 4
VMEM = pl.BlockSpec(memory_space=pltpu.VMEM)
HBM = pl.BlockSpec(memory_space=pltpu.HBM)


def in_hbm(array):
    return pltpu.with_memory_space_constraint(array, pltpu.HBM)


def params():
    return pltpu.CompilerParams(vmem_limit_bytes=VMEM_LIMIT)


def ring_order(size):
    if size % 4:
        return list(range(size))
    columns = size // 4
    order = [0]
    for row in range(4):
        across = range(1, columns) if row % 2 == 0 else range(columns - 1, 0, -1)
        order += [row * columns + column for column in across]
    return order + [row * columns for row in (3, 2, 1)]


def contract(left, right):
    return lax.dot_general(left, right, (((1,), (1,)), ((), ())), preferred_element_type=F32)


def extra_rows(columns):
    return 2 * -(-columns // 1024) * 8


def shard_kernel(
    depth,
    rank,
    factor_ref,
    factor_out_ref,
    demand_ref,
    lengths_ref,
    holder_ref,
    slots_ref,
    first_ref,
    second_ref,
    bounds_ref,
    demand,
    lengths,
    holder,
    slots,
    sems,
):
    group, place = lax.axis_index("groups"), lax.axis_index("batch")
    cut = first_ref.shape[1]
    here = pl.multiple_of(group * depth, 128)
    after = pl.multiple_of(group * depth + cut, 128)
    small = [
        pltpu.make_async_copy(demand_ref, demand, sems.at[0]),
        pltpu.make_async_copy(lengths_ref, lengths, sems.at[1]),
        pltpu.make_async_copy(holder_ref, holder, sems.at[2]),
        pltpu.make_async_copy(slots_ref.at[pl.ds(place, 1)], slots, sems.at[3]),
    ]
    large = [
        pltpu.make_async_copy(factor_ref.at[:, pl.ds(here, cut)], first_ref, sems.at[4]),
        pltpu.make_async_copy(
            factor_ref.at[:, pl.ds(after, depth - cut)], second_ref.at[:, : depth - cut], sems.at[5]
        ),
        pltpu.make_async_copy(factor_out_ref, second_ref.at[:, depth - cut :], sems.at[6]),
    ]
    for copy in small + large:
        copy.start()
    for copy in small:
        copy.wait()
    count = slots.shape[2]
    items = demand.shape[1]
    column = lax.broadcasted_iota(I32, (1, count * rank), 1)
    zero = jnp.int32(0)

    def chunk_mask(chunk):
        return (column >= chunk * rank) & (column < (chunk + 1) * rank)

    low = high = jnp.zeros((1, count * rank), I32)
    if items * count <= 64:
        start = zero
        spans = []
        for item in range(items):
            end = start + lengths[0, item]
            spans.append((holder[demand[0, item]], start, end))
            start = end
        for chunk in range(count):
            slot = slots[0, 0, chunk]
            begin = end = zero
            for owner, first, last in spans:
                begin = jnp.where(owner == slot, first, begin)
                end = jnp.where(owner == slot, last, end)
            low = jnp.where(chunk_mask(chunk), begin, low)
            high = jnp.where(chunk_mask(chunk), end, high)
    else:

        def chunk_ends(chunk, carry):
            low, high = carry
            slot = slots[0, 0, chunk]

            def item_ends(item, state):
                start, begin, end = state
                last = start + lengths[0, item]
                hit = holder[demand[0, item]] == slot
                return last, jnp.where(hit, start, begin), jnp.where(hit, last, end)

            _, begin, end = lax.fori_loop(0, items, item_ends, (zero, zero, zero))
            mask = chunk_mask(chunk)
            return jnp.where(mask, begin, low), jnp.where(mask, end, high)

        low, high = lax.fori_loop(0, count, chunk_ends, (low, high))
    bounds_ref[0:1, :] = low
    bounds_ref[1:2, :] = high
    bounds_ref[2:8, :] = jnp.zeros((6, count * rank), I32)
    for copy in large:
        copy.wait()


def shard_call(factor, factor_out, demand, lengths, holder_slot, slots, depth):
    rank, width = factor_out.shape
    cut = (depth + width) // 2
    count = slots.shape[2]
    return pl.pallas_call(
        functools.partial(shard_kernel, depth, rank),
        out_shape=(
            jax.ShapeDtypeStruct((rank, cut), factor.dtype),
            jax.ShapeDtypeStruct((rank, cut), factor.dtype),
            jax.ShapeDtypeStruct((8, count * rank), I32),
        ),
        in_specs=[HBM] * 6,
        out_specs=(VMEM,) * 3,
        scratch_shapes=[
            pltpu.SMEM(demand.shape, I32),
            pltpu.SMEM(lengths.shape, I32),
            pltpu.SMEM(holder_slot.shape, I32),
            pltpu.SMEM((1, 1, count), I32),
            pltpu.SemaphoreType.DMA((7,)),
        ],
        compiler_params=params(),
        cost_estimate=LONG,
    )(*map(in_hbm, (factor, factor_out, demand, lengths, holder_slot, slots)))


def rows_kernel(depth, hidden_ref, bounds_ref, to_other_ref, bounds_out_ref):
    rows = hidden_ref.shape[0]
    there = pl.multiple_of((1 - lax.axis_index("groups")) * depth, 128)
    for i in range(depth // 128):
        to_other_ref[i * rows : (i + 1) * rows, :] = hidden_ref[:, pl.ds(there + i * 128, 128)]
    columns = bounds_ref.shape[1]
    extra = extra_rows(columns)
    line = lax.broadcasted_iota(I32, (extra, 128), 0)
    ends = jnp.zeros((extra, 128), I32)
    for i in range(columns // 128):
        span = slice(i * 128, (i + 1) * 128)
        ends = jnp.where(line == i, bounds_ref[0:1, span], ends)
        ends = jnp.where(line == extra // 2 + i, bounds_ref[1:2, span], ends)
    to_other_ref[-extra:, :] = ends.astype(F32).astype(BF16)
    bounds_out_ref[...] = bounds_ref[...]


def rows_call(hidden, bounds):
    rows, features = hidden.shape
    depth = features // 2
    tall = depth // 128 * rows + extra_rows(bounds.shape[1])
    return pl.pallas_call(
        functools.partial(rows_kernel, depth),
        out_shape=(
            jax.ShapeDtypeStruct((tall, 128), hidden.dtype),
            jax.ShapeDtypeStruct(bounds.shape, I32),
        ),
        in_specs=[VMEM] * 2,
        out_specs=(VMEM,) * 2,
        compiler_params=params(),
        cost_estimate=LONG,
    )(hidden, bounds)


def mark_kernel(bounds_ref, out_ref):
    out_ref[...] = bounds_ref[...]


def mark(bounds):
    return pl.pallas_call(
        mark_kernel,
        out_shape=jax.ShapeDtypeStruct(bounds.shape, bounds.dtype),
        in_specs=[VMEM],
        out_specs=VMEM,
        compiler_params=params(),
        cost_estimate=LONG,
    )(bounds)


def base_kernel(size, rows_ref, weight_ref, bounds_ref, near_ref, far_ref, mask_ref):
    width = near_ref.shape[1]
    core = lax.axis_index("tensor")
    for out_ref, side in ((near_ref, core), (far_ref, 1 - core)):
        columns = pl.ds(pl.multiple_of(side * width, 128), width)
        out_ref[...] = jnp.dot(
            rows_ref[...], weight_ref[:, columns], preferred_element_type=F32
        )
    for group in range(mask_ref.shape[1] // size):
        mask = group_mask(*own_ends(bounds_ref, group, size), (rows_ref.shape[0], size))
        mask_ref[:, group * size : (group + 1) * size] = jnp.where(mask, 1.0, 0.0).astype(BF16)


def base_call(rows, weight, bounds, size):
    mask = jax.ShapeDtypeStruct((rows.shape[0], bounds.shape[1]), BF16)
    out = jax.ShapeDtypeStruct((rows.shape[0], weight.shape[1] // 2), F32)
    return pl.pallas_call(
        functools.partial(base_kernel, size),
        out_shape=(out, out, mask),
        in_specs=[VMEM] * 3,
        out_specs=(VMEM,) * 3,
        compiler_params=params(),
        cost_estimate=HALF,
    )(rows, weight, bounds)


def group_mask(low, high, shape):
    row = lax.broadcasted_iota(I32, shape, 0)
    return (row >= low) & (row < high)


def own_ends(bounds_ref, group, size):
    columns = slice(group * size, (group + 1) * size)
    return bounds_ref[0:1, columns], bounds_ref[1:2, columns]


def other_ends(other_ref, extra, group, size):
    ends = other_ref[-extra:, :].astype(F32).astype(I32)
    lines = range(group * size // 128, (group + 1) * size // 128)
    low = jnp.concatenate([ends[i : i + 1] for i in lines], axis=1)
    high = jnp.concatenate([ends[extra // 2 + i : extra // 2 + i + 1] for i in lines], axis=1)
    return low, high


def fold(masked):
    total = masked[:, :128]
    for begin in range(128, masked.shape[1], 128):
        total = total + masked[:, begin : begin + 128]
    return total


def rank_kernel(sides, groups, depth, last, *refs):
    refs = list(refs)
    rows_refs, refs = refs[: len(sides)], refs[len(sides) :]
    bounds_ref, pieces = refs[0], refs[1:]
    pieces, rest = pieces[: 2 * GROUP * len(groups)], pieces[2 * GROUP * len(groups) :]
    starts, outs = (rest[: len(sides)], rest[len(sides) :]) if last else ((), rest)
    cut = pieces[0].shape[1]
    rank = pieces[0].shape[0]
    size = GROUP * rank
    extra = extra_rows(bounds_ref.shape[1])
    rows = []
    for side, ref in zip(sides, rows_refs):
        if side == 0:
            offset = pl.multiple_of(lax.axis_index("groups") * depth, 128)
            rows.append(ref[:, pl.ds(offset, depth)])
        else:
            blocks = depth // 128
            tall = (ref.shape[0] - extra) // blocks
            rows.append(
                jnp.concatenate([ref[i * tall : (i + 1) * tall, :] for i in range(blocks)], axis=1)
            )
    count = rows[0].shape[0]
    rows = jnp.concatenate(rows, axis=0)
    totals = [ref[...] for ref in starts] if last else [None] * len(sides)
    for i, group in enumerate(groups):
        held = pieces[2 * GROUP * i : 2 * GROUP * (i + 1)]
        first = jnp.concatenate([ref[...] for ref in held[:GROUP]], axis=0)
        second = jnp.concatenate([ref[:, : depth - cut] for ref in held[GROUP:]], axis=0)
        part = contract(rows, jnp.concatenate([first, second], axis=1))
        for s, side in enumerate(sides):
            if side == 0:
                ends = own_ends(bounds_ref, group, size)
            else:
                ends = other_ends(rows_refs[s], extra, group, size)
            here = part[s * count : (s + 1) * count]
            kept = fold(jnp.where(group_mask(*ends, here.shape), here, 0.0))
            totals[s] = kept if totals[s] is None else totals[s] + kept
    if last:
        (total,) = totals
        total = total + pltpu.roll(total, rank, 1)
        half = count // 2
        lane = lax.broadcasted_iota(I32, (half, 2 * rank), 1)
        total = jnp.where(lane < rank, total[:half], total[half:])
        size = outs[0].shape[0]
        totals = [total[i * size : (i + 1) * size] for i in range(len(outs))]
    for total, out_ref in zip(totals, outs):
        out_ref[...] = total.astype(out_ref.dtype)


def rank_call(sides, groups, depth, count, rows, bounds, pieces, starts):
    rank = pieces[0].shape[0]
    last = len(starts) > 0
    if not last:
        out = (jax.ShapeDtypeStruct((count, 2 * rank), F32),) * len(sides)
    elif sides == (1,):
        out = (jax.ShapeDtypeStruct((count // 2, 2 * rank), BF16),)
    else:
        out = (jax.ShapeDtypeStruct((count // 4, 2 * rank), F32),) * 2
    operands = [*rows, bounds, *pieces, *starts]
    return pl.pallas_call(
        functools.partial(rank_kernel, sides, groups, depth, last),
        out_shape=out,
        in_specs=[VMEM] * len(operands),
        out_specs=(VMEM,) * len(out),
        compiler_params=params(),
        cost_estimate=HALF if last and sides == (0,) else LONG,
    )(*operands)


def final_kernel(mask_ref, top, low, one_top, one_low, three, two, near_ref, far_ref, *refs):
    factors, (out_ref, done, sems) = refs[:-3], refs[-3:]
    rank, width = factors[0].shape[0], out_ref.shape[1]
    begin = factors[0].shape[1] - width
    here = jnp.concatenate([top[...] + one_top[...], low[...] + one_low[...]], axis=0)
    packed = here + (two[...].astype(F32) + three[...].astype(F32))
    turned = pltpu.roll(packed, rank, 1)
    lane = lax.broadcasted_iota(I32, packed.shape, 1)
    factor = jnp.concatenate([ref[:, begin:] for ref in factors], axis=0)
    half = packed.shape[0]
    copies = []
    for i in (0, 1):
        values = jnp.where((lane < rank) == (i == 0), packed, turned).astype(BF16)
        span = slice(i * half, (i + 1) * half)
        chosen = jnp.concatenate([values] * (len(factors) // 2), axis=1) * mask_ref[span, :]
        total = jnp.dot(chosen, factor, preferred_element_type=F32)
        adapted = total.astype(BF16).astype(F32)
        done[span, :] = ((near_ref[span, :] + far_ref[span, :]) + adapted).astype(BF16)
        copies.append(pltpu.make_async_copy(done.at[span], out_ref.at[span], sems.at[i]))
        copies[-1].start()
    for copy in copies:
        copy.wait()


def per_device(hidden, demand, lengths, holder_slot, value_weight, factor_in, factor_out):
    rows, features = hidden.shape
    owners = lax.axis_size("batch")
    rank, width = factor_out.shape[1:]
    depth = features // 2
    order = ring_order(owners)
    forward = [(order[i], order[(i + 1) % owners]) for i in range(owners)]
    backward = [(b, a) for a, b in forward]
    swap = [(0, 1), (1, 0)]

    full = (owners - 1) // 2
    distances = [0]
    for step in range(1, full + 1):
        distances += [step, -step]
    distances.append(owners // 2)
    table = [
        [[order[(order.index(me) - distance) % owners] for distance in distances]]
        for me in range(owners)
    ]
    first, second, bounds = shard_call(
        factor_in[0].T, factor_out[0], demand, lengths, holder_slot, jnp.asarray(table, I32), depth
    )
    to_other, bounds = rows_call(hidden, bounds)
    bounds, first_later = lax.optimization_barrier((mark(bounds), first))

    firsts, seconds = [first], [second]
    ahead, behind = (first, second), (first_later, second)
    for step in range(1, full + 1):
        a = lax.ppermute(ahead[0], "batch", forward)
        d = lax.ppermute(behind[1], "batch", backward)
        b = lax.ppermute(ahead[1], "batch", forward)
        c = lax.ppermute(behind[0], "batch", backward)
        ahead, behind = (a, b), (c, d)
        firsts += [a, c]
        seconds += [b, d]
    firsts.append(lax.ppermute(ahead[0], "batch", forward))
    seconds.append(lax.ppermute(behind[1], "batch", backward))
    near, far, mask = base_call(hidden, value_weight, bounds, GROUP * rank)
    hidden, near, far = lax.optimization_barrier((hidden, near, far))
    other = lax.ppermute(to_other, "groups", swap)

    count = owners // GROUP
    early = range(count - 1)
    pieces = []
    for group in early:
        pieces += firsts[group * GROUP : (group + 1) * GROUP]
        pieces += seconds[group * GROUP : (group + 1) * GROUP]
    both = (hidden, other)
    start_mine, start_theirs = rank_call(
        (0, 1), tuple(early), depth, rows, both, bounds, pieces, ()
    )
    start_theirs, far = lax.optimization_barrier((start_theirs, far))
    far = lax.ppermute(far, "tensor", swap)
    pieces = firsts[-GROUP:] + seconds[-GROUP:]
    late = (count - 1,)
    (theirs,) = rank_call((1,), late, depth, rows, (other,), bounds, pieces, (start_theirs,))
    mine = rank_call((0,), late, depth, rows, (hidden,), bounds, pieces, (start_mine,))

    three = lax.ppermute(theirs, ("groups", "tensor"), [(0, 3), (1, 2), (2, 1), (3, 0)])
    two = lax.ppermute(theirs, "groups", swap)
    one = [lax.ppermute(part, "tensor", swap) for part in mine]

    operands = [mask, *mine, *one, three, two, near, far, *seconds]
    return pl.pallas_call(
        final_kernel,
        out_shape=jax.ShapeDtypeStruct((rows, width), BF16),
        in_specs=[VMEM] * len(operands),
        out_specs=HBM,
        scratch_shapes=[pltpu.VMEM((rows, width), BF16), pltpu.SemaphoreType.DMA((2,))],
        compiler_params=params(),
    )(*operands)


def solution(mesh):
    return jax.shard_map(
        per_device,
        mesh=mesh,
        in_specs=(
            P(("groups", "batch"), "tensor"),
            P(("groups", "batch"), None),
            P(("groups", "batch"), None),
            P(),
            P("tensor", None),
            P("batch", "tensor", None),
            P("batch", None, "tensor"),
        ),
        out_specs=P(("groups", "batch"), "tensor"),
        check_vma=False,
    )
```

```python
import functools

import jax
import jax.numpy as jnp
from jax import lax
from jax.experimental import pallas as pl
from jax.experimental.pallas import tpu as pltpu
from jax.sharding import PartitionSpec as P

F32, BF16, I32 = jnp.float32, jnp.bfloat16, jnp.int32
VMEM_LIMIT = 24 * 1024 * 1024
HALF = pl.CostEstimate(flops=0, bytes_accessed=1 << 22, transcendentals=0)
LONG = pl.CostEstimate(flops=1 << 33, bytes_accessed=1 << 24, transcendentals=0)
GROUP = 4
VMEM = pl.BlockSpec(memory_space=pltpu.VMEM)
HBM = pl.BlockSpec(memory_space=pltpu.HBM)


def in_hbm(array):
    return pltpu.with_memory_space_constraint(array, pltpu.HBM)


def params():
    return pltpu.CompilerParams(vmem_limit_bytes=VMEM_LIMIT)


def ring_order(size):
    if size % 4:
        return list(range(size))
    columns = size // 4
    order = [0]
    for row in range(4):
        across = range(1, columns) if row % 2 == 0 else range(columns - 1, 0, -1)
        order += [row * columns + column for column in across]
    return order + [row * columns for row in (3, 2, 1)]


def contract(left, right):
    return lax.dot_general(left, right, (((1,), (1,)), ((), ())), preferred_element_type=F32)


def extra_rows(columns):
    return 2 * -(-columns // 1024) * 8


def shard_kernel(
    depth,
    rank,
    factor_ref,
    factor_out_ref,
    demand_ref,
    lengths_ref,
    holder_ref,
    slots_ref,
    first_ref,
    second_ref,
    bounds_ref,
    demand,
    lengths,
    holder,
    slots,
    sems,
):
    group, place = lax.axis_index("groups"), lax.axis_index("batch")
    cut = first_ref.shape[1]
    here = pl.multiple_of(group * depth, 128)
    after = pl.multiple_of(group * depth + cut, 128)
    small = [
        pltpu.make_async_copy(demand_ref, demand, sems.at[0]),
        pltpu.make_async_copy(lengths_ref, lengths, sems.at[1]),
        pltpu.make_async_copy(holder_ref, holder, sems.at[2]),
        pltpu.make_async_copy(slots_ref.at[pl.ds(place, 1)], slots, sems.at[3]),
    ]
    large = [
        pltpu.make_async_copy(factor_ref.at[:, pl.ds(here, cut)], first_ref, sems.at[4]),
        pltpu.make_async_copy(
            factor_ref.at[:, pl.ds(after, depth - cut)], second_ref.at[:, : depth - cut], sems.at[5]
        ),
        pltpu.make_async_copy(factor_out_ref, second_ref.at[:, depth - cut :], sems.at[6]),
    ]
    for copy in small + large:
        copy.start()
    for copy in small:
        copy.wait()
    count = slots.shape[2]
    items = demand.shape[1]
    column = lax.broadcasted_iota(I32, (1, count * rank), 1)
    zero = jnp.int32(0)

    def chunk_mask(chunk):
        return (column >= chunk * rank) & (column < (chunk + 1) * rank)

    low = high = jnp.zeros((1, count * rank), I32)
    if items * count <= 64:
        start = zero
        spans = []
        for item in range(items):
            end = start + lengths[0, item]
            spans.append((holder[demand[0, item]], start, end))
            start = end
        for chunk in range(count):
            slot = slots[0, 0, chunk]
            begin = end = zero
            for owner, first, last in spans:
                begin = jnp.where(owner == slot, first, begin)
                end = jnp.where(owner == slot, last, end)
            low = jnp.where(chunk_mask(chunk), begin, low)
            high = jnp.where(chunk_mask(chunk), end, high)
    else:

        def chunk_ends(chunk, carry):
            low, high = carry
            slot = slots[0, 0, chunk]

            def item_ends(item, state):
                start, begin, end = state
                last = start + lengths[0, item]
                hit = holder[demand[0, item]] == slot
                return last, jnp.where(hit, start, begin), jnp.where(hit, last, end)

            _, begin, end = lax.fori_loop(0, items, item_ends, (zero, zero, zero))
            mask = chunk_mask(chunk)
            return jnp.where(mask, begin, low), jnp.where(mask, end, high)

        low, high = lax.fori_loop(0, count, chunk_ends, (low, high))
    bounds_ref[0:1, :] = low
    bounds_ref[1:2, :] = high
    bounds_ref[2:8, :] = jnp.zeros((6, count * rank), I32)
    for copy in large:
        copy.wait()


def shard_call(factor, factor_out, demand, lengths, holder_slot, slots, depth):
    rank, width = factor_out.shape
    cut = (depth + width) // 2
    count = slots.shape[2]
    return pl.pallas_call(
        functools.partial(shard_kernel, depth, rank),
        out_shape=(
            jax.ShapeDtypeStruct((rank, cut), factor.dtype),
            jax.ShapeDtypeStruct((rank, cut), factor.dtype),
            jax.ShapeDtypeStruct((8, count * rank), I32),
        ),
        in_specs=[HBM] * 6,
        out_specs=(VMEM,) * 3,
        scratch_shapes=[
            pltpu.SMEM(demand.shape, I32),
            pltpu.SMEM(lengths.shape, I32),
            pltpu.SMEM(holder_slot.shape, I32),
            pltpu.SMEM((1, 1, count), I32),
            pltpu.SemaphoreType.DMA((7,)),
        ],
        compiler_params=params(),
        cost_estimate=LONG,
    )(*map(in_hbm, (factor, factor_out, demand, lengths, holder_slot, slots)))


def rows_kernel(depth, hidden_ref, bounds_ref, to_other_ref, bounds_out_ref):
    rows = hidden_ref.shape[0]
    there = pl.multiple_of((1 - lax.axis_index("groups")) * depth, 128)
    for i in range(depth // 128):
        to_other_ref[i * rows : (i + 1) * rows, :] = hidden_ref[:, pl.ds(there + i * 128, 128)]
    columns = bounds_ref.shape[1]
    extra = extra_rows(columns)
    line = lax.broadcasted_iota(I32, (extra, 128), 0)
    ends = jnp.zeros((extra, 128), I32)
    for i in range(columns // 128):
        span = slice(i * 128, (i + 1) * 128)
        ends = jnp.where(line == i, bounds_ref[0:1, span], ends)
        ends = jnp.where(line == extra // 2 + i, bounds_ref[1:2, span], ends)
    to_other_ref[-extra:, :] = ends.astype(F32).astype(BF16)
    bounds_out_ref[...] = bounds_ref[...]


def rows_call(hidden, bounds):
    rows, features = hidden.shape
    depth = features // 2
    tall = depth // 128 * rows + extra_rows(bounds.shape[1])
    return pl.pallas_call(
        functools.partial(rows_kernel, depth),
        out_shape=(
            jax.ShapeDtypeStruct((tall, 128), hidden.dtype),
            jax.ShapeDtypeStruct(bounds.shape, I32),
        ),
        in_specs=[VMEM] * 2,
        out_specs=(VMEM,) * 2,
        compiler_params=params(),
        cost_estimate=LONG,
    )(hidden, bounds)


def mark_kernel(bounds_ref, out_ref):
    out_ref[...] = bounds_ref[...]


def mark(bounds):
    return pl.pallas_call(
        mark_kernel,
        out_shape=jax.ShapeDtypeStruct(bounds.shape, bounds.dtype),
        in_specs=[VMEM],
        out_specs=VMEM,
        compiler_params=params(),
        cost_estimate=LONG,
    )(bounds)


def base_kernel(size, rows_ref, weight_ref, bounds_ref, near_ref, far_ref, mask_ref):
    width = near_ref.shape[1]
    core = lax.axis_index("tensor")
    for out_ref, side in ((near_ref, core), (far_ref, 1 - core)):
        columns = pl.ds(pl.multiple_of(side * width, 128), width)
        out_ref[...] = jnp.dot(
            rows_ref[...], weight_ref[:, columns], preferred_element_type=F32
        )
    for group in range(mask_ref.shape[1] // size):
        mask = group_mask(*own_ends(bounds_ref, group, size), (rows_ref.shape[0], size))
        mask_ref[:, group * size : (group + 1) * size] = jnp.where(mask, 1.0, 0.0).astype(BF16)


def base_call(rows, weight, bounds, size):
    mask = jax.ShapeDtypeStruct((rows.shape[0], bounds.shape[1]), BF16)
    out = jax.ShapeDtypeStruct((rows.shape[0], weight.shape[1] // 2), F32)
    return pl.pallas_call(
        functools.partial(base_kernel, size),
        out_shape=(out, out, mask),
        in_specs=[VMEM] * 3,
        out_specs=(VMEM,) * 3,
        compiler_params=params(),
        cost_estimate=HALF,
    )(rows, weight, bounds)


def group_mask(low, high, shape):
    row = lax.broadcasted_iota(I32, shape, 0)
    return (row >= low) & (row < high)


def own_ends(bounds_ref, group, size):
    columns = slice(group * size, (group + 1) * size)
    return bounds_ref[0:1, columns], bounds_ref[1:2, columns]


def other_ends(other_ref, extra, group, size):
    ends = other_ref[-extra:, :].astype(F32).astype(I32)
    lines = range(group * size // 128, (group + 1) * size // 128)
    low = jnp.concatenate([ends[i : i + 1] for i in lines], axis=1)
    high = jnp.concatenate([ends[extra // 2 + i : extra // 2 + i + 1] for i in lines], axis=1)
    return low, high


def fold(masked):
    total = masked[:, :128]
    for begin in range(128, masked.shape[1], 128):
        total = total + masked[:, begin : begin + 128]
    return total


def rank_kernel(sides, groups, depth, last, *refs):
    refs = list(refs)
    rows_refs, refs = refs[: len(sides)], refs[len(sides) :]
    bounds_ref, pieces = refs[0], refs[1:]
    pieces, rest = pieces[: 2 * GROUP * len(groups)], pieces[2 * GROUP * len(groups) :]
    starts, outs = (rest[: len(sides)], rest[len(sides) :]) if last else ((), rest)
    cut = pieces[0].shape[1]
    rank = pieces[0].shape[0]
    size = GROUP * rank
    extra = extra_rows(bounds_ref.shape[1])
    rows = []
    for side, ref in zip(sides, rows_refs):
        if side == 0:
            offset = pl.multiple_of(lax.axis_index("groups") * depth, 128)
            rows.append(ref[:, pl.ds(offset, depth)])
        else:
            blocks = depth // 128
            tall = (ref.shape[0] - extra) // blocks
            rows.append(
                jnp.concatenate([ref[i * tall : (i + 1) * tall, :] for i in range(blocks)], axis=1)
            )
    count = rows[0].shape[0]
    rows = jnp.concatenate(rows, axis=0)
    totals = [ref[...] for ref in starts] if last else [None] * len(sides)
    for i, group in enumerate(groups):
        held = pieces[2 * GROUP * i : 2 * GROUP * (i + 1)]
        first = jnp.concatenate([ref[...] for ref in held[:GROUP]], axis=0)
        second = jnp.concatenate([ref[:, : depth - cut] for ref in held[GROUP:]], axis=0)
        part = contract(rows, jnp.concatenate([first, second], axis=1))
        for s, side in enumerate(sides):
            if side == 0:
                ends = own_ends(bounds_ref, group, size)
            else:
                ends = other_ends(rows_refs[s], extra, group, size)
            here = part[s * count : (s + 1) * count]
            kept = fold(jnp.where(group_mask(*ends, here.shape), here, 0.0))
            totals[s] = kept if totals[s] is None else totals[s] + kept
    if last:
        (total,) = totals
        total = total + pltpu.roll(total, rank, 1)
        half = count // 2
        lane = lax.broadcasted_iota(I32, (half, 2 * rank), 1)
        total = jnp.where(lane < rank, total[:half], total[half:])
        size = outs[0].shape[0]
        totals = [total[i * size : (i + 1) * size] for i in range(len(outs))]
    for total, out_ref in zip(totals, outs):
        out_ref[...] = total.astype(out_ref.dtype)


def rank_call(sides, groups, depth, count, rows, bounds, pieces, starts):
    rank = pieces[0].shape[0]
    last = len(starts) > 0
    if not last:
        out = (jax.ShapeDtypeStruct((count, 2 * rank), F32),) * len(sides)
    elif sides == (1,):
        out = (jax.ShapeDtypeStruct((count // 2, 2 * rank), BF16),)
    else:
        out = (jax.ShapeDtypeStruct((count // 4, 2 * rank), F32),) * 2
    operands = [*rows, bounds, *pieces, *starts]
    return pl.pallas_call(
        functools.partial(rank_kernel, sides, groups, depth, last),
        out_shape=out,
        in_specs=[VMEM] * len(operands),
        out_specs=(VMEM,) * len(out),
        compiler_params=params(),
        cost_estimate=HALF if last and sides == (0,) else LONG,
    )(*operands)


def final_kernel(mask_ref, top, low, one_top, one_low, two, three, near_ref, far_ref, *refs):
    factors, (out_ref, done, sems) = refs[:-3], refs[-3:]
    rank, width = factors[0].shape[0], out_ref.shape[1]
    begin = factors[0].shape[1] - width
    here = jnp.concatenate([top[...] + one_top[...], low[...] + one_low[...]], axis=0)
    packed = here + (two[...].astype(F32) + three[...].astype(F32))
    turned = pltpu.roll(packed, rank, 1)
    lane = lax.broadcasted_iota(I32, packed.shape, 1)
    factor = jnp.concatenate([ref[:, begin:] for ref in factors], axis=0)
    half = packed.shape[0]
    copies = []
    for i in (0, 1):
        values = jnp.where((lane < rank) == (i == 0), packed, turned).astype(BF16)
        span = slice(i * half, (i + 1) * half)
        chosen = jnp.concatenate([values] * (len(factors) // 2), axis=1) * mask_ref[span, :]
        total = jnp.dot(chosen, factor, preferred_element_type=F32)
        adapted = total.astype(BF16).astype(F32)
        done[span, :] = ((near_ref[span, :] + far_ref[span, :]) + adapted).astype(BF16)
        copies.append(pltpu.make_async_copy(done.at[span], out_ref.at[span], sems.at[i]))
        copies[-1].start()
    for copy in copies:
        copy.wait()


def per_device(hidden, demand, lengths, holder_slot, value_weight, factor_in, factor_out):
    rows, features = hidden.shape
    owners = lax.axis_size("batch")
    rank, width = factor_out.shape[1:]
    depth = features // 2
    order = ring_order(owners)
    forward = [(order[i], order[(i + 1) % owners]) for i in range(owners)]
    backward = [(b, a) for a, b in forward]
    swap = [(0, 1), (1, 0)]

    full = (owners - 1) // 2
    distances = [0]
    for step in range(1, full + 1):
        distances += [step, -step]
    distances.append(owners // 2)
    table = [
        [[order[(order.index(me) - distance) % owners] for distance in distances]]
        for me in range(owners)
    ]
    first, second, bounds = shard_call(
        factor_in[0].T, factor_out[0], demand, lengths, holder_slot, jnp.asarray(table, I32), depth
    )
    to_other, bounds = rows_call(hidden, bounds)
    bounds, first_later = lax.optimization_barrier((mark(bounds), first))

    firsts, seconds = [first], [second]
    ahead, behind = (first, second), (first_later, second)
    for step in range(1, full + 1):
        a = lax.ppermute(ahead[0], "batch", forward)
        d = lax.ppermute(behind[1], "batch", backward)
        b = lax.ppermute(ahead[1], "batch", forward)
        c = lax.ppermute(behind[0], "batch", backward)
        ahead, behind = (a, b), (c, d)
        firsts += [a, c]
        seconds += [b, d]
    firsts.append(lax.ppermute(ahead[0], "batch", forward))
    seconds.append(lax.ppermute(behind[1], "batch", backward))
    near, far, mask = base_call(hidden, value_weight, bounds, GROUP * rank)
    hidden, near, far = lax.optimization_barrier((hidden, near, far))
    other = lax.ppermute(to_other, "groups", swap)

    count = owners // GROUP
    early = range(count - 1)
    pieces = []
    for group in early:
        pieces += firsts[group * GROUP : (group + 1) * GROUP]
        pieces += seconds[group * GROUP : (group + 1) * GROUP]
    both = (hidden, other)
    start_mine, start_theirs = rank_call(
        (0, 1), tuple(early), depth, rows, both, bounds, pieces, ()
    )
    start_theirs, far = lax.optimization_barrier((start_theirs, far))
    far = lax.ppermute(far, "tensor", swap)
    pieces = firsts[-GROUP:] + seconds[-GROUP:]
    late = (count - 1,)
    (theirs,) = rank_call((1,), late, depth, rows, (other,), bounds, pieces, (start_theirs,))
    mine = rank_call((0,), late, depth, rows, (hidden,), bounds, pieces, (start_mine,))

    three = lax.ppermute(theirs, ("groups", "tensor"), [(0, 3), (1, 2), (2, 1), (3, 0)])
    two = lax.ppermute(theirs, "groups", swap)
    one = [lax.ppermute(part, "tensor", swap) for part in mine]

    operands = [mask, *mine, *one, two, three, near, far, *seconds]
    return pl.pallas_call(
        final_kernel,
        out_shape=jax.ShapeDtypeStruct((rows, width), BF16),
        in_specs=[VMEM] * len(operands),
        out_specs=HBM,
        scratch_shapes=[pltpu.VMEM((rows, width), BF16), pltpu.SemaphoreType.DMA((2,))],
        compiler_params=params(),
    )(*operands)


def solution(mesh):
    return jax.shard_map(
        per_device,
        mesh=mesh,
        in_specs=(
            P(("groups", "batch"), "tensor"),
            P(("groups", "batch"), None),
            P(("groups", "batch"), None),
            P(),
            P("tensor", None),
            P("batch", "tensor", None),
            P("batch", None, "tensor"),
        ),
        out_specs=P(("groups", "batch"), "tensor"),
        check_vma=False,
    )
```
